32 devices in a mesh: hours: 16 (over z, x, core), region: 2 (over y).
Axes of the slice: x: 2, y: 2, z: 4, core: 2. Of those that a mesh axis runs over, the one named last changes fastest.
Arguments:
- availability: float32 [1024, 16, 256], P('hours', None, 'region'), may hold values from 0.1 to 1
- demand: float32 [1024, 256], P('hours', 'region'), may hold values from 2 to 72, as said below
- gen_cost: float32 [16, 256], P(None, 'region'), may hold values from 0.05 to 1
- cap_cost: float32 [2, 2048], P('region', 'hours'), may hold values from 51.2 to 512
- owner_map: int32 [2, 2048], P('region'), may hold values from 0 to 2047, each once within a row
- line_ends: int32 [2, 512], P(None, 'region'), may hold values from 0 to 127
- line_limit: float32 [512], P('region'), may hold values from 0.5 to 4
- cross_ends: int32 [2, 2, 64], P(None, 'region'), may hold values from 0 to 127
- cross_limit: float32 [2, 64], P('region'), may hold values from 0.5 to 4
- pair_counts: int32 [2, 2], P('region'), may hold values from 0 to 32, as said below
- store_node: int32 [512], P('region'), may hold values from 0 to 127
- store_energy: float32 [512], P('region'), may hold values from 0.02 to 0.4
- store_power: float32 [512], P('region'), may hold values from 0.2 to 2
- price_start: float32 [1024, 256], P('hours', 'region'), may hold values from -3 to 0.5
Outputs:
- dispatch: float32 [1024, 16, 256], P('hours', None, 'region')
- capacity: float32 [2, 2048], P('region', 'hours')
- prices: float32 [1024, 256], P('hours', 'region')
- charge_state: float32 [1024, 512], P('hours', 'region')
The draws below stay inside these ranges and needn't reach their ends.
Inputs may be any that keep to these rules, and one draw needn't show every extreme that they name: `demand`: loads are positive. `owner_map`: each row lists every capacity column of its region once. `pair_counts`: cross lines in use among the 32 slots of each ordered pair of regions; a region has none to itself; some pair uses all 32.
All inputs are finite; a program needn't handle non-finite values.
Results may differ from the reference program's by a relative error of at most 0.00018.
Values sent between devices are 32-bit elements; how exact they have to be, the bound alone decides.
No kernel may reach another device: no remote copies, remote signals or barrier semaphores. Data moves between devices by JAX's collectives and lax.ppermute only.
A program may use at most 64 MiB of HBM per device.

```python
import math
import jax
import jax.numpy as jnp
from jax import lax

K = 16
NODE_DEV = 128
LIN_DEV = 256
XW = 32
S_DEV = 256
ITERS = 4
HOURS = 1024
NODES = 256
LINES = 512
SLOTS = 64
STORES = 512
COLS = 2048
N_REGION = 2


def draw_demand(key, part):
    first_key = jax.random.fold_in(jax.random.fold_in(key, 11), 0)
    hour_ramp = 1.0 + 2.0 * jnp.arange(HOURS, dtype=jnp.float32)[:, None] / (HOURS - 1)
    base_load = jax.random.uniform(first_key, (HOURS, NODES), jnp.float32, 4.0, 12.0)
    return (base_load * hour_ramp).astype(jnp.float32)


def draw_pair_counts(key, part):
    first_key, second_key = jax.random.split(jax.random.fold_in(key, 23))
    counts = jax.random.randint(first_key, (N_REGION, N_REGION), 1, XW + 1)
    chosen = jax.random.randint(second_key, (), 0, N_REGION * (N_REGION - 1))
    source = chosen // (N_REGION - 1)
    offset = chosen % (N_REGION - 1)
    target = offset + (offset >= source).astype(jnp.int32)
    counts = counts.at[source, target].set(XW)
    labels = jnp.arange(N_REGION, dtype=jnp.int32)
    counts = jnp.where(labels[:, None] == labels[None, :], 0, counts)
    return counts.astype(jnp.int32)


def set_ends(array, own_key, low, high):
    place = [jax.random.randint(jax.random.fold_in(own_key, axis), (), 0, length) for axis, length in enumerate(array.shape)]
    longest = array.shape.index(max(array.shape))
    next_to = place[:longest] + [(place[longest] + 1) % array.shape[longest]] + place[longest + 1:]
    return array.at[tuple(place)].set(low).at[tuple(next_to)].set(high)


def block_levels(stream_key, shape, shards, least, largest):
    loudness, own = 1.0, jax.random.fold_in(stream_key, 6)
    for dim, shards_of in shards:
        draws = jnp.exp(jax.random.uniform(jax.random.fold_in(own, dim), (shards_of,), jnp.float32, least / len(shards), largest / len(shards)))
        loudness = loudness * jnp.repeat(draws, shape[dim] // shards_of).reshape([-1 if axis == dim else 1 for axis in range(len(shape))])
    return loudness


def setup_inputs(seed: int = 0) -> dict:
    streams_of = jax.random.split(jax.random.key(seed), 15)
    availability = jnp.clip(0.1 + 0.9 * jax.random.uniform(streams_of[0], (HOURS, K, NODES), jnp.float32) ** block_levels(streams_of[0], (HOURS, K, NODES), ((0, 16), (2, 2)), -0.2, 0.2), 0.1, 1.0)
    demand = draw_demand(jax.random.fold_in(streams_of[14], 71), 0)
    gen_cost = jnp.clip(jnp.exp(math.log(1.0) - 2.9957323 * jax.random.uniform(streams_of[2], (K, NODES), jnp.float32) ** block_levels(streams_of[2], (K, NODES), ((1, 2),), -0.2, 0.2)), 0.05, 1.0)
    cap_cost = jnp.clip(jnp.exp(math.log(512.0) - 2.3025851 * jax.random.uniform(streams_of[3], (N_REGION, COLS), jnp.float32) ** block_levels(streams_of[3], (N_REGION, COLS), ((0, 2), (1, 16)), -0.2, 0.2)), 51.2, 512.0)
    owner_map = jax.vmap(lambda own: jax.random.permutation(own, COLS))(jax.random.split(streams_of[4], N_REGION)).reshape((N_REGION, COLS)).astype(jnp.int32)
    line_ends = set_ends(jax.random.randint(streams_of[5], (2, LINES), 0, NODE_DEV), jax.random.fold_in(streams_of[5], 1), 0, NODE_DEV - 1).astype(jnp.int32)
    line_limit = jnp.clip(jnp.exp(math.log(4.0) - 2.0794415 * jax.random.uniform(streams_of[6], (LINES,), jnp.float32) ** block_levels(streams_of[6], (LINES,), ((0, 2),), -0.2, 0.2)), 0.5, 4.0)
    cross_ends = set_ends(jax.random.randint(streams_of[7], (2, N_REGION, SLOTS), 0, NODE_DEV), jax.random.fold_in(streams_of[7], 1), 0, NODE_DEV - 1).astype(jnp.int32)
    cross_limit = jnp.clip(jnp.exp(math.log(4.0) - 2.0794415 * jax.random.uniform(streams_of[8], (N_REGION, SLOTS), jnp.float32) ** block_levels(streams_of[8], (N_REGION, SLOTS), ((0, 2),), -0.2, 0.2)), 0.5, 4.0)
    pair_counts = draw_pair_counts(jax.random.fold_in(streams_of[14], 71), 0)
    store_node = set_ends(jax.random.randint(streams_of[10], (STORES,), 0, NODE_DEV), jax.random.fold_in(streams_of[10], 1), 0, NODE_DEV - 1).astype(jnp.int32)
    store_energy = jnp.clip(jnp.exp(math.log(0.4) - 2.9957323 * jax.random.uniform(streams_of[11], (STORES,), jnp.float32) ** block_levels(streams_of[11], (STORES,), ((0, 2),), -0.2, 0.2)), 0.02, 0.4)
    store_power = jnp.clip(jnp.exp(math.log(2.0) - 2.3025851 * jax.random.uniform(streams_of[12], (STORES,), jnp.float32) ** block_levels(streams_of[12], (STORES,), ((0, 2),), -0.2, 0.2)), 0.2, 2.0)
    price_start = jnp.clip(-3.0 + 3.5 * jax.random.uniform(streams_of[13], (HOURS, NODES), jnp.float32) ** block_levels(streams_of[13], (HOURS, NODES), ((0, 16), (1, 2)), -0.2, 0.2), -3.0, 0.5)
    return dict(availability=availability, demand=demand, gen_cost=gen_cost, cap_cost=cap_cost, owner_map=owner_map, line_ends=line_ends, line_limit=line_limit, cross_ends=cross_ends, cross_limit=cross_limit, pair_counts=pair_counts, store_node=store_node, store_energy=store_energy, store_power=store_power, price_start=price_start)


epsilon = 1e-06

def reference(availability, demand, gen_cost, cap_cost, owner_map, line_ends, line_limit, cross_ends, cross_limit, pair_counts, store_node, store_energy, store_power, price_start):
    region_base = jnp.arange(N_REGION, dtype=jnp.int32) * NODE_DEV
    line_region = jnp.arange(LINES, dtype=jnp.int32) // LIN_DEV
    line_from = region_base[line_region] + line_ends[0]
    line_to = region_base[line_region] + line_ends[1]
    slot_ids = jnp.arange(SLOTS, dtype=jnp.int32)
    slot_dest = slot_ids // XW
    cross_from = (region_base[:, None] + cross_ends[0]).reshape(-1)
    cross_to = (region_base[slot_dest][None, :] + cross_ends[1]).reshape(-1)
    slot_used = (slot_ids % XW)[None, :] < pair_counts[:, slot_dest]
    cross_bound = jnp.where(slot_used, cross_limit, 0.0).reshape(-1)
    store_at = region_base[jnp.arange(STORES, dtype=jnp.int32) // S_DEV] + store_node
    region_rows = jnp.arange(N_REGION, dtype=jnp.int32)[:, None]

    def to_dense(owned_values):
        flat_cols = jnp.zeros((N_REGION, COLS), owned_values.dtype).at[region_rows, owner_map].set(owned_values)
        return flat_cols.reshape(N_REGION, K, NODE_DEV).transpose(1, 0, 2).reshape(K, NODES)

    def to_owner(dense_values):
        region_cols = dense_values.reshape(K, N_REGION, NODE_DEV).transpose(1, 0, 2).reshape(N_REGION, COLS)
        return jnp.take_along_axis(region_cols, owner_map, axis=1)
    col_weight = to_owner(lax.optimization_barrier(jnp.sum(availability, axis=0)))
    dispatch = jnp.zeros((HOURS, K, NODES), jnp.float32)
    capacity = jnp.zeros((N_REGION, COLS), jnp.float32)
    inner_flow = jnp.zeros((HOURS, LINES), jnp.float32)
    cross_flow = jnp.zeros((HOURS, N_REGION * SLOTS), jnp.float32)
    discharge = jnp.zeros((HOURS, STORES), jnp.float32)
    charge = jnp.zeros((HOURS, STORES), jnp.float32)
    prices = price_start
    cap_duals = jnp.zeros((HOURS, K, NODES), jnp.float32)
    store_duals = jnp.zeros((HOURS, STORES), jnp.float32)
    weight = jnp.float32(1.0)
    for iteration in range(ITERS):
        primal_step = 0.5 / weight
        dispatch_new = jnp.maximum(dispatch - primal_step * (gen_cost[None] + prices[:, None, :] + cap_duals), 0.0)
        cap_pull = to_owner(lax.optimization_barrier(jnp.sum(availability * cap_duals, axis=0)))
        capacity_new = jnp.maximum(capacity - (cap_cost - cap_pull) / (weight * col_weight), 0.0)
        inner_new = jnp.clip(inner_flow - primal_step * (prices[:, line_to] - prices[:, line_from]), -line_limit, line_limit)
        cross_new = jnp.clip(cross_flow - primal_step * (prices[:, cross_to] - prices[:, cross_from]), -cross_bound, cross_bound)
        discharge_new = jnp.clip(discharge - primal_step * (prices[:, store_at] + store_duals), -store_power, store_power)
        charge_new = jnp.clip(charge - primal_step * (store_duals - jnp.roll(store_duals, -1, axis=0)), 0.0, store_energy)
        dispatch_bar = 2.0 * dispatch_new - dispatch
        capacity_bar = 2.0 * capacity_new - capacity
        inner_bar = 2.0 * inner_new - inner_flow
        cross_bar = 2.0 * cross_new - cross_flow
        discharge_bar = 2.0 * discharge_new - discharge
        charge_bar = 2.0 * charge_new - charge
        balance = lax.optimization_barrier(jnp.sum(dispatch_bar, axis=1))
        balance = balance.at[:, line_to].add(inner_bar).at[:, line_from].add(-inner_bar)
        balance = balance.at[:, cross_to].add(cross_bar).at[:, cross_from].add(-cross_bar)
        balance = balance.at[:, store_at].add(discharge_bar)
        balance = balance - demand
        cap_rows = dispatch_bar - availability * to_dense(capacity_bar)[None]
        storage_rows = charge_bar - jnp.roll(charge_bar, 1, axis=0) + discharge_bar
        prices_new = prices + weight / (K + 8.0) * balance
        cap_new = jnp.maximum(cap_duals + weight / 2.0 * cap_rows, 0.0)
        store_new = store_duals + weight / 3.0 * storage_rows
        if iteration < ITERS - 1:
            primal_sq = jnp.sum((dispatch_new - dispatch) ** 2) + jnp.sum((capacity_new - capacity) ** 2) + jnp.sum((inner_new - inner_flow) ** 2) + jnp.sum((cross_new - cross_flow) ** 2) + jnp.sum((discharge_new - discharge) ** 2) + jnp.sum((charge_new - charge) ** 2)
            dual_sq = jnp.sum((prices_new - prices) ** 2) + jnp.sum((cap_new - cap_duals) ** 2) + jnp.sum((store_new - store_duals) ** 2)
            weight = jnp.sqrt(weight * jnp.sqrt((dual_sq + epsilon) / (primal_sq + epsilon)))
        dispatch, capacity, inner_flow, cross_flow = (dispatch_new, capacity_new, inner_new, cross_new)
        discharge, charge = (discharge_new, charge_new)
        prices, cap_duals, store_duals = (prices_new, cap_new, store_new)
    return (dispatch, capacity, prices, charge)
```

```python
import functools

import jax
import jax.numpy as jnp
from jax import lax
from jax.experimental import pallas as pl
from jax.experimental.pallas import tpu as pltpu
from jax.sharding import PartitionSpec as P

ITERS = 4
EPSILON = 1e-06
LANES = 128
VMEM_BYTES = 24 * 1024 * 1024


def round_up(value, multiple):
    return (value + multiple - 1) // multiple * multiple


def split3(value):
    high = value.astype(jnp.bfloat16)
    rest = value - high.astype(jnp.float32)
    middle = rest.astype(jnp.bfloat16)
    low = (rest - middle.astype(jnp.float32)).astype(jnp.bfloat16)
    return jnp.concatenate([high, middle, low], axis=0)


def dot3(value, matrix, transposed):
    rows = value.shape[0]
    contract = ((1,), (1 if transposed else 0,))
    product = lax.dot_general(
        split3(value), matrix, (contract, ((), ())), preferred_element_type=jnp.float32
    )
    return product[:rows] + product[rows : 2 * rows] + product[2 * rows :]


def row_sum(value):
    return jnp.sum(value, axis=0, keepdims=True)


def fold_lanes(row):
    total = row[:, :LANES]
    for start in range(LANES, row.shape[1], LANES):
        total = total + row[:, start : start + LANES]
    return total


def owned_one_hots(owner_ref, tech_count, node_count):
    owned = owner_ref[pl.ds(lax.axis_index("hours"), 1), :]
    shape_t = (tech_count, owned.shape[1])
    shape_n = (node_count, owned.shape[1])
    tech = lax.broadcasted_iota(jnp.int32, shape_t, 0) == owned // node_count
    node = lax.broadcasted_iota(jnp.int32, shape_n, 0) == owned % node_count
    return tech, node.astype(jnp.float32).astype(jnp.bfloat16)


def setup_kernel(
    sizes,
    avail_ref,
    price_ref,
    cost_ref,
    owner_ref,
    ends_ref,
    limit_ref,
    pairs_ref,
    avail_t_ref,
    sums_ref,
    region_ref,
):
    hours, regions, rows, techs, nodes, slots = sizes
    width = slots // regions
    own = lax.axis_index("region")
    total = jnp.zeros((techs, nodes), jnp.float32)
    for hour in range(rows):
        total = total + avail_ref[hour * techs : (hour + 1) * techs, :]
    for tech in range(techs):
        avail_t_ref[tech] = avail_ref[pl.ds(tech, rows, stride=techs), :]
    tech_hot, node_hot = owned_one_hots(owner_ref, techs, nodes)
    costs = jnp.where(tech_hot, cost_ref[...], 0.0)
    sums_ref[:techs, :] = total
    sums_ref[techs : 2 * techs, :] = dot3(costs, node_hot, True)
    slot = lax.broadcasted_iota(jnp.int32, (1, slots), 1)
    pair = slot // width
    in_use = jnp.zeros((1, slots), jnp.int32)
    for target in range(regions):
        in_use = jnp.where(pair == target, pairs_ref[0, target], in_use)
    bound = jnp.where(slot % width < in_use, limit_ref[...], 0.0)
    start = ends_ref[0:1, :] + own * nodes
    end = ends_ref[1:2, :] + pair * nodes
    info = jnp.concatenate(
        [start.astype(jnp.float32), end.astype(jnp.float32), bound, jnp.zeros((13, slots), jnp.float32)],
        axis=0,
    )
    place = lax.broadcasted_iota(jnp.int32, (slots, regions * slots), 1) == (
        own * slots + lax.broadcasted_iota(jnp.int32, (slots, regions * slots), 0)
    )
    info = dot3(info, place.astype(jnp.float32).astype(jnp.bfloat16), False)
    region_ref[:rows, :] = price_ref[...]
    for chunk in range(regions * slots // LANES):
        region_ref[rows + 8 * chunk : rows + 8 * chunk + 8, :] = info[
            :8, chunk * LANES : (chunk + 1) * LANES
        ]


def sweep_kernel(sizes, iteration, names_in, names_out, *refs):
    hours, regions, rows, techs, nodes, slots = sizes
    first = iteration == 0
    last = iteration == ITERS - 1
    given = dict(zip(names_in, refs[: len(names_in)]))
    gives = dict(zip(names_out, refs[len(names_in) :]))
    own = lax.axis_index("region")
    hour_index = lax.axis_index("hours")
    received, gathered = given["received"], given["gathered"]

    sums = received[0]
    for sender in range(1, hours):
        sums = sums + received[sender]
    if first:
        weight = jnp.ones((1, 1), jnp.float32)
        col_weight, cost = sums[:techs], sums[techs : 2 * techs]
        gives["col_weight"][...] = col_weight
        gives["cost"][...] = cost
        chunks = []
        for chunk in range(regions * slots // LANES):
            part = gathered[0, rows + 8 * chunk : rows + 8 * chunk + 8, :]
            for region in range(1, regions):
                part = part + gathered[region, rows + 8 * chunk : rows + 8 * chunk + 8, :]
            chunks.append(part)
        info = jnp.concatenate(chunks, axis=1) if len(chunks) > 1 else chunks[0]
        base = own * nodes
        line_ends, stores = given["line_ends"][...], given["store_node"][...]
        start = jnp.concatenate(
            [line_ends[0:1] + base, jnp.full_like(stores, -1), info[0:1].astype(jnp.int32)], axis=1
        )
        end = jnp.concatenate(
            [line_ends[1:2] + base, stores + base, info[1:2].astype(jnp.int32)], axis=1
        )
        limits = jnp.concatenate(
            [given["line_limit"][...], given["store_power"][...], info[2:3]], axis=1
        )
        node = lax.broadcasted_iota(jnp.int32, (regions * nodes, start.shape[1]), 0)
        maps = (node == end).astype(jnp.float32) - (node == start).astype(jnp.float32)
        gives["maps"][...] = maps.astype(jnp.bfloat16)
        gives["limits"][...] = limits
        maps_ref = gives["maps"]
    else:
        maps_ref = given["maps"]
        limits = given["limits"][...]
        col_weight, cost = given["col_weight"][...], given["cost"][...]
        squares = jnp.sum(sums[techs : techs + 2], axis=1, keepdims=True)
        weight = given["weight"][...][:, :1]
        weight = jnp.sqrt(
            weight * jnp.sqrt((squares[1:2] + EPSILON) / (squares[0:1] + EPSILON))
        )
    primal_step = 0.5 / weight
    lines = sizes_lines(maps_ref, regions, slots, given["store_energy"].shape[1])
    units = given["store_energy"].shape[1]
    energy = given["store_energy"][...]

    prices_all = jnp.concatenate([gathered[region, :rows, :] for region in range(regions)], axis=1)
    prices = gathered[own, :rows, :]
    difference = dot3(prices_all, maps_ref[...], False)

    if first:
        capacity_new = jnp.maximum(-cost / (weight * col_weight), 0.0)
        capacity_bar = 2.0 * capacity_new
        capacity_change = capacity_new
    else:
        capacity = given["capacity"][...]
        capacity_new = jnp.maximum(
            capacity - (cost - sums[:techs]) / (weight * col_weight), 0.0
        )
        capacity_bar = 2.0 * capacity_new - capacity
        capacity_change = capacity_new - capacity

    row_id = lax.broadcasted_iota(jnp.int32, (rows, units), 0)
    if not first:
        before = lax.rem(hour_index + hours - 1, hours)
        after = lax.rem(hour_index + 1, hours)
        halo = techs + 2
        span = units // LANES
        next_row = jnp.concatenate(
            [received[after, halo + i : halo + i + 1, :] for i in range(span)], axis=1
        )
        prev_row = jnp.concatenate(
            [received[before, halo + span + i : halo + span + i + 1, :] for i in range(span)],
            axis=1,
        )
        store_duals = given["store_duals"][...]
        next_duals = jnp.where(row_id == rows - 1, next_row, pltpu.roll(store_duals, rows - 1, 0))
        if iteration == 1:
            charge = jnp.zeros((rows, units), jnp.float32)
            charge_before = jnp.zeros((1, units), jnp.float32)
        else:
            charge = given["charge"][...]
            charge_before = given["charge_before"][...]
        charge_new = jnp.clip(charge - primal_step * (store_duals - next_duals), 0.0, energy)
        gives["charge"][...] = charge_new

    flows_new, flows_bar = [], []
    primal_row = jnp.zeros((1, LANES), jnp.float32)
    total_flows = limits.shape[1]
    for low, high in ((0, lines), (lines, lines + units), (lines + units, total_flows)):
        slope = difference[:, low:high]
        if low == lines and not first:
            slope = slope + store_duals
        bound = limits[:, low:high]
        old = None if first else given["flows"][:, low:high]
        moved = -primal_step * slope if first else old - primal_step * slope
        new = jnp.clip(moved, -bound, bound)
        flows_new.append(new)
        flows_bar.append(2.0 * new if first else 2.0 * new - old)
        if not last:
            gives["flows"][:, low:high] = new
            change = row_sum((new if first else new - old) ** 2)
            if low == lines + units:
                slot = lax.broadcasted_iota(jnp.int32, change.shape, 1)
                change = jnp.where(slot // slots == own, change, 0.0)
            primal_row = primal_row + fold_lanes(change)
    maps_own = maps_ref[pl.ds(pl.multiple_of(own * nodes, nodes), nodes), :]
    balance = dot3(jnp.concatenate(flows_bar, axis=1), maps_own, True) - given["demand"][...]

    gen_cost = given["gen_cost"][...]
    half_weight = weight / 2.0
    primal_acc = jnp.zeros((rows, nodes), jnp.float32)
    dual_acc = jnp.zeros((rows, nodes), jnp.float32)
    for tech in range(techs):
        slope = gen_cost[tech : tech + 1] + prices
        if first:
            dispatch_new = jnp.maximum(-primal_step * slope, 0.0)
            dispatch_bar = 2.0 * dispatch_new
        else:
            duals = given["cap_duals"][tech]
            dispatch = given["dispatch"][tech]
            dispatch_new = jnp.maximum(dispatch - primal_step * (slope + duals), 0.0)
            dispatch_bar = 2.0 * dispatch_new - dispatch
        balance = balance + dispatch_bar
        if last:
            gives["dispatch"][pl.ds(tech, rows, stride=techs), :] = dispatch_new
            continue
        gives["dispatch"][tech] = dispatch_new
        avail = given["availability"][tech]
        cap_rows = dispatch_bar - avail * capacity_bar[tech : tech + 1]
        if first:
            primal_acc = primal_acc + dispatch_new * dispatch_new
            duals_new = jnp.maximum(half_weight * cap_rows, 0.0)
            dual_acc = dual_acc + duals_new * duals_new
        else:
            primal_acc = primal_acc + (dispatch_new - dispatch) ** 2
            duals_new = jnp.maximum(duals + half_weight * cap_rows, 0.0)
            dual_acc = dual_acc + (duals_new - duals) ** 2
        gives["cap_duals"][tech] = duals_new
        gives["sums"][tech : tech + 1, :] = row_sum(avail * duals_new)

    step_up = weight / (techs + 8.0) * balance
    if last:
        gives["prices"][...] = prices + step_up
        tech_hot, node_hot = owned_one_hots(given["owner"], techs, nodes)
        chosen = dot3(capacity_new, node_hot, False)
        gives["capacity"][...] = row_sum(jnp.where(tech_hot, chosen, 0.0))
        return
    gives["region"][:rows, :] = prices + step_up
    gives["weight"][...] = jnp.broadcast_to(weight, (1, LANES))
    gives["capacity"][...] = capacity_new
    dual_row = row_sum(dual_acc + step_up * step_up)
    primal_row = primal_row + row_sum(primal_acc)
    primal_row = primal_row + jnp.where(hour_index == 0, row_sum(capacity_change**2), 0.0)

    discharge_bar = flows_bar[1]
    if first:
        store_step = weight / 3.0 * discharge_bar
        store_new = store_step
    else:
        charge_bar = 2.0 * charge_new - charge
        before_new = jnp.clip(
            charge_before - primal_step * (prev_row - store_duals[0:1]), 0.0, energy
        )
        gives["charge_before"][...] = before_new
        before_bar = 2.0 * before_new - charge_before
        shifted = jnp.where(row_id == 0, before_bar, pltpu.roll(charge_bar, 1, 0))
        store_step = weight / 3.0 * (charge_bar - shifted + discharge_bar)
        store_new = store_duals + store_step
        primal_row = primal_row + fold_lanes(row_sum((charge_new - charge) ** 2))
    gives["store_duals"][...] = store_new
    dual_row = dual_row + fold_lanes(row_sum(store_step * store_step))
    gives["region"][rows : rows + 8, :] = jnp.concatenate(
        [primal_row, dual_row, jnp.zeros((6, LANES), jnp.float32)], axis=0
    )
    halo = techs + 2
    span = units // LANES
    gives["sums"][techs:halo, :] = jnp.concatenate([primal_row, dual_row], axis=0)
    for i in range(span):
        gives["sums"][halo + i : halo + i + 1, :] = store_new[:1, i * LANES : (i + 1) * LANES]
        gives["sums"][halo + span + i : halo + span + i + 1, :] = store_new[
            rows - 1 :, i * LANES : (i + 1) * LANES
        ]
    for row in range(halo + 2 * span, gives["sums"].shape[0]):
        gives["sums"][row : row + 1, :] = jnp.zeros((1, LANES), jnp.float32)


def sizes_lines(maps_ref, regions, slots, units):
    return maps_ref.shape[1] - units - regions * slots


def call(kernel, arguments, shapes, in_smem=()):
    return pl.pallas_call(
        kernel,
        out_shape=shapes,
        in_specs=[
            pl.BlockSpec(memory_space=pltpu.SMEM if i in in_smem else pltpu.VMEM)
            for i in range(len(arguments))
        ],
        out_specs=[pl.BlockSpec(memory_space=pltpu.VMEM)] * len(shapes),
        compiler_params=pltpu.CompilerParams(vmem_limit_bytes=VMEM_BYTES),
    )(*arguments)


def to_all_hours(message):
    count = lax.axis_size("hours")
    copies = jnp.broadcast_to(message[None], (count, *message.shape))
    return lax.all_to_all(copies, "hours", split_axis=0, concat_axis=0)


def body(
    availability,
    demand,
    gen_cost,
    cap_cost,
    owner_map,
    line_ends,
    line_limit,
    cross_ends,
    cross_limit,
    pair_counts,
    store_node,
    store_energy,
    store_power,
    price_start,
):
    rows, techs, nodes = availability.shape
    hours, regions = lax.axis_size("hours"), lax.axis_size("region")
    slots = cross_limit.shape[1]
    owned = cap_cost.shape[1]
    units, lines = store_node.shape[0], line_limit.shape[0]
    total_flows = lines + units + regions * slots
    info_rows = 8 * (regions * slots // LANES)
    sizes = (hours, regions, rows, techs, nodes, slots)
    owner_rows = owner_map.reshape(hours, owned)
    energy = store_energy[None]

    def shape(*dims, dtype=jnp.float32):
        return jax.ShapeDtypeStruct(dims, dtype)

    avail_t, message, to_regions = call(
        functools.partial(setup_kernel, sizes),
        (
            availability.reshape(rows * techs, nodes),
            price_start,
            cap_cost,
            owner_rows,
            cross_ends[:, 0],
            cross_limit,
            pair_counts,
        ),
        (shape(techs, rows, nodes), shape(2 * techs, nodes), shape(rows + info_rows, nodes)),
        in_smem=(6,),
    )
    gathered = lax.all_gather(to_regions, "region")
    received = to_all_hours(message)
    state = {
        "availability": avail_t,
        "demand": demand,
        "gen_cost": gen_cost,
        "store_energy": energy,
    }
    message_rows = round_up(techs + 2 + 2 * (units // LANES), 8)
    kept = {
        "dispatch": shape(techs, rows, nodes),
        "cap_duals": shape(techs, rows, nodes),
        "flows": shape(rows, total_flows),
        "store_duals": shape(rows, units),
        "capacity": shape(techs, nodes),
        "weight": shape(1, LANES),
        "region": shape(rows + 8, nodes),
        "sums": shape(message_rows, nodes),
    }
    charges = {"charge": shape(rows, units), "charge_before": shape(1, units)}
    for iteration in range(ITERS):
        given = dict(state, received=received, gathered=gathered)
        if iteration == 0:
            given.update(
                line_ends=line_ends,
                line_limit=line_limit[None],
                store_node=store_node[None],
                store_power=store_power[None],
            )
            outs = dict(
                kept,
                col_weight=shape(techs, nodes),
                cost=shape(techs, nodes),
                maps=shape(regions * nodes, total_flows, dtype=jnp.bfloat16),
                limits=shape(1, total_flows),
            )
        elif iteration < ITERS - 1:
            outs = dict(kept, **charges)
        else:
            given["owner"] = owner_rows
            outs = {
                "dispatch": shape(rows * techs, nodes),
                "capacity": shape(1, owned),
                "prices": shape(rows, nodes),
                "charge": shape(rows, units),
            }
        values = call(
            functools.partial(sweep_kernel, sizes, iteration, tuple(given), tuple(outs)),
            tuple(given.values()),
            tuple(outs.values()),
        )
        results = dict(zip(outs, values))
        if iteration == ITERS - 1:
            break
        to_regions, message = results.pop("region"), results.pop("sums")
        gathered = lax.all_gather(to_regions, "region")
        squares = jnp.sum(gathered[:, rows : rows + 2], axis=0)
        received = to_all_hours(message.at[techs : techs + 2].set(squares))
        state.update(results)
    return (
        results["dispatch"].reshape(rows, techs, nodes),
        results["capacity"],
        results["prices"],
        results["charge"],
    )


def solution(mesh):
    placed = (
        P("hours", None, "region"),
        P("hours", "region"),
        P(None, "region"),
        P("region", "hours"),
        P("region", None),
        P(None, "region"),
        P("region"),
        P(None, "region", None),
        P("region", None),
        P("region", None),
        P("region"),
        P("region"),
        P("region"),
        P("hours", "region"),
    )
    return jax.shard_map(
        body,
        mesh=mesh,
        in_specs=placed,
        out_specs=(
            P("hours", None, "region"),
            P("region", "hours"),
            P("hours", "region"),
            P("hours", "region"),
        ),
        check_vma=False,
    )
```

```python
import functools

import jax
import jax.numpy as jnp
from jax import lax
from jax.experimental import pallas as pl
from jax.experimental.pallas import tpu as pltpu
from jax.sharding import PartitionSpec as P

ITERS = 4
EPSILON = 1e-06
LANES = 128
VMEM_BYTES = 24 * 1024 * 1024


def split3(value):
    high = value.astype(jnp.bfloat16)
    rest = value - high.astype(jnp.float32)
    middle = rest.astype(jnp.bfloat16)
    low = (rest - middle.astype(jnp.float32)).astype(jnp.bfloat16)
    return jnp.concatenate([high, middle, low], axis=0)


def dot3(value, matrix, transposed):
    rows = value.shape[0]
    contract = ((1,), (1 if transposed else 0,))
    product = lax.dot_general(
        split3(value), matrix, (contract, ((), ())), preferred_element_type=jnp.float32
    )
    return product[:rows] + product[rows : 2 * rows] + product[2 * rows :]


def row_sum(value):
    return jnp.sum(value, axis=0, keepdims=True)


def fold_lanes(row):
    total = row[:, :LANES]
    for start in range(LANES, row.shape[1], LANES):
        total = total + row[:, start : start + LANES]
    return total


def owned_one_hots(owner_ref, tech_count, node_count):
    owned = owner_ref[pl.ds(lax.axis_index("hours"), 1), :]
    shape_t = (tech_count, owned.shape[1])
    shape_n = (node_count, owned.shape[1])
    tech = lax.broadcasted_iota(jnp.int32, shape_t, 0) == owned // node_count
    node = lax.broadcasted_iota(jnp.int32, shape_n, 0) == owned % node_count
    return tech, node.astype(jnp.float32).astype(jnp.bfloat16)


def setup_kernel(
    sizes,
    avail_ref,
    price_ref,
    cost_ref,
    owner_ref,
    ends_ref,
    limit_ref,
    pairs_ref,
    avail_t_ref,
    sums_ref,
    region_ref,
):
    hours, regions, rows, techs, nodes, slots = sizes
    width = slots // regions
    own = lax.axis_index("region")
    total = jnp.zeros((techs, nodes), jnp.float32)
    for hour in range(rows):
        total = total + avail_ref[hour * techs : (hour + 1) * techs, :]
    for tech in range(techs):
        avail_t_ref[tech] = avail_ref[pl.ds(tech, rows, stride=techs), :]
    tech_hot, node_hot = owned_one_hots(owner_ref, techs, nodes)
    costs = jnp.where(tech_hot, cost_ref[...], 0.0)
    sums_ref[:techs, :] = total
    sums_ref[techs : 2 * techs, :] = dot3(costs, node_hot, True)
    slot = lax.broadcasted_iota(jnp.int32, (1, slots), 1)
    pair = slot // width
    in_use = jnp.zeros((1, slots), jnp.int32)
    for target in range(regions):
        in_use = jnp.where(pair == target, pairs_ref[0, target], in_use)
    bound = jnp.where(slot % width < in_use, limit_ref[...], 0.0)
    start = ends_ref[0:1, :] + own * nodes
    end = ends_ref[1:2, :] + pair * nodes
    info = jnp.concatenate(
        [start.astype(jnp.float32), end.astype(jnp.float32), bound, jnp.zeros((13, slots), jnp.float32)],
        axis=0,
    )
    place = lax.broadcasted_iota(jnp.int32, (slots, regions * slots), 1) == (
        own * slots + lax.broadcasted_iota(jnp.int32, (slots, regions * slots), 0)
    )
    info = dot3(info, place.astype(jnp.float32).astype(jnp.bfloat16), False)
    region_ref[:rows, :] = price_ref[...]
    for chunk in range(regions * slots // LANES):
        region_ref[rows + 8 * chunk : rows + 8 * chunk + 8, :] = info[
            :8, chunk * LANES : (chunk + 1) * LANES
        ]


def sweep_kernel(sizes, iteration, names_in, names_out, *refs):
    hours, regions, rows, techs, nodes, slots = sizes
    first = iteration == 0
    last = iteration == ITERS - 1
    given = dict(zip(names_in, refs[: len(names_in)]))
    gives = dict(zip(names_out, refs[len(names_in) :]))
    own = lax.axis_index("region")
    hour_index = lax.axis_index("hours")
    gathered = given["gathered"]
    sums = given["totals"][...]
    if first:
        weight = jnp.ones((1, 1), jnp.float32)
        col_weight, cost = sums[:techs], sums[techs : 2 * techs]
        gives["col_weight"][...] = col_weight
        gives["cost"][...] = cost
        chunks = []
        for chunk in range(regions * slots // LANES):
            part = gathered[0, rows + 8 * chunk : rows + 8 * chunk + 8, :]
            for region in range(1, regions):
                part = part + gathered[region, rows + 8 * chunk : rows + 8 * chunk + 8, :]
            chunks.append(part)
        info = jnp.concatenate(chunks, axis=1) if len(chunks) > 1 else chunks[0]
        base = own * nodes
        line_ends, stores = given["line_ends"][...], given["store_node"][...]
        start = jnp.concatenate(
            [line_ends[0:1] + base, jnp.full_like(stores, -1), info[0:1].astype(jnp.int32)], axis=1
        )
        end = jnp.concatenate(
            [line_ends[1:2] + base, stores + base, info[1:2].astype(jnp.int32)], axis=1
        )
        limits = jnp.concatenate(
            [given["line_limit"][...], given["store_power"][...], info[2:3]], axis=1
        )
        node = lax.broadcasted_iota(jnp.int32, (regions * nodes, start.shape[1]), 0)
        maps = (node == end).astype(jnp.float32) - (node == start).astype(jnp.float32)
        gives["maps"][...] = maps.astype(jnp.bfloat16)
        gives["limits"][...] = limits
        maps_ref = gives["maps"]
    else:
        maps_ref = given["maps"]
        limits = given["limits"][...]
        col_weight, cost = given["col_weight"][...], given["cost"][...]
        squares = jnp.sum(sums[techs : techs + 2], axis=1, keepdims=True)
        weight = given["weight"][...][:, :1]
        weight = jnp.sqrt(
            weight * jnp.sqrt((squares[1:2] + EPSILON) / (squares[0:1] + EPSILON))
        )
    primal_step = 0.5 / weight
    lines = sizes_lines(maps_ref, regions, slots, given["store_energy"].shape[1])
    units = given["store_energy"].shape[1]
    energy = given["store_energy"][...]

    prices_all = jnp.concatenate([gathered[region, :rows, :] for region in range(regions)], axis=1)
    prices = gathered[own, :rows, :]
    difference = dot3(prices_all, maps_ref[...], False)

    if first:
        capacity_new = jnp.maximum(-cost / (weight * col_weight), 0.0)
        capacity_bar = 2.0 * capacity_new
        capacity_change = capacity_new
    else:
        capacity = given["capacity"][...]
        capacity_new = jnp.maximum(
            capacity - (cost - sums[:techs]) / (weight * col_weight), 0.0
        )
        capacity_bar = 2.0 * capacity_new - capacity
        capacity_change = capacity_new - capacity

    row_id = lax.broadcasted_iota(jnp.int32, (rows, units), 0)
    if not first:
        span = units // LANES
        next_row = jnp.concatenate([given["next_row"][i : i + 1, :] for i in range(span)], axis=1)
        prev_row = jnp.concatenate([given["prev_row"][i : i + 1, :] for i in range(span)], axis=1)
        store_duals = given["store_duals"][...]
        next_duals = jnp.where(row_id == rows - 1, next_row, pltpu.roll(store_duals, rows - 1, 0))
        if iteration == 1:
            charge = jnp.zeros((rows, units), jnp.float32)
            charge_before = jnp.zeros((1, units), jnp.float32)
        else:
            charge = given["charge"][...]
            charge_before = given["charge_before"][...]
        charge_new = jnp.clip(charge - primal_step * (store_duals - next_duals), 0.0, energy)
        gives["charge"][...] = charge_new

    flows_new, flows_bar = [], []
    primal_row = jnp.zeros((1, LANES), jnp.float32)
    total_flows = limits.shape[1]
    for low, high in ((0, lines), (lines, lines + units), (lines + units, total_flows)):
        slope = difference[:, low:high]
        if low == lines and not first:
            slope = slope + store_duals
        bound = limits[:, low:high]
        old = None if first else given["flows"][:, low:high]
        moved = -primal_step * slope if first else old - primal_step * slope
        new = jnp.clip(moved, -bound, bound)
        flows_new.append(new)
        flows_bar.append(2.0 * new if first else 2.0 * new - old)
        if not last:
            gives["flows"][:, low:high] = new
            change = row_sum((new if first else new - old) ** 2)
            if low == lines + units:
                slot = lax.broadcasted_iota(jnp.int32, change.shape, 1)
                change = jnp.where(slot // slots == own, change, 0.0)
            primal_row = primal_row + fold_lanes(change)
    maps_own = maps_ref[pl.ds(pl.multiple_of(own * nodes, nodes), nodes), :]
    balance = dot3(jnp.concatenate(flows_bar, axis=1), maps_own, True) - given["demand"][...]

    gen_cost = given["gen_cost"][...]
    half_weight = weight / 2.0
    primal_acc = jnp.zeros((rows, nodes), jnp.float32)
    dual_acc = jnp.zeros((rows, nodes), jnp.float32)
    for tech in range(techs):
        slope = gen_cost[tech : tech + 1] + prices
        if first:
            dispatch_new = jnp.maximum(-primal_step * slope, 0.0)
            dispatch_bar = 2.0 * dispatch_new
        else:
            duals = given["cap_duals"][tech]
            dispatch = given["dispatch"][tech]
            dispatch_new = jnp.maximum(dispatch - primal_step * (slope + duals), 0.0)
            dispatch_bar = 2.0 * dispatch_new - dispatch
        balance = balance + dispatch_bar
        if last:
            gives["dispatch"][pl.ds(tech, rows, stride=techs), :] = dispatch_new
            continue
        gives["dispatch"][tech] = dispatch_new
        avail = given["availability"][tech]
        cap_rows = dispatch_bar - avail * capacity_bar[tech : tech + 1]
        if first:
            primal_acc = primal_acc + dispatch_new * dispatch_new
            duals_new = jnp.maximum(half_weight * cap_rows, 0.0)
            dual_acc = dual_acc + duals_new * duals_new
        else:
            primal_acc = primal_acc + (dispatch_new - dispatch) ** 2
            duals_new = jnp.maximum(duals + half_weight * cap_rows, 0.0)
            dual_acc = dual_acc + (duals_new - duals) ** 2
        gives["cap_duals"][tech] = duals_new
        gives["sums"][tech : tech + 1, :] = row_sum(avail * duals_new)

    step_up = weight / (techs + 8.0) * balance
    if last:
        gives["prices"][...] = prices + step_up
        tech_hot, node_hot = owned_one_hots(given["owner"], techs, nodes)
        chosen = dot3(capacity_new, node_hot, False)
        gives["capacity"][...] = row_sum(jnp.where(tech_hot, chosen, 0.0))
        return
    gives["region"][:rows, :] = prices + step_up
    gives["weight"][...] = jnp.broadcast_to(weight, (1, LANES))
    gives["capacity"][...] = capacity_new
    dual_row = row_sum(dual_acc + step_up * step_up)
    primal_row = primal_row + row_sum(primal_acc)
    primal_row = primal_row + jnp.where(hour_index == 0, row_sum(capacity_change**2), 0.0)

    discharge_bar = flows_bar[1]
    if first:
        store_step = weight / 3.0 * discharge_bar
        store_new = store_step
    else:
        charge_bar = 2.0 * charge_new - charge
        before_new = jnp.clip(
            charge_before - primal_step * (prev_row - store_duals[0:1]), 0.0, energy
        )
        gives["charge_before"][...] = before_new
        before_bar = 2.0 * before_new - charge_before
        shifted = jnp.where(row_id == 0, before_bar, pltpu.roll(charge_bar, 1, 0))
        store_step = weight / 3.0 * (charge_bar - shifted + discharge_bar)
        store_new = store_duals + store_step
        primal_row = primal_row + fold_lanes(row_sum((charge_new - charge) ** 2))
    gives["store_duals"][...] = store_new
    dual_row = dual_row + fold_lanes(row_sum(store_step * store_step))
    gives["region"][rows : rows + 8, :] = jnp.concatenate(
        [primal_row, dual_row, jnp.zeros((6, LANES), jnp.float32)], axis=0
    )
    span = units // LANES
    gives["sums"][techs:, :] = jnp.concatenate(
        [primal_row, dual_row, jnp.zeros((6, LANES), jnp.float32)], axis=0
    )
    for i in range(span):
        part = slice(i * LANES, (i + 1) * LANES)
        gives["first_row"][i : i + 1, :] = store_new[:1, part]
        gives["last_row"][i : i + 1, :] = store_new[rows - 1 :, part]


def sizes_lines(maps_ref, regions, slots, units):
    return maps_ref.shape[1] - units - regions * slots


def call(kernel, arguments, shapes, in_smem=()):
    return pl.pallas_call(
        kernel,
        out_shape=shapes,
        in_specs=[
            pl.BlockSpec(memory_space=pltpu.SMEM if i in in_smem else pltpu.VMEM)
            for i in range(len(arguments))
        ],
        out_specs=[pl.BlockSpec(memory_space=pltpu.VMEM)] * len(shapes),
        compiler_params=pltpu.CompilerParams(vmem_limit_bytes=VMEM_BYTES),
    )(*arguments)


def swap(value, hour_bit, region_bit):
    hours, regions = lax.axis_size("hours"), lax.axis_size("region")
    pairs = [
        (hour * regions + region, (hour ^ hour_bit) * regions + (region ^ region_bit))
        for hour in range(hours)
        for region in range(regions)
    ]
    return lax.ppermute(value, ("hours", "region"), pairs)


def shifted(value, steps):
    count = lax.axis_size("hours")
    return lax.ppermute(value, "hours", [(i, (i + steps) % count) for i in range(count)])


def exchange(to_regions, sums, squares_at=None, first_row=None, last_row=None):
    hours, regions = lax.axis_size("hours"), lax.axis_size("region")
    hour, region = lax.axis_index("hours"), lax.axis_index("region")
    sweeping = squares_at is not None
    next_row = prev_row = None
    if regions != 2 or hours < 4 or hours & (hours - 1):
        gathered = lax.all_gather(to_regions, "region")
        if sweeping:
            rows = to_regions.shape[0] - 8
            squares = jnp.sum(gathered[:, rows : rows + 8], axis=0)
            sums = sums.at[squares_at:].set(squares)
            next_row, prev_row = shifted(first_row, -1), shifted(last_row, 1)
        return gathered, lax.psum(sums, "hours"), next_row, prev_row
    even = hour % 2 == 0
    message = sums
    if sweeping:
        message = jnp.concatenate([sums, jnp.where(even, last_row, first_row)], axis=0)
        beside = jnp.where(even, first_row, last_row)
        across = [
            (h * regions + r, (h + 1 if h % 2 else h - 1) % hours * regions + r)
            for h in range(hours)
            for r in range(regions)
        ]
    partner = swap(message, 1, 0)
    other = swap(to_regions, 0, 1)
    count = sums.shape[0]
    totals = sums + partner[:count]
    if sweeping:
        rows = to_regions.shape[0] - 8
        diagonal = swap(sums[squares_at:], 1, 1)
        arrived = lax.ppermute(beside, ("hours", "region"), across)
        next_row = jnp.where(even, partner[count:], arrived)
        prev_row = jnp.where(even, arrived, partner[count:])
        totals = totals.at[squares_at:].add(other[rows:] + diagonal)
    bit = 2
    while bit < hours:
        totals = totals + swap(totals, bit, 0)
        bit *= 2
    gathered = jnp.where(
        region == 0, jnp.stack([to_regions, other]), jnp.stack([other, to_regions])
    )
    return gathered, totals, next_row, prev_row


def body(
    availability,
    demand,
    gen_cost,
    cap_cost,
    owner_map,
    line_ends,
    line_limit,
    cross_ends,
    cross_limit,
    pair_counts,
    store_node,
    store_energy,
    store_power,
    price_start,
):
    rows, techs, nodes = availability.shape
    hours, regions = lax.axis_size("hours"), lax.axis_size("region")
    slots = cross_limit.shape[1]
    owned = cap_cost.shape[1]
    units, lines = store_node.shape[0], line_limit.shape[0]
    total_flows = lines + units + regions * slots
    info_rows = 8 * (regions * slots // LANES)
    sizes = (hours, regions, rows, techs, nodes, slots)
    owner_rows = owner_map.reshape(hours, owned)
    energy = store_energy[None]

    def shape(*dims, dtype=jnp.float32):
        return jax.ShapeDtypeStruct(dims, dtype)

    avail_t, message, to_regions = call(
        functools.partial(setup_kernel, sizes),
        (
            availability.reshape(rows * techs, nodes),
            price_start,
            cap_cost,
            owner_rows,
            cross_ends[:, 0],
            cross_limit,
            pair_counts,
        ),
        (shape(techs, rows, nodes), shape(2 * techs, nodes), shape(rows + info_rows, nodes)),
        in_smem=(6,),
    )
    gathered, totals, next_row, prev_row = exchange(to_regions, message)
    state = {
        "availability": avail_t,
        "demand": demand,
        "gen_cost": gen_cost,
        "store_energy": energy,
    }
    kept = {
        "dispatch": shape(techs, rows, nodes),
        "cap_duals": shape(techs, rows, nodes),
        "flows": shape(rows, total_flows),
        "store_duals": shape(rows, units),
        "capacity": shape(techs, nodes),
        "weight": shape(1, LANES),
        "region": shape(rows + 8, nodes),
        "sums": shape(techs + 8, nodes),
        "first_row": shape(units // LANES, LANES),
        "last_row": shape(units // LANES, LANES),
    }
    charges = {"charge": shape(rows, units), "charge_before": shape(1, units)}
    for iteration in range(ITERS):
        given = dict(state, totals=totals, gathered=gathered)
        if iteration == 0:
            given.update(
                line_ends=line_ends,
                line_limit=line_limit[None],
                store_node=store_node[None],
                store_power=store_power[None],
            )
            outs = dict(
                kept,
                col_weight=shape(techs, nodes),
                cost=shape(techs, nodes),
                maps=shape(regions * nodes, total_flows, dtype=jnp.bfloat16),
                limits=shape(1, total_flows),
            )
        else:
            given.update(next_row=next_row, prev_row=prev_row)
            outs = dict(kept, **charges)
        if iteration == ITERS - 1:
            given["owner"] = owner_rows
            outs = {
                "dispatch": shape(rows * techs, nodes),
                "capacity": shape(1, owned),
                "prices": shape(rows, nodes),
                "charge": shape(rows, units),
            }
        values = call(
            functools.partial(sweep_kernel, sizes, iteration, tuple(given), tuple(outs)),
            tuple(given.values()),
            tuple(outs.values()),
        )
        results = dict(zip(outs, values))
        if iteration == ITERS - 1:
            break
        gathered, totals, next_row, prev_row = exchange(
            results.pop("region"),
            results.pop("sums"),
            techs,
            results.pop("first_row"),
            results.pop("last_row"),
        )
        state.update(results)
    return (
        results["dispatch"].reshape(rows, techs, nodes),
        results["capacity"],
        results["prices"],
        results["charge"],
    )


def solution(mesh):
    placed = (
        P("hours", None, "region"),
        P("hours", "region"),
        P(None, "region"),
        P("region", "hours"),
        P("region", None),
        P(None, "region"),
        P("region"),
        P(None, "region", None),
        P("region", None),
        P("region", None),
        P("region"),
        P("region"),
        P("region"),
        P("hours", "region"),
    )
    return jax.shard_map(
        body,
        mesh=mesh,
        in_specs=placed,
        out_specs=(
            P("hours", None, "region"),
            P("region", "hours"),
            P("hours", "region"),
            P("hours", "region"),
        ),
        check_vma=False,
    )
```

```python
import functools

import jax
import jax.numpy as jnp
from jax import lax
from jax.experimental import pallas as pl
from jax.experimental.pallas import tpu as pltpu
from jax.sharding import PartitionSpec as P

ITERS = 4
EPSILON = 1e-06
LANES = 128
VMEM_BYTES = 24 * 1024 * 1024


def split3(value):
    high = value.astype(jnp.bfloat16)
    rest = value - high.astype(jnp.float32)
    middle = rest.astype(jnp.bfloat16)
    low = (rest - middle.astype(jnp.float32)).astype(jnp.bfloat16)
    return jnp.concatenate([high, middle, low], axis=0)


def dot3(value, matrix, transposed):
    rows = value.shape[0]
    contract = ((1,), (1 if transposed else 0,))
    product = lax.dot_general(
        split3(value), matrix, (contract, ((), ())), preferred_element_type=jnp.float32
    )
    return product[:rows] + product[rows : 2 * rows] + product[2 * rows :]


def row_sum(value):
    return jnp.sum(value, axis=0, keepdims=True)


def fold_lanes(row):
    total = row[:, :LANES]
    for start in range(LANES, row.shape[1], LANES):
        total = total + row[:, start : start + LANES]
    return total


def owned_one_hots(owner_ref, tech_count, node_count):
    owned = owner_ref[pl.ds(lax.axis_index("hours"), 1), :]
    shape_t = (tech_count, owned.shape[1])
    shape_n = (node_count, owned.shape[1])
    tech = lax.broadcasted_iota(jnp.int32, shape_t, 0) == owned // node_count
    node = lax.broadcasted_iota(jnp.int32, shape_n, 0) == owned % node_count
    return tech, node.astype(jnp.float32).astype(jnp.bfloat16)


def setup_kernel(
    sizes,
    avail_ref,
    price_ref,
    cost_ref,
    owner_ref,
    ends_ref,
    limit_ref,
    pairs_ref,
    avail_t_ref,
    sums_ref,
    region_ref,
):
    hours, regions, rows, techs, nodes, slots = sizes
    width = slots // regions
    own = lax.axis_index("region")
    total = jnp.zeros((techs, nodes), jnp.float32)
    for hour in range(rows):
        total = total + avail_ref[hour * techs : (hour + 1) * techs, :]
    for tech in range(techs):
        avail_t_ref[tech] = avail_ref[pl.ds(tech, rows, stride=techs), :]
    tech_hot, node_hot = owned_one_hots(owner_ref, techs, nodes)
    costs = jnp.where(tech_hot, cost_ref[...], 0.0)
    sums_ref[:techs, :] = total
    sums_ref[techs : 2 * techs, :] = dot3(costs, node_hot, True)
    slot = lax.broadcasted_iota(jnp.int32, (1, slots), 1)
    pair = slot // width
    in_use = jnp.zeros((1, slots), jnp.int32)
    for target in range(regions):
        in_use = jnp.where(pair == target, pairs_ref[0, target], in_use)
    bound = jnp.where(slot % width < in_use, limit_ref[...], 0.0)
    start = ends_ref[0:1, :] + own * nodes
    end = ends_ref[1:2, :] + pair * nodes
    info = jnp.concatenate(
        [start.astype(jnp.float32), end.astype(jnp.float32), bound, jnp.zeros((13, slots), jnp.float32)],
        axis=0,
    )
    place = lax.broadcasted_iota(jnp.int32, (slots, regions * slots), 1) == (
        own * slots + lax.broadcasted_iota(jnp.int32, (slots, regions * slots), 0)
    )
    info = dot3(info, place.astype(jnp.float32).astype(jnp.bfloat16), False)
    region_ref[:rows, :] = price_ref[...]
    for chunk in range(regions * slots // LANES):
        region_ref[rows + 8 * chunk : rows + 8 * chunk + 8, :] = info[
            :8, chunk * LANES : (chunk + 1) * LANES
        ]


def neighbour_rows(given, hour_index, halo, span):
    def row_of(name, offset):
        return jnp.concatenate(
            [given[name][offset + i : offset + i + 1, :] for i in range(span)], axis=1
        )

    if "totals" in given:
        return row_of("next_row", 0), row_of("prev_row", 0)
    first, last = halo, halo + span
    core, x_place, slab = hour_index % 2, hour_index // 2 % 2, hour_index // 4 % 2
    next_row = jnp.where(slab == 0, row_of("near", first), row_of("far", first))
    prev_row = jnp.where(slab == 0, row_of("far", last), row_of("near", last))
    next_row = jnp.where(x_place == 0, row_of("across", first), next_row)
    prev_row = jnp.where(x_place == 0, prev_row, row_of("across", last))
    next_row = jnp.where(core == 0, row_of("partner", first), next_row)
    prev_row = jnp.where(core == 0, prev_row, row_of("partner", last))
    return next_row, prev_row


def sweep_kernel(sizes, iteration, names_in, names_out, *refs):
    hours, regions, rows, techs, nodes, slots = sizes
    first = iteration == 0
    last = iteration == ITERS - 1
    given = dict(zip(names_in, refs[: len(names_in)]))
    gives = dict(zip(names_out, refs[len(names_in) :]))
    own = lax.axis_index("region")
    hour_index = lax.axis_index("hours")
    gathered = given["gathered"]
    if "totals" in given:
        sums = given["totals"][...]
    else:
        sums = (given["slab"][...] + given["near"][...]) + (
            given["middle"][...] + given["far"][...]
        )
    if first:
        weight = jnp.ones((1, 1), jnp.float32)
        col_weight, cost = sums[:techs], sums[techs : 2 * techs]
        gives["col_weight"][...] = col_weight
        gives["cost"][...] = cost
        chunks = []
        for chunk in range(regions * slots // LANES):
            part = gathered[0, rows + 8 * chunk : rows + 8 * chunk + 8, :]
            for region in range(1, regions):
                part = part + gathered[region, rows + 8 * chunk : rows + 8 * chunk + 8, :]
            chunks.append(part)
        info = jnp.concatenate(chunks, axis=1) if len(chunks) > 1 else chunks[0]
        base = own * nodes
        line_ends, stores = given["line_ends"][...], given["store_node"][...]
        start = jnp.concatenate(
            [line_ends[0:1] + base, jnp.full_like(stores, -1), info[0:1].astype(jnp.int32)], axis=1
        )
        end = jnp.concatenate(
            [line_ends[1:2] + base, stores + base, info[1:2].astype(jnp.int32)], axis=1
        )
        limits = jnp.concatenate(
            [given["line_limit"][...], given["store_power"][...], info[2:3]], axis=1
        )
        node = lax.broadcasted_iota(jnp.int32, (regions * nodes, start.shape[1]), 0)
        maps = (node == end).astype(jnp.float32) - (node == start).astype(jnp.float32)
        gives["maps"][...] = maps.astype(jnp.bfloat16)
        gives["limits"][...] = limits
        maps_ref = gives["maps"]
    else:
        maps_ref = given["maps"]
        limits = given["limits"][...]
        col_weight, cost = given["col_weight"][...], given["cost"][...]
        squares = jnp.sum(sums[techs : techs + 2], axis=1, keepdims=True)
        weight = given["weight"][...][:, :1]
        weight = jnp.sqrt(
            weight * jnp.sqrt((squares[1:2] + EPSILON) / (squares[0:1] + EPSILON))
        )
    primal_step = 0.5 / weight
    lines = sizes_lines(maps_ref, regions, slots, given["store_energy"].shape[1])
    units = given["store_energy"].shape[1]
    energy = given["store_energy"][...]

    prices_all = jnp.concatenate([gathered[region, :rows, :] for region in range(regions)], axis=1)
    prices = gathered[own, :rows, :]
    difference = dot3(prices_all, maps_ref[...], False)

    if first:
        capacity_new = jnp.maximum(-cost / (weight * col_weight), 0.0)
        capacity_bar = 2.0 * capacity_new
        capacity_change = capacity_new
    else:
        capacity = given["capacity"][...]
        capacity_new = jnp.maximum(
            capacity - (cost - sums[:techs]) / (weight * col_weight), 0.0
        )
        capacity_bar = 2.0 * capacity_new - capacity
        capacity_change = capacity_new - capacity

    row_id = lax.broadcasted_iota(jnp.int32, (rows, units), 0)
    if not first:
        span = units // LANES
        next_row, prev_row = neighbour_rows(given, hour_index, techs + 2, span)
        store_duals = given["store_duals"][...]
        next_duals = jnp.where(row_id == rows - 1, next_row, pltpu.roll(store_duals, rows - 1, 0))
        if iteration == 1:
            charge = jnp.zeros((rows, units), jnp.float32)
            charge_before = jnp.zeros((1, units), jnp.float32)
        else:
            charge = given["charge"][...]
            charge_before = given["charge_before"][...]
        charge_new = jnp.clip(charge - primal_step * (store_duals - next_duals), 0.0, energy)
        gives["charge"][...] = charge_new

    flows_new, flows_bar = [], []
    primal_row = jnp.zeros((1, LANES), jnp.float32)
    total_flows = limits.shape[1]
    for low, high in ((0, lines), (lines, lines + units), (lines + units, total_flows)):
        slope = difference[:, low:high]
        if low == lines and not first:
            slope = slope + store_duals
        bound = limits[:, low:high]
        old = None if first else given["flows"][:, low:high]
        moved = -primal_step * slope if first else old - primal_step * slope
        new = jnp.clip(moved, -bound, bound)
        flows_new.append(new)
        flows_bar.append(2.0 * new if first else 2.0 * new - old)
        if not last:
            gives["flows"][:, low:high] = new
            change = row_sum((new if first else new - old) ** 2)
            if low == lines + units:
                slot = lax.broadcasted_iota(jnp.int32, change.shape, 1)
                change = jnp.where(slot // slots == own, change, 0.0)
            primal_row = primal_row + fold_lanes(change)
    maps_own = maps_ref[pl.ds(pl.multiple_of(own * nodes, nodes), nodes), :]
    balance = dot3(jnp.concatenate(flows_bar, axis=1), maps_own, True) - given["demand"][...]

    gen_cost = given["gen_cost"][...]
    half_weight = weight / 2.0
    primal_acc = jnp.zeros((rows, nodes), jnp.float32)
    dual_acc = jnp.zeros((rows, nodes), jnp.float32)
    for tech in range(techs):
        slope = gen_cost[tech : tech + 1] + prices
        if first:
            dispatch_new = jnp.maximum(-primal_step * slope, 0.0)
            dispatch_bar = 2.0 * dispatch_new
        else:
            duals = given["cap_duals"][tech]
            dispatch = given["dispatch"][tech]
            dispatch_new = jnp.maximum(dispatch - primal_step * (slope + duals), 0.0)
            dispatch_bar = 2.0 * dispatch_new - dispatch
        balance = balance + dispatch_bar
        if last:
            gives["dispatch"][pl.ds(tech, rows, stride=techs), :] = dispatch_new
            continue
        gives["dispatch"][tech] = dispatch_new
        avail = given["availability"][tech]
        cap_rows = dispatch_bar - avail * capacity_bar[tech : tech + 1]
        if first:
            primal_acc = primal_acc + dispatch_new * dispatch_new
            duals_new = jnp.maximum(half_weight * cap_rows, 0.0)
            dual_acc = dual_acc + duals_new * duals_new
        else:
            primal_acc = primal_acc + (dispatch_new - dispatch) ** 2
            duals_new = jnp.maximum(duals + half_weight * cap_rows, 0.0)
            dual_acc = dual_acc + (duals_new - duals) ** 2
        gives["cap_duals"][tech] = duals_new
        gives["sums"][tech : tech + 1, :] = row_sum(avail * duals_new)

    step_up = weight / (techs + 8.0) * balance
    if last:
        gives["prices"][...] = prices + step_up
        tech_hot, node_hot = owned_one_hots(given["owner"], techs, nodes)
        chosen = dot3(capacity_new, node_hot, False)
        gives["capacity"][...] = row_sum(jnp.where(tech_hot, chosen, 0.0))
        return
    gives["region"][:rows, :] = prices + step_up
    gives["weight"][...] = jnp.broadcast_to(weight, (1, LANES))
    gives["capacity"][...] = capacity_new
    dual_row = row_sum(dual_acc + step_up * step_up)
    primal_row = primal_row + row_sum(primal_acc)
    primal_row = primal_row + jnp.where(hour_index == 0, row_sum(capacity_change**2), 0.0)

    discharge_bar = flows_bar[1]
    if first:
        store_step = weight / 3.0 * discharge_bar
        store_new = store_step
    else:
        charge_bar = 2.0 * charge_new - charge
        before_new = jnp.clip(
            charge_before - primal_step * (prev_row - store_duals[0:1]), 0.0, energy
        )
        gives["charge_before"][...] = before_new
        before_bar = 2.0 * before_new - charge_before
        shifted = jnp.where(row_id == 0, before_bar, pltpu.roll(charge_bar, 1, 0))
        store_step = weight / 3.0 * (charge_bar - shifted + discharge_bar)
        store_new = store_duals + store_step
        primal_row = primal_row + fold_lanes(row_sum((charge_new - charge) ** 2))
    gives["store_duals"][...] = store_new
    dual_row = dual_row + fold_lanes(row_sum(store_step * store_step))
    gives["region"][rows : rows + 8, :] = jnp.concatenate(
        [primal_row, dual_row, jnp.zeros((6, LANES), jnp.float32)], axis=0
    )
    halo, span = techs + 2, units // LANES
    gives["sums"][techs:halo, :] = jnp.concatenate([primal_row, dual_row], axis=0)
    for i in range(span):
        part = slice(i * LANES, (i + 1) * LANES)
        gives["sums"][halo + i : halo + i + 1, :] = store_new[:1, part]
        gives["sums"][halo + span + i : halo + span + i + 1, :] = store_new[rows - 1 :, part]
    used = halo + 2 * span
    total_rows = gives["sums"].shape[0]
    gives["sums"][used:, :] = jnp.zeros((total_rows - used, LANES), jnp.float32)


def sizes_lines(maps_ref, regions, slots, units):
    return maps_ref.shape[1] - units - regions * slots


def call(kernel, arguments, shapes, in_smem=()):
    return pl.pallas_call(
        kernel,
        out_shape=shapes,
        in_specs=[
            pl.BlockSpec(memory_space=pltpu.SMEM if i in in_smem else pltpu.VMEM)
            for i in range(len(arguments))
        ],
        out_specs=[pl.BlockSpec(memory_space=pltpu.VMEM)] * len(shapes),
        compiler_params=pltpu.CompilerParams(vmem_limit_bytes=VMEM_BYTES),
    )(*arguments)


def swap(value, hour_bit, region_bit):
    hours, regions = lax.axis_size("hours"), lax.axis_size("region")
    pairs = [
        (hour * regions + region, (hour ^ hour_bit) * regions + (region ^ region_bit))
        for hour in range(hours)
        for region in range(regions)
    ]
    return lax.ppermute(value, ("hours", "region"), pairs)


def shifted(value, steps):
    count = lax.axis_size("hours")
    return lax.ppermute(value, "hours", [(i, (i + steps) % count) for i in range(count)])


def exchange(to_regions, sums, techs, span):
    hours, regions = lax.axis_size("hours"), lax.axis_size("region")
    region = lax.axis_index("region")
    sweeping = span > 0
    halo = techs + 2
    if regions != 2 or hours != 16:
        gathered = lax.all_gather(to_regions, "region")
        if not sweeping:
            return gathered, {"totals": lax.psum(sums, "hours")}
        rows = to_regions.shape[0] - 8
        squares = jnp.sum(gathered[:, rows : rows + 2], axis=0)
        totals = lax.psum(sums.at[techs:halo].set(squares)[:halo], "hours")
        next_row = shifted(sums[halo : halo + span], -1)
        prev_row = shifted(sums[halo + span : halo + 2 * span], 1)
        return gathered, {"totals": totals, "next_row": next_row, "prev_row": prev_row}

    def merged(mine, yours, mine_first):
        total = mine + yours
        if not sweeping:
            return total
        edge = lax.broadcasted_iota(jnp.int32, total.shape, 0)
        keep = jnp.where(edge < halo + span, mine_first, jnp.logical_not(mine_first))
        return jnp.where(edge < halo, total, jnp.where(keep, mine, yours))

    hour = lax.axis_index("hours")
    partner = swap(sums, 1, 0)
    chip = merged(sums, partner, hour % 2 == 0)
    across = swap(chip, 2, 0)
    if sweeping:
        rows = to_regions.shape[0] - 8
        other = swap(to_regions.at[rows : rows + 2].set(chip[techs:halo]), 0, 1)
        diagonal = swap(chip[techs:halo], 2, 1)
    else:
        other = swap(to_regions, 0, 1)
    slab = merged(chip, across, hour // 2 % 2 == 0)
    if sweeping:
        slab = slab.at[techs:halo].add(other[rows : rows + 2] + diagonal)
    near, middle, far = [swap(slab, 4 * step, 0) for step in (1, 2, 3)]
    gathered = jnp.where(
        region == 0, jnp.stack([to_regions, other]), jnp.stack([other, to_regions])
    )
    parts = {"slab": slab, "near": near, "middle": middle, "far": far}
    if sweeping:
        parts.update(partner=partner, across=across)
    return gathered, parts


def body(
    availability,
    demand,
    gen_cost,
    cap_cost,
    owner_map,
    line_ends,
    line_limit,
    cross_ends,
    cross_limit,
    pair_counts,
    store_node,
    store_energy,
    store_power,
    price_start,
):
    rows, techs, nodes = availability.shape
    hours, regions = lax.axis_size("hours"), lax.axis_size("region")
    slots = cross_limit.shape[1]
    owned = cap_cost.shape[1]
    units, lines = store_node.shape[0], line_limit.shape[0]
    total_flows = lines + units + regions * slots
    info_rows = 8 * (regions * slots // LANES)
    sizes = (hours, regions, rows, techs, nodes, slots)
    owner_rows = owner_map.reshape(hours, owned)
    energy = store_energy[None]

    def shape(*dims, dtype=jnp.float32):
        return jax.ShapeDtypeStruct(dims, dtype)

    avail_t, message, to_regions = call(
        functools.partial(setup_kernel, sizes),
        (
            availability.reshape(rows * techs, nodes),
            price_start,
            cap_cost,
            owner_rows,
            cross_ends[:, 0],
            cross_limit,
            pair_counts,
        ),
        (shape(techs, rows, nodes), shape(2 * techs, nodes), shape(rows + info_rows, nodes)),
        in_smem=(6,),
    )
    gathered, parts = exchange(to_regions, message, techs, 0)
    state = {
        "availability": avail_t,
        "demand": demand,
        "gen_cost": gen_cost,
        "store_energy": energy,
    }
    span = units // LANES
    kept = {
        "dispatch": shape(techs, rows, nodes),
        "cap_duals": shape(techs, rows, nodes),
        "flows": shape(rows, total_flows),
        "store_duals": shape(rows, units),
        "capacity": shape(techs, nodes),
        "weight": shape(1, LANES),
        "region": shape(rows + 8, nodes),
        "sums": shape((techs + 2 + 2 * span) // 8 * 8 + 8, nodes),
    }
    charges = {"charge": shape(rows, units), "charge_before": shape(1, units)}
    for iteration in range(ITERS):
        given = dict(state, **parts, gathered=gathered)
        if iteration == 0:
            given.update(
                line_ends=line_ends,
                line_limit=line_limit[None],
                store_node=store_node[None],
                store_power=store_power[None],
            )
            outs = dict(
                kept,
                col_weight=shape(techs, nodes),
                cost=shape(techs, nodes),
                maps=shape(regions * nodes, total_flows, dtype=jnp.bfloat16),
                limits=shape(1, total_flows),
            )
        else:
            outs = dict(kept, **charges)
        if iteration == ITERS - 1:
            given["owner"] = owner_rows
            outs = {
                "dispatch": shape(rows * techs, nodes),
                "capacity": shape(1, owned),
                "prices": shape(rows, nodes),
                "charge": shape(rows, units),
            }
        values = call(
            functools.partial(sweep_kernel, sizes, iteration, tuple(given), tuple(outs)),
            tuple(given.values()),
            tuple(outs.values()),
        )
        results = dict(zip(outs, values))
        if iteration == ITERS - 1:
            break
        gathered, parts = exchange(results.pop("region"), results.pop("sums"), techs, span)
        state.update(results)
    return (
        results["dispatch"].reshape(rows, techs, nodes),
        results["capacity"],
        results["prices"],
        results["charge"],
    )


def solution(mesh):
    placed = (
        P("hours", None, "region"),
        P("hours", "region"),
        P(None, "region"),
        P("region", "hours"),
        P("region", None),
        P(None, "region"),
        P("region"),
        P(None, "region", None),
        P("region", None),
        P("region", None),
        P("region"),
        P("region"),
        P("region"),
        P("hours", "region"),
    )
    return jax.shard_map(
        body,
        mesh=mesh,
        in_specs=placed,
        out_specs=(
            P("hours", None, "region"),
            P("region", "hours"),
            P("hours", "region"),
            P("hours", "region"),
        ),
        check_vma=False,
    )
```

```python
import functools

import jax
import jax.numpy as jnp
from jax import lax
from jax.experimental import pallas as pl
from jax.experimental.pallas import tpu as pltpu
from jax.sharding import PartitionSpec as P

ITERS = 4
EPSILON = 1e-06
LANES = 128
VMEM_BYTES = 24 * 1024 * 1024


def split3(value):
    high = value.astype(jnp.bfloat16)
    rest = value - high.astype(jnp.float32)
    middle = rest.astype(jnp.bfloat16)
    low = (rest - middle.astype(jnp.float32)).astype(jnp.bfloat16)
    return jnp.concatenate([high, middle, low], axis=0)


def dot3(value, matrix, transposed):
    rows = value.shape[0]
    contract = ((1,), (1 if transposed else 0,))
    product = lax.dot_general(
        split3(value), matrix, (contract, ((), ())), preferred_element_type=jnp.float32
    )
    return product[:rows] + product[rows : 2 * rows] + product[2 * rows :]


def row_sum(value):
    return jnp.sum(value, axis=0, keepdims=True)


def fold_lanes(row):
    total = row[:, :LANES]
    for start in range(LANES, row.shape[1], LANES):
        total = total + row[:, start : start + LANES]
    return total


def owned_one_hots(owner_ref, tech_count, node_count):
    owned = owner_ref[pl.ds(lax.axis_index("hours"), 1), :]
    shape_t = (tech_count, owned.shape[1])
    shape_n = (node_count, owned.shape[1])
    tech = lax.broadcasted_iota(jnp.int32, shape_t, 0) == owned // node_count
    node = lax.broadcasted_iota(jnp.int32, shape_n, 0) == owned % node_count
    return tech, node.astype(jnp.float32).astype(jnp.bfloat16)


def setup_kernel(
    sizes,
    avail_ref,
    price_ref,
    cost_ref,
    owner_ref,
    ends_ref,
    limit_ref,
    pairs_ref,
    avail_t_ref,
    sums_ref,
    region_ref,
):
    hours, regions, rows, techs, nodes, slots = sizes
    width = slots // regions
    own = lax.axis_index("region")
    total = jnp.zeros((techs, nodes), jnp.float32)
    for hour in range(rows):
        total = total + avail_ref[hour * techs : (hour + 1) * techs, :]
    for tech in range(techs):
        avail_t_ref[tech] = avail_ref[pl.ds(tech, rows, stride=techs), :]
    tech_hot, node_hot = owned_one_hots(owner_ref, techs, nodes)
    costs = jnp.where(tech_hot, cost_ref[...], 0.0)
    sums_ref[:techs, :] = total
    sums_ref[techs : 2 * techs, :] = dot3(costs, node_hot, True)
    slot = lax.broadcasted_iota(jnp.int32, (1, slots), 1)
    pair = slot // width
    in_use = jnp.zeros((1, slots), jnp.int32)
    for target in range(regions):
        in_use = jnp.where(pair == target, pairs_ref[0, target], in_use)
    bound = jnp.where(slot % width < in_use, limit_ref[...], 0.0)
    start = ends_ref[0:1, :] + own * nodes
    end = ends_ref[1:2, :] + pair * nodes
    info = jnp.concatenate(
        [start.astype(jnp.float32), end.astype(jnp.float32), bound, jnp.zeros((13, slots), jnp.float32)],
        axis=0,
    )
    place = lax.broadcasted_iota(jnp.int32, (slots, regions * slots), 1) == (
        own * slots + lax.broadcasted_iota(jnp.int32, (slots, regions * slots), 0)
    )
    info = dot3(info, place.astype(jnp.float32).astype(jnp.bfloat16), False)
    region_ref[:rows, :] = price_ref[...]
    for chunk in range(regions * slots // LANES):
        region_ref[rows + 8 * chunk : rows + 8 * chunk + 8, :] = info[
            :8, chunk * LANES : (chunk + 1) * LANES
        ]


def neighbour_rows(given, hour_index, halo, span):
    def row_of(ref, *place):
        start = place[-1]
        return jnp.concatenate(
            [ref[(*place[:-1], slice(start + i, start + i + 1))] for i in range(span)], axis=1
        )

    if "totals" in given:
        return row_of(given["next_row"], 0), row_of(given["prev_row"], 0)
    places, slabs = given["places"], given["slabs"]
    inner, outer = places.shape[0], slabs.shape[0]
    place, slab = hour_index % inner, hour_index // inner
    next_row = jnp.where(
        place == inner - 1,
        row_of(slabs, (slab + 1) % outer, halo),
        row_of(places, (place + 1) % inner, halo),
    )
    prev_row = jnp.where(
        place == 0,
        row_of(slabs, (slab + outer - 1) % outer, halo + span),
        row_of(places, (place + inner - 1) % inner, halo + span),
    )
    return next_row, prev_row


def sweep_kernel(sizes, iteration, names_in, names_out, *refs):
    hours, regions, rows, techs, nodes, slots = sizes
    first = iteration == 0
    last = iteration == ITERS - 1
    given = dict(zip(names_in, refs[: len(names_in)]))
    gives = dict(zip(names_out, refs[len(names_in) :]))
    own = lax.axis_index("region")
    hour_index = lax.axis_index("hours")
    gathered = given["gathered"]
    if "totals" in given:
        sums = given["totals"][...]
    else:
        sums = jnp.sum(given["slabs"][...], axis=0)
    if first:
        weight = jnp.ones((1, 1), jnp.float32)
        col_weight, cost = sums[:techs], sums[techs : 2 * techs]
        gives["col_weight"][...] = col_weight
        gives["cost"][...] = cost
        chunks = []
        for chunk in range(regions * slots // LANES):
            part = gathered[0, rows + 8 * chunk : rows + 8 * chunk + 8, :]
            for region in range(1, regions):
                part = part + gathered[region, rows + 8 * chunk : rows + 8 * chunk + 8, :]
            chunks.append(part)
        info = jnp.concatenate(chunks, axis=1) if len(chunks) > 1 else chunks[0]
        base = own * nodes
        line_ends, stores = given["line_ends"][...], given["store_node"][...]
        start = jnp.concatenate(
            [line_ends[0:1] + base, jnp.full_like(stores, -1), info[0:1].astype(jnp.int32)], axis=1
        )
        end = jnp.concatenate(
            [line_ends[1:2] + base, stores + base, info[1:2].astype(jnp.int32)], axis=1
        )
        limits = jnp.concatenate(
            [given["line_limit"][...], given["store_power"][...], info[2:3]], axis=1
        )
        node = lax.broadcasted_iota(jnp.int32, (regions * nodes, start.shape[1]), 0)
        maps = (node == end).astype(jnp.float32) - (node == start).astype(jnp.float32)
        gives["maps"][...] = maps.astype(jnp.bfloat16)
        gives["limits"][...] = limits
        maps_ref = gives["maps"]
    else:
        maps_ref = given["maps"]
        limits = given["limits"][...]
        col_weight, cost = given["col_weight"][...], given["cost"][...]
        squares = jnp.sum(sums[techs : techs + 2], axis=1, keepdims=True)
        weight = given["weight"][...][:, :1]
        weight = jnp.sqrt(
            weight * jnp.sqrt((squares[1:2] + EPSILON) / (squares[0:1] + EPSILON))
        )
    primal_step = 0.5 / weight
    lines = sizes_lines(maps_ref, regions, slots, given["store_energy"].shape[1])
    units = given["store_energy"].shape[1]
    energy = given["store_energy"][...]

    prices_all = jnp.concatenate([gathered[region, :rows, :] for region in range(regions)], axis=1)
    prices = gathered[own, :rows, :]
    difference = dot3(prices_all, maps_ref[...], False)

    if first:
        capacity_new = jnp.maximum(-cost / (weight * col_weight), 0.0)
        capacity_bar = 2.0 * capacity_new
        capacity_change = capacity_new
    else:
        capacity = given["capacity"][...]
        capacity_new = jnp.maximum(
            capacity - (cost - sums[:techs]) / (weight * col_weight), 0.0
        )
        capacity_bar = 2.0 * capacity_new - capacity
        capacity_change = capacity_new - capacity

    row_id = lax.broadcasted_iota(jnp.int32, (rows, units), 0)
    if not first:
        span = units // LANES
        next_row, prev_row = neighbour_rows(given, hour_index, techs + 2, span)
        store_duals = given["store_duals"][...]
        next_duals = jnp.where(row_id == rows - 1, next_row, pltpu.roll(store_duals, rows - 1, 0))
        if iteration == 1:
            charge = jnp.zeros((rows, units), jnp.float32)
            charge_before = jnp.zeros((1, units), jnp.float32)
        else:
            charge = given["charge"][...]
            charge_before = given["charge_before"][...]
        charge_new = jnp.clip(charge - primal_step * (store_duals - next_duals), 0.0, energy)
        gives["charge"][...] = charge_new

    flows_new, flows_bar = [], []
    primal_row = jnp.zeros((1, LANES), jnp.float32)
    total_flows = limits.shape[1]
    for low, high in ((0, lines), (lines, lines + units), (lines + units, total_flows)):
        slope = difference[:, low:high]
        if low == lines and not first:
            slope = slope + store_duals
        bound = limits[:, low:high]
        old = None if first else given["flows"][:, low:high]
        moved = -primal_step * slope if first else old - primal_step * slope
        new = jnp.clip(moved, -bound, bound)
        flows_new.append(new)
        flows_bar.append(2.0 * new if first else 2.0 * new - old)
        if not last:
            gives["flows"][:, low:high] = new
            change = row_sum((new if first else new - old) ** 2)
            if low == lines + units:
                slot = lax.broadcasted_iota(jnp.int32, change.shape, 1)
                change = jnp.where(slot // slots == own, change, 0.0)
            primal_row = primal_row + fold_lanes(change)
    maps_own = maps_ref[pl.ds(pl.multiple_of(own * nodes, nodes), nodes), :]
    balance = dot3(jnp.concatenate(flows_bar, axis=1), maps_own, True) - given["demand"][...]

    gen_cost = given["gen_cost"][...]
    half_weight = weight / 2.0
    primal_acc = jnp.zeros((rows, nodes), jnp.float32)
    dual_acc = jnp.zeros((rows, nodes), jnp.float32)
    for tech in range(techs):
        slope = gen_cost[tech : tech + 1] + prices
        if first:
            dispatch_new = jnp.maximum(-primal_step * slope, 0.0)
            dispatch_bar = 2.0 * dispatch_new
        else:
            duals = given["cap_duals"][tech]
            dispatch = given["dispatch"][tech]
            dispatch_new = jnp.maximum(dispatch - primal_step * (slope + duals), 0.0)
            dispatch_bar = 2.0 * dispatch_new - dispatch
        balance = balance + dispatch_bar
        if last:
            gives["dispatch"][pl.ds(tech, rows, stride=techs), :] = dispatch_new
            continue
        gives["dispatch"][tech] = dispatch_new
        avail = given["availability"][tech]
        cap_rows = dispatch_bar - avail * capacity_bar[tech : tech + 1]
        if first:
            primal_acc = primal_acc + dispatch_new * dispatch_new
            duals_new = jnp.maximum(half_weight * cap_rows, 0.0)
            dual_acc = dual_acc + duals_new * duals_new
        else:
            primal_acc = primal_acc + (dispatch_new - dispatch) ** 2
            duals_new = jnp.maximum(duals + half_weight * cap_rows, 0.0)
            dual_acc = dual_acc + (duals_new - duals) ** 2
        gives["cap_duals"][tech] = duals_new
        gives["sums"][tech : tech + 1, :] = row_sum(avail * duals_new)

    step_up = weight / (techs + 8.0) * balance
    if last:
        gives["prices"][...] = prices + step_up
        tech_hot, node_hot = owned_one_hots(given["owner"], techs, nodes)
        chosen = dot3(capacity_new, node_hot, False)
        gives["capacity"][...] = row_sum(jnp.where(tech_hot, chosen, 0.0))
        return
    gives["region"][:rows, :] = prices + step_up
    gives["weight"][...] = jnp.broadcast_to(weight, (1, LANES))
    gives["capacity"][...] = capacity_new
    dual_row = row_sum(dual_acc + step_up * step_up)
    primal_row = primal_row + row_sum(primal_acc)
    primal_row = primal_row + jnp.where(hour_index == 0, row_sum(capacity_change**2), 0.0)

    discharge_bar = flows_bar[1]
    if first:
        store_step = weight / 3.0 * discharge_bar
        store_new = store_step
    else:
        charge_bar = 2.0 * charge_new - charge
        before_new = jnp.clip(
            charge_before - primal_step * (prev_row - store_duals[0:1]), 0.0, energy
        )
        gives["charge_before"][...] = before_new
        before_bar = 2.0 * before_new - charge_before
        shifted = jnp.where(row_id == 0, before_bar, pltpu.roll(charge_bar, 1, 0))
        store_step = weight / 3.0 * (charge_bar - shifted + discharge_bar)
        store_new = store_duals + store_step
        primal_row = primal_row + fold_lanes(row_sum((charge_new - charge) ** 2))
    gives["store_duals"][...] = store_new
    dual_row = dual_row + fold_lanes(row_sum(store_step * store_step))
    gives["region"][rows : rows + 8, :] = jnp.concatenate(
        [primal_row, dual_row, jnp.zeros((6, LANES), jnp.float32)], axis=0
    )
    halo, span = techs + 2, units // LANES
    gives["sums"][techs:halo, :] = jnp.concatenate([primal_row, dual_row], axis=0)
    for i in range(span):
        part = slice(i * LANES, (i + 1) * LANES)
        gives["sums"][halo + i : halo + i + 1, :] = store_new[:1, part]
        gives["sums"][halo + span + i : halo + span + i + 1, :] = store_new[rows - 1 :, part]
    used = halo + 2 * span
    total_rows = gives["sums"].shape[0]
    gives["sums"][used:, :] = jnp.zeros((total_rows - used, LANES), jnp.float32)


def sizes_lines(maps_ref, regions, slots, units):
    return maps_ref.shape[1] - units - regions * slots


def call(kernel, arguments, shapes, in_smem=()):
    return pl.pallas_call(
        kernel,
        out_shape=shapes,
        in_specs=[
            pl.BlockSpec(memory_space=pltpu.SMEM if i in in_smem else pltpu.VMEM)
            for i in range(len(arguments))
        ],
        out_specs=[pl.BlockSpec(memory_space=pltpu.VMEM)] * len(shapes),
        compiler_params=pltpu.CompilerParams(vmem_limit_bytes=VMEM_BYTES),
    )(*arguments)


def swap(value, hour_bit, region_bit):
    hours, regions = lax.axis_size("hours"), lax.axis_size("region")
    pairs = [
        (hour * regions + region, (hour ^ hour_bit) * regions + (region ^ region_bit))
        for hour in range(hours)
        for region in range(regions)
    ]
    return lax.ppermute(value, ("hours", "region"), pairs)


def to_all(message, groups):
    copies = jnp.broadcast_to(message[None], (len(groups[0]), *message.shape))
    return lax.all_to_all(
        copies, ("hours", "region"), split_axis=0, concat_axis=0, axis_index_groups=groups
    )


def shifted(value, steps):
    count = lax.axis_size("hours")
    return lax.ppermute(value, "hours", [(i, (i + steps) % count) for i in range(count)])


def exchange(to_regions, sums, techs, span):
    hours, regions = lax.axis_size("hours"), lax.axis_size("region")
    region = lax.axis_index("region")
    sweeping = span > 0
    halo = techs + 2
    if regions != 2 or hours != 16:
        gathered = lax.all_gather(to_regions, "region")
        if not sweeping:
            return gathered, {"totals": lax.psum(sums, "hours")}
        rows = to_regions.shape[0] - 8
        squares = jnp.sum(gathered[:, rows : rows + 2], axis=0)
        totals = lax.psum(sums.at[techs:halo].set(squares)[:halo], "hours")
        next_row = shifted(sums[halo : halo + span], -1)
        prev_row = shifted(sums[halo + span : halo + 2 * span], 1)
        return gathered, {"totals": totals, "next_row": next_row, "prev_row": prev_row}

    near = [
        [(z * 4 + place) * regions + side for place in range(4) for side in range(regions)]
        for z in range(hours // 4)
    ]
    far = [
        [(z * 4 + place) * regions + side for z in range(hours // 4)]
        for place in range(4)
        for side in range(regions)
    ]
    other = swap(to_regions, 0, 1)
    slab = to_all(sums, near)
    if sweeping:
        squares = jnp.sum(slab[:, techs:halo], axis=0)
    mine = slab.reshape(4, regions, *sums.shape)
    mine = jnp.where(region == 0, mine[:, 0], mine[:, 1])
    message = jnp.sum(mine, axis=0)
    if sweeping:
        message = jnp.concatenate(
            [
                message[:techs],
                squares,
                mine[0, halo : halo + span],
                mine[-1, halo + span : halo + 2 * span],
                message[halo + 2 * span :],
            ],
            axis=0,
        )
    slabs = to_all(message, far)
    gathered = jnp.where(
        region == 0, jnp.stack([to_regions, other]), jnp.stack([other, to_regions])
    )
    parts = {"slabs": slabs}
    if sweeping:
        parts["places"] = mine
    return gathered, parts


def body(
    availability,
    demand,
    gen_cost,
    cap_cost,
    owner_map,
    line_ends,
    line_limit,
    cross_ends,
    cross_limit,
    pair_counts,
    store_node,
    store_energy,
    store_power,
    price_start,
):
    rows, techs, nodes = availability.shape
    hours, regions = lax.axis_size("hours"), lax.axis_size("region")
    slots = cross_limit.shape[1]
    owned = cap_cost.shape[1]
    units, lines = store_node.shape[0], line_limit.shape[0]
    total_flows = lines + units + regions * slots
    info_rows = 8 * (regions * slots // LANES)
    sizes = (hours, regions, rows, techs, nodes, slots)
    owner_rows = owner_map.reshape(hours, owned)
    energy = store_energy[None]

    def shape(*dims, dtype=jnp.float32):
        return jax.ShapeDtypeStruct(dims, dtype)

    avail_t, message, to_regions = call(
        functools.partial(setup_kernel, sizes),
        (
            availability.reshape(rows * techs, nodes),
            price_start,
            cap_cost,
            owner_rows,
            cross_ends[:, 0],
            cross_limit,
            pair_counts,
        ),
        (shape(techs, rows, nodes), shape(2 * techs, nodes), shape(rows + info_rows, nodes)),
        in_smem=(6,),
    )
    gathered, parts = exchange(to_regions, message, techs, 0)
    state = {
        "availability": avail_t,
        "demand": demand,
        "gen_cost": gen_cost,
        "store_energy": energy,
    }
    span = units // LANES
    kept = {
        "dispatch": shape(techs, rows, nodes),
        "cap_duals": shape(techs, rows, nodes),
        "flows": shape(rows, total_flows),
        "store_duals": shape(rows, units),
        "capacity": shape(techs, nodes),
        "weight": shape(1, LANES),
        "region": shape(rows + 8, nodes),
        "sums": shape((techs + 2 + 2 * span) // 8 * 8 + 8, nodes),
    }
    charges = {"charge": shape(rows, units), "charge_before": shape(1, units)}
    for iteration in range(ITERS):
        given = dict(state, **parts, gathered=gathered)
        if iteration == 0:
            given.update(
                line_ends=line_ends,
                line_limit=line_limit[None],
                store_node=store_node[None],
                store_power=store_power[None],
            )
            outs = dict(
                kept,
                col_weight=shape(techs, nodes),
                cost=shape(techs, nodes),
                maps=shape(regions * nodes, total_flows, dtype=jnp.bfloat16),
                limits=shape(1, total_flows),
            )
        else:
            outs = dict(kept, **charges)
        if iteration == ITERS - 1:
            given["owner"] = owner_rows
            outs = {
                "dispatch": shape(rows * techs, nodes),
                "capacity": shape(1, owned),
                "prices": shape(rows, nodes),
                "charge": shape(rows, units),
            }
        values = call(
            functools.partial(sweep_kernel, sizes, iteration, tuple(given), tuple(outs)),
            tuple(given.values()),
            tuple(outs.values()),
        )
        results = dict(zip(outs, values))
        if iteration == ITERS - 1:
            break
        gathered, parts = exchange(results.pop("region"), results.pop("sums"), techs, span)
        state.update(results)
    return (
        results["dispatch"].reshape(rows, techs, nodes),
        results["capacity"],
        results["prices"],
        results["charge"],
    )


def solution(mesh):
    placed = (
        P("hours", None, "region"),
        P("hours", "region"),
        P(None, "region"),
        P("region", "hours"),
        P("region", None),
        P(None, "region"),
        P("region"),
        P(None, "region", None),
        P("region", None),
        P("region", None),
        P("region"),
        P("region"),
        P("region"),
        P("hours", "region"),
    )
    return jax.shard_map(
        body,
        mesh=mesh,
        in_specs=placed,
        out_specs=(
            P("hours", None, "region"),
            P("region", "hours"),
            P("hours", "region"),
            P("hours", "region"),
        ),
        check_vma=False,
    )
```

```python
import functools

import jax
import jax.numpy as jnp
from jax import lax
from jax.experimental import pallas as pl
from jax.experimental.pallas import tpu as pltpu
from jax.sharding import PartitionSpec as P

ITERS = 4
EPSILON = 1e-06
LANES = 128
VMEM_BYTES = 24 * 1024 * 1024
SQUARES = 3


def split3(value):
    high = value.astype(jnp.bfloat16)
    rest = value - high.astype(jnp.float32)
    middle = rest.astype(jnp.bfloat16)
    low = (rest - middle.astype(jnp.float32)).astype(jnp.bfloat16)
    return jnp.concatenate([high, middle, low], axis=0)


def dot3(value, matrix, transposed):
    rows = value.shape[0]
    contract = ((1,), (1 if transposed else 0,))
    product = lax.dot_general(
        split3(value), matrix, (contract, ((), ())), preferred_element_type=jnp.float32
    )
    return product[:rows] + product[rows : 2 * rows] + product[2 * rows :]


def row_sum(value):
    return jnp.sum(value, axis=0, keepdims=True)


def fold_lanes(row):
    total = row[:, :LANES]
    for start in range(LANES, row.shape[1], LANES):
        total = total + row[:, start : start + LANES]
    return total


def owned_one_hots(owner_ref, tech_count, node_count):
    owned = owner_ref[pl.ds(lax.axis_index("hours"), 1), :]
    shape_t = (tech_count, owned.shape[1])
    shape_n = (node_count, owned.shape[1])
    tech = lax.broadcasted_iota(jnp.int32, shape_t, 0) == owned // node_count
    node = lax.broadcasted_iota(jnp.int32, shape_n, 0) == owned % node_count
    return tech, node.astype(jnp.float32).astype(jnp.bfloat16)


def incidence(start, end, count):
    node = lax.broadcasted_iota(jnp.int32, (count, start.shape[1]), 0)
    maps = (node == end).astype(jnp.float32) - (node == start).astype(jnp.float32)
    return maps.astype(jnp.bfloat16)


def halo_at(sizes):
    return sizes["techs"] + SQUARES


def sums_rows(sizes):
    return (halo_at(sizes) + 2 * sizes["units"] // LANES + 7) // 8 * 8


def write_halo(sizes, sums_ref, store_new):
    halo, span, rows = halo_at(sizes), sizes["units"] // LANES, sizes["rows"]
    for i in range(span):
        part = slice(i * LANES, (i + 1) * LANES)
        sums_ref[halo + i : halo + i + 1, :] = store_new[:1, part]
        sums_ref[halo + span + i : halo + span + i + 1, :] = store_new[rows - 1 :, part]
    used, end = halo + 2 * span, sums_rows(sizes)
    if used < end:
        sums_ref[used:end, :] = jnp.zeros((end - used, LANES), jnp.float32)


def regions_kernel(sizes, price, ends, limit, pairs_ref, region_ref, ends_ref, limit_ref, sems):
    rows, nodes, slots, regions = (sizes[name] for name in ("rows", "nodes", "slots", "regions"))
    copies = [
        pltpu.make_async_copy(ends, ends_ref, sems.at[0]),
        pltpu.make_async_copy(limit, limit_ref, sems.at[1]),
        pltpu.make_async_copy(price, region_ref.at[pl.ds(0, rows)], sems.at[2]),
    ]
    for copy in copies:
        copy.start()
    own = lax.axis_index("region")
    width = slots // regions
    slot = lax.broadcasted_iota(jnp.int32, (1, slots), 1)
    pair = slot // width
    in_use = jnp.zeros((1, slots), jnp.int32)
    for target in range(regions):
        in_use = jnp.where(pair == target, pairs_ref[0, target], in_use)
    place = lax.broadcasted_iota(jnp.int32, (slots, regions * slots), 1) == (
        own * slots + lax.broadcasted_iota(jnp.int32, (slots, regions * slots), 0)
    )
    place = place.astype(jnp.float32).astype(jnp.bfloat16)
    copies[0].wait()
    copies[1].wait()
    bound = jnp.where(slot % width < in_use, limit_ref[...], 0.0)
    start = ends_ref[0:1, :] + own * nodes
    end = ends_ref[1:2, :] + pair * nodes
    info = jnp.concatenate(
        [start.astype(jnp.float32), end.astype(jnp.float32), bound, jnp.zeros((13, slots), jnp.float32)],
        axis=0,
    )
    info = dot3(info, place, False)
    for chunk in range(regions * slots // LANES):
        region_ref[rows + 8 * chunk : rows + 8 * chunk + 8, :] = info[
            :8, chunk * LANES : (chunk + 1) * LANES
        ]
    copies[2].wait()


def start_kernel(sizes, sources, outs, *refs):
    given = dict(zip(sources, refs[: len(sources)]))
    gives = dict(zip(outs, refs[len(sources) : len(sources) + len(outs)]))
    held = dict(zip(START_SCRATCH, refs[len(sources) + len(outs) : -1]))
    sems = refs[-1]
    targets = {name: gives[name] if name in gives else held[name] for name in sources}
    copies = {
        name: pltpu.make_async_copy(given[name], targets[name], sems.at[i])
        for i, name in enumerate(sources)
    }
    for copy in copies.values():
        copy.start()
    rows, techs, nodes = sizes["rows"], sizes["techs"], sizes["nodes"]
    lines = sizes["lines"]
    for name in ("line_ends", "store_node", "line_limit", "store_power", "price"):
        copies[name].wait()
    line_ends, stores = held["line_ends"][...], held["store_node"][...]
    start = jnp.concatenate([line_ends[0:1], jnp.full_like(stores, -1)], axis=1)
    end = jnp.concatenate([line_ends[1:2], stores], axis=1)
    maps = incidence(start, end, nodes)
    limits = jnp.concatenate([held["line_limit"][...], held["store_power"][...]], axis=1)
    gives["maps_local"][...] = maps
    gives["limits_local"][...] = limits
    prices = held["price"][...]
    flows = jnp.clip(-0.5 * dot3(prices, maps, False), -limits, limits)
    gives["flows_local"][...] = flows
    store_new = (1.0 / 3.0) * (2.0 * flows[:, lines:])
    gives["store_duals"][...] = store_new
    primal_row = fold_lanes(row_sum(flows * flows))
    dual_row = fold_lanes(row_sum(store_new * store_new))
    balance = dot3(2.0 * flows, maps, True)
    copies["demand"].wait()
    balance = balance - gives["demand"][...]
    copies["gen_cost"].wait()
    gen_cost = gives["gen_cost"][...]
    copies["availability"].wait()
    acc = jnp.zeros((rows, nodes), jnp.float32)
    weights = jnp.zeros((techs, nodes), jnp.float32)
    for hour in range(rows):
        weights = weights + held["availability"][hour * techs : (hour + 1) * techs, :]
    for tech in range(techs):
        avail = held["availability"][pl.ds(tech, rows, stride=techs), :]
        gives["available"][tech] = avail
        dispatch = jnp.maximum(-0.5 * (gen_cost[tech : tech + 1] + prices), 0.0)
        gives["dispatch"][tech] = dispatch
        dispatch_bar = 2.0 * dispatch
        balance = balance + dispatch_bar
        duals = jnp.maximum(0.5 * dispatch_bar, 0.0)
        acc = acc + dispatch * dispatch
        gives["sums"][tech : tech + 1, :] = row_sum(avail * duals)
    gives["balance"][...] = balance
    squares = row_sum(acc)
    copies["cap_cost"].wait()
    copies["owner"].wait()
    cost = held["cap_cost"][...]
    negative = jnp.sum((cost < 0.0).astype(jnp.float32), axis=1, keepdims=True)
    write_halo(sizes, gives["sums"], store_new)
    gives["sums"][techs : techs + SQUARES, :] = jnp.concatenate(
        [primal_row + squares, dual_row + squares, jnp.broadcast_to(negative, (1, LANES))], axis=0
    )
    tech_hot, node_hot = owned_one_hots(gives["owner"], techs, nodes)
    first = sums_rows(sizes)
    gives["sums"][first : first + techs, :] = weights
    gives["sums"][first + techs : first + 2 * techs, :] = dot3(
        jnp.where(tech_hot, cost, 0.0), node_hot, True
    )
    for name in ("store_energy",):
        copies[name].wait()


START_SCRATCH = (
    "availability",
    "price",
    "cap_cost",
    "line_ends",
    "line_limit",
    "store_node",
    "store_power",
)


def close_kernel(
    sizes,
    gathered,
    balance_ref,
    sums_in_ref,
    maps_ref,
    limits_ref,
    flows_ref,
    region_ref,
    sums_ref,
):
    rows, techs, nodes, slots, regions = (
        sizes[name] for name in ("rows", "techs", "nodes", "slots", "regions")
    )
    own = lax.axis_index("region")
    chunks = []
    for chunk in range(regions * slots // LANES):
        at = slice(rows + 8 * chunk, rows + 8 * chunk + 8)
        part = gathered[0, at, :]
        for region in range(1, regions):
            part = part + gathered[region, at, :]
        chunks.append(part)
    info = jnp.concatenate(chunks, axis=1) if len(chunks) > 1 else chunks[0]
    maps_ref[...] = incidence(
        info[0:1].astype(jnp.int32), info[1:2].astype(jnp.int32), regions * nodes
    )
    limits = info[2:3]
    limits_ref[...] = limits
    prices_all = jnp.concatenate([gathered[region, :rows, :] for region in range(regions)], axis=1)
    flows = jnp.clip(-0.5 * dot3(prices_all, maps_ref[...], False), -limits, limits)
    flows_ref[...] = flows
    maps_own = maps_ref[pl.ds(pl.multiple_of(own * nodes, nodes), nodes), :]
    balance = balance_ref[...] + dot3(2.0 * flows, maps_own, True)
    step_up = (1.0 / (techs + 8.0)) * balance
    region_ref[:rows, :] = gathered[own, :rows, :] + step_up
    change = row_sum(flows * flows)
    slot = lax.broadcasted_iota(jnp.int32, change.shape, 1)
    primal = fold_lanes(jnp.where(slot // slots == own, change, 0.0))
    more = jnp.concatenate(
        [primal, row_sum(step_up * step_up), jnp.zeros((SQUARES - 2, LANES), jnp.float32)], axis=0
    )
    sums_ref[...] = sums_in_ref[...]
    squares = sums_in_ref[techs : techs + SQUARES, :] + more
    sums_ref[techs : techs + SQUARES, :] = squares
    region_ref[rows:, :] = jnp.concatenate(
        [squares, jnp.zeros((8 - SQUARES, LANES), jnp.float32)], axis=0
    )


def neighbour_rows(sizes, given, hour_index):
    span = sizes["units"] // LANES

    def row_of(name, offset):
        return jnp.concatenate(
            [given[name][offset + i : offset + i + 1, :] for i in range(span)], axis=1
        )

    if "totals" in given:
        return row_of("next_row", 0), row_of("prev_row", 0)
    first = halo_at(sizes)
    last = first + span
    core, x_place, slab = hour_index % 2, hour_index // 2 % 2, hour_index // 4 % 2
    next_row = jnp.where(slab == 0, row_of("near", first), row_of("far", first))
    prev_row = jnp.where(slab == 0, row_of("far", last), row_of("near", last))
    next_row = jnp.where(x_place == 0, row_of("across", first), next_row)
    prev_row = jnp.where(x_place == 0, prev_row, row_of("across", last))
    next_row = jnp.where(core == 0, row_of("partner", first), next_row)
    prev_row = jnp.where(core == 0, prev_row, row_of("partner", last))
    return next_row, prev_row


def total_of(parts):
    if "totals" in parts:
        return parts["totals"][...]
    return (parts["slab"][...] + parts["near"][...]) + (parts["middle"][...] + parts["far"][...])


def sweep_kernel(sizes, iteration, names_in, names_out, *refs):
    rows, techs, nodes, slots, regions, lines, units = (
        sizes[name] for name in ("rows", "techs", "nodes", "slots", "regions", "lines", "units")
    )
    second = iteration == 1
    last = iteration == ITERS - 1
    given = dict(zip(names_in, refs[: len(names_in)]))
    gives = dict(zip(names_out, refs[len(names_in) :]))
    own = lax.axis_index("region")
    hour_index = lax.axis_index("hours")
    gathered = given["gathered"]

    sums = total_of(given)
    squares = jnp.sum(sums[techs : techs + 2], axis=1, keepdims=True)
    old_weight = jnp.ones((1, 1), jnp.float32) if second else given["weight"][...][:, :1]
    weight = jnp.sqrt(
        old_weight * jnp.sqrt((squares[1:2] + EPSILON) / (squares[0:1] + EPSILON))
    )
    primal_step = 0.5 / weight
    if second:
        first = sums_rows(sizes)
        col_weight, cost = sums[first : first + techs], sums[first + techs : first + 2 * techs]
        gives["col_weight"][...] = col_weight
        gives["cost"][...] = cost
        capacity = jnp.maximum(-cost / col_weight, 0.0)
        first_bar = 2.0 * capacity
    else:
        col_weight, cost = given["col_weight"][...], given["cost"][...]
        capacity = given["capacity"][...]
    capacity_new = jnp.maximum(capacity - (cost - sums[:techs]) / (weight * col_weight), 0.0)
    capacity_bar = 2.0 * capacity_new - capacity

    prices_all = jnp.concatenate([gathered[region, :rows, :] for region in range(regions)], axis=1)
    prices = gathered[own, :rows, :]
    maps_local = given["maps_local"][...]
    slope_local = dot3(prices, maps_local, False)
    slope_cross = dot3(prices_all, given["maps_cross"][...], False)

    energy = given["store_energy"][...]
    row_id = lax.broadcasted_iota(jnp.int32, (rows, units), 0)
    next_row, prev_row = neighbour_rows(sizes, given, hour_index)
    store_duals = given["store_duals"][...]
    next_duals = jnp.where(row_id == rows - 1, next_row, pltpu.roll(store_duals, rows - 1, 0))
    if second:
        charge = jnp.zeros((rows, units), jnp.float32)
        charge_before = jnp.zeros((1, units), jnp.float32)
    else:
        charge = given["charge"][...]
        charge_before = given["charge_before"][...]
    charge_new = jnp.clip(charge - primal_step * (store_duals - next_duals), 0.0, energy)
    gives["charge"][...] = charge_new

    primal_row = jnp.zeros((1, LANES), jnp.float32)
    bars = []
    for name, slope, low, high in (
        ("flows_local", slope_local, 0, lines),
        ("flows_local", slope_local, lines, lines + units),
        ("flows_cross", slope_cross, 0, regions * slots),
    ):
        slope = slope[:, low:high]
        if low:
            slope = slope + store_duals
        bound = given[name.replace("flows", "limits")][:, low:high]
        old = given[name][:, low:high]
        new = jnp.clip(old - primal_step * slope, -bound, bound)
        bars.append(2.0 * new - old)
        if not last:
            gives[name][:, low:high] = new
            change = row_sum((new - old) ** 2)
            if name == "flows_cross":
                slot = lax.broadcasted_iota(jnp.int32, change.shape, 1)
                change = jnp.where(slot // slots == own, change, 0.0)
            primal_row = primal_row + fold_lanes(change)
    maps_own = given["maps_cross"][pl.ds(pl.multiple_of(own * nodes, nodes), nodes), :]
    balance = dot3(jnp.concatenate(bars[:2], axis=1), maps_local, True) - given["demand"][...]
    balance = balance + dot3(bars[2], maps_own, True)

    gen_cost = given["gen_cost"][...]
    half_weight = weight / 2.0
    primal_acc = jnp.zeros((rows, nodes), jnp.float32)
    dual_acc = jnp.zeros((rows, nodes), jnp.float32)
    for tech in range(techs):
        slope = gen_cost[tech : tech + 1] + prices
        dispatch = given["dispatch"][tech]
        avail = given["available"][tech]
        if second:
            duals = jnp.maximum(0.5 * (2.0 * dispatch - avail * first_bar[tech : tech + 1]), 0.0)
        else:
            duals = given["cap_duals"][tech]
        dispatch_new = jnp.maximum(dispatch - primal_step * (slope + duals), 0.0)
        dispatch_bar = 2.0 * dispatch_new - dispatch
        balance = balance + dispatch_bar
        if last:
            gives["dispatch"][pl.ds(tech, rows, stride=techs), :] = dispatch_new
            continue
        gives["dispatch"][tech] = dispatch_new
        cap_rows = dispatch_bar - avail * capacity_bar[tech : tech + 1]
        primal_acc = primal_acc + (dispatch_new - dispatch) ** 2
        duals_new = jnp.maximum(duals + half_weight * cap_rows, 0.0)
        dual_acc = dual_acc + (duals_new - duals) ** 2
        gives["cap_duals"][tech] = duals_new
        gives["sums"][tech : tech + 1, :] = row_sum(avail * duals_new)

    step_up = weight / (techs + 8.0) * balance
    if last:
        gives["prices"][...] = prices + step_up
        tech_hot, node_hot = owned_one_hots(given["owner"], techs, nodes)
        chosen = dot3(capacity_new, node_hot, False)
        gives["capacity"][...] = row_sum(jnp.where(tech_hot, chosen, 0.0))
        return
    gives["region"][:rows, :] = prices + step_up
    gives["weight"][...] = jnp.broadcast_to(weight, (1, LANES))
    gives["capacity"][...] = capacity_new
    charge_bar = 2.0 * charge_new - charge
    before_new = jnp.clip(charge_before - primal_step * (prev_row - store_duals[0:1]), 0.0, energy)
    gives["charge_before"][...] = before_new
    before_bar = 2.0 * before_new - charge_before
    shifted_bar = jnp.where(row_id == 0, before_bar, pltpu.roll(charge_bar, 1, 0))
    store_step = weight / 3.0 * (charge_bar - shifted_bar + bars[1])
    store_new = store_duals + store_step
    gives["store_duals"][...] = store_new
    primal_row = primal_row + row_sum(primal_acc) + fold_lanes(row_sum((charge_new - charge) ** 2))
    primal_row = primal_row + jnp.where(
        hour_index == 0, row_sum((capacity_new - capacity) ** 2), 0.0
    )
    dual_row = row_sum(dual_acc + step_up * step_up) + fold_lanes(row_sum(store_step * store_step))
    squares = jnp.concatenate(
        [primal_row, dual_row, jnp.zeros((SQUARES - 2, LANES), jnp.float32)], axis=0
    )
    gives["region"][rows:, :] = jnp.concatenate(
        [squares, jnp.zeros((8 - SQUARES, LANES), jnp.float32)], axis=0
    )
    gives["sums"][techs : techs + SQUARES, :] = squares
    write_halo(sizes, gives["sums"], store_new)


def call(kernel, arguments, shapes, scratch=(), spaces=None, cost=None):
    spaces = spaces or [pltpu.VMEM] * len(arguments)
    return pl.pallas_call(
        kernel,
        out_shape=shapes,
        in_specs=[pl.BlockSpec(memory_space=space) for space in spaces],
        out_specs=[pl.BlockSpec(memory_space=pltpu.VMEM)] * len(shapes),
        scratch_shapes=scratch,
        cost_estimate=cost,
        compiler_params=pltpu.CompilerParams(vmem_limit_bytes=VMEM_BYTES),
    )(*arguments)


def swap(value, hour_bit, region_bit):
    hours, regions = lax.axis_size("hours"), lax.axis_size("region")
    pairs = [
        (hour * regions + region, (hour ^ hour_bit) * regions + (region ^ region_bit))
        for hour in range(hours)
        for region in range(regions)
    ]
    return lax.ppermute(value, ("hours", "region"), pairs)


def shifted(value, steps):
    count = lax.axis_size("hours")
    return lax.ppermute(value, "hours", [(i, (i + steps) % count) for i in range(count)])


def both_regions(block):
    if lax.axis_size("region") != 2:
        return lax.all_gather(block, "region")
    return in_order(block, swap(block, 0, 1))


def in_order(block, other):
    return jnp.where(
        lax.axis_index("region") == 0, jnp.stack([block, other]), jnp.stack([other, block])
    )


def exchange(sizes, block, sums):
    hours, regions = lax.axis_size("hours"), lax.axis_size("region")
    techs, rows, span = sizes["techs"], sizes["rows"], sizes["units"] // LANES
    halo = halo_at(sizes)
    if regions != 2 or hours != 16:
        gathered = lax.all_gather(block, "region")
        squares = jnp.sum(gathered[:, rows : rows + SQUARES], axis=0)
        totals = lax.psum(sums.at[techs:halo].set(squares), "hours")
        next_row = shifted(sums[halo : halo + span], -1)
        prev_row = shifted(sums[halo + span : halo + 2 * span], 1)
        return gathered, {"totals": totals, "next_row": next_row, "prev_row": prev_row}

    def merged(mine, yours, mine_first):
        row = lax.broadcasted_iota(jnp.int32, mine.shape, 0)
        keep = jnp.where(row < halo + span, mine_first, jnp.logical_not(mine_first))
        edge = (row >= halo) & (row < halo + 2 * span)
        return jnp.where(edge, jnp.where(keep, mine, yours), mine + yours)

    hour = lax.axis_index("hours")
    partner = swap(sums, 1, 0)
    chip = merged(sums, partner, hour % 2 == 0)
    across = swap(chip, 2, 0)
    other = swap(block.at[rows : rows + SQUARES].set(chip[techs:halo]), 0, 1)
    diagonal = swap(chip[techs:halo], 2, 1)
    slab = merged(chip, across, hour // 2 % 2 == 0)
    slab = slab.at[techs:halo].add(other[rows : rows + SQUARES] + diagonal)
    near, middle, far = [swap(slab, 4 * step, 0) for step in (1, 2, 3)]
    parts = {"slab": slab, "near": near, "middle": middle, "far": far}
    parts.update(partner=partner, across=across)
    return in_order(block, other), parts


def body(
    availability,
    demand,
    gen_cost,
    cap_cost,
    owner_map,
    line_ends,
    line_limit,
    cross_ends,
    cross_limit,
    pair_counts,
    store_node,
    store_energy,
    store_power,
    price_start,
):
    rows, techs, nodes = availability.shape
    hours, regions = lax.axis_size("hours"), lax.axis_size("region")
    slots, owned = cross_limit.shape[1], cap_cost.shape[1]
    units, lines = store_node.shape[0], line_limit.shape[0]
    sizes = dict(
        rows=rows, techs=techs, nodes=nodes, regions=regions, slots=slots, lines=lines, units=units
    )
    cross = regions * slots
    info_rows = 8 * (cross // LANES)

    def shape(*dims, dtype=jnp.float32):
        return jax.ShapeDtypeStruct(dims, dtype)

    def scratch_like(array):
        return pltpu.VMEM(array.shape, array.dtype)

    ends = cross_ends[:, 0]
    (block,) = call(
        functools.partial(regions_kernel, sizes),
        (price_start, ends, cross_limit, pair_counts),
        (shape(rows + info_rows, nodes),),
        scratch=[scratch_like(ends), scratch_like(cross_limit), pltpu.SemaphoreType.DMA((3,))],
        spaces=[pltpu.HBM] * 3 + [pltpu.SMEM],
    )
    gathered = both_regions(block)

    sources = {
        "line_ends": line_ends,
        "store_node": store_node[None],
        "line_limit": line_limit[None],
        "store_power": store_power[None],
        "price": price_start,
        "demand": demand,
        "gen_cost": gen_cost,
        "availability": availability.reshape(rows * techs, nodes),
        "cap_cost": cap_cost,
        "owner": owner_map.reshape(hours, owned),
        "store_energy": store_energy[None],
    }
    outs = {
        "demand": shape(rows, nodes),
        "gen_cost": shape(techs, nodes),
        "owner": shape(hours, owned, dtype=jnp.int32),
        "store_energy": shape(1, units),
        "available": shape(techs, rows, nodes),
        "maps_local": shape(nodes, lines + units, dtype=jnp.bfloat16),
        "limits_local": shape(1, lines + units),
        "flows_local": shape(rows, lines + units),
        "store_duals": shape(rows, units),
        "dispatch": shape(techs, rows, nodes),
        "balance": shape(rows, nodes),
        "sums": shape(sums_rows(sizes) + 2 * techs, nodes),
    }
    values = call(
        functools.partial(start_kernel, sizes, tuple(sources), tuple(outs)),
        tuple(sources.values()),
        tuple(outs.values()),
        scratch=[scratch_like(sources[name]) for name in START_SCRATCH]
        + [pltpu.SemaphoreType.DMA((len(sources),))],
        spaces=[pltpu.HBM] * len(sources),
        cost=pl.CostEstimate(flops=10**7, bytes_accessed=4 * 10**6, transcendentals=0),
    )
    state = dict(zip(outs, values))
    sums = state.pop("sums")
    closed = call(
        functools.partial(close_kernel, sizes),
        (gathered, state.pop("balance"), sums),
        (
            shape(regions * nodes, cross, dtype=jnp.bfloat16),
            shape(1, cross),
            shape(rows, cross),
            shape(rows + 8, nodes),
            shape(*sums.shape),
        ),
    )
    state.update(zip(("maps_cross", "limits_cross", "flows_cross"), closed))
    block, sums = closed[3:]
    gathered, parts = exchange(sizes, block, sums)

    def again(parts):
        totals = total_of(parts)
        first = sums_rows(sizes)
        col_weight, cost = totals[first : first + techs], totals[first + techs :]
        capacity = jnp.maximum(-cost / col_weight, 0.0)
        taken = state["dispatch"]
        rows_of = 2.0 * taken - state["available"] * (2.0 * capacity)[:, None, :]
        duals = jnp.maximum(0.5 * rows_of, 0.0)
        own = jnp.where(lax.axis_index("hours") == 0, jnp.sum(capacity**2, axis=0), 0.0)
        fixed = sums.at[:techs].set(jnp.sum(state["available"] * duals, axis=1))
        fixed = fixed.at[techs].add(own)
        fixed = fixed.at[techs + 1].add(jnp.sum(duals**2 - taken**2, axis=(0, 1)))
        blocks = block.at[rows : rows + SQUARES].set(fixed[techs : techs + SQUARES])
        return exchange(sizes, blocks, fixed)[1]

    negative = total_of(parts)[techs + 2, 0]
    parts = lax.cond(negative > 0.0, again, lambda parts: parts, parts)

    for iteration in range(1, ITERS):
        given = dict(state, **parts, gathered=gathered)
        if iteration < ITERS - 1:
            given.pop("owner")
            outs = {
                "dispatch": shape(techs, rows, nodes),
                "cap_duals": shape(techs, rows, nodes),
                "flows_local": shape(rows, lines + units),
                "flows_cross": shape(rows, cross),
                "store_duals": shape(rows, units),
                "capacity": shape(techs, nodes),
                "weight": shape(1, LANES),
                "charge": shape(rows, units),
                "charge_before": shape(1, units),
                "region": shape(rows + 8, nodes),
                "sums": shape(sums_rows(sizes), nodes),
            }
            if iteration == 1:
                outs.update(col_weight=shape(techs, nodes), cost=shape(techs, nodes))
        else:
            outs = {
                "dispatch": shape(rows * techs, nodes),
                "capacity": shape(1, owned),
                "prices": shape(rows, nodes),
                "charge": shape(rows, units),
            }
        values = call(
            functools.partial(sweep_kernel, sizes, iteration, tuple(given), tuple(outs)),
            tuple(given.values()),
            tuple(outs.values()),
        )
        results = dict(zip(outs, values))
        if iteration < ITERS - 1:
            gathered, parts = exchange(sizes, results.pop("region"), results.pop("sums"))
            state.update(results)
    return (
        results["dispatch"].reshape(rows, techs, nodes),
        results["capacity"],
        results["prices"],
        results["charge"],
    )


def solution(mesh):
    placed = (
        P("hours", None, "region"),
        P("hours", "region"),
        P(None, "region"),
        P("region", "hours"),
        P("region", None),
        P(None, "region"),
        P("region"),
        P(None, "region", None),
        P("region", None),
        P("region", None),
        P("region"),
        P("region"),
        P("region"),
        P("hours", "region"),
    )
    return jax.shard_map(
        body,
        mesh=mesh,
        in_specs=placed,
        out_specs=(
            P("hours", None, "region"),
            P("region", "hours"),
            P("hours", "region"),
            P("hours", "region"),
        ),
        check_vma=False,
    )
```

```python
import functools
from types import SimpleNamespace as Bag

import jax
import jax.numpy as jnp
from jax import lax
from jax.experimental import pallas as pl
from jax.experimental.pallas import tpu as pltpu
from jax.sharding import PartitionSpec as P

ITERS = 4
EPSILON = 1e-06
LANES = 128
VMEM_BYTES = 24 * 1024 * 1024
SQUARES = 3


def split3(value):
    high = value.astype(jnp.bfloat16)
    rest = value - high.astype(jnp.float32)
    middle = rest.astype(jnp.bfloat16)
    low = (rest - middle.astype(jnp.float32)).astype(jnp.bfloat16)
    return jnp.concatenate([high, middle, low], axis=0)


def dot3(value, matrix, transposed):
    rows = value.shape[0]
    contract = ((1,), (1 if transposed else 0,))
    product = lax.dot_general(
        split3(value), matrix, (contract, ((), ())), preferred_element_type=jnp.float32
    )
    return product[:rows] + product[rows : 2 * rows] + product[2 * rows :]


def row_sum(value):
    return jnp.sum(value, axis=0, keepdims=True)


def fold_lanes(row):
    total = row[:, :LANES]
    for start in range(LANES, row.shape[1], LANES):
        total = total + row[:, start : start + LANES]
    return total


def owned_one_hots(owner_ref, tech_count, node_count):
    owned = owner_ref[pl.ds(lax.axis_index("hours"), 1), :]
    shape_t = (tech_count, owned.shape[1])
    shape_n = (node_count, owned.shape[1])
    tech = lax.broadcasted_iota(jnp.int32, shape_t, 0) == owned // node_count
    node = lax.broadcasted_iota(jnp.int32, shape_n, 0) == owned % node_count
    return tech, node.astype(jnp.float32).astype(jnp.bfloat16)


def incidence(start, end, count):
    node = lax.broadcasted_iota(jnp.int32, (count, start.shape[1]), 0)
    maps = (node == end).astype(jnp.float32) - (node == start).astype(jnp.float32)
    return maps.astype(jnp.bfloat16)


def halo_at(sizes):
    return sizes.techs + SQUARES


def sums_rows(sizes):
    return (halo_at(sizes) + 2 * sizes.units // LANES + 7) // 8 * 8


def write_halo(sizes, sums_ref, store_new):
    halo, span, rows = halo_at(sizes), sizes.units // LANES, sizes.rows
    for i in range(span):
        part = slice(i * LANES, (i + 1) * LANES)
        sums_ref[halo + i : halo + i + 1, :] = store_new[:1, part]
        sums_ref[halo + span + i : halo + span + i + 1, :] = store_new[rows - 1 :, part]
    used, end = halo + 2 * span, sums_rows(sizes)
    if used < end:
        sums_ref[used:end, :] = jnp.zeros((end - used, LANES), jnp.float32)


def slots_kernel(sizes, ends_ref, limit_ref, pairs_ref, info_ref):
    nodes, slots, regions = sizes.nodes, sizes.slots, sizes.regions
    own = lax.axis_index("region")
    width = slots // regions
    slot = lax.broadcasted_iota(jnp.int32, (1, slots), 1)
    pair = slot // width
    in_use = jnp.zeros((1, slots), jnp.int32)
    for target in range(regions):
        in_use = jnp.where(pair == target, pairs_ref[0, target], in_use)
    place = lax.broadcasted_iota(jnp.int32, (slots, regions * slots), 1) == (
        own * slots + lax.broadcasted_iota(jnp.int32, (slots, regions * slots), 0)
    )
    place = place.astype(jnp.float32).astype(jnp.bfloat16)
    bound = jnp.where(slot % width < in_use, limit_ref[...], 0.0)
    start = (ends_ref[0:1, :] + own * nodes).astype(jnp.float32)
    end = (ends_ref[1:2, :] + pair * nodes).astype(jnp.float32)
    rest = jnp.zeros((13, slots), jnp.float32)
    info = dot3(jnp.concatenate([start, end, bound, rest], axis=0), place, False)
    for chunk in range(regions * slots // LANES):
        info_ref[8 * chunk : 8 * chunk + 8, :] = info[:8, chunk * LANES : (chunk + 1) * LANES]


def start_kernel(sizes, names_in, names_out, *refs):
    given = Bag(**dict(zip(names_in, refs[: len(names_in)])))
    gives = Bag(**dict(zip(names_out, refs[len(names_in) :])))
    rows, techs, nodes, lines = sizes.rows, sizes.techs, sizes.nodes, sizes.lines
    gives.demand[...] = given.demand[...]
    gives.gen_cost[...] = given.gen_cost[...]
    gives.owner[...] = given.owner[...]
    gives.store_energy[...] = given.store_energy[...]
    line_ends, stores = given.line_ends[...], given.store_node[...]
    start = jnp.concatenate([line_ends[0:1], jnp.full_like(stores, -1)], axis=1)
    end = jnp.concatenate([line_ends[1:2], stores], axis=1)
    maps = incidence(start, end, nodes)
    limits = jnp.concatenate([given.line_limit[...], given.store_power[...]], axis=1)
    gives.maps_local[...] = maps
    gives.limits_local[...] = limits
    prices = given.price[...]
    flows = jnp.clip(-0.5 * dot3(prices, maps, False), -limits, limits)
    gives.flows_local[...] = flows
    store_new = (1.0 / 3.0) * (2.0 * flows[:, lines:])
    gives.store_duals[...] = store_new
    primal_row = fold_lanes(row_sum(flows * flows))
    dual_row = fold_lanes(row_sum(store_new * store_new))
    balance = dot3(2.0 * flows, maps, True) - given.demand[...]
    gen_cost = given.gen_cost[...]
    acc = jnp.zeros((rows, nodes), jnp.float32)
    weights = jnp.zeros((techs, nodes), jnp.float32)
    for hour in range(rows):
        weights = weights + given.availability[hour * techs : (hour + 1) * techs, :]
    for tech in range(techs):
        avail = given.availability[pl.ds(tech, rows, stride=techs), :]
        gives.available[tech] = avail
        dispatch = jnp.maximum(-0.5 * (gen_cost[tech : tech + 1] + prices), 0.0)
        gives.dispatch[tech] = dispatch
        dispatch_bar = 2.0 * dispatch
        balance = balance + dispatch_bar
        duals = jnp.maximum(0.5 * dispatch_bar, 0.0)
        acc = acc + dispatch * dispatch
        gives.sums[tech : tech + 1, :] = row_sum(avail * duals)
    gives.balance[...] = balance
    squares = row_sum(acc)
    cost = given.cap_cost[...]
    negative = jnp.sum((cost < 0.0).astype(jnp.float32), axis=1, keepdims=True)
    write_halo(sizes, gives.sums, store_new)
    gives.sums[techs : techs + SQUARES, :] = jnp.concatenate(
        [primal_row + squares, dual_row + squares, jnp.broadcast_to(negative, (1, LANES))], axis=0
    )
    tech_hot, node_hot = owned_one_hots(given.owner, techs, nodes)
    first = sums_rows(sizes)
    gives.sums[first : first + techs, :] = weights
    gives.sums[first + techs : first + 2 * techs, :] = dot3(
        jnp.where(tech_hot, cost, 0.0), node_hot, True
    )


def close_kernel(
    sizes,
    gathered,
    info_ref,
    balance_ref,
    sums_in_ref,
    maps_ref,
    limits_ref,
    flows_ref,
    region_ref,
    sums_ref,
):
    rows, techs, nodes = sizes.rows, sizes.techs, sizes.nodes
    slots, regions = sizes.slots, sizes.regions
    own = lax.axis_index("region")
    chunks = []
    for chunk in range(regions * slots // LANES):
        at = slice(8 * chunk, 8 * chunk + 8)
        part = info_ref[0, at, :]
        for region in range(1, regions):
            part = part + info_ref[region, at, :]
        chunks.append(part)
    info = jnp.concatenate(chunks, axis=1) if len(chunks) > 1 else chunks[0]
    maps_ref[...] = incidence(
        info[0:1].astype(jnp.int32), info[1:2].astype(jnp.int32), regions * nodes
    )
    limits = info[2:3]
    limits_ref[...] = limits
    prices_all = jnp.concatenate([gathered[region, :rows, :] for region in range(regions)], axis=1)
    flows = jnp.clip(-0.5 * dot3(prices_all, maps_ref[...], False), -limits, limits)
    flows_ref[...] = flows
    maps_own = maps_ref[pl.ds(pl.multiple_of(own * nodes, nodes), nodes), :]
    balance = balance_ref[...] + dot3(2.0 * flows, maps_own, True)
    step_up = (1.0 / (techs + 8.0)) * balance
    region_ref[:rows, :] = gathered[own, :rows, :] + step_up
    change = row_sum(flows * flows)
    slot = lax.broadcasted_iota(jnp.int32, change.shape, 1)
    primal = fold_lanes(jnp.where(slot // slots == own, change, 0.0))
    more = jnp.concatenate(
        [primal, row_sum(step_up * step_up), jnp.zeros((SQUARES - 2, LANES), jnp.float32)], axis=0
    )
    sums_ref[...] = sums_in_ref[...]
    squares = sums_in_ref[techs : techs + SQUARES, :] + more
    sums_ref[techs : techs + SQUARES, :] = squares
    region_ref[rows:, :] = jnp.concatenate(
        [squares, jnp.zeros((8 - SQUARES, LANES), jnp.float32)], axis=0
    )


def neighbour_rows(sizes, given, hour_index):
    span = sizes.units // LANES

    def row_of(ref, offset):
        return jnp.concatenate([ref[offset + i : offset + i + 1, :] for i in range(span)], axis=1)

    if hasattr(given, "totals"):
        return row_of(given.next_row, 0), row_of(given.prev_row, 0)
    first = halo_at(sizes)
    last = first + span
    core, x_place, slab = hour_index % 2, hour_index // 2 % 2, hour_index // 4 % 2
    next_row = jnp.where(slab == 0, row_of(given.near, first), row_of(given.far, first))
    prev_row = jnp.where(slab == 0, row_of(given.far, last), row_of(given.near, last))
    next_row = jnp.where(x_place == 0, row_of(given.across, first), next_row)
    prev_row = jnp.where(x_place == 0, prev_row, row_of(given.across, last))
    next_row = jnp.where(core == 0, row_of(given.partner, first), next_row)
    prev_row = jnp.where(core == 0, prev_row, row_of(given.partner, last))
    return next_row, prev_row


def total_of(parts):
    if hasattr(parts, "totals"):
        return parts.totals[...]
    return (parts.slab[...] + parts.near[...]) + (parts.middle[...] + parts.far[...])


def sweep_kernel(sizes, iteration, names_in, names_out, *refs):
    rows, techs, nodes = sizes.rows, sizes.techs, sizes.nodes
    slots, regions, lines, units = sizes.slots, sizes.regions, sizes.lines, sizes.units
    second = iteration == 1
    last = iteration == ITERS - 1
    given = Bag(**dict(zip(names_in, refs[: len(names_in)])))
    gives = Bag(**dict(zip(names_out, refs[len(names_in) :])))
    own = lax.axis_index("region")
    hour_index = lax.axis_index("hours")
    gathered = given.gathered

    sums = total_of(given)
    squares = jnp.sum(sums[techs : techs + 2], axis=1, keepdims=True)
    old_weight = jnp.ones((1, 1), jnp.float32) if second else given.weight[...][:, :1]
    weight = jnp.sqrt(
        old_weight * jnp.sqrt((squares[1:2] + EPSILON) / (squares[0:1] + EPSILON))
    )
    primal_step = 0.5 / weight
    if second:
        first = sums_rows(sizes)
        col_weight, cost = sums[first : first + techs], sums[first + techs : first + 2 * techs]
        gives.col_weight[...] = col_weight
        gives.cost[...] = cost
        gives.negative[...] = sums[techs + 2 : techs + 3]
        capacity = jnp.maximum(-cost / col_weight, 0.0)
        first_bar = 2.0 * capacity
    else:
        col_weight, cost = given.col_weight[...], given.cost[...]
        capacity = given.capacity[...]
    capacity_new = jnp.maximum(capacity - (cost - sums[:techs]) / (weight * col_weight), 0.0)
    capacity_bar = 2.0 * capacity_new - capacity

    prices_all = jnp.concatenate([gathered[region, :rows, :] for region in range(regions)], axis=1)
    prices = gathered[own, :rows, :]
    maps_local = given.maps_local[...]
    slope_local = dot3(prices, maps_local, False)
    slope_cross = dot3(prices_all, given.maps_cross[...], False)

    energy = given.store_energy[...]
    row_id = lax.broadcasted_iota(jnp.int32, (rows, units), 0)
    next_row, prev_row = neighbour_rows(sizes, given, hour_index)
    store_duals = given.store_duals[...]
    next_duals = jnp.where(row_id == rows - 1, next_row, pltpu.roll(store_duals, rows - 1, 0))
    if second:
        charge = jnp.zeros((rows, units), jnp.float32)
        charge_before = jnp.zeros((1, units), jnp.float32)
    else:
        charge = given.charge[...]
        charge_before = given.charge_before[...]
    charge_new = jnp.clip(charge - primal_step * (store_duals - next_duals), 0.0, energy)
    gives.charge[...] = charge_new

    primal_row = jnp.zeros((1, LANES), jnp.float32)
    bars = []
    local_out = None if last else gives.flows_local
    cross_out = None if last else gives.flows_cross
    for flows, out, limits, slope, low, high in (
        (given.flows_local, local_out, given.limits_local, slope_local, 0, lines),
        (given.flows_local, local_out, given.limits_local, slope_local, lines, lines + units),
        (given.flows_cross, cross_out, given.limits_cross, slope_cross, 0, regions * slots),
    ):
        slope = slope[:, low:high]
        if low:
            slope = slope + store_duals
        bound = limits[:, low:high]
        old = flows[:, low:high]
        new = jnp.clip(old - primal_step * slope, -bound, bound)
        bars.append(2.0 * new - old)
        if not last:
            out[:, low:high] = new
            change = row_sum((new - old) ** 2)
            if out is cross_out:
                slot = lax.broadcasted_iota(jnp.int32, change.shape, 1)
                change = jnp.where(slot // slots == own, change, 0.0)
            primal_row = primal_row + fold_lanes(change)
    maps_own = given.maps_cross[pl.ds(pl.multiple_of(own * nodes, nodes), nodes), :]
    balance = dot3(jnp.concatenate(bars[:2], axis=1), maps_local, True) - given.demand[...]
    balance = balance + dot3(bars[2], maps_own, True)

    gen_cost = given.gen_cost[...]
    half_weight = weight / 2.0
    primal_acc = jnp.zeros((rows, nodes), jnp.float32)
    dual_acc = jnp.zeros((rows, nodes), jnp.float32)
    for tech in range(techs):
        slope = gen_cost[tech : tech + 1] + prices
        dispatch = given.dispatch[tech]
        avail = given.available[tech]
        if second:
            duals = jnp.maximum(0.5 * (2.0 * dispatch - avail * first_bar[tech : tech + 1]), 0.0)
        else:
            duals = given.cap_duals[tech]
        dispatch_new = jnp.maximum(dispatch - primal_step * (slope + duals), 0.0)
        dispatch_bar = 2.0 * dispatch_new - dispatch
        balance = balance + dispatch_bar
        if last:
            gives.dispatch[pl.ds(tech, rows, stride=techs), :] = dispatch_new
            continue
        gives.dispatch[tech] = dispatch_new
        cap_rows = dispatch_bar - avail * capacity_bar[tech : tech + 1]
        primal_acc = primal_acc + (dispatch_new - dispatch) ** 2
        duals_new = jnp.maximum(duals + half_weight * cap_rows, 0.0)
        dual_acc = dual_acc + (duals_new - duals) ** 2
        gives.cap_duals[tech] = duals_new
        gives.sums[tech : tech + 1, :] = row_sum(avail * duals_new)

    step_up = weight / (techs + 8.0) * balance
    if last:
        gives.prices[...] = prices + step_up
        tech_hot, node_hot = owned_one_hots(given.owner, techs, nodes)
        chosen = dot3(capacity_new, node_hot, False)
        gives.capacity[...] = row_sum(jnp.where(tech_hot, chosen, 0.0))
        return
    gives.block[:rows, :] = prices + step_up
    gives.weight[...] = jnp.broadcast_to(weight, (1, LANES))
    gives.capacity[...] = capacity_new
    charge_bar = 2.0 * charge_new - charge
    before_new = jnp.clip(charge_before - primal_step * (prev_row - store_duals[0:1]), 0.0, energy)
    gives.charge_before[...] = before_new
    before_bar = 2.0 * before_new - charge_before
    shifted_bar = jnp.where(row_id == 0, before_bar, pltpu.roll(charge_bar, 1, 0))
    store_step = weight / 3.0 * (charge_bar - shifted_bar + bars[1])
    store_new = store_duals + store_step
    gives.store_duals[...] = store_new
    primal_row = primal_row + row_sum(primal_acc) + fold_lanes(row_sum((charge_new - charge) ** 2))
    primal_row = primal_row + jnp.where(
        hour_index == 0, row_sum((capacity_new - capacity) ** 2), 0.0
    )
    dual_row = row_sum(dual_acc + step_up * step_up) + fold_lanes(row_sum(store_step * store_step))
    squares = jnp.concatenate(
        [primal_row, dual_row, jnp.zeros((SQUARES - 2, LANES), jnp.float32)], axis=0
    )
    gives.block[rows:, :] = jnp.concatenate(
        [squares, jnp.zeros((8 - SQUARES, LANES), jnp.float32)], axis=0
    )
    gives.sums[techs : techs + SQUARES, :] = squares
    write_halo(sizes, gives.sums, store_new)


def call(kernel, given, outs, flops=0, smem=()):
    names_in, names_out = tuple(vars(given)), tuple(vars(outs))
    values = pl.pallas_call(
        functools.partial(kernel, names_in, names_out),
        out_shape=tuple(vars(outs).values()),
        in_specs=[
            pl.BlockSpec(memory_space=pltpu.SMEM if i in smem else pltpu.VMEM)
            for i in range(len(names_in))
        ],
        out_specs=[pl.BlockSpec(memory_space=pltpu.VMEM)] * len(names_out),
        cost_estimate=pl.CostEstimate(flops=flops, bytes_accessed=4 * flops, transcendentals=0),
        compiler_params=pltpu.CompilerParams(vmem_limit_bytes=VMEM_BYTES),
    )(*vars(given).values())
    return Bag(**dict(zip(names_out, values)))


def swap(value, hour_bit, region_bit):
    hours, regions = lax.axis_size("hours"), lax.axis_size("region")
    pairs = [
        (hour * regions + region, (hour ^ hour_bit) * regions + (region ^ region_bit))
        for hour in range(hours)
        for region in range(regions)
    ]
    return lax.ppermute(value, ("hours", "region"), pairs)


def shifted(value, steps):
    count = lax.axis_size("hours")
    return lax.ppermute(value, "hours", [(i, (i + steps) % count) for i in range(count)])


def both_regions(block):
    if lax.axis_size("region") != 2:
        return lax.all_gather(block, "region")
    return in_order(block, swap(block, 0, 1))


def in_order(block, other):
    return jnp.where(
        lax.axis_index("region") == 0, jnp.stack([block, other]), jnp.stack([other, block])
    )


def exchange(sizes, block, sums):
    hours, regions = lax.axis_size("hours"), lax.axis_size("region")
    techs, rows, span = sizes.techs, sizes.rows, sizes.units // LANES
    halo = halo_at(sizes)
    if regions != 2 or hours != 16:
        gathered = lax.all_gather(block, "region")
        squares = jnp.sum(gathered[:, rows : rows + SQUARES], axis=0)
        totals = lax.psum(sums.at[techs:halo].set(squares), "hours")
        next_row = shifted(sums[halo : halo + span], -1)
        prev_row = shifted(sums[halo + span : halo + 2 * span], 1)
        return gathered, Bag(totals=totals, next_row=next_row, prev_row=prev_row)

    def merged(mine, yours, mine_first):
        row = lax.broadcasted_iota(jnp.int32, mine.shape, 0)
        keep = jnp.where(row < halo + span, mine_first, jnp.logical_not(mine_first))
        edge = (row >= halo) & (row < halo + 2 * span)
        return jnp.where(edge, jnp.where(keep, mine, yours), mine + yours)

    hour = lax.axis_index("hours")
    partner = swap(sums, 1, 0)
    chip = merged(sums, partner, hour % 2 == 0)
    across = swap(chip, 2, 0)
    other = swap(block.at[rows : rows + SQUARES].set(chip[techs:halo]), 0, 1)
    diagonal = swap(chip[techs:halo], 2, 1)
    slab = merged(chip, across, hour // 2 % 2 == 0)
    slab = slab.at[techs:halo].add(other[rows : rows + SQUARES] + diagonal)
    near, middle, far = [swap(slab, 4 * step, 0) for step in (1, 2, 3)]
    parts = Bag(slab=slab, near=near, middle=middle, far=far, partner=partner, across=across)
    return in_order(block, other), parts


def shape(*dims, dtype=jnp.float32):
    return jax.ShapeDtypeStruct(dims, dtype)


def corrected(sizes, state, block, sums, parts):
    techs, rows = sizes.techs, sizes.rows
    totals = total_of(parts)
    first = sums_rows(sizes)
    col_weight, cost = totals[first : first + techs], totals[first + techs :]
    capacity = jnp.maximum(-cost / col_weight, 0.0)
    taken = state.dispatch
    rows_of = 2.0 * taken - state.available * (2.0 * capacity)[:, None, :]
    duals = jnp.maximum(0.5 * rows_of, 0.0)
    own = jnp.where(lax.axis_index("hours") == 0, jnp.sum(capacity**2, axis=0), 0.0)
    fixed = sums.at[:techs].set(jnp.sum(state.available * duals, axis=1))
    fixed = fixed.at[techs].add(own)
    fixed = fixed.at[techs + 1].add(jnp.sum(duals**2 - taken**2, axis=(0, 1)))
    block = block.at[rows : rows + SQUARES].set(fixed[techs : techs + SQUARES])
    return exchange(sizes, block, fixed)[1]


def run(args, exact):
    rows, techs, nodes = args.availability.shape
    hours, regions = lax.axis_size("hours"), lax.axis_size("region")
    slots, owned = args.cross_limit.shape[1], args.cap_cost.shape[1]
    units, lines = args.store_node.shape[0], args.line_limit.shape[0]
    sizes = Bag(
        rows=rows, techs=techs, nodes=nodes, regions=regions, slots=slots, lines=lines, units=units
    )
    cross = regions * slots

    gathered = both_regions(args.price_start)
    info = call(
        lambda names_in, names_out, *refs: slots_kernel(sizes, *refs),
        Bag(ends=args.cross_ends[:, 0], limit=args.cross_limit, pairs=args.pair_counts),
        Bag(info=shape(8 * (cross // LANES), nodes)),
        smem=(2,),
    ).info
    info = both_regions(info)
    state = call(
        functools.partial(start_kernel, sizes),
        Bag(
            availability=args.availability.reshape(rows * techs, nodes),
            price=args.price_start,
            demand=args.demand,
            gen_cost=args.gen_cost,
            cap_cost=args.cap_cost,
            owner=args.owner_map.reshape(hours, owned),
            line_ends=args.line_ends,
            line_limit=args.line_limit[None],
            store_node=args.store_node[None],
            store_power=args.store_power[None],
            store_energy=args.store_energy[None],
        ),
        Bag(
            demand=shape(rows, nodes),
            gen_cost=shape(techs, nodes),
            owner=shape(hours, owned, dtype=jnp.int32),
            store_energy=shape(1, units),
            available=shape(techs, rows, nodes),
            maps_local=shape(nodes, lines + units, dtype=jnp.bfloat16),
            limits_local=shape(1, lines + units),
            flows_local=shape(rows, lines + units),
            store_duals=shape(rows, units),
            dispatch=shape(techs, rows, nodes),
            balance=shape(rows, nodes),
            sums=shape(sums_rows(sizes) + 2 * techs, nodes),
        ),
        flops=10**6,
    )
    closed = call(
        lambda names_in, names_out, *refs: close_kernel(sizes, *refs),
        Bag(gathered=gathered, info=info, balance=state.balance, sums=state.sums),
        Bag(
            maps=shape(regions * nodes, cross, dtype=jnp.bfloat16),
            limits=shape(1, cross),
            flows=shape(rows, cross),
            block=shape(rows + 8, nodes),
            sums=shape(*state.sums.shape),
        ),
    )
    del state.sums, state.balance
    state.maps_cross, state.limits_cross = closed.maps, closed.limits
    state.flows_cross = closed.flows
    gathered, parts = exchange(sizes, closed.block, closed.sums)
    if exact:
        parts = corrected(sizes, state, closed.block, closed.sums, parts)

    negative = None
    for iteration in range(1, ITERS):
        given = Bag(**vars(state), **vars(parts), gathered=gathered)
        if iteration < ITERS - 1:
            del given.owner
            outs = Bag(
                dispatch=shape(techs, rows, nodes),
                cap_duals=shape(techs, rows, nodes),
                flows_local=shape(rows, lines + units),
                flows_cross=shape(rows, cross),
                store_duals=shape(rows, units),
                capacity=shape(techs, nodes),
                weight=shape(1, LANES),
                charge=shape(rows, units),
                charge_before=shape(1, units),
                block=shape(rows + 8, nodes),
                sums=shape(sums_rows(sizes), nodes),
            )
            if iteration == 1:
                outs.col_weight, outs.cost = shape(techs, nodes), shape(techs, nodes)
                outs.negative = shape(1, LANES)
        else:
            outs = Bag(
                dispatch=shape(rows * techs, nodes),
                capacity=shape(1, owned),
                prices=shape(rows, nodes),
                charge=shape(rows, units),
            )
        results = call(functools.partial(sweep_kernel, sizes, iteration), given, outs)
        if iteration == 1:
            negative = results.negative[0, 0]
            del results.negative
        if iteration < ITERS - 1:
            gathered, parts = exchange(sizes, results.block, results.sums)
            del results.block, results.sums
            vars(state).update(vars(results))
    dispatch = results.dispatch.reshape(rows, techs, nodes)
    return (dispatch, results.capacity, results.prices, results.charge), negative


def body(
    availability,
    demand,
    gen_cost,
    cap_cost,
    owner_map,
    line_ends,
    line_limit,
    cross_ends,
    cross_limit,
    pair_counts,
    store_node,
    store_energy,
    store_power,
    price_start,
):
    args = Bag(**locals())
    outputs, negative = run(args, False)
    return lax.cond(negative > 0.0, lambda: run(args, True)[0], lambda: outputs)


def solution(mesh):
    placed = (
        P("hours", None, "region"),
        P("hours", "region"),
        P(None, "region"),
        P("region", "hours"),
        P("region", None),
        P(None, "region"),
        P("region"),
        P(None, "region", None),
        P("region", None),
        P("region", None),
        P("region"),
        P("region"),
        P("region"),
        P("hours", "region"),
    )
    return jax.shard_map(
        body,
        mesh=mesh,
        in_specs=placed,
        out_specs=(
            P("hours", None, "region"),
            P("region", "hours"),
            P("hours", "region"),
            P("hours", "region"),
        ),
        check_vma=False,
    )
```

```python
import functools
from types import SimpleNamespace as Bag

import jax
import jax.numpy as jnp
from jax import lax
from jax.experimental import pallas as pl
from jax.experimental.pallas import tpu as pltpu
from jax.sharding import PartitionSpec as P

ITERS = 4
EPSILON = 1e-06
LANES = 128
VMEM_BYTES = 24 * 1024 * 1024
SQUARES = 3


def split3(value):
    high = value.astype(jnp.bfloat16)
    rest = value - high.astype(jnp.float32)
    middle = rest.astype(jnp.bfloat16)
    low = (rest - middle.astype(jnp.float32)).astype(jnp.bfloat16)
    return jnp.concatenate([high, middle, low], axis=0)


def dot3(value, matrix, transposed):
    rows = value.shape[0]
    contract = ((1,), (1 if transposed else 0,))
    product = lax.dot_general(
        split3(value), matrix, (contract, ((), ())), preferred_element_type=jnp.float32
    )
    return product[:rows] + product[rows : 2 * rows] + product[2 * rows :]


def row_sum(value):
    return jnp.sum(value, axis=0, keepdims=True)


def fold_lanes(row):
    total = row[:, :LANES]
    for start in range(LANES, row.shape[1], LANES):
        total = total + row[:, start : start + LANES]
    return total


def owned_one_hots(owned, tech_count, node_count):
    shape_t = (tech_count, owned.shape[1])
    shape_n = (node_count, owned.shape[1])
    tech = lax.broadcasted_iota(jnp.int32, shape_t, 0) == owned // node_count
    node = lax.broadcasted_iota(jnp.int32, shape_n, 0) == owned % node_count
    return tech, node.astype(jnp.float32).astype(jnp.bfloat16)


def incidence(start, end, count):
    node = lax.broadcasted_iota(jnp.int32, (count, start.shape[1]), 0)
    maps = (node == end).astype(jnp.float32) - (node == start).astype(jnp.float32)
    return maps.astype(jnp.bfloat16)


def halo_at(sizes):
    return sizes.techs + SQUARES


def sums_rows(sizes):
    return (halo_at(sizes) + 2 * sizes.units // LANES + 7) // 8 * 8


def write_halo(sizes, sums_ref, store_new):
    halo, span, rows = halo_at(sizes), sizes.units // LANES, sizes.rows
    write_lanes(sums_ref, halo, store_new[:1])
    write_lanes(sums_ref, halo + span, store_new[rows - 1 :])
    used, end = halo + 2 * span, sums_rows(sizes)
    if used < end:
        sums_ref[used:end, :] = jnp.zeros((end - used, LANES), jnp.float32)


def write_lanes(ref, start, row):
    for i in range(row.shape[1] // LANES):
        ref[start + i : start + i + 1, :] = row[:, i * LANES : (i + 1) * LANES]


def read_lanes(ref, start, length):
    return jnp.concatenate(
        [ref[start + i : start + i + 1, :] for i in range(length // LANES)], axis=1
    )


def places(sizes):
    span = sizes.units // LANES
    limits = sizes.techs
    energy = limits + (sizes.lines + sizes.units) // LANES
    return Bag(
        limits=limits,
        energy=energy,
        owned=energy + span,
        weight=sizes.techs,
        before=sizes.techs + 1,
        negative=sizes.techs + 1 + span,
    )


def slots_kernel(sizes, ends_ref, limit_ref, pairs_ref, info_ref):
    nodes, slots, regions = sizes.nodes, sizes.slots, sizes.regions
    own = lax.axis_index("region")
    width = slots // regions
    slot = lax.broadcasted_iota(jnp.int32, (1, slots), 1)
    pair = slot // width
    in_use = jnp.zeros((1, slots), jnp.int32)
    for target in range(regions):
        in_use = jnp.where(pair == target, pairs_ref[0, target], in_use)
    place = lax.broadcasted_iota(jnp.int32, (slots, regions * slots), 1) == (
        own * slots + lax.broadcasted_iota(jnp.int32, (slots, regions * slots), 0)
    )
    place = place.astype(jnp.float32).astype(jnp.bfloat16)
    bound = jnp.where(slot % width < in_use, limit_ref[...], 0.0)
    start = (ends_ref[0:1, :] + own * nodes).astype(jnp.float32)
    end = (ends_ref[1:2, :] + pair * nodes).astype(jnp.float32)
    rest = jnp.zeros((13, slots), jnp.float32)
    info = dot3(jnp.concatenate([start, end, bound, rest], axis=0), place, False)
    for chunk in range(regions * slots // LANES):
        info_ref[8 * chunk : 8 * chunk + 8, :] = info[:8, chunk * LANES : (chunk + 1) * LANES]


def start_kernel(sizes, names_in, names_out, *refs):
    given = Bag(**dict(zip(names_in, refs[: len(names_in)])))
    gives = Bag(**dict(zip(names_out, refs[len(names_in) :])))
    rows, techs, nodes, lines = sizes.rows, sizes.techs, sizes.nodes, sizes.lines
    at = places(sizes)
    fixed = gives.available.at[techs + 1]
    gives.available[techs] = given.demand[...]
    fixed[:techs, :] = given.gen_cost[...]
    write_lanes(fixed, at.energy, given.store_energy[...])
    owned = given.owner[pl.ds(lax.axis_index("hours"), 1), :]
    fixed[at.owned : at.owned + 1, : owned.shape[1]] = owned.astype(jnp.float32)
    line_ends, stores = given.line_ends[...], given.store_node[...]
    start = jnp.concatenate([line_ends[0:1], jnp.full_like(stores, -1)], axis=1)
    end = jnp.concatenate([line_ends[1:2], stores], axis=1)
    maps = incidence(start, end, nodes)
    limits = jnp.concatenate([given.line_limit[...], given.store_power[...]], axis=1)
    gives.maps_local[...] = maps
    write_lanes(fixed, at.limits, limits)
    prices = given.price[...]
    flows = jnp.clip(-0.5 * dot3(prices, maps, False), -limits, limits)
    gives.flows_local[...] = flows
    store_new = (1.0 / 3.0) * (2.0 * flows[:, lines:])
    gives.store_duals[...] = store_new
    primal_row = fold_lanes(row_sum(flows * flows))
    dual_row = fold_lanes(row_sum(store_new * store_new))
    balance = dot3(2.0 * flows, maps, True) - given.demand[...]
    gen_cost = given.gen_cost[...]
    acc = jnp.zeros((rows, nodes), jnp.float32)
    weights = jnp.zeros((techs, nodes), jnp.float32)
    for hour in range(rows):
        weights = weights + given.availability[hour * techs : (hour + 1) * techs, :]
    for tech in range(techs):
        avail = given.availability[pl.ds(tech, rows, stride=techs), :]
        gives.available[tech] = avail
        dispatch = jnp.maximum(-0.5 * (gen_cost[tech : tech + 1] + prices), 0.0)
        gives.dispatch[tech] = dispatch
        dispatch_bar = 2.0 * dispatch
        balance = balance + dispatch_bar
        duals = jnp.maximum(0.5 * dispatch_bar, 0.0)
        acc = acc + dispatch * dispatch
        gives.sums[tech : tech + 1, :] = row_sum(avail * duals)
    gives.balance[...] = balance
    squares = row_sum(acc)
    cost = given.cap_cost[...]
    negative = jnp.sum((cost < 0.0).astype(jnp.float32), axis=1, keepdims=True)
    write_halo(sizes, gives.sums, store_new)
    gives.sums[techs : techs + SQUARES, :] = jnp.concatenate(
        [primal_row + squares, dual_row + squares, jnp.broadcast_to(negative, (1, LANES))], axis=0
    )
    tech_hot, node_hot = owned_one_hots(owned, techs, nodes)
    first = sums_rows(sizes)
    gives.sums[first : first + techs, :] = weights
    gives.sums[first + techs : first + 2 * techs, :] = dot3(
        jnp.where(tech_hot, cost, 0.0), node_hot, True
    )


def close_kernel(
    sizes,
    gathered,
    info_ref,
    balance_ref,
    sums_in_ref,
    maps_ref,
    flows_ref,
    region_ref,
    sums_ref,
):
    rows, techs, nodes = sizes.rows, sizes.techs, sizes.nodes
    slots, regions = sizes.slots, sizes.regions
    own = lax.axis_index("region")
    chunks = []
    for chunk in range(regions * slots // LANES):
        at = slice(8 * chunk, 8 * chunk + 8)
        part = info_ref[0, at, :]
        for region in range(1, regions):
            part = part + info_ref[region, at, :]
        chunks.append(part)
    info = jnp.concatenate(chunks, axis=1) if len(chunks) > 1 else chunks[0]
    maps_ref[...] = incidence(
        info[0:1].astype(jnp.int32), info[1:2].astype(jnp.int32), regions * nodes
    )
    limits = info[2:3]
    prices_all = jnp.concatenate([gathered[region, :rows, :] for region in range(regions)], axis=1)
    flows = jnp.clip(-0.5 * dot3(prices_all, maps_ref[...], False), -limits, limits)
    flows_ref[:rows, :] = flows
    flows_ref[rows : rows + 1, :] = limits
    maps_own = maps_ref[pl.ds(pl.multiple_of(own * nodes, nodes), nodes), :]
    balance = balance_ref[...] + dot3(2.0 * flows, maps_own, True)
    step_up = (1.0 / (techs + 8.0)) * balance
    region_ref[:rows, :] = gathered[own, :rows, :] + step_up
    change = row_sum(flows * flows)
    slot = lax.broadcasted_iota(jnp.int32, change.shape, 1)
    primal = fold_lanes(jnp.where(slot // slots == own, change, 0.0))
    more = jnp.concatenate(
        [primal, row_sum(step_up * step_up), jnp.zeros((SQUARES - 2, LANES), jnp.float32)], axis=0
    )
    sums_ref[...] = sums_in_ref[...]
    squares = sums_in_ref[techs : techs + SQUARES, :] + more
    sums_ref[techs : techs + SQUARES, :] = squares
    region_ref[rows:, :] = jnp.concatenate(
        [squares, jnp.zeros((8 - SQUARES, LANES), jnp.float32)], axis=0
    )


def neighbour_rows(sizes, given, hour_index):
    units = sizes.units
    if hasattr(given, "totals"):
        return read_lanes(given.next_row, 0, units), read_lanes(given.prev_row, 0, units)
    first = halo_at(sizes)
    last = first + units // LANES
    count = given.slabs.shape[0]
    core, x_place, slab = hour_index % 2, hour_index // 2 % 2, hour_index // 4
    next_row = read_lanes(given.slabs.at[(slab + 1) % count], first, units)
    prev_row = read_lanes(given.slabs.at[(slab + count - 1) % count], last, units)
    next_row = jnp.where(x_place == 0, read_lanes(given.across, first, units), next_row)
    prev_row = jnp.where(x_place == 0, prev_row, read_lanes(given.across, last, units))
    next_row = jnp.where(core == 0, read_lanes(given.partner, first, units), next_row)
    prev_row = jnp.where(core == 0, prev_row, read_lanes(given.partner, last, units))
    return next_row, prev_row


def total_of(parts):
    if hasattr(parts, "totals"):
        return parts.totals[...]
    return jnp.sum(parts.slabs[...], axis=0)


def sweep_kernel(sizes, iteration, names_in, names_out, *refs):
    rows, techs, nodes = sizes.rows, sizes.techs, sizes.nodes
    slots, regions, lines, units = sizes.slots, sizes.regions, sizes.lines, sizes.units
    second = iteration == 1
    last = iteration == ITERS - 1
    given = Bag(**dict(zip(names_in, refs[: len(names_in)])))
    gives = Bag(**dict(zip(names_out, refs[len(names_in) :])))
    own = lax.axis_index("region")
    hour_index = lax.axis_index("hours")
    gathered = given.gathered

    at = places(sizes)
    fixed = given.available.at[techs + 1]
    small = given.dispatch.at[techs]
    sums = total_of(given)
    squares = jnp.sum(sums[techs : techs + 2], axis=1, keepdims=True)
    old_weight = jnp.ones((1, 1), jnp.float32) if second else small[at.weight : at.weight + 1, :1]
    weight = jnp.sqrt(
        old_weight * jnp.sqrt((squares[1:2] + EPSILON) / (squares[0:1] + EPSILON))
    )
    primal_step = 0.5 / weight
    if second:
        first = sums_rows(sizes)
        col_weight, cost = sums[first : first + techs], sums[first + techs : first + 2 * techs]
        negative = sums[techs + 2 : techs + 3]
        capacity = jnp.maximum(-cost / col_weight, 0.0)
        first_bar = 2.0 * capacity
    else:
        col_weight = given.cap_duals[techs, :techs, :]
        cost = given.cap_duals[techs, techs : 2 * techs, :]
        capacity = small[:techs, :]
        negative = small[at.negative : at.negative + 1, :]
    capacity_new = jnp.maximum(capacity - (cost - sums[:techs]) / (weight * col_weight), 0.0)
    capacity_bar = 2.0 * capacity_new - capacity

    prices_all = jnp.concatenate([gathered[region, :rows, :] for region in range(regions)], axis=1)
    prices = gathered[own, :rows, :]
    maps_local = given.maps_local[...]
    slope_local = dot3(prices, maps_local, False)
    slope_cross = dot3(prices_all, given.maps_cross[...], False)

    energy = read_lanes(fixed, at.energy, units)
    row_id = lax.broadcasted_iota(jnp.int32, (rows, units), 0)
    next_row, prev_row = neighbour_rows(sizes, given, hour_index)
    store_duals = given.store_duals[...]
    next_duals = jnp.where(row_id == rows - 1, next_row, pltpu.roll(store_duals, rows - 1, 0))
    if second:
        charge = jnp.zeros((rows, units), jnp.float32)
        charge_before = jnp.zeros((1, units), jnp.float32)
    else:
        charge = given.charge[...]
        charge_before = read_lanes(small, at.before, units)
    charge_new = jnp.clip(charge - primal_step * (store_duals - next_duals), 0.0, energy)
    gives.charge[...] = charge_new

    primal_row = jnp.zeros((1, LANES), jnp.float32)
    bars = []
    local_out = None if last else gives.flows_local
    cross_out = None if last else gives.flows_cross
    local_limits = read_lanes(fixed, at.limits, lines + units)
    cross_limits = given.flows_cross[rows : rows + 1, :]
    for flows, out, limits, slope, low, high in (
        (given.flows_local, local_out, local_limits, slope_local, 0, lines),
        (given.flows_local, local_out, local_limits, slope_local, lines, lines + units),
        (given.flows_cross, cross_out, cross_limits, slope_cross, 0, regions * slots),
    ):
        slope = slope[:, low:high]
        if low:
            slope = slope + store_duals
        bound = limits[:, low:high]
        old = flows[:rows, low:high]
        new = jnp.clip(old - primal_step * slope, -bound, bound)
        bars.append(2.0 * new - old)
        if not last:
            out[:rows, low:high] = new
            change = row_sum((new - old) ** 2)
            if out is cross_out:
                slot = lax.broadcasted_iota(jnp.int32, change.shape, 1)
                change = jnp.where(slot // slots == own, change, 0.0)
            primal_row = primal_row + fold_lanes(change)
    maps_own = given.maps_cross[pl.ds(pl.multiple_of(own * nodes, nodes), nodes), :]
    balance = dot3(jnp.concatenate(bars[:2], axis=1), maps_local, True) - given.available[techs]
    balance = balance + dot3(bars[2], maps_own, True)

    gen_cost = fixed[:techs, :]
    half_weight = weight / 2.0
    primal_acc = jnp.zeros((rows, nodes), jnp.float32)
    dual_acc = jnp.zeros((rows, nodes), jnp.float32)
    for tech in range(techs):
        slope = gen_cost[tech : tech + 1] + prices
        dispatch = given.dispatch[tech]
        avail = given.available[tech]
        if second:
            duals = jnp.maximum(0.5 * (2.0 * dispatch - avail * first_bar[tech : tech + 1]), 0.0)
        else:
            duals = given.cap_duals[tech]
        dispatch_new = jnp.maximum(dispatch - primal_step * (slope + duals), 0.0)
        dispatch_bar = 2.0 * dispatch_new - dispatch
        balance = balance + dispatch_bar
        if last:
            gives.dispatch[pl.ds(tech, rows, stride=techs), :] = dispatch_new
            continue
        gives.dispatch[tech] = dispatch_new
        cap_rows = dispatch_bar - avail * capacity_bar[tech : tech + 1]
        primal_acc = primal_acc + (dispatch_new - dispatch) ** 2
        duals_new = jnp.maximum(duals + half_weight * cap_rows, 0.0)
        dual_acc = dual_acc + (duals_new - duals) ** 2
        gives.cap_duals[tech] = duals_new
        gives.sums[tech : tech + 1, :] = row_sum(avail * duals_new)

    step_up = weight / (techs + 8.0) * balance
    if last:
        gives.prices[...] = prices + step_up
        owned = fixed[at.owned : at.owned + 1, : gives.capacity.shape[1]].astype(jnp.int32)
        tech_hot, node_hot = owned_one_hots(owned, techs, nodes)
        chosen = dot3(capacity_new, node_hot, False)
        gives.capacity[...] = row_sum(jnp.where(tech_hot, chosen, 0.0))
        gives.negative[...] = negative
        return
    gives.block[:rows, :] = prices + step_up
    gives.flows_cross[rows : rows + 1, :] = cross_limits
    gives.cap_duals[techs, :techs, :] = col_weight
    gives.cap_duals[techs, techs : 2 * techs, :] = cost
    small_new = gives.dispatch.at[techs]
    small_new[:techs, :] = capacity_new
    small_new[at.weight : at.weight + 1, :] = jnp.broadcast_to(weight, (1, LANES))
    small_new[at.negative : at.negative + 1, :] = negative
    charge_bar = 2.0 * charge_new - charge
    before_new = jnp.clip(charge_before - primal_step * (prev_row - store_duals[0:1]), 0.0, energy)
    write_lanes(small_new, at.before, before_new)
    before_bar = 2.0 * before_new - charge_before
    shifted_bar = jnp.where(row_id == 0, before_bar, pltpu.roll(charge_bar, 1, 0))
    store_step = weight / 3.0 * (charge_bar - shifted_bar + bars[1])
    store_new = store_duals + store_step
    gives.store_duals[...] = store_new
    primal_row = primal_row + row_sum(primal_acc) + fold_lanes(row_sum((charge_new - charge) ** 2))
    primal_row = primal_row + jnp.where(
        hour_index == 0, row_sum((capacity_new - capacity) ** 2), 0.0
    )
    dual_row = row_sum(dual_acc + step_up * step_up) + fold_lanes(row_sum(store_step * store_step))
    squares = jnp.concatenate(
        [primal_row, dual_row, jnp.zeros((SQUARES - 2, LANES), jnp.float32)], axis=0
    )
    gives.block[rows:, :] = jnp.concatenate(
        [squares, jnp.zeros((8 - SQUARES, LANES), jnp.float32)], axis=0
    )
    gives.sums[techs : techs + SQUARES, :] = squares
    write_halo(sizes, gives.sums, store_new)


def call(kernel, given, outs, flops=0, smem=()):
    names_in, names_out = tuple(vars(given)), tuple(vars(outs))
    values = pl.pallas_call(
        functools.partial(kernel, names_in, names_out),
        out_shape=tuple(vars(outs).values()),
        in_specs=[
            pl.BlockSpec(memory_space=pltpu.SMEM if i in smem else pltpu.VMEM)
            for i in range(len(names_in))
        ],
        out_specs=[pl.BlockSpec(memory_space=pltpu.VMEM)] * len(names_out),
        cost_estimate=pl.CostEstimate(flops=flops, bytes_accessed=4 * flops, transcendentals=0),
        compiler_params=pltpu.CompilerParams(vmem_limit_bytes=VMEM_BYTES),
    )(*vars(given).values())
    return Bag(**dict(zip(names_out, values)))


def swap(value, hour_bit, region_bit):
    hours, regions = lax.axis_size("hours"), lax.axis_size("region")
    pairs = [
        (hour * regions + region, (hour ^ hour_bit) * regions + (region ^ region_bit))
        for hour in range(hours)
        for region in range(regions)
    ]
    return lax.ppermute(value, ("hours", "region"), pairs)


def shifted(value, steps):
    count = lax.axis_size("hours")
    return lax.ppermute(value, "hours", [(i, (i + steps) % count) for i in range(count)])


def both_regions(block):
    if lax.axis_size("region") != 2:
        return lax.all_gather(block, "region")
    return in_order(block, swap(block, 0, 1))


def in_order(block, other):
    return jnp.where(
        lax.axis_index("region") == 0, jnp.stack([block, other]), jnp.stack([other, block])
    )


def exchange(sizes, block, sums):
    hours, regions = lax.axis_size("hours"), lax.axis_size("region")
    techs, rows, span = sizes.techs, sizes.rows, sizes.units // LANES
    halo = halo_at(sizes)
    if regions != 2 or hours != 16:
        gathered = lax.all_gather(block, "region")
        squares = jnp.sum(gathered[:, rows : rows + SQUARES], axis=0)
        totals = lax.psum(sums.at[techs:halo].set(squares), "hours")
        next_row = shifted(sums[halo : halo + span], -1)
        prev_row = shifted(sums[halo + span : halo + 2 * span], 1)
        return gathered, Bag(totals=totals, next_row=next_row, prev_row=prev_row)

    def merged(mine, yours, mine_first):
        last = halo + span
        edges = [
            jnp.where(mine_first, mine[halo:last], yours[halo:last]),
            jnp.where(mine_first, yours[last : last + span], mine[last : last + span]),
        ]
        total = mine + yours
        return jnp.concatenate([total[:halo], *edges, total[last + span :]], axis=0)

    hour, region = lax.axis_index("hours"), lax.axis_index("region")
    partner = swap(sums, 1, 0)
    other = swap(block[:rows], 0, 1)
    chip = merged(sums, partner, hour % 2 == 0)
    square = gather_from(
        chip,
        [
            [(4 * z + 2 * x + core) * regions + side for x in range(2) for side in range(regions)]
            for z in range(hours // 4)
            for core in range(2)
        ],
    )
    left = jnp.where(region == 0, square[0], square[1])
    right = jnp.where(region == 0, square[2], square[3])
    across = jnp.where(hour // 2 % 2 == 0, right, left)
    slab = merged(left, right, True)
    slab = slab.at[techs:halo].set(jnp.sum(square[:, techs:halo], axis=0))
    slabs = gather_from(
        slab,
        [
            [(4 * z + place) * regions + side for z in range(hours // 4)]
            for place in range(4)
            for side in range(regions)
        ],
    )
    return in_order(block[:rows], other), Bag(slabs=slabs, partner=partner, across=across)


def gather_from(value, groups):
    return lax.all_gather(value, ("hours", "region"), axis_index_groups=groups)


def shape(*dims, dtype=jnp.float32):
    return jax.ShapeDtypeStruct(dims, dtype)


def corrected(sizes, state, block, sums, parts):
    techs, rows = sizes.techs, sizes.rows
    totals = total_of(parts)
    first = sums_rows(sizes)
    col_weight, cost = totals[first : first + techs], totals[first + techs :]
    capacity = jnp.maximum(-cost / col_weight, 0.0)
    taken = state.dispatch[:techs]
    rows_of = 2.0 * taken - state.available[:techs] * (2.0 * capacity)[:, None, :]
    duals = jnp.maximum(0.5 * rows_of, 0.0)
    own = jnp.where(lax.axis_index("hours") == 0, jnp.sum(capacity**2, axis=0), 0.0)
    fixed = sums.at[:techs].set(jnp.sum(state.available[:techs] * duals, axis=1))
    fixed = fixed.at[techs].add(own)
    fixed = fixed.at[techs + 1].add(jnp.sum(duals**2 - taken**2, axis=(0, 1)))
    block = block.at[rows : rows + SQUARES].set(fixed[techs : techs + SQUARES])
    return exchange(sizes, block, fixed)[1]


def run(args, exact):
    rows, techs, nodes = args.availability.shape
    hours, regions = lax.axis_size("hours"), lax.axis_size("region")
    slots, owned = args.cross_limit.shape[1], args.cap_cost.shape[1]
    units, lines = args.store_node.shape[0], args.line_limit.shape[0]
    sizes = Bag(
        rows=rows, techs=techs, nodes=nodes, regions=regions, slots=slots, lines=lines, units=units
    )
    cross = regions * slots

    gathered = both_regions(args.price_start)
    info = call(
        lambda names_in, names_out, *refs: slots_kernel(sizes, *refs),
        Bag(ends=args.cross_ends[:, 0], limit=args.cross_limit, pairs=args.pair_counts),
        Bag(info=shape(8 * (cross // LANES), nodes)),
        smem=(2,),
    ).info
    info = both_regions(info)
    state = call(
        functools.partial(start_kernel, sizes),
        Bag(
            availability=args.availability.reshape(rows * techs, nodes),
            price=args.price_start,
            demand=args.demand,
            gen_cost=args.gen_cost,
            cap_cost=args.cap_cost,
            owner=args.owner_map.reshape(hours, owned),
            line_ends=args.line_ends,
            line_limit=args.line_limit[None],
            store_node=args.store_node[None],
            store_power=args.store_power[None],
            store_energy=args.store_energy[None],
        ),
        Bag(
            available=shape(techs + 2, rows, nodes),
            maps_local=shape(nodes, lines + units, dtype=jnp.bfloat16),
            flows_local=shape(rows, lines + units),
            store_duals=shape(rows, units),
            dispatch=shape(techs + 1, rows, nodes),
            balance=shape(rows, nodes),
            sums=shape(sums_rows(sizes) + 2 * techs, nodes),
        ),
        flops=10**6,
    )
    closed = call(
        lambda names_in, names_out, *refs: close_kernel(sizes, *refs),
        Bag(gathered=gathered, info=info, balance=state.balance, sums=state.sums),
        Bag(
            maps=shape(regions * nodes, cross, dtype=jnp.bfloat16),
            flows=shape(rows + 8, cross),
            block=shape(rows + 8, nodes),
            sums=shape(*state.sums.shape),
        ),
    )
    del state.sums, state.balance
    state.maps_cross, state.flows_cross = closed.maps, closed.flows
    gathered, parts = exchange(sizes, closed.block, closed.sums)
    if exact:
        parts = corrected(sizes, state, closed.block, closed.sums, parts)

    for iteration in range(1, ITERS):
        given = Bag(**vars(state), **vars(parts), gathered=gathered)
        if iteration < ITERS - 1:
            outs = Bag(
                dispatch=shape(techs + 1, rows, nodes),
                cap_duals=shape(techs + 1, rows, nodes),
                flows_local=shape(rows, lines + units),
                flows_cross=shape(rows + 8, cross),
                store_duals=shape(rows, units),
                charge=shape(rows, units),
                block=shape(rows + 8, nodes),
                sums=shape(sums_rows(sizes), nodes),
            )
        else:
            outs = Bag(
                dispatch=shape(rows * techs, nodes),
                capacity=shape(1, owned),
                prices=shape(rows, nodes),
                charge=shape(rows, units),
                negative=shape(1, LANES),
            )
        results = call(functools.partial(sweep_kernel, sizes, iteration), given, outs)
        if iteration < ITERS - 1:
            gathered, parts = exchange(sizes, results.block, results.sums)
            del results.block, results.sums
            vars(state).update(vars(results))
    dispatch = results.dispatch.reshape(rows, techs, nodes)
    outputs = (dispatch, results.capacity, results.prices, results.charge)
    return outputs, results.negative[0, 0]


def body(
    availability,
    demand,
    gen_cost,
    cap_cost,
    owner_map,
    line_ends,
    line_limit,
    cross_ends,
    cross_limit,
    pair_counts,
    store_node,
    store_energy,
    store_power,
    price_start,
):
    args = Bag(**locals())
    outputs, negative = run(args, False)
    return lax.cond(negative > 0.0, lambda: run(args, True)[0], lambda: outputs)


def solution(mesh):
    placed = (
        P("hours", None, "region"),
        P("hours", "region"),
        P(None, "region"),
        P("region", "hours"),
        P("region", None),
        P(None, "region"),
        P("region"),
        P(None, "region", None),
        P("region", None),
        P("region", None),
        P("region"),
        P("region"),
        P("region"),
        P("hours", "region"),
    )
    return jax.shard_map(
        body,
        mesh=mesh,
        in_specs=placed,
        out_specs=(
            P("hours", None, "region"),
            P("region", "hours"),
            P("hours", "region"),
            P("hours", "region"),
        ),
        check_vma=False,
    )
```

```python
import functools
from types import SimpleNamespace as Bag

import jax
import jax.numpy as jnp
from jax import lax
from jax.experimental import pallas as pl
from jax.experimental.pallas import tpu as pltpu
from jax.sharding import PartitionSpec as P

ITERS = 4
EPSILON = 1e-06
LANES = 128
VMEM_BYTES = 24 * 1024 * 1024
SQUARES = 3


def split3(value):
    high = value.astype(jnp.bfloat16)
    rest = value - high.astype(jnp.float32)
    middle = rest.astype(jnp.bfloat16)
    low = (rest - middle.astype(jnp.float32)).astype(jnp.bfloat16)
    return jnp.concatenate([high, middle, low], axis=0)


def dot3(value, matrix, transposed):
    rows = value.shape[0]
    contract = ((1,), (1 if transposed else 0,))
    product = lax.dot_general(
        split3(value), matrix, (contract, ((), ())), preferred_element_type=jnp.float32
    )
    return product[:rows] + product[rows : 2 * rows] + product[2 * rows :]


def row_sum(value):
    return jnp.sum(value, axis=0, keepdims=True)


def fold_lanes(row):
    total = row[:, :LANES]
    for start in range(LANES, row.shape[1], LANES):
        total = total + row[:, start : start + LANES]
    return total


def owned_one_hots(owned, tech_count, node_count):
    shape_t = (tech_count, owned.shape[1])
    shape_n = (node_count, owned.shape[1])
    tech = lax.broadcasted_iota(jnp.int32, shape_t, 0) == owned // node_count
    node = lax.broadcasted_iota(jnp.int32, shape_n, 0) == owned % node_count
    return tech, node.astype(jnp.float32).astype(jnp.bfloat16)


def incidence(start, end, count):
    node = lax.broadcasted_iota(jnp.int32, (count, start.shape[1]), 0)
    maps = (node == end).astype(jnp.float32) - (node == start).astype(jnp.float32)
    return maps.astype(jnp.bfloat16)


def halo_at(sizes):
    return sizes.techs + SQUARES


def sums_rows(sizes):
    return (halo_at(sizes) + 2 * sizes.units // LANES + 7) // 8 * 8


def write_halo(sizes, sums_ref, store_new):
    halo, span, rows = halo_at(sizes), sizes.units // LANES, sizes.rows
    write_lanes(sums_ref, halo, store_new[:1])
    write_lanes(sums_ref, halo + span, store_new[rows - 1 :])
    used, end = halo + 2 * span, sums_rows(sizes)
    if used < end:
        sums_ref[used:end, :] = jnp.zeros((end - used, LANES), jnp.float32)


def write_lanes(ref, start, row):
    for i in range(row.shape[1] // LANES):
        ref[start + i : start + i + 1, :] = row[:, i * LANES : (i + 1) * LANES]


def read_lanes(ref, start, length):
    return jnp.concatenate(
        [ref[start + i : start + i + 1, :] for i in range(length // LANES)], axis=1
    )


def places(sizes):
    span = sizes.units // LANES
    limits = sizes.techs
    energy = limits + (sizes.lines + sizes.units) // LANES
    return Bag(
        limits=limits,
        energy=energy,
        owned=energy + span,
        weight=sizes.techs,
        before=sizes.techs + 1,
        negative=sizes.techs + 1 + span,
    )


def slots_kernel(sizes, ends_ref, limit_ref, pairs_ref, info_ref):
    nodes, slots, regions = sizes.nodes, sizes.slots, sizes.regions
    own = lax.axis_index("region")
    width = slots // regions
    slot = lax.broadcasted_iota(jnp.int32, (1, slots), 1)
    pair = slot // width
    in_use = jnp.zeros((1, slots), jnp.int32)
    for target in range(regions):
        in_use = jnp.where(pair == target, pairs_ref[0, target], in_use)
    place = lax.broadcasted_iota(jnp.int32, (slots, regions * slots), 1) == (
        own * slots + lax.broadcasted_iota(jnp.int32, (slots, regions * slots), 0)
    )
    place = place.astype(jnp.float32).astype(jnp.bfloat16)
    bound = jnp.where(slot % width < in_use, limit_ref[...], 0.0)
    start = (ends_ref[0:1, :] + own * nodes).astype(jnp.float32)
    end = (ends_ref[1:2, :] + pair * nodes).astype(jnp.float32)
    rest = jnp.zeros((13, slots), jnp.float32)
    info = dot3(jnp.concatenate([start, end, bound, rest], axis=0), place, False)
    for chunk in range(regions * slots // LANES):
        info_ref[8 * chunk : 8 * chunk + 8, :] = info[:8, chunk * LANES : (chunk + 1) * LANES]


def start_kernel(sizes, names_in, names_out, *refs):
    given = Bag(**dict(zip(names_in, refs[: len(names_in)])))
    gives = Bag(**dict(zip(names_out, refs[len(names_in) :])))
    rows, techs, nodes, lines = sizes.rows, sizes.techs, sizes.nodes, sizes.lines
    at = places(sizes)
    fixed = gives.available.at[techs + 1]
    gives.available[techs] = given.demand[...]
    fixed[:techs, :] = given.gen_cost[...]
    write_lanes(fixed, at.energy, given.store_energy[...])
    owned = given.owner[pl.ds(lax.axis_index("hours"), 1), :]
    fixed[at.owned : at.owned + 1, : owned.shape[1]] = owned.astype(jnp.float32)
    line_ends, stores = given.line_ends[...], given.store_node[...]
    start = jnp.concatenate([line_ends[0:1], jnp.full_like(stores, -1)], axis=1)
    end = jnp.concatenate([line_ends[1:2], stores], axis=1)
    maps = incidence(start, end, nodes)
    limits = jnp.concatenate([given.line_limit[...], given.store_power[...]], axis=1)
    gives.maps_local[...] = maps
    write_lanes(fixed, at.limits, limits)
    prices = given.price[...]
    flows = jnp.clip(-0.5 * dot3(prices, maps, False), -limits, limits)
    gives.flows_local[...] = flows
    store_new = (1.0 / 3.0) * (2.0 * flows[:, lines:])
    gives.store_duals[...] = store_new
    primal_row = fold_lanes(row_sum(flows * flows))
    dual_row = fold_lanes(row_sum(store_new * store_new))
    balance = dot3(2.0 * flows, maps, True) - given.demand[...]
    gen_cost = given.gen_cost[...]
    acc = jnp.zeros((rows, nodes), jnp.float32)
    weights = jnp.zeros((techs, nodes), jnp.float32)
    for hour in range(rows):
        weights = weights + given.availability[hour * techs : (hour + 1) * techs, :]
    for tech in range(techs):
        avail = given.availability[pl.ds(tech, rows, stride=techs), :]
        gives.available[tech] = avail
        dispatch = jnp.maximum(-0.5 * (gen_cost[tech : tech + 1] + prices), 0.0)
        gives.dispatch[tech] = dispatch
        dispatch_bar = 2.0 * dispatch
        balance = balance + dispatch_bar
        duals = jnp.maximum(0.5 * dispatch_bar, 0.0)
        acc = acc + dispatch * dispatch
        gives.sums[tech : tech + 1, :] = row_sum(avail * duals)
    gives.balance[...] = balance
    squares = row_sum(acc)
    cost = given.cap_cost[...]
    negative = jnp.sum((cost < 0.0).astype(jnp.float32), axis=1, keepdims=True)
    write_halo(sizes, gives.sums, store_new)
    gives.sums[techs : techs + SQUARES, :] = jnp.concatenate(
        [primal_row + squares, dual_row + squares, jnp.broadcast_to(negative, (1, LANES))], axis=0
    )
    tech_hot, node_hot = owned_one_hots(owned, techs, nodes)
    first = sums_rows(sizes)
    gives.sums[first : first + techs, :] = weights
    gives.sums[first + techs : first + 2 * techs, :] = dot3(
        jnp.where(tech_hot, cost, 0.0), node_hot, True
    )


def close_kernel(
    sizes,
    gathered,
    info_ref,
    balance_ref,
    sums_in_ref,
    maps_ref,
    flows_ref,
    region_ref,
    sums_ref,
):
    rows, techs, nodes = sizes.rows, sizes.techs, sizes.nodes
    slots, regions = sizes.slots, sizes.regions
    own = lax.axis_index("region")
    chunks = []
    for chunk in range(regions * slots // LANES):
        at = slice(8 * chunk, 8 * chunk + 8)
        part = info_ref[0, at, :]
        for region in range(1, regions):
            part = part + info_ref[region, at, :]
        chunks.append(part)
    info = jnp.concatenate(chunks, axis=1) if len(chunks) > 1 else chunks[0]
    maps_ref[...] = incidence(
        info[0:1].astype(jnp.int32), info[1:2].astype(jnp.int32), regions * nodes
    )
    limits = info[2:3]
    prices_all = jnp.concatenate([gathered[region, :rows, :] for region in range(regions)], axis=1)
    flows = jnp.clip(-0.5 * dot3(prices_all, maps_ref[...], False), -limits, limits)
    flows_ref[:rows, :] = flows
    flows_ref[rows : rows + 1, :] = limits
    maps_own = maps_ref[pl.ds(pl.multiple_of(own * nodes, nodes), nodes), :]
    balance = balance_ref[...] + dot3(2.0 * flows, maps_own, True)
    step_up = (1.0 / (techs + 8.0)) * balance
    region_ref[:rows, :] = gathered[own, :rows, :] + step_up
    change = row_sum(flows * flows)
    slot = lax.broadcasted_iota(jnp.int32, change.shape, 1)
    primal = fold_lanes(jnp.where(slot // slots == own, change, 0.0))
    more = jnp.concatenate(
        [primal, row_sum(step_up * step_up), jnp.zeros((SQUARES - 2, LANES), jnp.float32)], axis=0
    )
    sums_ref[...] = sums_in_ref[...]
    squares = sums_in_ref[techs : techs + SQUARES, :] + more
    sums_ref[techs : techs + SQUARES, :] = squares
    region_ref[rows:, :] = jnp.concatenate(
        [squares, jnp.zeros((8 - SQUARES, LANES), jnp.float32)], axis=0
    )


def sweep_kernel(sizes, iteration, names_in, names_out, *refs):
    rows, techs, nodes = sizes.rows, sizes.techs, sizes.nodes
    slots, regions, lines, units = sizes.slots, sizes.regions, sizes.lines, sizes.units
    second = iteration == 1
    last = iteration == ITERS - 1
    given = Bag(**dict(zip(names_in, refs[: len(names_in)])))
    gives = Bag(**dict(zip(names_out, refs[len(names_in) :])))
    own = lax.axis_index("region")
    hour_index = lax.axis_index("hours")
    gathered = given.gathered

    at = places(sizes)
    fixed = given.available.at[techs + 1]
    small = given.dispatch.at[techs]
    sums = given.totals
    squares = jnp.sum(sums[techs : techs + 2, :], axis=1, keepdims=True)
    old_weight = jnp.ones((1, 1), jnp.float32) if second else small[at.weight : at.weight + 1, :1]
    weight = jnp.sqrt(
        old_weight * jnp.sqrt((squares[1:2] + EPSILON) / (squares[0:1] + EPSILON))
    )
    primal_step = 0.5 / weight
    if second:
        first = sums_rows(sizes)
        col_weight, cost = sums[first : first + techs, :], sums[first + techs :, :]
        negative = sums[techs + 2 : techs + 3, :]
        capacity = jnp.maximum(-cost / col_weight, 0.0)
        first_bar = 2.0 * capacity
    else:
        col_weight = given.cap_duals[techs, :techs, :]
        cost = given.cap_duals[techs, techs : 2 * techs, :]
        capacity = small[:techs, :]
        negative = small[at.negative : at.negative + 1, :]
    capacity_new = jnp.maximum(capacity - (cost - sums[:techs, :]) / (weight * col_weight), 0.0)
    capacity_bar = 2.0 * capacity_new - capacity

    prices_all = jnp.concatenate([gathered[region, :rows, :] for region in range(regions)], axis=1)
    prices = gathered[own, :rows, :]
    maps_local = given.maps_local[...]
    slope_local = dot3(prices, maps_local, False)
    slope_cross = dot3(prices_all, given.maps_cross[...], False)

    energy = read_lanes(fixed, at.energy, units)
    row_id = lax.broadcasted_iota(jnp.int32, (rows, units), 0)
    halo = halo_at(sizes)
    next_row = read_lanes(sums, halo, units)
    prev_row = read_lanes(sums, halo + units // LANES, units)
    store_duals = given.store_duals[...]
    next_duals = jnp.where(row_id == rows - 1, next_row, pltpu.roll(store_duals, rows - 1, 0))
    if second:
        charge = jnp.zeros((rows, units), jnp.float32)
        charge_before = jnp.zeros((1, units), jnp.float32)
    else:
        charge = given.charge[...]
        charge_before = read_lanes(small, at.before, units)
    charge_new = jnp.clip(charge - primal_step * (store_duals - next_duals), 0.0, energy)
    gives.charge[...] = charge_new

    primal_row = jnp.zeros((1, LANES), jnp.float32)
    bars = []
    local_out = None if last else gives.flows_local
    cross_out = None if last else gives.flows_cross
    local_limits = read_lanes(fixed, at.limits, lines + units)
    cross_limits = given.flows_cross[rows : rows + 1, :]
    for flows, out, limits, slope, low, high in (
        (given.flows_local, local_out, local_limits, slope_local, 0, lines),
        (given.flows_local, local_out, local_limits, slope_local, lines, lines + units),
        (given.flows_cross, cross_out, cross_limits, slope_cross, 0, regions * slots),
    ):
        slope = slope[:, low:high]
        if low:
            slope = slope + store_duals
        bound = limits[:, low:high]
        old = flows[:rows, low:high]
        new = jnp.clip(old - primal_step * slope, -bound, bound)
        bars.append(2.0 * new - old)
        if not last:
            out[:rows, low:high] = new
            change = row_sum((new - old) ** 2)
            if out is cross_out:
                slot = lax.broadcasted_iota(jnp.int32, change.shape, 1)
                change = jnp.where(slot // slots == own, change, 0.0)
            primal_row = primal_row + fold_lanes(change)
    maps_own = given.maps_cross[pl.ds(pl.multiple_of(own * nodes, nodes), nodes), :]
    balance = dot3(jnp.concatenate(bars[:2], axis=1), maps_local, True) - given.available[techs]
    balance = balance + dot3(bars[2], maps_own, True)

    gen_cost = fixed[:techs, :]
    half_weight = weight / 2.0
    primal_acc = jnp.zeros((rows, nodes), jnp.float32)
    dual_acc = jnp.zeros((rows, nodes), jnp.float32)
    for tech in range(techs):
        slope = gen_cost[tech : tech + 1] + prices
        dispatch = given.dispatch[tech]
        avail = given.available[tech]
        if second:
            duals = jnp.maximum(0.5 * (2.0 * dispatch - avail * first_bar[tech : tech + 1]), 0.0)
        else:
            duals = given.cap_duals[tech]
        dispatch_new = jnp.maximum(dispatch - primal_step * (slope + duals), 0.0)
        dispatch_bar = 2.0 * dispatch_new - dispatch
        balance = balance + dispatch_bar
        if last:
            gives.dispatch[pl.ds(tech, rows, stride=techs), :] = dispatch_new
            continue
        gives.dispatch[tech] = dispatch_new
        cap_rows = dispatch_bar - avail * capacity_bar[tech : tech + 1]
        primal_acc = primal_acc + (dispatch_new - dispatch) ** 2
        duals_new = jnp.maximum(duals + half_weight * cap_rows, 0.0)
        dual_acc = dual_acc + (duals_new - duals) ** 2
        gives.cap_duals[tech] = duals_new
        gives.sums[tech : tech + 1, :] = row_sum(avail * duals_new)

    step_up = weight / (techs + 8.0) * balance
    if last:
        gives.prices[...] = prices + step_up
        owned = fixed[at.owned : at.owned + 1, : gives.capacity.shape[1]].astype(jnp.int32)
        tech_hot, node_hot = owned_one_hots(owned, techs, nodes)
        chosen = dot3(capacity_new, node_hot, False)
        gives.capacity[...] = row_sum(jnp.where(tech_hot, chosen, 0.0))
        gives.negative[...] = negative
        return
    gives.block[:rows, :] = prices + step_up
    gives.flows_cross[rows : rows + 1, :] = cross_limits
    gives.cap_duals[techs, :techs, :] = col_weight
    gives.cap_duals[techs, techs : 2 * techs, :] = cost
    small_new = gives.dispatch.at[techs]
    small_new[:techs, :] = capacity_new
    small_new[at.weight : at.weight + 1, :] = jnp.broadcast_to(weight, (1, LANES))
    small_new[at.negative : at.negative + 1, :] = negative
    charge_bar = 2.0 * charge_new - charge
    before_new = jnp.clip(charge_before - primal_step * (prev_row - store_duals[0:1]), 0.0, energy)
    write_lanes(small_new, at.before, before_new)
    before_bar = 2.0 * before_new - charge_before
    shifted_bar = jnp.where(row_id == 0, before_bar, pltpu.roll(charge_bar, 1, 0))
    store_step = weight / 3.0 * (charge_bar - shifted_bar + bars[1])
    store_new = store_duals + store_step
    gives.store_duals[...] = store_new
    primal_row = primal_row + row_sum(primal_acc) + fold_lanes(row_sum((charge_new - charge) ** 2))
    primal_row = primal_row + jnp.where(
        hour_index == 0, row_sum((capacity_new - capacity) ** 2), 0.0
    )
    dual_row = row_sum(dual_acc + step_up * step_up) + fold_lanes(row_sum(store_step * store_step))
    squares = jnp.concatenate(
        [primal_row, dual_row, jnp.zeros((SQUARES - 2, LANES), jnp.float32)], axis=0
    )
    gives.block[rows:, :] = jnp.concatenate(
        [squares, jnp.zeros((8 - SQUARES, LANES), jnp.float32)], axis=0
    )
    gives.sums[techs : techs + SQUARES, :] = squares
    write_halo(sizes, gives.sums, store_new)


def call(kernel, given, outs, flops=0, smem=()):
    names_in, names_out = tuple(vars(given)), tuple(vars(outs))
    values = pl.pallas_call(
        functools.partial(kernel, names_in, names_out),
        out_shape=tuple(vars(outs).values()),
        in_specs=[
            pl.BlockSpec(memory_space=pltpu.SMEM if i in smem else pltpu.VMEM)
            for i in range(len(names_in))
        ],
        out_specs=[pl.BlockSpec(memory_space=pltpu.VMEM)] * len(names_out),
        cost_estimate=pl.CostEstimate(flops=flops, bytes_accessed=4 * flops, transcendentals=0),
        compiler_params=pltpu.CompilerParams(vmem_limit_bytes=VMEM_BYTES),
    )(*vars(given).values())
    return Bag(**dict(zip(names_out, values)))


def permute(value, target, takes_part=lambda hour: True):
    hours, regions = lax.axis_size("hours"), lax.axis_size("region")
    pairs = []
    for hour in range(hours):
        for region in range(regions):
            if takes_part(hour):
                to_hour, to_region = target(hour, region)
                pairs.append((hour * regions + region, to_hour * regions + to_region))
    return lax.ppermute(value, ("hours", "region"), pairs)


def other_region(hour, region):
    return hour, region ^ 1


def core_of(hour):
    return hour % 2


def first_core(hour):
    return hour % 2 == 0


def shifted(value, steps):
    count = lax.axis_size("hours")
    return lax.ppermute(value, "hours", [(i, (i + steps) % count) for i in range(count)])


def both_regions(block):
    if lax.axis_size("region") != 2:
        return lax.all_gather(block, "region")
    return in_order(block, permute(block, other_region))


def in_order(block, other):
    return jnp.where(
        lax.axis_index("region") == 0, jnp.stack([block, other]), jnp.stack([other, block])
    )


def exchange(sizes, block, sums):
    hours, regions = lax.axis_size("hours"), lax.axis_size("region")
    techs, rows, span = sizes.techs, sizes.rows, sizes.units // LANES
    halo = halo_at(sizes)
    last, end = halo + span, halo + 2 * span

    def with_edges(total, first_rows, last_rows):
        return jnp.concatenate([total[:halo], first_rows, last_rows, total[end:]], axis=0)

    if regions != 2 or hours != 16:
        gathered = lax.all_gather(block, "region")
        squares = jnp.sum(gathered[:, rows : rows + SQUARES], axis=0)
        totals = lax.psum(sums.at[techs:halo].set(squares), "hours")
        return gathered, with_edges(
            totals, shifted(sums[halo:last], -1), shifted(sums[last:end], 1)
        )

    hour = lax.axis_index("hours")
    prices = block[:rows]
    lower = permute(sums, lambda h, r: (h + 1, r), first_core)
    upper_prices = permute(prices, lambda h, r: (h - 1, r), core_of)
    far_prices = permute(
        jnp.concatenate([prices, upper_prices], axis=0), other_region, first_core
    )
    given_prices = permute(far_prices[rows:], lambda h, r: (h + 1, r), first_core)
    other = jnp.where(core_of(hour) == 0, far_prices[:rows], given_prices)

    chip = with_edges(sums + lower, lower[halo:last], sums[last:end])
    across = permute(chip, lambda h, r: (h ^ 2, r), core_of)
    squares = chip[techs:halo]
    diagonal = permute(squares, lambda h, r: (h ^ 2, r ^ 1), core_of)
    beside = permute(squares, other_region, core_of)
    on_left = hour // 2 % 2 == 0
    slab = chip + across
    slab = slab.at[techs:halo].add(diagonal + beside)
    slab = with_edges(
        slab,
        jnp.where(on_left, chip[halo:last], across[halo:last]),
        jnp.where(on_left, across[last:end], chip[last:end]),
    )
    near, middle, far = [
        permute(slab, lambda h, r, step=step: (h ^ 4 * step, r), core_of) for step in (1, 2, 3)
    ]
    even = hour // 4 % 2 == 0
    totals = (slab + near) + (middle + far)
    next_rows = jnp.where(even, near[halo:last], far[halo:last])
    next_rows = jnp.where(on_left, across[halo:last], next_rows)
    prev_rows = jnp.where(even, far[last:end], near[last:end])
    prev_rows = jnp.where(on_left, prev_rows, across[last:end])
    mine = with_edges(totals, next_rows, lower[last:end])
    down = permute(
        with_edges(totals, sums[halo:last], prev_rows), lambda h, r: (h - 1, r), core_of
    )
    return in_order(prices, other), jnp.where(core_of(hour) == 0, down, mine)


def shape(*dims, dtype=jnp.float32):
    return jax.ShapeDtypeStruct(dims, dtype)


def corrected(sizes, state, block, sums, totals):
    techs, rows = sizes.techs, sizes.rows
    first = sums_rows(sizes)
    col_weight, cost = totals[first : first + techs], totals[first + techs :]
    capacity = jnp.maximum(-cost / col_weight, 0.0)
    taken = state.dispatch[:techs]
    rows_of = 2.0 * taken - state.available[:techs] * (2.0 * capacity)[:, None, :]
    duals = jnp.maximum(0.5 * rows_of, 0.0)
    own = jnp.where(lax.axis_index("hours") == 0, jnp.sum(capacity**2, axis=0), 0.0)
    fixed = sums.at[:techs].set(jnp.sum(state.available[:techs] * duals, axis=1))
    fixed = fixed.at[techs].add(own)
    fixed = fixed.at[techs + 1].add(jnp.sum(duals**2 - taken**2, axis=(0, 1)))
    block = block.at[rows : rows + SQUARES].set(fixed[techs : techs + SQUARES])
    return exchange(sizes, block, fixed)[1]


def run(args, exact):
    rows, techs, nodes = args.availability.shape
    hours, regions = lax.axis_size("hours"), lax.axis_size("region")
    slots, owned = args.cross_limit.shape[1], args.cap_cost.shape[1]
    units, lines = args.store_node.shape[0], args.line_limit.shape[0]
    sizes = Bag(
        rows=rows, techs=techs, nodes=nodes, regions=regions, slots=slots, lines=lines, units=units
    )
    cross = regions * slots

    gathered = both_regions(args.price_start)
    info = call(
        lambda names_in, names_out, *refs: slots_kernel(sizes, *refs),
        Bag(ends=args.cross_ends[:, 0], limit=args.cross_limit, pairs=args.pair_counts),
        Bag(info=shape(8 * (cross // LANES), nodes)),
        smem=(2,),
    ).info
    info = both_regions(info)
    state = call(
        functools.partial(start_kernel, sizes),
        Bag(
            availability=args.availability.reshape(rows * techs, nodes),
            price=args.price_start,
            demand=args.demand,
            gen_cost=args.gen_cost,
            cap_cost=args.cap_cost,
            owner=args.owner_map.reshape(hours, owned),
            line_ends=args.line_ends,
            line_limit=args.line_limit[None],
            store_node=args.store_node[None],
            store_power=args.store_power[None],
            store_energy=args.store_energy[None],
        ),
        Bag(
            available=shape(techs + 2, rows, nodes),
            maps_local=shape(nodes, lines + units, dtype=jnp.bfloat16),
            flows_local=shape(rows, lines + units),
            store_duals=shape(rows, units),
            dispatch=shape(techs + 1, rows, nodes),
            balance=shape(rows, nodes),
            sums=shape(sums_rows(sizes) + 2 * techs, nodes),
        ),
        flops=10**6,
    )
    closed = call(
        lambda names_in, names_out, *refs: close_kernel(sizes, *refs),
        Bag(gathered=gathered, info=info, balance=state.balance, sums=state.sums),
        Bag(
            maps=shape(regions * nodes, cross, dtype=jnp.bfloat16),
            flows=shape(rows + 8, cross),
            block=shape(rows + 8, nodes),
            sums=shape(*state.sums.shape),
        ),
    )
    del state.sums, state.balance
    state.maps_cross, state.flows_cross = closed.maps, closed.flows
    gathered, totals = exchange(sizes, closed.block, closed.sums)
    if exact:
        totals = corrected(sizes, state, closed.block, closed.sums, totals)

    for iteration in range(1, ITERS):
        given = Bag(**vars(state), totals=totals, gathered=gathered)
        if iteration < ITERS - 1:
            outs = Bag(
                dispatch=shape(techs + 1, rows, nodes),
                cap_duals=shape(techs + 1, rows, nodes),
                flows_local=shape(rows, lines + units),
                flows_cross=shape(rows + 8, cross),
                store_duals=shape(rows, units),
                charge=shape(rows, units),
                block=shape(rows + 8, nodes),
                sums=shape(sums_rows(sizes), nodes),
            )
        else:
            outs = Bag(
                dispatch=shape(rows * techs, nodes),
                capacity=shape(1, owned),
                prices=shape(rows, nodes),
                charge=shape(rows, units),
                negative=shape(1, LANES),
            )
        results = call(functools.partial(sweep_kernel, sizes, iteration), given, outs)
        if iteration < ITERS - 1:
            gathered, totals = exchange(sizes, results.block, results.sums)
            del results.block, results.sums
            vars(state).update(vars(results))
    dispatch = results.dispatch.reshape(rows, techs, nodes)
    outputs = (dispatch, results.capacity, results.prices, results.charge)
    return outputs, results.negative[0, 0]


def body(
    availability,
    demand,
    gen_cost,
    cap_cost,
    owner_map,
    line_ends,
    line_limit,
    cross_ends,
    cross_limit,
    pair_counts,
    store_node,
    store_energy,
    store_power,
    price_start,
):
    args = Bag(**locals())
    outputs, negative = run(args, False)
    return lax.cond(negative > 0.0, lambda: run(args, True)[0], lambda: outputs)


def solution(mesh):
    placed = (
        P("hours", None, "region"),
        P("hours", "region"),
        P(None, "region"),
        P("region", "hours"),
        P("region", None),
        P(None, "region"),
        P("region"),
        P(None, "region", None),
        P("region", None),
        P("region", None),
        P("region"),
        P("region"),
        P("region"),
        P("hours", "region"),
    )
    return jax.shard_map(
        body,
        mesh=mesh,
        in_specs=placed,
        out_specs=(
            P("hours", None, "region"),
            P("region", "hours"),
            P("hours", "region"),
            P("hours", "region"),
        ),
        check_vma=False,
    )
```

```python
import functools
from types import SimpleNamespace as Bag

import jax
import jax.numpy as jnp
from jax import lax
from jax.experimental import pallas as pl
from jax.experimental.pallas import tpu as pltpu
from jax.sharding import PartitionSpec as P

ITERS = 4
EPSILON = 1e-06
LANES = 128
VMEM_BYTES = 24 * 1024 * 1024
SQUARES = 3


def split3(value):
    high = value.astype(jnp.bfloat16)
    rest = value - high.astype(jnp.float32)
    middle = rest.astype(jnp.bfloat16)
    low = (rest - middle.astype(jnp.float32)).astype(jnp.bfloat16)
    return jnp.concatenate([high, middle, low], axis=0)


def dot3(value, matrix, transposed):
    rows = value.shape[0]
    contract = ((1,), (1 if transposed else 0,))
    product = lax.dot_general(
        split3(value), matrix, (contract, ((), ())), preferred_element_type=jnp.float32
    )
    return product[:rows] + product[rows : 2 * rows] + product[2 * rows :]


def row_sum(value):
    return jnp.sum(value, axis=0, keepdims=True)


def fold_lanes(row):
    total = row[:, :LANES]
    for start in range(LANES, row.shape[1], LANES):
        total = total + row[:, start : start + LANES]
    return total


def owned_one_hots(owned, tech_count, node_count):
    shape_t = (tech_count, owned.shape[1])
    shape_n = (node_count, owned.shape[1])
    tech = lax.broadcasted_iota(jnp.int32, shape_t, 0) == owned // node_count
    node = lax.broadcasted_iota(jnp.int32, shape_n, 0) == owned % node_count
    return tech, node.astype(jnp.float32).astype(jnp.bfloat16)


def incidence(start, end, count):
    node = lax.broadcasted_iota(jnp.int32, (count, start.shape[1]), 0)
    maps = (node == end).astype(jnp.float32) - (node == start).astype(jnp.float32)
    return maps.astype(jnp.bfloat16)


def halo_at(sizes):
    return sizes.techs + SQUARES


def sums_rows(sizes):
    return (halo_at(sizes) + 2 * sizes.units // LANES + 7) // 8 * 8


def write_halo(sizes, sums_ref, store_new):
    halo, span, rows = halo_at(sizes), sizes.units // LANES, sizes.rows
    write_lanes(sums_ref, halo, store_new[:1])
    write_lanes(sums_ref, halo + span, store_new[rows - 1 :])
    used, end = halo + 2 * span, sums_rows(sizes)
    if used < end:
        sums_ref[used:end, :] = jnp.zeros((end - used, LANES), jnp.float32)


def write_lanes(ref, start, row):
    for i in range(row.shape[1] // LANES):
        ref[start + i : start + i + 1, :] = row[:, i * LANES : (i + 1) * LANES]


def read_lanes(ref, start, length):
    return jnp.concatenate(
        [ref[start + i : start + i + 1, :] for i in range(length // LANES)], axis=1
    )


def places(sizes):
    span = sizes.units // LANES
    limits = sizes.techs
    energy = limits + (sizes.lines + sizes.units) // LANES
    return Bag(
        limits=limits,
        energy=energy,
        owned=energy + span,
        weight=sizes.techs,
        before=sizes.techs + 1,
        negative=sizes.techs + 1 + span,
    )


def slots_kernel(sizes, ends_ref, limit_ref, pairs_ref, info_ref):
    nodes, slots, regions = sizes.nodes, sizes.slots, sizes.regions
    own = lax.axis_index("region")
    width = slots // regions
    slot = lax.broadcasted_iota(jnp.int32, (1, slots), 1)
    pair = slot // width
    in_use = jnp.zeros((1, slots), jnp.int32)
    for target in range(regions):
        in_use = jnp.where(pair == target, pairs_ref[0, target], in_use)
    place = lax.broadcasted_iota(jnp.int32, (slots, regions * slots), 1) == (
        own * slots + lax.broadcasted_iota(jnp.int32, (slots, regions * slots), 0)
    )
    place = place.astype(jnp.float32).astype(jnp.bfloat16)
    bound = jnp.where(slot % width < in_use, limit_ref[...], 0.0)
    start = (ends_ref[0:1, :] + own * nodes).astype(jnp.float32)
    end = (ends_ref[1:2, :] + pair * nodes).astype(jnp.float32)
    rest = jnp.zeros((13, slots), jnp.float32)
    info = dot3(jnp.concatenate([start, end, bound, rest], axis=0), place, False)
    for chunk in range(regions * slots // LANES):
        info_ref[8 * chunk : 8 * chunk + 8, :] = info[:8, chunk * LANES : (chunk + 1) * LANES]


def start_kernel(sizes, names_in, names_out, *refs):
    given = Bag(**dict(zip(names_in, refs[: len(names_in)])))
    gives = Bag(**dict(zip(names_out, refs[len(names_in) :])))
    rows, techs, nodes, lines = sizes.rows, sizes.techs, sizes.nodes, sizes.lines
    at = places(sizes)
    fixed = gives.available.at[techs + 1]
    gives.available[techs] = given.demand[...]
    fixed[:techs, :] = given.gen_cost[...]
    write_lanes(fixed, at.energy, given.store_energy[...])
    owned = given.owner[pl.ds(lax.axis_index("hours"), 1), :]
    fixed[at.owned : at.owned + 1, : owned.shape[1]] = owned.astype(jnp.float32)
    line_ends, stores = given.line_ends[...], given.store_node[...]
    start = jnp.concatenate([line_ends[0:1], jnp.full_like(stores, -1)], axis=1)
    end = jnp.concatenate([line_ends[1:2], stores], axis=1)
    maps = incidence(start, end, nodes)
    limits = jnp.concatenate([given.line_limit[...], given.store_power[...]], axis=1)
    gives.maps_local[...] = maps
    write_lanes(fixed, at.limits, limits)
    prices = given.price[...]
    flows = jnp.clip(-0.5 * dot3(prices, maps, False), -limits, limits)
    gives.flows_local[...] = flows
    store_new = (1.0 / 3.0) * (2.0 * flows[:, lines:])
    gives.store_duals[...] = store_new
    primal_row = fold_lanes(row_sum(flows * flows))
    dual_row = fold_lanes(row_sum(store_new * store_new))
    balance = dot3(2.0 * flows, maps, True) - given.demand[...]
    gen_cost = given.gen_cost[...]
    acc = jnp.zeros((rows, nodes), jnp.float32)
    weights = jnp.zeros((techs, nodes), jnp.float32)
    for hour in range(rows):
        weights = weights + given.availability[hour * techs : (hour + 1) * techs, :]
    for tech in range(techs):
        avail = given.availability[pl.ds(tech, rows, stride=techs), :]
        gives.available[tech] = avail
        dispatch = jnp.maximum(-0.5 * (gen_cost[tech : tech + 1] + prices), 0.0)
        gives.dispatch[tech] = dispatch
        dispatch_bar = 2.0 * dispatch
        balance = balance + dispatch_bar
        duals = jnp.maximum(0.5 * dispatch_bar, 0.0)
        acc = acc + dispatch * dispatch
        gives.sums[tech : tech + 1, :] = row_sum(avail * duals)
    gives.balance[...] = balance
    squares = row_sum(acc)
    cost = given.cap_cost[...]
    negative = jnp.sum((cost < 0.0).astype(jnp.float32), axis=1, keepdims=True)
    write_halo(sizes, gives.sums, store_new)
    gives.sums[techs : techs + SQUARES, :] = jnp.concatenate(
        [primal_row + squares, dual_row + squares, jnp.broadcast_to(negative, (1, LANES))], axis=0
    )
    tech_hot, node_hot = owned_one_hots(owned, techs, nodes)
    first = sums_rows(sizes)
    gives.sums[first : first + techs, :] = weights
    gives.sums[first + techs : first + 2 * techs, :] = dot3(
        jnp.where(tech_hot, cost, 0.0), node_hot, True
    )


def close_kernel(
    sizes,
    gathered,
    info_ref,
    balance_ref,
    sums_in_ref,
    maps_ref,
    flows_ref,
    block_ref,
):
    rows, techs, nodes = sizes.rows, sizes.techs, sizes.nodes
    slots, regions = sizes.slots, sizes.regions
    own = lax.axis_index("region")
    chunks = []
    for chunk in range(regions * slots // LANES):
        at = slice(8 * chunk, 8 * chunk + 8)
        part = info_ref[0, at, :]
        for region in range(1, regions):
            part = part + info_ref[region, at, :]
        chunks.append(part)
    info = jnp.concatenate(chunks, axis=1) if len(chunks) > 1 else chunks[0]
    maps_ref[...] = incidence(
        info[0:1].astype(jnp.int32), info[1:2].astype(jnp.int32), regions * nodes
    )
    limits = info[2:3]
    prices_all = jnp.concatenate([gathered[region, :rows, :] for region in range(regions)], axis=1)
    flows = jnp.clip(-0.5 * dot3(prices_all, maps_ref[...], False), -limits, limits)
    flows_ref[:rows, :] = flows
    flows_ref[rows : rows + 1, :] = limits
    maps_own = maps_ref[pl.ds(pl.multiple_of(own * nodes, nodes), nodes), :]
    balance = balance_ref[...] + dot3(2.0 * flows, maps_own, True)
    step_up = (1.0 / (techs + 8.0)) * balance
    block_ref[:rows, :] = gathered[own, :rows, :] + step_up
    change = row_sum(flows * flows)
    slot = lax.broadcasted_iota(jnp.int32, change.shape, 1)
    primal = fold_lanes(jnp.where(slot // slots == own, change, 0.0))
    more = jnp.concatenate(
        [primal, row_sum(step_up * step_up), jnp.zeros((SQUARES - 2, LANES), jnp.float32)], axis=0
    )
    block_ref[rows:, :] = sums_in_ref[...]
    block_ref[rows + techs : rows + techs + SQUARES, :] = (
        sums_in_ref[techs : techs + SQUARES, :] + more
    )


def sweep_kernel(sizes, iteration, names_in, names_out, *refs):
    rows, techs, nodes = sizes.rows, sizes.techs, sizes.nodes
    slots, regions, lines, units = sizes.slots, sizes.regions, sizes.lines, sizes.units
    second = iteration == 1
    last = iteration == ITERS - 1
    given = Bag(**dict(zip(names_in, refs[: len(names_in)])))
    gives = Bag(**dict(zip(names_out, refs[len(names_in) :])))
    own = lax.axis_index("region")
    hour_index = lax.axis_index("hours")
    gathered = given.gathered

    at = places(sizes)
    fixed = given.available.at[techs + 1]
    small = given.dispatch.at[techs]
    out_sums = None if last else gives.block.at[pl.ds(rows, sums_rows(sizes))]
    sums = given.totals
    squares = jnp.sum(sums[techs : techs + 2, :], axis=1, keepdims=True)
    old_weight = jnp.ones((1, 1), jnp.float32) if second else small[at.weight : at.weight + 1, :1]
    weight = jnp.sqrt(
        old_weight * jnp.sqrt((squares[1:2] + EPSILON) / (squares[0:1] + EPSILON))
    )
    primal_step = 0.5 / weight
    if second:
        first = sums_rows(sizes)
        col_weight, cost = sums[first : first + techs, :], sums[first + techs :, :]
        negative = sums[techs + 2 : techs + 3, :]
        capacity = jnp.maximum(-cost / col_weight, 0.0)
        first_bar = 2.0 * capacity
    else:
        col_weight = given.cap_duals[techs, :techs, :]
        cost = given.cap_duals[techs, techs : 2 * techs, :]
        capacity = small[:techs, :]
        negative = small[at.negative : at.negative + 1, :]
    capacity_new = jnp.maximum(capacity - (cost - sums[:techs, :]) / (weight * col_weight), 0.0)
    capacity_bar = 2.0 * capacity_new - capacity

    prices_all = jnp.concatenate([gathered[region, :rows, :] for region in range(regions)], axis=1)
    prices = gathered[own, :rows, :]
    maps_local = given.maps_local[...]
    slope_local = dot3(prices, maps_local, False)
    slope_cross = dot3(prices_all, given.maps_cross[...], False)

    energy = read_lanes(fixed, at.energy, units)
    row_id = lax.broadcasted_iota(jnp.int32, (rows, units), 0)
    halo = halo_at(sizes)
    next_row = read_lanes(sums, halo, units)
    prev_row = read_lanes(sums, halo + units // LANES, units)
    store_duals = given.store_duals[...]
    next_duals = jnp.where(row_id == rows - 1, next_row, pltpu.roll(store_duals, rows - 1, 0))
    if second:
        charge = jnp.zeros((rows, units), jnp.float32)
        charge_before = jnp.zeros((1, units), jnp.float32)
    else:
        charge = given.charge[...]
        charge_before = read_lanes(small, at.before, units)
    charge_new = jnp.clip(charge - primal_step * (store_duals - next_duals), 0.0, energy)
    gives.charge[...] = charge_new

    primal_row = jnp.zeros((1, LANES), jnp.float32)
    bars = []
    local_out = None if last else gives.flows_local
    cross_out = None if last else gives.flows_cross
    local_limits = read_lanes(fixed, at.limits, lines + units)
    cross_limits = given.flows_cross[rows : rows + 1, :]
    for flows, out, limits, slope, low, high in (
        (given.flows_local, local_out, local_limits, slope_local, 0, lines),
        (given.flows_local, local_out, local_limits, slope_local, lines, lines + units),
        (given.flows_cross, cross_out, cross_limits, slope_cross, 0, regions * slots),
    ):
        slope = slope[:, low:high]
        if low:
            slope = slope + store_duals
        bound = limits[:, low:high]
        old = flows[:rows, low:high]
        new = jnp.clip(old - primal_step * slope, -bound, bound)
        bars.append(2.0 * new - old)
        if not last:
            out[:rows, low:high] = new
            change = row_sum((new - old) ** 2)
            if out is cross_out:
                slot = lax.broadcasted_iota(jnp.int32, change.shape, 1)
                change = jnp.where(slot // slots == own, change, 0.0)
            primal_row = primal_row + fold_lanes(change)
    maps_own = given.maps_cross[pl.ds(pl.multiple_of(own * nodes, nodes), nodes), :]
    balance = dot3(jnp.concatenate(bars[:2], axis=1), maps_local, True) - given.available[techs]
    balance = balance + dot3(bars[2], maps_own, True)

    gen_cost = fixed[:techs, :]
    half_weight = weight / 2.0
    primal_acc = jnp.zeros((rows, nodes), jnp.float32)
    dual_acc = jnp.zeros((rows, nodes), jnp.float32)
    for tech in range(techs):
        slope = gen_cost[tech : tech + 1] + prices
        dispatch = given.dispatch[tech]
        avail = given.available[tech]
        if second:
            duals = jnp.maximum(0.5 * (2.0 * dispatch - avail * first_bar[tech : tech + 1]), 0.0)
        else:
            duals = given.cap_duals[tech]
        dispatch_new = jnp.maximum(dispatch - primal_step * (slope + duals), 0.0)
        dispatch_bar = 2.0 * dispatch_new - dispatch
        balance = balance + dispatch_bar
        if last:
            gives.dispatch[pl.ds(tech, rows, stride=techs), :] = dispatch_new
            continue
        gives.dispatch[tech] = dispatch_new
        cap_rows = dispatch_bar - avail * capacity_bar[tech : tech + 1]
        primal_acc = primal_acc + (dispatch_new - dispatch) ** 2
        duals_new = jnp.maximum(duals + half_weight * cap_rows, 0.0)
        dual_acc = dual_acc + (duals_new - duals) ** 2
        gives.cap_duals[tech] = duals_new
        out_sums[tech : tech + 1, :] = row_sum(avail * duals_new)

    step_up = weight / (techs + 8.0) * balance
    if last:
        gives.prices[...] = prices + step_up
        owned = fixed[at.owned : at.owned + 1, : gives.capacity.shape[1]].astype(jnp.int32)
        tech_hot, node_hot = owned_one_hots(owned, techs, nodes)
        chosen = dot3(capacity_new, node_hot, False)
        gives.capacity[...] = row_sum(jnp.where(tech_hot, chosen, 0.0))
        gives.negative[...] = negative
        return
    gives.block[:rows, :] = prices + step_up
    gives.flows_cross[rows : rows + 1, :] = cross_limits
    gives.cap_duals[techs, :techs, :] = col_weight
    gives.cap_duals[techs, techs : 2 * techs, :] = cost
    small_new = gives.dispatch.at[techs]
    small_new[:techs, :] = capacity_new
    small_new[at.weight : at.weight + 1, :] = jnp.broadcast_to(weight, (1, LANES))
    small_new[at.negative : at.negative + 1, :] = negative
    charge_bar = 2.0 * charge_new - charge
    before_new = jnp.clip(charge_before - primal_step * (prev_row - store_duals[0:1]), 0.0, energy)
    write_lanes(small_new, at.before, before_new)
    before_bar = 2.0 * before_new - charge_before
    shifted_bar = jnp.where(row_id == 0, before_bar, pltpu.roll(charge_bar, 1, 0))
    store_step = weight / 3.0 * (charge_bar - shifted_bar + bars[1])
    store_new = store_duals + store_step
    gives.store_duals[...] = store_new
    primal_row = primal_row + row_sum(primal_acc) + fold_lanes(row_sum((charge_new - charge) ** 2))
    primal_row = primal_row + jnp.where(
        hour_index == 0, row_sum((capacity_new - capacity) ** 2), 0.0
    )
    dual_row = row_sum(dual_acc + step_up * step_up) + fold_lanes(row_sum(store_step * store_step))
    squares = jnp.concatenate(
        [primal_row, dual_row, jnp.zeros((SQUARES - 2, LANES), jnp.float32)], axis=0
    )
    out_sums[techs : techs + SQUARES, :] = squares
    write_halo(sizes, out_sums, store_new)


def call(kernel, given, outs, flops=0, smem=()):
    names_in, names_out = tuple(vars(given)), tuple(vars(outs))
    values = pl.pallas_call(
        functools.partial(kernel, names_in, names_out),
        out_shape=tuple(vars(outs).values()),
        in_specs=[
            pl.BlockSpec(memory_space=pltpu.SMEM if i in smem else pltpu.VMEM)
            for i in range(len(names_in))
        ],
        out_specs=[pl.BlockSpec(memory_space=pltpu.VMEM)] * len(names_out),
        cost_estimate=pl.CostEstimate(flops=flops, bytes_accessed=4 * flops, transcendentals=0),
        compiler_params=pltpu.CompilerParams(vmem_limit_bytes=VMEM_BYTES),
    )(*vars(given).values())
    return Bag(**dict(zip(names_out, values)))


def swap(value, hour_bit, region_bit, core=None):
    hours, regions = lax.axis_size("hours"), lax.axis_size("region")
    pairs = []
    for hour in range(hours):
        for region in range(regions):
            here = hour * regions + region
            there = (hour ^ hour_bit) * regions + (region ^ region_bit)
            pairs.append((here, there if core in (None, hour % 2) else here))
    return lax.ppermute(value, ("hours", "region"), pairs)


def shifted(value, steps):
    count = lax.axis_size("hours")
    return lax.ppermute(value, "hours", [(i, (i + steps) % count) for i in range(count)])


def both_regions(block):
    if lax.axis_size("region") != 2:
        return lax.all_gather(block, "region")
    return in_order(block, swap(block, 0, 1))


def in_order(block, other):
    return jnp.where(
        lax.axis_index("region") == 0, jnp.stack([block, other]), jnp.stack([other, block])
    )


def exchange(sizes, block):
    hours, regions = lax.axis_size("hours"), lax.axis_size("region")
    techs, rows, span = sizes.techs, sizes.rows, sizes.units // LANES
    halo = halo_at(sizes)
    last, end = halo + span, halo + 2 * span
    prices, sums = block[:rows], block[rows:]

    def with_edges(total, first_rows, last_rows):
        return jnp.concatenate([total[:halo], first_rows, last_rows, total[end:]], axis=0)

    if regions != 2 or hours != 16:
        gathered = lax.all_gather(block[: rows + halo], "region")
        squares = jnp.sum(gathered[:, rows + techs :], axis=0)
        gathered = gathered[:, :rows]
        totals = lax.psum(sums.at[techs:halo].set(squares), "hours")
        return gathered, with_edges(
            totals, shifted(sums[halo:last], -1), shifted(sums[last:end], 1)
        )

    core = lax.axis_index("hours") % 2
    on_left = lax.axis_index("hours") // 2 % 2 == 0
    even = lax.axis_index("hours") // 4 % 2 == 0
    partner = swap(block, 1, 0)
    lower = partner[rows:]
    far_prices = swap(jnp.concatenate([prices, partner[:rows]], axis=0), 0, 1, core=0)
    chip = with_edges(sums + lower, lower[halo:last], sums[last:end])
    across = swap(chip, 2, 0, core=1)
    squares = chip[techs:halo]
    diagonal = swap(squares, 2, 1, core=1)
    beside = swap(squares, 0, 1, core=1)
    slab = chip + across
    slab = slab.at[techs:halo].add(diagonal + beside)
    slab = with_edges(
        slab,
        jnp.where(on_left, chip[halo:last], across[halo:last]),
        jnp.where(on_left, across[last:end], chip[last:end]),
    )
    near, middle, far = [swap(slab, 4 * step, 0, core=1) for step in (1, 2, 3)]
    totals = (slab + near) + (middle + far)
    next_rows = jnp.where(even, near[halo:last], far[halo:last])
    next_rows = jnp.where(on_left, across[halo:last], next_rows)
    prev_rows = jnp.where(even, far[last:end], near[last:end])
    prev_rows = jnp.where(on_left, prev_rows, across[last:end])
    mine = with_edges(totals, next_rows, lower[last:end])
    message = with_edges(totals, sums[halo:last], prev_rows)
    message = jnp.pad(message, ((0, rows - message.shape[0]), (0, 0)))
    arrived = swap(jnp.where(core == 0, far_prices[rows:], message), 1, 0)
    other = jnp.where(core == 0, far_prices[:rows], arrived)
    return in_order(prices, other), jnp.where(core == 0, arrived[: sums.shape[0]], mine)


def shape(*dims, dtype=jnp.float32):
    return jax.ShapeDtypeStruct(dims, dtype)


def corrected(sizes, state, block, totals):
    techs, rows = sizes.techs, sizes.rows
    first = sums_rows(sizes)
    col_weight, cost = totals[first : first + techs], totals[first + techs :]
    capacity = jnp.maximum(-cost / col_weight, 0.0)
    taken = state.dispatch[:techs]
    rows_of = 2.0 * taken - state.available[:techs] * (2.0 * capacity)[:, None, :]
    duals = jnp.maximum(0.5 * rows_of, 0.0)
    own = jnp.where(lax.axis_index("hours") == 0, jnp.sum(capacity**2, axis=0), 0.0)
    at = rows + techs
    block = block.at[rows:at].set(jnp.sum(state.available[:techs] * duals, axis=1))
    block = block.at[at].add(own)
    block = block.at[at + 1].add(jnp.sum(duals**2 - taken**2, axis=(0, 1)))
    return exchange(sizes, block)[1]


def run(args, exact):
    rows, techs, nodes = args.availability.shape
    hours, regions = lax.axis_size("hours"), lax.axis_size("region")
    slots, owned = args.cross_limit.shape[1], args.cap_cost.shape[1]
    units, lines = args.store_node.shape[0], args.line_limit.shape[0]
    sizes = Bag(
        rows=rows, techs=techs, nodes=nodes, regions=regions, slots=slots, lines=lines, units=units
    )
    cross = regions * slots

    gathered = both_regions(args.price_start)
    info = call(
        lambda names_in, names_out, *refs: slots_kernel(sizes, *refs),
        Bag(ends=args.cross_ends[:, 0], limit=args.cross_limit, pairs=args.pair_counts),
        Bag(info=shape(8 * (cross // LANES), nodes)),
        smem=(2,),
    ).info
    info = both_regions(info)
    state = call(
        functools.partial(start_kernel, sizes),
        Bag(
            availability=args.availability.reshape(rows * techs, nodes),
            price=args.price_start,
            demand=args.demand,
            gen_cost=args.gen_cost,
            cap_cost=args.cap_cost,
            owner=args.owner_map.reshape(hours, owned),
            line_ends=args.line_ends,
            line_limit=args.line_limit[None],
            store_node=args.store_node[None],
            store_power=args.store_power[None],
            store_energy=args.store_energy[None],
        ),
        Bag(
            available=shape(techs + 2, rows, nodes),
            maps_local=shape(nodes, lines + units, dtype=jnp.bfloat16),
            flows_local=shape(rows, lines + units),
            store_duals=shape(rows, units),
            dispatch=shape(techs + 1, rows, nodes),
            balance=shape(rows, nodes),
            sums=shape(sums_rows(sizes) + 2 * techs, nodes),
        ),
        flops=10**6,
    )
    closed = call(
        lambda names_in, names_out, *refs: close_kernel(sizes, *refs),
        Bag(gathered=gathered, info=info, balance=state.balance, sums=state.sums),
        Bag(
            maps=shape(regions * nodes, cross, dtype=jnp.bfloat16),
            flows=shape(rows + 8, cross),
            block=shape(rows + state.sums.shape[0], nodes),
        ),
    )
    del state.sums, state.balance
    state.maps_cross, state.flows_cross = closed.maps, closed.flows
    gathered, totals = exchange(sizes, closed.block)
    if exact:
        totals = corrected(sizes, state, closed.block, totals)

    for iteration in range(1, ITERS):
        given = Bag(**vars(state), totals=totals, gathered=gathered)
        if iteration < ITERS - 1:
            outs = Bag(
                dispatch=shape(techs + 1, rows, nodes),
                cap_duals=shape(techs + 1, rows, nodes),
                flows_local=shape(rows, lines + units),
                flows_cross=shape(rows + 8, cross),
                store_duals=shape(rows, units),
                charge=shape(rows, units),
                block=shape(rows + sums_rows(sizes), nodes),
            )
        else:
            outs = Bag(
                dispatch=shape(rows * techs, nodes),
                capacity=shape(1, owned),
                prices=shape(rows, nodes),
                charge=shape(rows, units),
                negative=shape(1, LANES),
            )
        results = call(functools.partial(sweep_kernel, sizes, iteration), given, outs)
        if iteration < ITERS - 1:
            gathered, totals = exchange(sizes, results.block)
            del results.block
            vars(state).update(vars(results))
    dispatch = results.dispatch.reshape(rows, techs, nodes)
    outputs = (dispatch, results.capacity, results.prices, results.charge)
    return outputs, results.negative[0, 0]


def body(
    availability,
    demand,
    gen_cost,
    cap_cost,
    owner_map,
    line_ends,
    line_limit,
    cross_ends,
    cross_limit,
    pair_counts,
    store_node,
    store_energy,
    store_power,
    price_start,
):
    args = Bag(**locals())
    outputs, negative = run(args, False)
    return lax.cond(negative > 0.0, lambda: run(args, True)[0], lambda: outputs)


def solution(mesh):
    placed = (
        P("hours", None, "region"),
        P("hours", "region"),
        P(None, "region"),
        P("region", "hours"),
        P("region", None),
        P(None, "region"),
        P("region"),
        P(None, "region", None),
        P("region", None),
        P("region", None),
        P("region"),
        P("region"),
        P("region"),
        P("hours", "region"),
    )
    return jax.shard_map(
        body,
        mesh=mesh,
        in_specs=placed,
        out_specs=(
            P("hours", None, "region"),
            P("region", "hours"),
            P("hours", "region"),
            P("hours", "region"),
        ),
        check_vma=False,
    )
```

```python
import functools
from types import SimpleNamespace as Bag

import jax
import jax.numpy as jnp
from jax import lax
from jax.experimental import pallas as pl
from jax.experimental.pallas import tpu as pltpu
from jax.sharding import PartitionSpec as P

ITERS = 4
EPSILON = 1e-06
LANES = 128
VMEM_BYTES = 24 * 1024 * 1024
SQUARES = 3


def split3(value):
    high = value.astype(jnp.bfloat16)
    rest = value - high.astype(jnp.float32)
    middle = rest.astype(jnp.bfloat16)
    low = (rest - middle.astype(jnp.float32)).astype(jnp.bfloat16)
    return jnp.concatenate([high, middle, low], axis=0)


def dot3(value, matrix, transposed):
    rows = value.shape[0]
    contract = ((1,), (1 if transposed else 0,))
    product = lax.dot_general(
        split3(value), matrix, (contract, ((), ())), preferred_element_type=jnp.float32
    )
    return product[:rows] + product[rows : 2 * rows] + product[2 * rows :]


def row_sum(value):
    return jnp.sum(value, axis=0, keepdims=True)


def fold_lanes(row):
    total = row[:, :LANES]
    for start in range(LANES, row.shape[1], LANES):
        total = total + row[:, start : start + LANES]
    return total


def owned_one_hots(owned, tech_count, node_count):
    shape_t = (tech_count, owned.shape[1])
    shape_n = (node_count, owned.shape[1])
    tech = lax.broadcasted_iota(jnp.int32, shape_t, 0) == owned // node_count
    node = lax.broadcasted_iota(jnp.int32, shape_n, 0) == owned % node_count
    return tech, node.astype(jnp.float32).astype(jnp.bfloat16)


def incidence(start, end, count):
    node = lax.broadcasted_iota(jnp.int32, (count, start.shape[1]), 0)
    maps = (node == end).astype(jnp.float32) - (node == start).astype(jnp.float32)
    return maps.astype(jnp.bfloat16)


def halo_at(sizes):
    return sizes.techs + SQUARES


def sums_rows(sizes):
    return (halo_at(sizes) + 2 * sizes.units // LANES + 7) // 8 * 8


def write_halo(sizes, sums_ref, store_new):
    halo, span, rows = halo_at(sizes), sizes.units // LANES, sizes.rows
    write_lanes(sums_ref, halo, store_new[:1])
    write_lanes(sums_ref, halo + span, store_new[rows - 1 :])
    used, end = halo + 2 * span, sums_rows(sizes)
    if used < end:
        sums_ref[used:end, :] = jnp.zeros((end - used, LANES), jnp.float32)


def write_lanes(ref, start, row):
    for i in range(row.shape[1] // LANES):
        ref[start + i : start + i + 1, :] = row[:, i * LANES : (i + 1) * LANES]


def read_lanes(ref, start, length):
    return jnp.concatenate(
        [ref[start + i : start + i + 1, :] for i in range(length // LANES)], axis=1
    )


def places(sizes):
    span = sizes.units // LANES
    limits = sizes.techs
    energy = limits + (sizes.lines + sizes.units) // LANES
    return Bag(
        limits=limits,
        energy=energy,
        owned=energy + span,
        weight=sizes.techs,
        before=sizes.techs + 1,
        negative=sizes.techs + 1 + span,
    )


def slots_kernel(sizes, ends_ref, limit_ref, pairs_ref, info_ref):
    nodes, slots, regions = sizes.nodes, sizes.slots, sizes.regions
    own = lax.axis_index("region")
    width = slots // regions
    slot = lax.broadcasted_iota(jnp.int32, (1, slots), 1)
    pair = slot // width
    in_use = jnp.zeros((1, slots), jnp.int32)
    for target in range(regions):
        in_use = jnp.where(pair == target, pairs_ref[0:1, target : target + 1], in_use)
    place = lax.broadcasted_iota(jnp.int32, (slots, regions * slots), 1) == (
        own * slots + lax.broadcasted_iota(jnp.int32, (slots, regions * slots), 0)
    )
    place = place.astype(jnp.float32).astype(jnp.bfloat16)
    bound = jnp.where(slot % width < in_use, limit_ref[...], 0.0)
    start = (ends_ref[0:1, :] + own * nodes).astype(jnp.float32)
    end = (ends_ref[1:2, :] + pair * nodes).astype(jnp.float32)
    rest = jnp.zeros((13, slots), jnp.float32)
    info = dot3(jnp.concatenate([start, end, bound, rest], axis=0), place, False)
    for chunk in range(regions * slots // LANES):
        info_ref[8 * chunk : 8 * chunk + 8, :] = info[:8, chunk * LANES : (chunk + 1) * LANES]


def start_kernel(sizes, names_in, names_out, *refs):
    given = Bag(**dict(zip(names_in, refs[: len(names_in)])))
    gives = Bag(**dict(zip(names_out, refs[len(names_in) :])))
    rows, techs, nodes, lines = sizes.rows, sizes.techs, sizes.nodes, sizes.lines
    at = places(sizes)
    fixed = gives.available.at[techs + 1]
    gives.available[techs] = given.demand[...]
    fixed[:techs, :] = given.gen_cost[...]
    write_lanes(fixed, at.energy, given.store_energy[...])
    owned = given.owner[pl.ds(lax.axis_index("hours"), 1), :]
    fixed[at.owned : at.owned + 1, : owned.shape[1]] = owned.astype(jnp.float32)
    line_ends, stores = given.line_ends[...], given.store_node[...]
    start = jnp.concatenate([line_ends[0:1], jnp.full_like(stores, -1)], axis=1)
    end = jnp.concatenate([line_ends[1:2], stores], axis=1)
    maps = incidence(start, end, nodes)
    limits = jnp.concatenate([given.line_limit[...], given.store_power[...]], axis=1)
    gives.maps_local[...] = maps
    write_lanes(fixed, at.limits, limits)
    prices = given.price[...]
    flows = jnp.clip(-0.5 * dot3(prices, maps, False), -limits, limits)
    gives.flows_local[...] = flows
    store_new = (1.0 / 3.0) * (2.0 * flows[:, lines:])
    gives.store_duals[...] = store_new
    primal_row = fold_lanes(row_sum(flows * flows))
    dual_row = fold_lanes(row_sum(store_new * store_new))
    balance = dot3(2.0 * flows, maps, True) - given.demand[...]
    gen_cost = given.gen_cost[...]
    acc = jnp.zeros((rows, nodes), jnp.float32)
    weights = jnp.zeros((techs, nodes), jnp.float32)
    for hour in range(rows):
        weights = weights + given.availability[hour * techs : (hour + 1) * techs, :]
    for tech in range(techs):
        avail = given.availability[pl.ds(tech, rows, stride=techs), :]
        gives.available[tech] = avail
        dispatch = jnp.maximum(-0.5 * (gen_cost[tech : tech + 1] + prices), 0.0)
        gives.dispatch[tech] = dispatch
        dispatch_bar = 2.0 * dispatch
        balance = balance + dispatch_bar
        duals = jnp.maximum(0.5 * dispatch_bar, 0.0)
        acc = acc + dispatch * dispatch
        gives.sums[tech : tech + 1, :] = row_sum(avail * duals)
    gives.balance[...] = balance
    squares = row_sum(acc)
    cost = given.cap_cost[...]
    negative = jnp.sum((cost < 0.0).astype(jnp.float32), axis=1, keepdims=True)
    write_halo(sizes, gives.sums, store_new)
    gives.sums[techs : techs + SQUARES, :] = jnp.concatenate(
        [primal_row + squares, dual_row + squares, jnp.broadcast_to(negative, (1, LANES))], axis=0
    )
    tech_hot, node_hot = owned_one_hots(owned, techs, nodes)
    first = sums_rows(sizes)
    gives.sums[first : first + techs, :] = weights
    gives.sums[first + techs : first + 2 * techs, :] = dot3(
        jnp.where(tech_hot, cost, 0.0), node_hot, True
    )


def close_kernel(
    sizes,
    gathered,
    info_ref,
    balance_ref,
    sums_in_ref,
    maps_ref,
    flows_ref,
    prices_ref,
    sums_ref,
):
    rows, techs, nodes = sizes.rows, sizes.techs, sizes.nodes
    slots, regions = sizes.slots, sizes.regions
    own = lax.axis_index("region")
    chunks = []
    for chunk in range(regions * slots // LANES):
        at = slice(8 * chunk, 8 * chunk + 8)
        part = info_ref[0, at, :]
        for region in range(1, regions):
            part = part + info_ref[region, at, :]
        chunks.append(part)
    info = jnp.concatenate(chunks, axis=1) if len(chunks) > 1 else chunks[0]
    maps_ref[...] = incidence(
        info[0:1].astype(jnp.int32), info[1:2].astype(jnp.int32), regions * nodes
    )
    limits = info[2:3]
    prices_all = jnp.concatenate([gathered[region, :rows, :] for region in range(regions)], axis=1)
    flows = jnp.clip(-0.5 * dot3(prices_all, maps_ref[...], False), -limits, limits)
    flows_ref[:rows, :] = flows
    flows_ref[rows : rows + 1, :] = limits
    maps_own = maps_ref[pl.ds(pl.multiple_of(own * nodes, nodes), nodes), :]
    balance = balance_ref[...] + dot3(2.0 * flows, maps_own, True)
    step_up = (1.0 / (techs + 8.0)) * balance
    prices_ref[...] = gathered[own, :rows, :] + step_up
    change = row_sum(flows * flows)
    slot = lax.broadcasted_iota(jnp.int32, change.shape, 1)
    primal = fold_lanes(jnp.where(slot // slots == own, change, 0.0))
    more = jnp.concatenate(
        [primal, row_sum(step_up * step_up), jnp.zeros((SQUARES - 2, LANES), jnp.float32)], axis=0
    )
    sums_ref[...] = sums_in_ref[...]
    squares = sums_in_ref[techs : techs + SQUARES, :] + more
    sums_ref[techs : techs + SQUARES, :] = squares


def neighbour_rows(sizes, given, hour_index):
    units = sizes.units
    if hasattr(given, "totals"):
        return read_lanes(given.next_row, 0, units), read_lanes(given.prev_row, 0, units)
    first = halo_at(sizes)
    last = first + units // LANES
    core, x_place, odd = hour_index % 2, hour_index // 2 % 2, hour_index // 4 % 2
    next_row = jnp.where(
        odd == 0, read_lanes(given.near, first, units), read_lanes(given.far, first, units)
    )
    prev_row = jnp.where(
        odd == 0, read_lanes(given.far, last, units), read_lanes(given.near, last, units)
    )
    next_row = jnp.where(x_place == 0, read_lanes(given.across, first, units), next_row)
    prev_row = jnp.where(x_place == 0, prev_row, read_lanes(given.across, last, units))
    next_row = jnp.where(core == 0, read_lanes(given.partner, first, units), next_row)
    prev_row = jnp.where(core == 0, prev_row, read_lanes(given.partner, last, units))
    return next_row, prev_row


def total_of(parts):
    if hasattr(parts, "totals"):
        return parts.totals[...]
    return (parts.slab[...] + parts.near[...]) + (parts.middle[...] + parts.far[...])


def sweep_kernel(sizes, iteration, names_in, names_out, *refs):
    rows, techs, nodes = sizes.rows, sizes.techs, sizes.nodes
    slots, regions, lines, units = sizes.slots, sizes.regions, sizes.lines, sizes.units
    second = iteration == 1
    last = iteration == ITERS - 1
    given = Bag(**dict(zip(names_in, refs[: len(names_in)])))
    gives = Bag(**dict(zip(names_out, refs[len(names_in) :])))
    own = lax.axis_index("region")
    hour_index = lax.axis_index("hours")
    gathered = given.gathered

    at = places(sizes)
    fixed = given.available.at[techs + 1]
    small = given.dispatch.at[techs]
    sums = total_of(given)
    squares = jnp.sum(sums[techs : techs + 2], axis=1, keepdims=True)
    old_weight = jnp.ones((1, 1), jnp.float32) if second else small[at.weight : at.weight + 1, :1]
    weight = jnp.sqrt(
        old_weight * jnp.sqrt((squares[1:2] + EPSILON) / (squares[0:1] + EPSILON))
    )
    primal_step = 0.5 / weight
    if second:
        first = sums_rows(sizes)
        col_weight, cost = sums[first : first + techs], sums[first + techs : first + 2 * techs]
        negative = sums[techs + 2 : techs + 3]
        capacity = jnp.maximum(-cost / col_weight, 0.0)
        first_bar = 2.0 * capacity
    else:
        col_weight = given.cap_duals[techs, :techs, :]
        cost = given.cap_duals[techs, techs : 2 * techs, :]
        capacity = small[:techs, :]
        negative = small[at.negative : at.negative + 1, :]
    capacity_new = jnp.maximum(capacity - (cost - sums[:techs]) / (weight * col_weight), 0.0)
    capacity_bar = 2.0 * capacity_new - capacity

    prices_all = jnp.concatenate([gathered[region, :rows, :] for region in range(regions)], axis=1)
    prices = gathered[own, :rows, :]
    maps_local = given.maps_local[...]
    slope_local = dot3(prices, maps_local, False)
    slope_cross = dot3(prices_all, given.maps_cross[...], False)

    energy = read_lanes(fixed, at.energy, units)
    row_id = lax.broadcasted_iota(jnp.int32, (rows, units), 0)
    next_row, prev_row = neighbour_rows(sizes, given, hour_index)
    store_duals = given.store_duals[...]
    next_duals = jnp.where(row_id == rows - 1, next_row, pltpu.roll(store_duals, rows - 1, 0))
    if second:
        charge = jnp.zeros((rows, units), jnp.float32)
        charge_before = jnp.zeros((1, units), jnp.float32)
    else:
        charge = given.charge[...]
        charge_before = read_lanes(small, at.before, units)
    charge_new = jnp.clip(charge - primal_step * (store_duals - next_duals), 0.0, energy)
    gives.charge[...] = charge_new

    primal_row = jnp.zeros((1, LANES), jnp.float32)
    bars = []
    local_out = None if last else gives.flows_local
    cross_out = None if last else gives.flows_cross
    local_limits = read_lanes(fixed, at.limits, lines + units)
    cross_limits = given.flows_cross[rows : rows + 1, :]
    for flows, out, limits, slope, low, high in (
        (given.flows_local, local_out, local_limits, slope_local, 0, lines),
        (given.flows_local, local_out, local_limits, slope_local, lines, lines + units),
        (given.flows_cross, cross_out, cross_limits, slope_cross, 0, regions * slots),
    ):
        slope = slope[:, low:high]
        if low:
            slope = slope + store_duals
        bound = limits[:, low:high]
        old = flows[:rows, low:high]
        new = jnp.clip(old - primal_step * slope, -bound, bound)
        bars.append(2.0 * new - old)
        if not last:
            out[:rows, low:high] = new
            change = row_sum((new - old) ** 2)
            if out is cross_out:
                slot = lax.broadcasted_iota(jnp.int32, change.shape, 1)
                change = jnp.where(slot // slots == own, change, 0.0)
            primal_row = primal_row + fold_lanes(change)
    maps_own = given.maps_cross[pl.ds(pl.multiple_of(own * nodes, nodes), nodes), :]
    balance = dot3(jnp.concatenate(bars[:2], axis=1), maps_local, True) - given.available[techs]
    balance = balance + dot3(bars[2], maps_own, True)

    gen_cost = fixed[:techs, :]
    half_weight = weight / 2.0
    primal_acc = jnp.zeros((rows, nodes), jnp.float32)
    dual_acc = jnp.zeros((rows, nodes), jnp.float32)
    for tech in range(techs):
        slope = gen_cost[tech : tech + 1] + prices
        dispatch = given.dispatch[tech]
        avail = given.available[tech]
        if second:
            duals = jnp.maximum(0.5 * (2.0 * dispatch - avail * first_bar[tech : tech + 1]), 0.0)
        else:
            duals = given.cap_duals[tech]
        dispatch_new = jnp.maximum(dispatch - primal_step * (slope + duals), 0.0)
        dispatch_bar = 2.0 * dispatch_new - dispatch
        balance = balance + dispatch_bar
        if last:
            gives.dispatch[pl.ds(tech, rows, stride=techs), :] = dispatch_new
            continue
        gives.dispatch[tech] = dispatch_new
        cap_rows = dispatch_bar - avail * capacity_bar[tech : tech + 1]
        primal_acc = primal_acc + (dispatch_new - dispatch) ** 2
        duals_new = jnp.maximum(duals + half_weight * cap_rows, 0.0)
        dual_acc = dual_acc + (duals_new - duals) ** 2
        gives.cap_duals[tech] = duals_new
        gives.sums[tech : tech + 1, :] = row_sum(avail * duals_new)

    step_up = weight / (techs + 8.0) * balance
    if last:
        gives.prices[...] = prices + step_up
        owned = fixed[at.owned : at.owned + 1, : gives.capacity.shape[1]].astype(jnp.int32)
        tech_hot, node_hot = owned_one_hots(owned, techs, nodes)
        chosen = dot3(capacity_new, node_hot, False)
        gives.capacity[...] = row_sum(jnp.where(tech_hot, chosen, 0.0))
        gives.negative[...] = negative
        return
    gives.prices[...] = prices + step_up
    gives.flows_cross[rows : rows + 1, :] = cross_limits
    gives.cap_duals[techs, :techs, :] = col_weight
    gives.cap_duals[techs, techs : 2 * techs, :] = cost
    small_new = gives.dispatch.at[techs]
    small_new[:techs, :] = capacity_new
    small_new[at.weight : at.weight + 1, :] = jnp.broadcast_to(weight, (1, LANES))
    small_new[at.negative : at.negative + 1, :] = negative
    charge_bar = 2.0 * charge_new - charge
    before_new = jnp.clip(charge_before - primal_step * (prev_row - store_duals[0:1]), 0.0, energy)
    write_lanes(small_new, at.before, before_new)
    before_bar = 2.0 * before_new - charge_before
    shifted_bar = jnp.where(row_id == 0, before_bar, pltpu.roll(charge_bar, 1, 0))
    store_step = weight / 3.0 * (charge_bar - shifted_bar + bars[1])
    store_new = store_duals + store_step
    gives.store_duals[...] = store_new
    primal_row = primal_row + row_sum(primal_acc) + fold_lanes(row_sum((charge_new - charge) ** 2))
    primal_row = primal_row + jnp.where(
        hour_index == 0, row_sum((capacity_new - capacity) ** 2), 0.0
    )
    dual_row = row_sum(dual_acc + step_up * step_up) + fold_lanes(row_sum(store_step * store_step))
    squares = jnp.concatenate(
        [primal_row, dual_row, jnp.zeros((SQUARES - 2, LANES), jnp.float32)], axis=0
    )
    gives.sums[techs : techs + SQUARES, :] = squares
    write_halo(sizes, gives.sums, store_new)


def call(kernel, given, outs, flops=0, smem=()):
    names_in, names_out = tuple(vars(given)), tuple(vars(outs))
    values = pl.pallas_call(
        functools.partial(kernel, names_in, names_out),
        out_shape=tuple(vars(outs).values()),
        in_specs=[
            pl.BlockSpec(memory_space=pltpu.SMEM if i in smem else pltpu.VMEM)
            for i in range(len(names_in))
        ],
        out_specs=[pl.BlockSpec(memory_space=pltpu.VMEM)] * len(names_out),
        cost_estimate=pl.CostEstimate(flops=flops, bytes_accessed=4 * flops, transcendentals=0),
        compiler_params=pltpu.CompilerParams(vmem_limit_bytes=VMEM_BYTES),
    )(*vars(given).values())
    return Bag(**dict(zip(names_out, values)))


def swap(value, hour_bit, region_bit):
    hours, regions = lax.axis_size("hours"), lax.axis_size("region")
    pairs = [
        (hour * regions + region, (hour ^ hour_bit) * regions + (region ^ region_bit))
        for hour in range(hours)
        for region in range(regions)
    ]
    return lax.ppermute(value, ("hours", "region"), pairs)


def shifted(value, steps):
    count = lax.axis_size("hours")
    return lax.ppermute(value, "hours", [(i, (i + steps) % count) for i in range(count)])


def both_regions(block):
    if lax.axis_size("region") != 2:
        return lax.all_gather(block, "region")
    return in_order(block, swap(block, 0, 1))


def in_order(block, other):
    return jnp.where(
        lax.axis_index("region") == 0, jnp.stack([block, other]), jnp.stack([other, block])
    )


def exchange(sizes, prices, sums):
    hours, regions = lax.axis_size("hours"), lax.axis_size("region")
    techs, span = sizes.techs, sizes.units // LANES
    halo = halo_at(sizes)
    if regions != 2 or hours != 16:
        gathered = lax.all_gather(prices, "region")
        totals = lax.psum(sums, "hours")
        totals = totals.at[techs:halo].set(lax.psum(totals[techs:halo], "region"))
        next_row = shifted(sums[halo : halo + span], -1)
        prev_row = shifted(sums[halo + span : halo + 2 * span], 1)
        return gathered, Bag(totals=totals, next_row=next_row, prev_row=prev_row)

    def merged(mine, yours, mine_first):
        last = halo + span
        edges = [
            jnp.where(mine_first, mine[halo:last], yours[halo:last]),
            jnp.where(mine_first, yours[last : last + span], mine[last : last + span]),
        ]
        total = mine + yours
        return jnp.concatenate([total[:halo], *edges, total[last + span :]], axis=0)

    hour = lax.axis_index("hours")
    partner = swap(sums, 1, 0)
    chip = merged(sums, partner, hour % 2 == 0)
    across = swap(chip, 2, 0)
    diagonal = swap(chip[techs:halo], 2, 1)
    beside = swap(jnp.concatenate([prices, chip[techs:halo]], axis=0), 0, 1)
    other, squares = beside[: sizes.rows], beside[sizes.rows :]
    slab = merged(chip, across, hour // 2 % 2 == 0)
    slab = slab.at[techs:halo].add(squares + diagonal)
    near, middle, far = [swap(slab, 4 * step, 0) for step in (1, 2, 3)]
    parts = Bag(slab=slab, near=near, middle=middle, far=far, partner=partner, across=across)
    return in_order(prices, other), parts


def shape(*dims, dtype=jnp.float32):
    return jax.ShapeDtypeStruct(dims, dtype)


def corrected(sizes, state, prices, sums, parts):
    techs = sizes.techs
    totals = total_of(parts)
    first = sums_rows(sizes)
    col_weight, cost = totals[first : first + techs], totals[first + techs :]
    capacity = jnp.maximum(-cost / col_weight, 0.0)
    taken = state.dispatch[:techs]
    rows_of = 2.0 * taken - state.available[:techs] * (2.0 * capacity)[:, None, :]
    duals = jnp.maximum(0.5 * rows_of, 0.0)
    own = jnp.where(lax.axis_index("hours") == 0, jnp.sum(capacity**2, axis=0), 0.0)
    fixed = sums.at[:techs].set(jnp.sum(state.available[:techs] * duals, axis=1))
    fixed = fixed.at[techs].add(own)
    fixed = fixed.at[techs + 1].add(jnp.sum(duals**2 - taken**2, axis=(0, 1)))
    return exchange(sizes, prices, fixed)[1]


def run(args, exact):
    rows, techs, nodes = args.availability.shape
    hours, regions = lax.axis_size("hours"), lax.axis_size("region")
    slots, owned = args.cross_limit.shape[1], args.cap_cost.shape[1]
    units, lines = args.store_node.shape[0], args.line_limit.shape[0]
    sizes = Bag(
        rows=rows, techs=techs, nodes=nodes, regions=regions, slots=slots, lines=lines, units=units
    )
    cross = regions * slots

    gathered = both_regions(args.price_start)
    info = call(
        lambda names_in, names_out, *refs: slots_kernel(sizes, *refs),
        Bag(ends=args.cross_ends[:, 0], limit=args.cross_limit, pairs=args.pair_counts),
        Bag(info=shape(8 * (cross // LANES), nodes)),
    ).info
    info = both_regions(info)
    state = call(
        functools.partial(start_kernel, sizes),
        Bag(
            availability=args.availability.reshape(rows * techs, nodes),
            price=args.price_start,
            demand=args.demand,
            gen_cost=args.gen_cost,
            cap_cost=args.cap_cost,
            owner=args.owner_map.reshape(hours, owned),
            line_ends=args.line_ends,
            line_limit=args.line_limit[None],
            store_node=args.store_node[None],
            store_power=args.store_power[None],
            store_energy=args.store_energy[None],
        ),
        Bag(
            available=shape(techs + 2, rows, nodes),
            maps_local=shape(nodes, lines + units, dtype=jnp.bfloat16),
            flows_local=shape(rows, lines + units),
            store_duals=shape(rows, units),
            dispatch=shape(techs + 1, rows, nodes),
            balance=shape(rows, nodes),
            sums=shape(sums_rows(sizes) + 2 * techs, nodes),
        ),
        flops=10**6,
    )
    closed = call(
        lambda names_in, names_out, *refs: close_kernel(sizes, *refs),
        Bag(gathered=gathered, info=info, balance=state.balance, sums=state.sums),
        Bag(
            maps=shape(regions * nodes, cross, dtype=jnp.bfloat16),
            flows=shape(rows + 8, cross),
            prices=shape(rows, nodes),
            sums=shape(*state.sums.shape),
        ),
    )
    del state.sums, state.balance
    state.maps_cross, state.flows_cross = closed.maps, closed.flows
    gathered, parts = exchange(sizes, closed.prices, closed.sums)
    if exact:
        parts = corrected(sizes, state, closed.prices, closed.sums, parts)

    for iteration in range(1, ITERS):
        given = Bag(**vars(state), **vars(parts), gathered=gathered)
        if iteration < ITERS - 1:
            outs = Bag(
                dispatch=shape(techs + 1, rows, nodes),
                cap_duals=shape(techs + 1, rows, nodes),
                flows_local=shape(rows, lines + units),
                flows_cross=shape(rows + 8, cross),
                store_duals=shape(rows, units),
                charge=shape(rows, units),
                prices=shape(rows, nodes),
                sums=shape(sums_rows(sizes), nodes),
            )
        else:
            outs = Bag(
                dispatch=shape(rows * techs, nodes),
                capacity=shape(1, owned),
                prices=shape(rows, nodes),
                charge=shape(rows, units),
                negative=shape(1, LANES),
            )
        results = call(functools.partial(sweep_kernel, sizes, iteration), given, outs)
        if iteration < ITERS - 1:
            gathered, parts = exchange(sizes, results.prices, results.sums)
            del results.prices, results.sums
            vars(state).update(vars(results))
    dispatch = results.dispatch.reshape(rows, techs, nodes)
    outputs = (dispatch, results.capacity, results.prices, results.charge)
    return outputs, results.negative[0, 0]


def body(
    availability,
    demand,
    gen_cost,
    cap_cost,
    owner_map,
    line_ends,
    line_limit,
    cross_ends,
    cross_limit,
    pair_counts,
    store_node,
    store_energy,
    store_power,
    price_start,
):
    args = Bag(**locals())
    outputs, negative = run(args, False)
    return lax.cond(negative > 0.0, lambda: run(args, True)[0], lambda: outputs)


def solution(mesh):
    placed = (
        P("hours", None, "region"),
        P("hours", "region"),
        P(None, "region"),
        P("region", "hours"),
        P("region", None),
        P(None, "region"),
        P("region"),
        P(None, "region", None),
        P("region", None),
        P("region", None),
        P("region"),
        P("region"),
        P("region"),
        P("hours", "region"),
    )
    return jax.shard_map(
        body,
        mesh=mesh,
        in_specs=placed,
        out_specs=(
            P("hours", None, "region"),
            P("region", "hours"),
            P("hours", "region"),
            P("hours", "region"),
        ),
        check_vma=False,
    )
```

```python
import functools
from types import SimpleNamespace as Bag

import jax
import jax.numpy as jnp
from jax import lax
from jax.experimental import pallas as pl
from jax.experimental.pallas import tpu as pltpu
from jax.sharding import PartitionSpec as P

ITERS = 4
EPSILON = 1e-06
LANES = 128
VMEM_BYTES = 24 * 1024 * 1024
SQUARES = 3


def split3(value):
    high = value.astype(jnp.bfloat16)
    rest = value - high.astype(jnp.float32)
    middle = rest.astype(jnp.bfloat16)
    low = (rest - middle.astype(jnp.float32)).astype(jnp.bfloat16)
    return jnp.concatenate([high, middle, low], axis=0)


def dot3(value, matrix, transposed):
    rows = value.shape[0]
    contract = ((1,), (1 if transposed else 0,))
    product = lax.dot_general(
        split3(value), matrix, (contract, ((), ())), preferred_element_type=jnp.float32
    )
    return product[:rows] + product[rows : 2 * rows] + product[2 * rows :]


def row_sum(value):
    return jnp.sum(value, axis=0, keepdims=True)


def fold_lanes(row):
    total = row[:, :LANES]
    for start in range(LANES, row.shape[1], LANES):
        total = total + row[:, start : start + LANES]
    return total


def owned_one_hots(owned, tech_count, node_count):
    shape_t = (tech_count, owned.shape[1])
    shape_n = (node_count, owned.shape[1])
    tech = lax.broadcasted_iota(jnp.int32, shape_t, 0) == owned // node_count
    node = lax.broadcasted_iota(jnp.int32, shape_n, 0) == owned % node_count
    return tech, node.astype(jnp.float32).astype(jnp.bfloat16)


def incidence(start, end, count):
    node = lax.broadcasted_iota(jnp.int32, (count, start.shape[1]), 0)
    maps = (node == end).astype(jnp.float32) - (node == start).astype(jnp.float32)
    return maps.astype(jnp.bfloat16)


def halo_at(sizes):
    return sizes.techs + SQUARES


def sums_rows(sizes):
    return (halo_at(sizes) + 2 * sizes.units // LANES + 7) // 8 * 8


def write_halo(sizes, sums_ref, store_new):
    halo, span, rows = halo_at(sizes), sizes.units // LANES, sizes.rows
    write_lanes(sums_ref, halo, store_new[:1])
    write_lanes(sums_ref, halo + span, store_new[rows - 1 :])
    used, end = halo + 2 * span, sums_rows(sizes)
    if used < end:
        sums_ref[used:end, :] = jnp.zeros((end - used, LANES), jnp.float32)


def write_lanes(ref, start, row):
    for i in range(row.shape[1] // LANES):
        ref[start + i : start + i + 1, :] = row[:, i * LANES : (i + 1) * LANES]


def read_lanes(ref, start, length):
    return jnp.concatenate(
        [ref[start + i : start + i + 1, :] for i in range(length // LANES)], axis=1
    )


def places(sizes):
    span = sizes.units // LANES
    limits = sizes.techs
    energy = limits + (sizes.lines + sizes.units) // LANES
    return Bag(
        limits=limits,
        energy=energy,
        owned=energy + span,
        weight=sizes.techs,
        before=sizes.techs + 1,
        negative=sizes.techs + 1 + span,
    )


def slots_kernel(sizes, ends_ref, limit_ref, pairs_ref, info_ref):
    nodes, slots, regions = sizes.nodes, sizes.slots, sizes.regions
    own = lax.axis_index("region")
    width = slots // regions
    slot = lax.broadcasted_iota(jnp.int32, (1, slots), 1)
    pair = slot // width
    in_use = jnp.zeros((1, slots), jnp.int32)
    for target in range(regions):
        in_use = jnp.where(pair == target, pairs_ref[0:1, target : target + 1], in_use)
    place = lax.broadcasted_iota(jnp.int32, (slots, regions * slots), 1) == (
        own * slots + lax.broadcasted_iota(jnp.int32, (slots, regions * slots), 0)
    )
    place = place.astype(jnp.float32).astype(jnp.bfloat16)
    bound = jnp.where(slot % width < in_use, limit_ref[...], 0.0)
    start = (ends_ref[0:1, :] + own * nodes).astype(jnp.float32)
    end = (ends_ref[1:2, :] + pair * nodes).astype(jnp.float32)
    rest = jnp.zeros((13, slots), jnp.float32)
    info = dot3(jnp.concatenate([start, end, bound, rest], axis=0), place, False)
    for chunk in range(regions * slots // LANES):
        info_ref[8 * chunk : 8 * chunk + 8, :] = info[:8, chunk * LANES : (chunk + 1) * LANES]


def start_kernel(sizes, names_in, names_out, *refs):
    given = Bag(**dict(zip(names_in, refs[: len(names_in)])))
    gives = Bag(**dict(zip(names_out, refs[len(names_in) :])))
    rows, techs, nodes, lines = sizes.rows, sizes.techs, sizes.nodes, sizes.lines
    at = places(sizes)
    fixed = gives.available.at[techs + 1]
    gives.available[techs] = given.demand[...]
    fixed[:techs, :] = given.gen_cost[...]
    write_lanes(fixed, at.energy, given.store_energy[...])
    owned = given.owner[pl.ds(lax.axis_index("hours"), 1), :]
    fixed[at.owned : at.owned + 1, : owned.shape[1]] = owned.astype(jnp.float32)
    line_ends, stores = given.line_ends[...], given.store_node[...]
    start = jnp.concatenate([line_ends[0:1], jnp.full_like(stores, -1)], axis=1)
    end = jnp.concatenate([line_ends[1:2], stores], axis=1)
    maps = incidence(start, end, nodes)
    limits = jnp.concatenate([given.line_limit[...], given.store_power[...]], axis=1)
    gives.maps_local[...] = maps
    write_lanes(fixed, at.limits, limits)
    prices = given.price[...]
    flows = jnp.clip(-0.5 * dot3(prices, maps, False), -limits, limits)
    gives.flows_local[...] = flows
    store_new = (1.0 / 3.0) * (2.0 * flows[:, lines:])
    gives.store_duals[...] = store_new
    primal_row = fold_lanes(row_sum(flows * flows))
    dual_row = fold_lanes(row_sum(store_new * store_new))
    balance = dot3(2.0 * flows, maps, True) - given.demand[...]
    gen_cost = given.gen_cost[...]
    acc = jnp.zeros((rows, nodes), jnp.float32)
    weights = jnp.zeros((techs, nodes), jnp.float32)
    for hour in range(rows):
        weights = weights + given.availability[hour * techs : (hour + 1) * techs, :]
    for tech in range(techs):
        avail = given.availability[pl.ds(tech, rows, stride=techs), :]
        gives.available[tech] = avail
        dispatch = jnp.maximum(-0.5 * (gen_cost[tech : tech + 1] + prices), 0.0)
        gives.dispatch[tech] = dispatch
        dispatch_bar = 2.0 * dispatch
        balance = balance + dispatch_bar
        duals = jnp.maximum(0.5 * dispatch_bar, 0.0)
        acc = acc + dispatch * dispatch
        gives.sums[tech : tech + 1, :] = row_sum(avail * duals)
    gives.balance[...] = balance
    squares = row_sum(acc)
    cost = given.cap_cost[...]
    negative = jnp.sum((cost < 0.0).astype(jnp.float32), axis=1, keepdims=True)
    write_halo(sizes, gives.sums, store_new)
    gives.sums[techs : techs + SQUARES, :] = jnp.concatenate(
        [primal_row + squares, dual_row + squares, jnp.broadcast_to(negative, (1, LANES))], axis=0
    )
    tech_hot, node_hot = owned_one_hots(owned, techs, nodes)
    first = sums_rows(sizes)
    gives.sums[first : first + techs, :] = weights
    gives.sums[first + techs : first + 2 * techs, :] = dot3(
        jnp.where(tech_hot, cost, 0.0), node_hot, True
    )


def close_kernel(
    sizes,
    gathered,
    info_ref,
    balance_ref,
    sums_in_ref,
    maps_ref,
    flows_ref,
    prices_ref,
    sums_ref,
):
    rows, techs, nodes = sizes.rows, sizes.techs, sizes.nodes
    slots, regions = sizes.slots, sizes.regions
    own = lax.axis_index("region")
    chunks = []
    for chunk in range(regions * slots // LANES):
        at = slice(8 * chunk, 8 * chunk + 8)
        part = info_ref[0, at, :]
        for region in range(1, regions):
            part = part + info_ref[region, at, :]
        chunks.append(part)
    info = jnp.concatenate(chunks, axis=1) if len(chunks) > 1 else chunks[0]
    maps_ref[...] = incidence(
        info[0:1].astype(jnp.int32), info[1:2].astype(jnp.int32), regions * nodes
    )
    limits = info[2:3]
    prices_all = jnp.concatenate([gathered[region, :rows, :] for region in range(regions)], axis=1)
    flows = jnp.clip(-0.5 * dot3(prices_all, maps_ref[...], False), -limits, limits)
    flows_ref[:rows, :] = flows
    flows_ref[rows : rows + 1, :] = limits
    maps_own = maps_ref[pl.ds(pl.multiple_of(own * nodes, nodes), nodes), :]
    balance = balance_ref[...] + dot3(2.0 * flows, maps_own, True)
    step_up = (1.0 / (techs + 8.0)) * balance
    prices_ref[...] = gathered[own, :rows, :] + step_up
    change = row_sum(flows * flows)
    slot = lax.broadcasted_iota(jnp.int32, change.shape, 1)
    primal = fold_lanes(jnp.where(slot // slots == own, change, 0.0))
    more = jnp.concatenate(
        [primal, row_sum(step_up * step_up), jnp.zeros((SQUARES - 2, LANES), jnp.float32)], axis=0
    )
    sums_ref[...] = sums_in_ref[...]
    squares = sums_in_ref[techs : techs + SQUARES, :] + more
    sums_ref[techs : techs + SQUARES, :] = squares


def neighbour_rows(sizes, given, hour_index):
    units = sizes.units
    if hasattr(given, "totals"):
        return read_lanes(given.next_row, 0, units), read_lanes(given.prev_row, 0, units)
    first = halo_at(sizes)
    last = first + units // LANES
    core, x_place, odd = hour_index % 2, hour_index // 2 % 2, hour_index // 4 % 2
    next_row = jnp.where(
        odd == 0, read_lanes(given.near, first, units), read_lanes(given.far, first, units)
    )
    prev_row = jnp.where(
        odd == 0, read_lanes(given.far, last, units), read_lanes(given.near, last, units)
    )
    next_row = jnp.where(x_place == 0, read_lanes(given.across, first, units), next_row)
    prev_row = jnp.where(x_place == 0, prev_row, read_lanes(given.across, last, units))
    next_row = jnp.where(core == 0, read_lanes(given.partner, first, units), next_row)
    prev_row = jnp.where(core == 0, prev_row, read_lanes(given.partner, last, units))
    return next_row, prev_row


def total_of(parts):
    if hasattr(parts, "totals"):
        return parts.totals[...]
    return (parts.slab[...] + parts.near[...]) + (parts.middle[...] + parts.far[...])


def sweep_kernel(sizes, iteration, names_in, names_out, *refs):
    rows, techs, nodes = sizes.rows, sizes.techs, sizes.nodes
    slots, regions, lines, units = sizes.slots, sizes.regions, sizes.lines, sizes.units
    second = iteration == 1
    last = iteration == ITERS - 1
    given = Bag(**dict(zip(names_in, refs[: len(names_in)])))
    gives = Bag(**dict(zip(names_out, refs[len(names_in) :])))
    own = lax.axis_index("region")
    hour_index = lax.axis_index("hours")
    gathered = given.gathered

    at = places(sizes)
    fixed = given.available.at[techs + 1]
    small = given.dispatch.at[techs]
    sums = total_of(given)
    squares = jnp.sum(sums[techs : techs + 2], axis=1, keepdims=True)
    old_weight = jnp.ones((1, 1), jnp.float32) if second else small[at.weight : at.weight + 1, :1]
    weight = jnp.sqrt(
        old_weight * jnp.sqrt((squares[1:2] + EPSILON) / (squares[0:1] + EPSILON))
    )
    primal_step = 0.5 / weight
    if second:
        first = sums_rows(sizes)
        col_weight, cost = sums[first : first + techs], sums[first + techs : first + 2 * techs]
        negative = sums[techs + 2 : techs + 3]
        capacity = jnp.maximum(-cost / col_weight, 0.0)
        first_bar = 2.0 * capacity
    else:
        col_weight = given.cap_duals[techs, :techs, :]
        cost = given.cap_duals[techs, techs : 2 * techs, :]
        capacity = small[:techs, :]
        negative = small[at.negative : at.negative + 1, :]
    capacity_new = jnp.maximum(capacity - (cost - sums[:techs]) / (weight * col_weight), 0.0)
    capacity_bar = 2.0 * capacity_new - capacity

    prices_all = jnp.concatenate([gathered[region, :rows, :] for region in range(regions)], axis=1)
    prices = gathered[own, :rows, :]
    maps_local = given.maps_local[...]
    slope_local = dot3(prices, maps_local, False)
    slope_cross = dot3(prices_all, given.maps_cross[...], False)

    energy = read_lanes(fixed, at.energy, units)
    row_id = lax.broadcasted_iota(jnp.int32, (rows, units), 0)
    next_row, prev_row = neighbour_rows(sizes, given, hour_index)
    store_duals = given.store_duals[...]
    next_duals = jnp.where(row_id == rows - 1, next_row, pltpu.roll(store_duals, rows - 1, 0))
    if second:
        charge = jnp.zeros((rows, units), jnp.float32)
        charge_before = jnp.zeros((1, units), jnp.float32)
    else:
        charge = given.charge[...]
        charge_before = read_lanes(small, at.before, units)
    charge_new = jnp.clip(charge - primal_step * (store_duals - next_duals), 0.0, energy)
    gives.charge[...] = charge_new

    primal_row = jnp.zeros((1, LANES), jnp.float32)
    bars = []
    local_out = None if last else gives.flows_local
    cross_out = None if last else gives.flows_cross
    local_limits = read_lanes(fixed, at.limits, lines + units)
    cross_limits = given.flows_cross[rows : rows + 1, :]
    for flows, out, limits, slope, low, high in (
        (given.flows_local, local_out, local_limits, slope_local, 0, lines),
        (given.flows_local, local_out, local_limits, slope_local, lines, lines + units),
        (given.flows_cross, cross_out, cross_limits, slope_cross, 0, regions * slots),
    ):
        slope = slope[:, low:high]
        if low:
            slope = slope + store_duals
        bound = limits[:, low:high]
        old = flows[:rows, low:high]
        new = jnp.clip(old - primal_step * slope, -bound, bound)
        bars.append(2.0 * new - old)
        if not last:
            out[:rows, low:high] = new
            change = row_sum((new - old) ** 2)
            if out is cross_out:
                slot = lax.broadcasted_iota(jnp.int32, change.shape, 1)
                change = jnp.where(slot // slots == own, change, 0.0)
            primal_row = primal_row + fold_lanes(change)
    maps_own = given.maps_cross[pl.ds(pl.multiple_of(own * nodes, nodes), nodes), :]
    balance = dot3(jnp.concatenate(bars[:2], axis=1), maps_local, True) - given.available[techs]
    balance = balance + dot3(bars[2], maps_own, True)

    gen_cost = fixed[:techs, :]
    half_weight = weight / 2.0
    primal_acc = jnp.zeros((rows, nodes), jnp.float32)
    dual_acc = jnp.zeros((rows, nodes), jnp.float32)
    for tech in range(techs):
        slope = gen_cost[tech : tech + 1] + prices
        dispatch = given.dispatch[tech]
        avail = given.available[tech]
        if second:
            duals = jnp.maximum(0.5 * (2.0 * dispatch - avail * first_bar[tech : tech + 1]), 0.0)
        else:
            duals = given.cap_duals[tech]
        dispatch_new = jnp.maximum(dispatch - primal_step * (slope + duals), 0.0)
        dispatch_bar = 2.0 * dispatch_new - dispatch
        balance = balance + dispatch_bar
        if last:
            gives.dispatch[pl.ds(tech, rows, stride=techs), :] = dispatch_new
            continue
        gives.dispatch[tech] = dispatch_new
        cap_rows = dispatch_bar - avail * capacity_bar[tech : tech + 1]
        primal_acc = primal_acc + (dispatch_new - dispatch) ** 2
        duals_new = jnp.maximum(duals + half_weight * cap_rows, 0.0)
        dual_acc = dual_acc + (duals_new - duals) ** 2
        gives.cap_duals[tech] = duals_new
        gives.sums[tech : tech + 1, :] = row_sum(avail * duals_new)

    step_up = weight / (techs + 8.0) * balance
    if last:
        gives.prices[...] = prices + step_up
        owned = fixed[at.owned : at.owned + 1, : gives.capacity.shape[1]].astype(jnp.int32)
        tech_hot, node_hot = owned_one_hots(owned, techs, nodes)
        chosen = dot3(capacity_new, node_hot, False)
        gives.capacity[...] = row_sum(jnp.where(tech_hot, chosen, 0.0))
        gives.negative[...] = negative
        return
    gives.prices[...] = prices + step_up
    gives.flows_cross[rows : rows + 1, :] = cross_limits
    gives.cap_duals[techs, :techs, :] = col_weight
    gives.cap_duals[techs, techs : 2 * techs, :] = cost
    small_new = gives.dispatch.at[techs]
    small_new[:techs, :] = capacity_new
    small_new[at.weight : at.weight + 1, :] = jnp.broadcast_to(weight, (1, LANES))
    small_new[at.negative : at.negative + 1, :] = negative
    charge_bar = 2.0 * charge_new - charge
    before_new = jnp.clip(charge_before - primal_step * (prev_row - store_duals[0:1]), 0.0, energy)
    write_lanes(small_new, at.before, before_new)
    before_bar = 2.0 * before_new - charge_before
    shifted_bar = jnp.where(row_id == 0, before_bar, pltpu.roll(charge_bar, 1, 0))
    store_step = weight / 3.0 * (charge_bar - shifted_bar + bars[1])
    store_new = store_duals + store_step
    gives.store_duals[...] = store_new
    primal_row = primal_row + row_sum(primal_acc) + fold_lanes(row_sum((charge_new - charge) ** 2))
    primal_row = primal_row + jnp.where(
        hour_index == 0, row_sum((capacity_new - capacity) ** 2), 0.0
    )
    dual_row = row_sum(dual_acc + step_up * step_up) + fold_lanes(row_sum(store_step * store_step))
    squares = jnp.concatenate(
        [primal_row, dual_row, jnp.zeros((SQUARES - 2, LANES), jnp.float32)], axis=0
    )
    gives.sums[techs : techs + SQUARES, :] = squares
    write_halo(sizes, gives.sums, store_new)


def call(kernel, given, outs, flops=0, smem=()):
    names_in, names_out = tuple(vars(given)), tuple(vars(outs))
    values = pl.pallas_call(
        functools.partial(kernel, names_in, names_out),
        out_shape=tuple(vars(outs).values()),
        in_specs=[
            pl.BlockSpec(memory_space=pltpu.SMEM if i in smem else pltpu.VMEM)
            for i in range(len(names_in))
        ],
        out_specs=[pl.BlockSpec(memory_space=pltpu.VMEM)] * len(names_out),
        cost_estimate=pl.CostEstimate(flops=flops, bytes_accessed=4 * flops, transcendentals=0),
        compiler_params=pltpu.CompilerParams(vmem_limit_bytes=VMEM_BYTES),
    )(*vars(given).values())
    return Bag(**dict(zip(names_out, values)))


def swap(value, hour_bit, region_bit):
    hours, regions = lax.axis_size("hours"), lax.axis_size("region")
    pairs = [
        (hour * regions + region, (hour ^ hour_bit) * regions + (region ^ region_bit))
        for hour in range(hours)
        for region in range(regions)
    ]
    return lax.ppermute(value, ("hours", "region"), pairs)


def shifted(value, steps):
    count = lax.axis_size("hours")
    return lax.ppermute(value, "hours", [(i, (i + steps) % count) for i in range(count)])


def both_regions(block):
    if lax.axis_size("region") != 2:
        return lax.all_gather(block, "region")
    return in_order(block, swap(block, 0, 1))


def in_order(block, other):
    return jnp.where(
        lax.axis_index("region") == 0, jnp.stack([block, other]), jnp.stack([other, block])
    )


def exchange(sizes, prices, sums):
    hours, regions = lax.axis_size("hours"), lax.axis_size("region")
    techs, span = sizes.techs, sizes.units // LANES
    halo = halo_at(sizes)
    if regions != 2 or hours != 16:
        gathered = lax.all_gather(prices, "region")
        totals = lax.psum(sums, "hours")
        totals = totals.at[techs:halo].set(lax.psum(totals[techs:halo], "region"))
        next_row = shifted(sums[halo : halo + span], -1)
        prev_row = shifted(sums[halo + span : halo + 2 * span], 1)
        return gathered, Bag(totals=totals, next_row=next_row, prev_row=prev_row)

    def merged(mine, yours, mine_first):
        last = halo + span
        edges = [
            jnp.where(mine_first, mine[halo:last], yours[halo:last]),
            jnp.where(mine_first, yours[last : last + span], mine[last : last + span]),
        ]
        total = mine + yours
        return jnp.concatenate([total[:halo], *edges, total[last + span :]], axis=0)

    hour = lax.axis_index("hours")
    partner = swap(sums, 1, 0)
    chip = merged(sums, partner, hour % 2 == 0)
    across = swap(chip, 2 + 1, 0)
    diagonal = swap(chip[techs:halo], 2 + 1, 1)
    beside = swap(jnp.concatenate([prices, chip[techs:halo]], axis=0), 0, 1)
    other, squares = beside[: sizes.rows], beside[sizes.rows :]
    slab = merged(chip, across, hour // 2 % 2 == 0)
    slab = slab.at[techs:halo].add(squares + diagonal)
    near, middle, far = [swap(slab, 4 * step + 1, 0) for step in (1, 2, 3)]
    parts = Bag(slab=slab, near=near, middle=middle, far=far, partner=partner, across=across)
    return in_order(prices, other), parts


def shape(*dims, dtype=jnp.float32):
    return jax.ShapeDtypeStruct(dims, dtype)


def corrected(sizes, state, prices, sums, parts):
    techs = sizes.techs
    totals = total_of(parts)
    first = sums_rows(sizes)
    col_weight, cost = totals[first : first + techs], totals[first + techs :]
    capacity = jnp.maximum(-cost / col_weight, 0.0)
    taken = state.dispatch[:techs]
    rows_of = 2.0 * taken - state.available[:techs] * (2.0 * capacity)[:, None, :]
    duals = jnp.maximum(0.5 * rows_of, 0.0)
    own = jnp.where(lax.axis_index("hours") == 0, jnp.sum(capacity**2, axis=0), 0.0)
    fixed = sums.at[:techs].set(jnp.sum(state.available[:techs] * duals, axis=1))
    fixed = fixed.at[techs].add(own)
    fixed = fixed.at[techs + 1].add(jnp.sum(duals**2 - taken**2, axis=(0, 1)))
    return exchange(sizes, prices, fixed)[1]


def run(args, exact):
    rows, techs, nodes = args.availability.shape
    hours, regions = lax.axis_size("hours"), lax.axis_size("region")
    slots, owned = args.cross_limit.shape[1], args.cap_cost.shape[1]
    units, lines = args.store_node.shape[0], args.line_limit.shape[0]
    sizes = Bag(
        rows=rows, techs=techs, nodes=nodes, regions=regions, slots=slots, lines=lines, units=units
    )
    cross = regions * slots

    gathered = both_regions(args.price_start)
    info = call(
        lambda names_in, names_out, *refs: slots_kernel(sizes, *refs),
        Bag(ends=args.cross_ends[:, 0], limit=args.cross_limit, pairs=args.pair_counts),
        Bag(info=shape(8 * (cross // LANES), nodes)),
    ).info
    info = both_regions(info)
    state = call(
        functools.partial(start_kernel, sizes),
        Bag(
            availability=args.availability.reshape(rows * techs, nodes),
            price=args.price_start,
            demand=args.demand,
            gen_cost=args.gen_cost,
            cap_cost=args.cap_cost,
            owner=args.owner_map.reshape(hours, owned),
            line_ends=args.line_ends,
            line_limit=args.line_limit[None],
            store_node=args.store_node[None],
            store_power=args.store_power[None],
            store_energy=args.store_energy[None],
        ),
        Bag(
            available=shape(techs + 2, rows, nodes),
            maps_local=shape(nodes, lines + units, dtype=jnp.bfloat16),
            flows_local=shape(rows, lines + units),
            store_duals=shape(rows, units),
            dispatch=shape(techs + 1, rows, nodes),
            balance=shape(rows, nodes),
            sums=shape(sums_rows(sizes) + 2 * techs, nodes),
        ),
        flops=10**6,
    )
    closed = call(
        lambda names_in, names_out, *refs: close_kernel(sizes, *refs),
        Bag(gathered=gathered, info=info, balance=state.balance, sums=state.sums),
        Bag(
            maps=shape(regions * nodes, cross, dtype=jnp.bfloat16),
            flows=shape(rows + 8, cross),
            prices=shape(rows, nodes),
            sums=shape(*state.sums.shape),
        ),
    )
    del state.sums, state.balance
    state.maps_cross, state.flows_cross = closed.maps, closed.flows
    gathered, parts = exchange(sizes, closed.prices, closed.sums)
    if exact:
        parts = corrected(sizes, state, closed.prices, closed.sums, parts)

    for iteration in range(1, ITERS):
        given = Bag(**vars(state), **vars(parts), gathered=gathered)
        if iteration < ITERS - 1:
            outs = Bag(
                dispatch=shape(techs + 1, rows, nodes),
                cap_duals=shape(techs + 1, rows, nodes),
                flows_local=shape(rows, lines + units),
                flows_cross=shape(rows + 8, cross),
                store_duals=shape(rows, units),
                charge=shape(rows, units),
                prices=shape(rows, nodes),
                sums=shape(sums_rows(sizes), nodes),
            )
        else:
            outs = Bag(
                dispatch=shape(rows * techs, nodes),
                capacity=shape(1, owned),
                prices=shape(rows, nodes),
                charge=shape(rows, units),
                negative=shape(1, LANES),
            )
        results = call(functools.partial(sweep_kernel, sizes, iteration), given, outs)
        if iteration < ITERS - 1:
            gathered, parts = exchange(sizes, results.prices, results.sums)
            del results.prices, results.sums
            vars(state).update(vars(results))
    dispatch = results.dispatch.reshape(rows, techs, nodes)
    outputs = (dispatch, results.capacity, results.prices, results.charge)
    return outputs, results.negative[0, 0]


def body(
    availability,
    demand,
    gen_cost,
    cap_cost,
    owner_map,
    line_ends,
    line_limit,
    cross_ends,
    cross_limit,
    pair_counts,
    store_node,
    store_energy,
    store_power,
    price_start,
):
    args = Bag(**locals())
    outputs, negative = run(args, False)
    return lax.cond(negative > 0.0, lambda: run(args, True)[0], lambda: outputs)


def solution(mesh):
    placed = (
        P("hours", None, "region"),
        P("hours", "region"),
        P(None, "region"),
        P("region", "hours"),
        P("region", None),
        P(None, "region"),
        P("region"),
        P(None, "region", None),
        P("region", None),
        P("region", None),
        P("region"),
        P("region"),
        P("region"),
        P("hours", "region"),
    )
    return jax.shard_map(
        body,
        mesh=mesh,
        in_specs=placed,
        out_specs=(
            P("hours", None, "region"),
            P("region", "hours"),
            P("hours", "region"),
            P("hours", "region"),
        ),
        check_vma=False,
    )
```

```python
import functools
from types import SimpleNamespace as Bag

import jax
import jax.numpy as jnp
from jax import lax
from jax.experimental import pallas as pl
from jax.experimental.pallas import tpu as pltpu
from jax.sharding import PartitionSpec as P

ITERS = 4
EPSILON = 1e-06
LANES = 128
VMEM_BYTES = 24 * 1024 * 1024
SQUARES = 3


def split3(value):
    high = value.astype(jnp.bfloat16)
    rest = value - high.astype(jnp.float32)
    middle = rest.astype(jnp.bfloat16)
    low = (rest - middle.astype(jnp.float32)).astype(jnp.bfloat16)
    return jnp.concatenate([high, middle, low], axis=0)


def dot3(value, matrix, transposed):
    rows = value.shape[0]
    contract = ((1,), (1 if transposed else 0,))
    product = lax.dot_general(
        split3(value), matrix, (contract, ((), ())), preferred_element_type=jnp.float32
    )
    return product[:rows] + product[rows : 2 * rows] + product[2 * rows :]


def row_sum(value):
    return jnp.sum(value, axis=0, keepdims=True)


def fold_lanes(row):
    total = row[:, :LANES]
    for start in range(LANES, row.shape[1], LANES):
        total = total + row[:, start : start + LANES]
    return total


def owned_one_hots(owned, tech_count, node_count):
    shape_t = (tech_count, owned.shape[1])
    shape_n = (node_count, owned.shape[1])
    tech = lax.broadcasted_iota(jnp.int32, shape_t, 0) == owned // node_count
    node = lax.broadcasted_iota(jnp.int32, shape_n, 0) == owned % node_count
    return tech, node.astype(jnp.float32).astype(jnp.bfloat16)


def incidence(start, end, count):
    node = lax.broadcasted_iota(jnp.int32, (count, start.shape[1]), 0)
    maps = (node == end).astype(jnp.float32) - (node == start).astype(jnp.float32)
    return maps.astype(jnp.bfloat16)


def halo_at(sizes):
    return sizes.techs + SQUARES


def sums_rows(sizes):
    return (halo_at(sizes) + 2 * sizes.units // LANES + 7) // 8 * 8


def write_halo(sizes, sums_ref, store_new):
    halo, span, rows = halo_at(sizes), sizes.units // LANES, sizes.rows
    write_lanes(sums_ref, halo, store_new[:1])
    write_lanes(sums_ref, halo + span, store_new[rows - 1 :])
    used, end = halo + 2 * span, sums_rows(sizes)
    if used < end:
        sums_ref[used:end, :] = jnp.zeros((end - used, LANES), jnp.float32)


def write_lanes(ref, start, row):
    for i in range(row.shape[1] // LANES):
        ref[start + i : start + i + 1, :] = row[:, i * LANES : (i + 1) * LANES]


def read_lanes(ref, start, length):
    return jnp.concatenate(
        [ref[start + i : start + i + 1, :] for i in range(length // LANES)], axis=1
    )


def places(sizes):
    span = sizes.units // LANES
    limits = sizes.techs
    energy = limits + (sizes.lines + sizes.units) // LANES
    return Bag(
        limits=limits,
        energy=energy,
        owned=energy + span,
        weight=sizes.techs,
        before=sizes.techs + 1,
        negative=sizes.techs + 1 + span,
    )


def first_kernel(sizes, sources, block_ref, ends_ref, limit_ref, pairs_ref, sems):
    rows = sizes.rows
    targets = (block_ref.at[pl.ds(0, rows)], ends_ref, limit_ref, pairs_ref)
    copies = [
        pltpu.make_async_copy(source, target, sems.at[i])
        for i, (source, target) in enumerate(zip(sources, targets))
    ]
    for copy in copies:
        copy.start()
    nodes, slots, regions = sizes.nodes, sizes.slots, sizes.regions
    own = lax.axis_index("region")
    width = slots // regions
    slot = lax.broadcasted_iota(jnp.int32, (1, slots), 1)
    pair = slot // width
    for copy in copies[1:]:
        copy.wait()
    in_use = jnp.zeros((1, slots), jnp.int32)
    for target in range(regions):
        in_use = jnp.where(pair == target, pairs_ref[0:1, target : target + 1], in_use)
    place = lax.broadcasted_iota(jnp.int32, (slots, regions * slots), 1) == (
        own * slots + lax.broadcasted_iota(jnp.int32, (slots, regions * slots), 0)
    )
    place = place.astype(jnp.float32).astype(jnp.bfloat16)
    bound = jnp.where(slot % width < in_use, limit_ref[...], 0.0)
    start = (ends_ref[0:1, :] + own * nodes).astype(jnp.float32)
    end = (ends_ref[1:2, :] + pair * nodes).astype(jnp.float32)
    rest = jnp.zeros((13, slots), jnp.float32)
    info = dot3(jnp.concatenate([start, end, bound, rest], axis=0), place, False)
    for chunk in range(regions * slots // LANES):
        block_ref[rows + 8 * chunk : rows + 8 * chunk + 8, :] = info[
            :8, chunk * LANES : (chunk + 1) * LANES
        ]
    copies[0].wait()


def start_kernel(sizes, names_in, names_out, *refs):
    given = Bag(**dict(zip(names_in, refs[: len(names_in)])))
    gives = Bag(**dict(zip(names_out, refs[len(names_in) : -2])))
    availability, sem = refs[-2:]
    copy = pltpu.make_async_copy(given.availability, availability, sem)
    copy.start()
    rows, techs, nodes, lines = sizes.rows, sizes.techs, sizes.nodes, sizes.lines
    at = places(sizes)
    fixed = gives.available.at[techs + 1]
    gives.available[techs] = given.demand[...]
    fixed[:techs, :] = given.gen_cost[...]
    write_lanes(fixed, at.energy, given.store_energy[...])
    owned = given.owner[pl.ds(lax.axis_index("hours"), 1), :]
    fixed[at.owned : at.owned + 1, : owned.shape[1]] = owned.astype(jnp.float32)
    line_ends, stores = given.line_ends[...], given.store_node[...]
    start = jnp.concatenate([line_ends[0:1], jnp.full_like(stores, -1)], axis=1)
    end = jnp.concatenate([line_ends[1:2], stores], axis=1)
    maps = incidence(start, end, nodes)
    limits = jnp.concatenate([given.line_limit[...], given.store_power[...]], axis=1)
    gives.maps_local[...] = maps
    write_lanes(fixed, at.limits, limits)
    prices = given.price[...]
    flows = jnp.clip(-0.5 * dot3(prices, maps, False), -limits, limits)
    gives.flows_local[...] = flows
    store_new = (1.0 / 3.0) * (2.0 * flows[:, lines:])
    gives.store_duals[...] = store_new
    primal_row = fold_lanes(row_sum(flows * flows))
    dual_row = fold_lanes(row_sum(store_new * store_new))
    balance = dot3(2.0 * flows, maps, True) - given.demand[...]
    gen_cost = given.gen_cost[...]
    copy.wait()
    acc = jnp.zeros((rows, nodes), jnp.float32)
    weights = jnp.zeros((techs, nodes), jnp.float32)
    for hour in range(rows):
        weights = weights + availability[hour * techs : (hour + 1) * techs, :]
    for tech in range(techs):
        avail = availability[pl.ds(tech, rows, stride=techs), :]
        gives.available[tech] = avail
        dispatch = jnp.maximum(-0.5 * (gen_cost[tech : tech + 1] + prices), 0.0)
        gives.dispatch[tech] = dispatch
        dispatch_bar = 2.0 * dispatch
        balance = balance + dispatch_bar
        duals = jnp.maximum(0.5 * dispatch_bar, 0.0)
        acc = acc + dispatch * dispatch
        gives.sums[tech : tech + 1, :] = row_sum(avail * duals)
    gives.balance[...] = balance
    squares = row_sum(acc)
    cost = given.cap_cost[...]
    negative = jnp.sum((cost < 0.0).astype(jnp.float32), axis=1, keepdims=True)
    write_halo(sizes, gives.sums, store_new)
    gives.sums[techs : techs + SQUARES, :] = jnp.concatenate(
        [primal_row + squares, dual_row + squares, jnp.broadcast_to(negative, (1, LANES))], axis=0
    )
    tech_hot, node_hot = owned_one_hots(owned, techs, nodes)
    first = sums_rows(sizes)
    gives.sums[first : first + techs, :] = weights
    gives.sums[first + techs : first + 2 * techs, :] = dot3(
        jnp.where(tech_hot, cost, 0.0), node_hot, True
    )


def close_kernel(
    sizes,
    gathered,
    local_ref,
    balance_ref,
    sums_in_ref,
    maps_ref,
    flows_ref,
    prices_ref,
    sums_ref,
):
    rows, techs, nodes = sizes.rows, sizes.techs, sizes.nodes
    slots, regions = sizes.slots, sizes.regions
    own = lax.axis_index("region")
    chunks = []
    for chunk in range(regions * slots // LANES):
        at = slice(rows + 8 * chunk, rows + 8 * chunk + 8)
        part = gathered[0, at, :]
        for region in range(1, regions):
            part = part + gathered[region, at, :]
        chunks.append(part)
    info = jnp.concatenate(chunks, axis=1) if len(chunks) > 1 else chunks[0]
    maps_ref[...] = incidence(
        info[0:1].astype(jnp.int32), info[1:2].astype(jnp.int32), regions * nodes
    )
    limits = info[2:3]
    prices_all = jnp.concatenate([gathered[region, :rows, :] for region in range(regions)], axis=1)
    flows = jnp.clip(-0.5 * dot3(prices_all, maps_ref[...], False), -limits, limits)
    local = local_ref.shape[1]
    flows_ref[:rows, :local] = local_ref[...]
    flows_ref[:rows, local:] = flows
    flows_ref[rows : rows + 1, local:] = limits
    maps_own = maps_ref[pl.ds(pl.multiple_of(own * nodes, nodes), nodes), :]
    balance = balance_ref[...] + dot3(2.0 * flows, maps_own, True)
    step_up = (1.0 / (techs + 8.0)) * balance
    prices_ref[...] = gathered[own, :rows, :] + step_up
    change = row_sum(flows * flows)
    slot = lax.broadcasted_iota(jnp.int32, change.shape, 1)
    primal = fold_lanes(jnp.where(slot // slots == own, change, 0.0))
    more = jnp.concatenate(
        [primal, row_sum(step_up * step_up), jnp.zeros((SQUARES - 2, LANES), jnp.float32)], axis=0
    )
    sums_ref[...] = sums_in_ref[...]
    squares = sums_in_ref[techs : techs + SQUARES, :] + more
    sums_ref[techs : techs + SQUARES, :] = squares


def neighbour_rows(sizes, given, hour_index):
    units = sizes.units
    if hasattr(given, "totals"):
        return read_lanes(given.next_row, 0, units), read_lanes(given.prev_row, 0, units)
    first = halo_at(sizes)
    last = first + units // LANES
    core, x_place, odd = hour_index % 2, hour_index // 2 % 2, hour_index // 4 % 2
    next_row = jnp.where(
        odd == 0, read_lanes(given.near, first, units), read_lanes(given.far, first, units)
    )
    prev_row = jnp.where(
        odd == 0, read_lanes(given.far, last, units), read_lanes(given.near, last, units)
    )
    next_row = jnp.where(x_place == 0, read_lanes(given.across, first, units), next_row)
    prev_row = jnp.where(x_place == 0, prev_row, read_lanes(given.across, last, units))
    next_row = jnp.where(core == 0, read_lanes(given.partner, first, units), next_row)
    prev_row = jnp.where(core == 0, prev_row, read_lanes(given.partner, last, units))
    return next_row, prev_row


def total_of(parts):
    if hasattr(parts, "totals"):
        return parts.totals[...]
    return (parts.slab[...] + parts.near[...]) + (parts.middle[...] + parts.far[...])


def sweep_kernel(sizes, iteration, names_in, names_out, *refs):
    rows, techs, nodes = sizes.rows, sizes.techs, sizes.nodes
    slots, regions, lines, units = sizes.slots, sizes.regions, sizes.lines, sizes.units
    second = iteration == 1
    last = iteration == ITERS - 1
    given = Bag(**dict(zip(names_in, refs[: len(names_in)])))
    gives = Bag(**dict(zip(names_out, refs[len(names_in) :])))
    own = lax.axis_index("region")
    hour_index = lax.axis_index("hours")
    gathered = given.gathered

    at = places(sizes)
    fixed = given.available.at[techs + 1]
    small = given.dispatch.at[techs]
    sums = total_of(given)
    squares = jnp.sum(sums[techs : techs + 2], axis=1, keepdims=True)
    old_weight = jnp.ones((1, 1), jnp.float32) if second else small[at.weight : at.weight + 1, :1]
    weight = jnp.sqrt(
        old_weight * jnp.sqrt((squares[1:2] + EPSILON) / (squares[0:1] + EPSILON))
    )
    primal_step = 0.5 / weight
    if second:
        first = sums_rows(sizes)
        col_weight, cost = sums[first : first + techs], sums[first + techs : first + 2 * techs]
        negative = sums[techs + 2 : techs + 3]
        capacity = jnp.maximum(-cost / col_weight, 0.0)
        first_bar = 2.0 * capacity
    else:
        col_weight = given.cap_duals[techs, :techs, :]
        cost = given.cap_duals[techs, techs : 2 * techs, :]
        capacity = small[:techs, :]
        negative = small[at.negative : at.negative + 1, :]
    capacity_new = jnp.maximum(capacity - (cost - sums[:techs]) / (weight * col_weight), 0.0)
    capacity_bar = 2.0 * capacity_new - capacity

    prices_all = jnp.concatenate([gathered[region, :rows, :] for region in range(regions)], axis=1)
    prices = gathered[own, :rows, :]
    maps_local = given.maps_local[...]
    slope_local = dot3(prices, maps_local, False)
    slope_cross = dot3(prices_all, given.maps_cross[...], False)

    energy = read_lanes(fixed, at.energy, units)
    row_id = lax.broadcasted_iota(jnp.int32, (rows, units), 0)
    next_row, prev_row = neighbour_rows(sizes, given, hour_index)
    store_duals = given.store_duals[...]
    next_duals = jnp.where(row_id == rows - 1, next_row, pltpu.roll(store_duals, rows - 1, 0))
    if second:
        charge = jnp.zeros((rows, units), jnp.float32)
        charge_before = jnp.zeros((1, units), jnp.float32)
    else:
        charge = given.charge[...]
        charge_before = read_lanes(small, at.before, units)
    charge_new = jnp.clip(charge - primal_step * (store_duals - next_duals), 0.0, energy)
    gives.charge[...] = charge_new

    primal_row = jnp.zeros((1, LANES), jnp.float32)
    bars = []
    local, total_flows = lines + units, lines + units + regions * slots
    local_limits = read_lanes(fixed, at.limits, local)
    cross_limits = given.flows[rows : rows + 1, local:]
    for bound, slope, low, high in (
        (local_limits[:, :lines], slope_local[:, :lines], 0, lines),
        (local_limits[:, lines:], slope_local[:, lines:] + store_duals, lines, local),
        (cross_limits, slope_cross, local, total_flows),
    ):
        old = given.flows[:rows, low:high]
        new = jnp.clip(old - primal_step * slope, -bound, bound)
        bars.append(2.0 * new - old)
        if not last:
            gives.flows[:rows, low:high] = new
            change = row_sum((new - old) ** 2)
            if low == local:
                slot = lax.broadcasted_iota(jnp.int32, change.shape, 1)
                change = jnp.where(slot // slots == own, change, 0.0)
            primal_row = primal_row + fold_lanes(change)
    maps_own = given.maps_cross[pl.ds(pl.multiple_of(own * nodes, nodes), nodes), :]
    balance = dot3(jnp.concatenate(bars[:2], axis=1), maps_local, True) - given.available[techs]
    balance = balance + dot3(bars[2], maps_own, True)

    gen_cost = fixed[:techs, :]
    half_weight = weight / 2.0
    primal_acc = jnp.zeros((rows, nodes), jnp.float32)
    dual_acc = jnp.zeros((rows, nodes), jnp.float32)
    for tech in range(techs):
        slope = gen_cost[tech : tech + 1] + prices
        dispatch = given.dispatch[tech]
        avail = given.available[tech]
        if second:
            duals = jnp.maximum(0.5 * (2.0 * dispatch - avail * first_bar[tech : tech + 1]), 0.0)
        else:
            duals = given.cap_duals[tech]
        dispatch_new = jnp.maximum(dispatch - primal_step * (slope + duals), 0.0)
        dispatch_bar = 2.0 * dispatch_new - dispatch
        balance = balance + dispatch_bar
        if last:
            gives.dispatch[pl.ds(tech, rows, stride=techs), :] = dispatch_new
            continue
        gives.dispatch[tech] = dispatch_new
        cap_rows = dispatch_bar - avail * capacity_bar[tech : tech + 1]
        primal_acc = primal_acc + (dispatch_new - dispatch) ** 2
        duals_new = jnp.maximum(duals + half_weight * cap_rows, 0.0)
        dual_acc = dual_acc + (duals_new - duals) ** 2
        gives.cap_duals[tech] = duals_new
        gives.sums[tech : tech + 1, :] = row_sum(avail * duals_new)

    step_up = weight / (techs + 8.0) * balance
    if last:
        gives.prices[...] = prices + step_up
        owned = fixed[at.owned : at.owned + 1, : gives.capacity.shape[1]].astype(jnp.int32)
        tech_hot, node_hot = owned_one_hots(owned, techs, nodes)
        chosen = dot3(capacity_new, node_hot, False)
        gives.capacity[...] = row_sum(jnp.where(tech_hot, chosen, 0.0))
        gives.negative[...] = negative
        return
    gives.prices[...] = prices + step_up
    gives.flows[rows : rows + 1, local:] = cross_limits
    gives.cap_duals[techs, :techs, :] = col_weight
    gives.cap_duals[techs, techs : 2 * techs, :] = cost
    small_new = gives.dispatch.at[techs]
    small_new[:techs, :] = capacity_new
    small_new[at.weight : at.weight + 1, :] = jnp.broadcast_to(weight, (1, LANES))
    small_new[at.negative : at.negative + 1, :] = negative
    charge_bar = 2.0 * charge_new - charge
    before_new = jnp.clip(charge_before - primal_step * (prev_row - store_duals[0:1]), 0.0, energy)
    write_lanes(small_new, at.before, before_new)
    before_bar = 2.0 * before_new - charge_before
    shifted_bar = jnp.where(row_id == 0, before_bar, pltpu.roll(charge_bar, 1, 0))
    store_step = weight / 3.0 * (charge_bar - shifted_bar + bars[1])
    store_new = store_duals + store_step
    gives.store_duals[...] = store_new
    primal_row = primal_row + row_sum(primal_acc) + fold_lanes(row_sum((charge_new - charge) ** 2))
    primal_row = primal_row + jnp.where(
        hour_index == 0, row_sum((capacity_new - capacity) ** 2), 0.0
    )
    dual_row = row_sum(dual_acc + step_up * step_up) + fold_lanes(row_sum(store_step * store_step))
    squares = jnp.concatenate(
        [primal_row, dual_row, jnp.zeros((SQUARES - 2, LANES), jnp.float32)], axis=0
    )
    gives.sums[techs : techs + SQUARES, :] = squares
    write_halo(sizes, gives.sums, store_new)


def call(kernel, given, outs, flops=0, left=(), scratch=(), limit=VMEM_BYTES):
    names_in, names_out = tuple(vars(given)), tuple(vars(outs))
    values = pl.pallas_call(
        functools.partial(kernel, names_in, names_out),
        out_shape=tuple(vars(outs).values()),
        in_specs=[
            pl.BlockSpec(memory_space=pl.ANY if i in left else pltpu.VMEM)
            for i in range(len(names_in))
        ],
        out_specs=[pl.BlockSpec(memory_space=pltpu.VMEM)] * len(names_out),
        scratch_shapes=scratch,
        cost_estimate=pl.CostEstimate(flops=flops, bytes_accessed=4 * flops, transcendentals=0),
        compiler_params=pltpu.CompilerParams(vmem_limit_bytes=limit),
    )(*vars(given).values())
    return Bag(**dict(zip(names_out, values)))


def swap(value, hour_bit, region_bit):
    hours, regions = lax.axis_size("hours"), lax.axis_size("region")
    pairs = [
        (hour * regions + region, (hour ^ hour_bit) * regions + (region ^ region_bit))
        for hour in range(hours)
        for region in range(regions)
    ]
    return lax.ppermute(value, ("hours", "region"), pairs)


def shifted(value, steps):
    count = lax.axis_size("hours")
    return lax.ppermute(value, "hours", [(i, (i + steps) % count) for i in range(count)])


def both_regions(block):
    if lax.axis_size("region") != 2:
        return lax.all_gather(block, "region")
    return in_order(block, swap(block, 0, 1))


def in_order(block, other):
    return jnp.where(
        lax.axis_index("region") == 0, jnp.stack([block, other]), jnp.stack([other, block])
    )


def exchange(sizes, prices, sums):
    hours, regions = lax.axis_size("hours"), lax.axis_size("region")
    techs, span = sizes.techs, sizes.units // LANES
    halo = halo_at(sizes)
    if regions != 2 or hours != 16:
        gathered = lax.all_gather(prices, "region")
        totals = lax.psum(sums, "hours")
        totals = totals.at[techs:halo].set(lax.psum(totals[techs:halo], "region"))
        next_row = shifted(sums[halo : halo + span], -1)
        prev_row = shifted(sums[halo + span : halo + 2 * span], 1)
        return gathered, Bag(totals=totals, next_row=next_row, prev_row=prev_row)

    def merged(mine, yours, mine_first):
        last = halo + span
        edges = [
            jnp.where(mine_first, mine[halo:last], yours[halo:last]),
            jnp.where(mine_first, yours[last : last + span], mine[last : last + span]),
        ]
        total = mine + yours
        return jnp.concatenate([total[:halo], *edges, total[last + span :]], axis=0)

    hour = lax.axis_index("hours")
    partner = swap(sums, 1, 0)
    chip = merged(sums, partner, hour % 2 == 0)
    across = swap(chip, 2 + 1, 0)
    diagonal = swap(chip[techs:halo], 2 + 1, 1)
    beside = swap(jnp.concatenate([prices, chip[techs:halo]], axis=0), 0, 1)
    other, squares = beside[: sizes.rows], beside[sizes.rows :]
    slab = merged(chip, across, hour // 2 % 2 == 0)
    slab = slab.at[techs:halo].add(squares + diagonal)
    near, middle, far = [swap(slab, 4 * step + 1, 0) for step in (1, 2, 3)]
    parts = Bag(slab=slab, near=near, middle=middle, far=far, partner=partner, across=across)
    return in_order(prices, other), parts


def shape(*dims, dtype=jnp.float32):
    return jax.ShapeDtypeStruct(dims, dtype)


def restarted(sizes, kept, price_start):
    rows, techs, nodes, lines = sizes.rows, sizes.techs, sizes.nodes, sizes.lines
    local, cross = lines + sizes.units, sizes.regions * sizes.slots
    at, own = places(sizes), lax.axis_index("region")
    first_hour = lax.axis_index("hours") == 0
    fixed, available = kept.available[techs + 1], kept.available[:techs]
    col_weight, cost = kept.cap_duals[techs, :techs], kept.cap_duals[techs, techs : 2 * techs]
    local_limits = fixed[at.limits : at.energy].reshape(1, local)
    cross_limits = kept.flows[rows : rows + 1, local:]
    maps_local = kept.maps_local.astype(jnp.float32)
    maps_cross = kept.maps_cross.astype(jnp.float32)
    maps_own = lax.dynamic_slice_in_dim(maps_cross, own * nodes, nodes)
    prices_all = jnp.concatenate(list(both_regions(price_start)), axis=1)
    highest = lax.Precision.HIGHEST

    capacity = jnp.maximum(-cost / col_weight, 0.0)
    slopes = fixed[:techs][:, None, :] + price_start[None]
    dispatch = jnp.maximum(-0.5 * slopes, 0.0)
    slope = jnp.dot(price_start, maps_local, precision=highest)
    flows_local = jnp.clip(-0.5 * slope, -local_limits, local_limits)
    slope = jnp.dot(prices_all, maps_cross, precision=highest)
    flows_cross = jnp.clip(-0.5 * slope, -cross_limits, cross_limits)
    balance = (
        jnp.sum(2.0 * dispatch, axis=0)
        + jnp.dot(2.0 * flows_local, maps_local.T, precision=highest)
        + jnp.dot(2.0 * flows_cross, maps_own.T, precision=highest)
        - kept.available[techs]
    )
    step_up = balance / (techs + 8.0)
    duals = jnp.maximum(0.5 * (2.0 * dispatch - available * (2.0 * capacity)[:, None, :]), 0.0)
    store_duals = 2.0 * flows_local[:, lines:] / 3.0
    slot = lax.broadcasted_iota(jnp.int32, (1, cross), 1) // sizes.slots
    primal = (
        jnp.sum(dispatch**2)
        + jnp.sum(flows_local**2)
        + jnp.sum(jnp.where(slot == own, flows_cross**2, 0.0))
        + jnp.where(first_hour, jnp.sum(capacity**2), 0.0)
    )
    dual = jnp.sum(step_up**2) + jnp.sum(duals**2) + jnp.sum(store_duals**2)
    rows_of = [
        jnp.sum(available * duals, axis=1),
        jnp.zeros((SQUARES, nodes)).at[0, 0].set(primal).at[1, 0].set(dual),
        store_duals[:1].reshape(-1, LANES),
        store_duals[rows - 1 :].reshape(-1, LANES),
    ]
    used = halo_at(sizes) + 2 * sizes.units // LANES
    rows_of.append(jnp.zeros((sums_rows(sizes) - used, nodes)))
    rows_of += [jnp.where(first_hour, part, 0.0) for part in (col_weight, cost)]
    gathered, parts = exchange(sizes, price_start + step_up, jnp.concatenate(rows_of, axis=0))
    flows = jnp.concatenate([flows_local, flows_cross], axis=1)
    limits = jnp.concatenate([local_limits, cross_limits], axis=1)
    state = Bag(
        available=kept.available,
        maps_local=kept.maps_local,
        maps_cross=kept.maps_cross,
        store_duals=store_duals,
        dispatch=jnp.concatenate([dispatch, jnp.zeros((1, rows, nodes))], axis=0),
        flows=jnp.concatenate([flows, jnp.broadcast_to(limits, (8, local + cross))], axis=0),
    )
    return state, gathered, parts


def run(args):
    rows, techs, nodes = args.availability.shape
    hours, regions = lax.axis_size("hours"), lax.axis_size("region")
    slots, owned = args.cross_limit.shape[1], args.cap_cost.shape[1]
    units, lines = args.store_node.shape[0], args.line_limit.shape[0]
    sizes = Bag(
        rows=rows, techs=techs, nodes=nodes, regions=regions, slots=slots, lines=lines, units=units
    )
    cross = regions * slots

    gathered = both_regions(
        call(
            lambda names_in, names_out, *refs: first_kernel(sizes, refs[:4], *refs[4:]),
            Bag(
                price=args.price_start,
                ends=args.cross_ends[:, 0],
                limit=args.cross_limit,
                pairs=args.pair_counts,
            ),
            Bag(block=shape(rows + 8 * (cross // LANES), nodes)),
            left=(0, 1, 2, 3),
            scratch=[
                pltpu.VMEM((2, slots), jnp.int32),
                pltpu.VMEM((1, slots), jnp.float32),
                pltpu.VMEM((1, regions), jnp.int32),
                pltpu.SemaphoreType.DMA((4,)),
            ],
            limit=None,
        ).block
    )
    state = call(
        functools.partial(start_kernel, sizes),
        Bag(
            availability=args.availability.reshape(rows * techs, nodes),
            price=args.price_start,
            demand=args.demand,
            gen_cost=args.gen_cost,
            cap_cost=args.cap_cost,
            owner=args.owner_map.reshape(hours, owned),
            line_ends=args.line_ends,
            line_limit=args.line_limit[None],
            store_node=args.store_node[None],
            store_power=args.store_power[None],
            store_energy=args.store_energy[None],
        ),
        Bag(
            available=shape(techs + 2, rows, nodes),
            maps_local=shape(nodes, lines + units, dtype=jnp.bfloat16),
            flows_local=shape(rows, lines + units),
            store_duals=shape(rows, units),
            dispatch=shape(techs + 1, rows, nodes),
            balance=shape(rows, nodes),
            sums=shape(sums_rows(sizes) + 2 * techs, nodes),
        ),
        flops=10**6,
        left=(0,),
        scratch=[pltpu.VMEM((rows * techs, nodes), jnp.float32), pltpu.SemaphoreType.DMA],
    )
    closed = call(
        lambda names_in, names_out, *refs: close_kernel(sizes, *refs),
        Bag(
            gathered=gathered,
            flows_local=state.flows_local,
            balance=state.balance,
            sums=state.sums,
        ),
        Bag(
            maps=shape(regions * nodes, cross, dtype=jnp.bfloat16),
            flows=shape(rows + 8, lines + units + cross),
            prices=shape(rows, nodes),
            sums=shape(*state.sums.shape),
        ),
    )
    del state.sums, state.balance, state.flows_local
    state.maps_cross, state.flows = closed.maps, closed.flows
    gathered, parts = exchange(sizes, closed.prices, closed.sums)
    outputs, kept, negative = sweeps(sizes, owned, state, gathered, parts)

    def again():
        return sweeps(sizes, owned, *restarted(sizes, kept, args.price_start))[0]

    return lax.cond(negative > 0.0, again, lambda: outputs)


def sweeps(sizes, owned, state, gathered, parts):
    rows, techs, nodes, lines, units = (
        sizes.rows,
        sizes.techs,
        sizes.nodes,
        sizes.lines,
        sizes.units,
    )
    state = Bag(**vars(state))
    for iteration in range(1, ITERS):
        given = Bag(**vars(state), **vars(parts), gathered=gathered)
        if iteration < ITERS - 1:
            outs = Bag(
                dispatch=shape(techs + 1, rows, nodes),
                cap_duals=shape(techs + 1, rows, nodes),
                flows=shape(rows + 8, lines + units + sizes.regions * sizes.slots),
                store_duals=shape(rows, units),
                charge=shape(rows, units),
                prices=shape(rows, nodes),
                sums=shape(sums_rows(sizes), nodes),
            )
        else:
            outs = Bag(
                dispatch=shape(rows * techs, nodes),
                capacity=shape(1, owned),
                prices=shape(rows, nodes),
                charge=shape(rows, units),
                negative=shape(1, LANES),
            )
        results = call(functools.partial(sweep_kernel, sizes, iteration), given, outs)
        if iteration < ITERS - 1:
            gathered, parts = exchange(sizes, results.prices, results.sums)
            del results.prices, results.sums
            vars(state).update(vars(results))
    dispatch = results.dispatch.reshape(rows, techs, nodes)
    outputs = (dispatch, results.capacity, results.prices, results.charge)
    return outputs, state, results.negative[0, 0]


def body(
    availability,
    demand,
    gen_cost,
    cap_cost,
    owner_map,
    line_ends,
    line_limit,
    cross_ends,
    cross_limit,
    pair_counts,
    store_node,
    store_energy,
    store_power,
    price_start,
):
    args = Bag(**locals())
    return run(args)


def solution(mesh):
    placed = (
        P("hours", None, "region"),
        P("hours", "region"),
        P(None, "region"),
        P("region", "hours"),
        P("region", None),
        P(None, "region"),
        P("region"),
        P(None, "region", None),
        P("region", None),
        P("region", None),
        P("region"),
        P("region"),
        P("region"),
        P("hours", "region"),
    )
    return jax.shard_map(
        body,
        mesh=mesh,
        in_specs=placed,
        out_specs=(
            P("hours", None, "region"),
            P("region", "hours"),
            P("hours", "region"),
            P("hours", "region"),
        ),
        check_vma=False,
    )
```

```python
import functools
from types import SimpleNamespace as Bag

import jax
import jax.numpy as jnp
from jax import lax
from jax.experimental import pallas as pl
from jax.experimental.pallas import tpu as pltpu
from jax.sharding import PartitionSpec as P

ITERS = 4
EPSILON = 1e-06
LANES = 128
VMEM_BYTES = 24 * 1024 * 1024
SQUARES = 3


def split3(value):
    high = value.astype(jnp.bfloat16)
    rest = value - high.astype(jnp.float32)
    middle = rest.astype(jnp.bfloat16)
    low = (rest - middle.astype(jnp.float32)).astype(jnp.bfloat16)
    return jnp.concatenate([high, middle, low], axis=0)


def dot3(value, matrix, transposed):
    rows = value.shape[0]
    contract = ((1,), (1 if transposed else 0,))
    product = lax.dot_general(
        split3(value), matrix, (contract, ((), ())), preferred_element_type=jnp.float32
    )
    return product[:rows] + product[rows : 2 * rows] + product[2 * rows :]


def row_sum(value):
    return jnp.sum(value, axis=0, keepdims=True)


def fold_lanes(row):
    total = row[:, :LANES]
    for start in range(LANES, row.shape[1], LANES):
        total = total + row[:, start : start + LANES]
    return total


def owned_one_hots(owned, tech_count, node_count):
    shape_t = (tech_count, owned.shape[1])
    shape_n = (node_count, owned.shape[1])
    tech = lax.broadcasted_iota(jnp.int32, shape_t, 0) == owned // node_count
    node = lax.broadcasted_iota(jnp.int32, shape_n, 0) == owned % node_count
    return tech, node.astype(jnp.float32).astype(jnp.bfloat16)


def incidence(start, end, count):
    node = lax.broadcasted_iota(jnp.int32, (count, start.shape[1]), 0)
    maps = (node == end).astype(jnp.float32) - (node == start).astype(jnp.float32)
    return maps.astype(jnp.bfloat16)


def halo_at(sizes):
    return sizes.techs + SQUARES


def sums_rows(sizes):
    return (halo_at(sizes) + 2 * sizes.units // LANES + 7) // 8 * 8


def write_halo(sizes, sums_ref, store_new):
    halo, span, rows = halo_at(sizes), sizes.units // LANES, sizes.rows
    write_lanes(sums_ref, halo, store_new[:1])
    write_lanes(sums_ref, halo + span, store_new[rows - 1 :])
    used, end = halo + 2 * span, sums_rows(sizes)
    if used < end:
        sums_ref[used:end, :] = jnp.zeros((end - used, LANES), jnp.float32)


def write_lanes(ref, start, row):
    for i in range(row.shape[1] // LANES):
        ref[start + i : start + i + 1, :] = row[:, i * LANES : (i + 1) * LANES]


def read_lanes(ref, start, length):
    return jnp.concatenate(
        [ref[start + i : start + i + 1, :] for i in range(length // LANES)], axis=1
    )


def places(sizes):
    span = sizes.units // LANES
    limits = sizes.techs
    energy = limits + (sizes.lines + sizes.units) // LANES
    return Bag(
        limits=limits,
        energy=energy,
        owned=energy + span,
        weight=sizes.techs,
        before=sizes.techs + 1,
        negative=sizes.techs + 1 + span,
    )


def first_kernel(sizes, sources, block_ref, ends_ref, limit_ref, pairs_ref, sems):
    rows = sizes.rows
    targets = (block_ref.at[pl.ds(0, rows)], ends_ref, limit_ref, pairs_ref)
    copies = [
        pltpu.make_async_copy(source, target, sems.at[i])
        for i, (source, target) in enumerate(zip(sources, targets))
    ]
    for copy in copies:
        copy.start()
    nodes, slots, regions = sizes.nodes, sizes.slots, sizes.regions
    own = lax.axis_index("region")
    width = slots // regions
    slot = lax.broadcasted_iota(jnp.int32, (1, slots), 1)
    pair = slot // width
    for copy in copies[1:]:
        copy.wait()
    in_use = jnp.zeros((1, slots), jnp.int32)
    for target in range(regions):
        in_use = jnp.where(pair == target, pairs_ref[0:1, target : target + 1], in_use)
    place = lax.broadcasted_iota(jnp.int32, (slots, regions * slots), 1) == (
        own * slots + lax.broadcasted_iota(jnp.int32, (slots, regions * slots), 0)
    )
    place = place.astype(jnp.float32).astype(jnp.bfloat16)
    bound = jnp.where(slot % width < in_use, limit_ref[...], 0.0)
    start = (ends_ref[0:1, :] + own * nodes).astype(jnp.float32)
    end = (ends_ref[1:2, :] + pair * nodes).astype(jnp.float32)
    rest = jnp.zeros((13, slots), jnp.float32)
    info = dot3(jnp.concatenate([start, end, bound, rest], axis=0), place, False)
    for chunk in range(regions * slots // LANES):
        block_ref[rows + 8 * chunk : rows + 8 * chunk + 8, :] = info[
            :8, chunk * LANES : (chunk + 1) * LANES
        ]
    copies[0].wait()


def start_kernel(sizes, names_in, names_out, *refs):
    given = Bag(**dict(zip(names_in, refs[: len(names_in)])))
    gives = Bag(**dict(zip(names_out, refs[len(names_in) : -2])))
    availability, sem = refs[-2:]
    copy = pltpu.make_async_copy(given.availability, availability, sem)
    copy.start()
    rows, techs, nodes, lines = sizes.rows, sizes.techs, sizes.nodes, sizes.lines
    at = places(sizes)
    fixed = gives.available.at[techs + 1]
    gives.available[techs] = given.demand[...]
    fixed[:techs, :] = given.gen_cost[...]
    write_lanes(fixed, at.energy, given.store_energy[...])
    owned = given.owner[pl.ds(lax.axis_index("hours"), 1), :]
    fixed[at.owned : at.owned + 1, : owned.shape[1]] = owned.astype(jnp.float32)
    line_ends, stores = given.line_ends[...], given.store_node[...]
    start = jnp.concatenate([line_ends[0:1], jnp.full_like(stores, -1)], axis=1)
    end = jnp.concatenate([line_ends[1:2], stores], axis=1)
    maps = incidence(start, end, nodes)
    limits = jnp.concatenate([given.line_limit[...], given.store_power[...]], axis=1)
    gives.maps_local[...] = maps
    write_lanes(fixed, at.limits, limits)
    prices = given.price[...]
    flows = jnp.clip(-0.5 * dot3(prices, maps, False), -limits, limits)
    gives.flows_local[...] = flows
    store_new = (1.0 / 3.0) * (2.0 * flows[:, lines:])
    gives.store_duals[...] = store_new
    primal_row = fold_lanes(row_sum(flows * flows))
    dual_row = fold_lanes(row_sum(store_new * store_new))
    balance = dot3(2.0 * flows, maps, True) - given.demand[...]
    gen_cost = given.gen_cost[...]
    copy.wait()
    acc = jnp.zeros((rows, nodes), jnp.float32)
    weights = jnp.zeros((techs, nodes), jnp.float32)
    for hour in range(rows):
        weights = weights + availability[hour * techs : (hour + 1) * techs, :]
    for tech in range(techs):
        avail = availability[pl.ds(tech, rows, stride=techs), :]
        gives.available[tech] = avail
        dispatch = jnp.maximum(-0.5 * (gen_cost[tech : tech + 1] + prices), 0.0)
        gives.dispatch[tech] = dispatch
        dispatch_bar = 2.0 * dispatch
        balance = balance + dispatch_bar
        duals = jnp.maximum(0.5 * dispatch_bar, 0.0)
        acc = acc + dispatch * dispatch
        gives.sums[tech : tech + 1, :] = row_sum(avail * duals)
    gives.balance[...] = balance
    squares = row_sum(acc)
    cost = given.cap_cost[...]
    negative = jnp.sum((cost < 0.0).astype(jnp.float32), axis=1, keepdims=True)
    write_halo(sizes, gives.sums, store_new)
    gives.sums[techs : techs + SQUARES, :] = jnp.concatenate(
        [primal_row + squares, dual_row + squares, jnp.broadcast_to(negative, (1, LANES))], axis=0
    )
    tech_hot, node_hot = owned_one_hots(owned, techs, nodes)
    first = sums_rows(sizes)
    gives.sums[first : first + techs, :] = weights
    gives.sums[first + techs : first + 2 * techs, :] = dot3(
        jnp.where(tech_hot, cost, 0.0), node_hot, True
    )


def close_kernel(
    sizes,
    gathered,
    local_ref,
    balance_ref,
    sums_in_ref,
    maps_ref,
    flows_ref,
    prices_ref,
    sums_ref,
):
    rows, techs, nodes = sizes.rows, sizes.techs, sizes.nodes
    slots, regions = sizes.slots, sizes.regions
    own = lax.axis_index("region")
    chunks = []
    for chunk in range(regions * slots // LANES):
        at = slice(rows + 8 * chunk, rows + 8 * chunk + 8)
        part = gathered[0, at, :]
        for region in range(1, regions):
            part = part + gathered[region, at, :]
        chunks.append(part)
    info = jnp.concatenate(chunks, axis=1) if len(chunks) > 1 else chunks[0]
    maps_ref[...] = incidence(
        info[0:1].astype(jnp.int32), info[1:2].astype(jnp.int32), regions * nodes
    )
    limits = info[2:3]
    prices_all = jnp.concatenate([gathered[region, :rows, :] for region in range(regions)], axis=1)
    flows = jnp.clip(-0.5 * dot3(prices_all, maps_ref[...], False), -limits, limits)
    local = local_ref.shape[1]
    flows_ref[:rows, :local] = local_ref[...]
    flows_ref[:rows, local:] = flows
    flows_ref[rows : rows + 1, local:] = limits
    maps_own = maps_ref[pl.ds(pl.multiple_of(own * nodes, nodes), nodes), :]
    balance = balance_ref[...] + dot3(2.0 * flows, maps_own, True)
    step_up = (1.0 / (techs + 8.0)) * balance
    prices_ref[...] = gathered[own, :rows, :] + step_up
    change = row_sum(flows * flows)
    slot = lax.broadcasted_iota(jnp.int32, change.shape, 1)
    primal = fold_lanes(jnp.where(slot // slots == own, change, 0.0))
    more = jnp.concatenate(
        [primal, row_sum(step_up * step_up), jnp.zeros((SQUARES - 2, LANES), jnp.float32)], axis=0
    )
    sums_ref[...] = sums_in_ref[...]
    squares = sums_in_ref[techs : techs + SQUARES, :] + more
    sums_ref[techs : techs + SQUARES, :] = squares


def neighbour_rows(sizes, given, hour_index):
    units = sizes.units
    if hasattr(given, "totals"):
        return read_lanes(given.next_row, 0, units), read_lanes(given.prev_row, 0, units)
    first = halo_at(sizes)
    last = first + units // LANES
    core, x_place, odd = hour_index % 2, hour_index // 2 % 2, hour_index // 4 % 2
    next_row = jnp.where(
        odd == 0, read_lanes(given.near, first, units), read_lanes(given.far, first, units)
    )
    prev_row = jnp.where(
        odd == 0, read_lanes(given.far, last, units), read_lanes(given.near, last, units)
    )
    next_row = jnp.where(x_place == 0, read_lanes(given.across, first, units), next_row)
    prev_row = jnp.where(x_place == 0, prev_row, read_lanes(given.across, last, units))
    next_row = jnp.where(core == 0, read_lanes(given.partner, first, units), next_row)
    prev_row = jnp.where(core == 0, prev_row, read_lanes(given.partner, last, units))
    return next_row, prev_row


def total_of(parts):
    if hasattr(parts, "totals"):
        return parts.totals[...]
    return (parts.slab[...] + parts.near[...]) + (parts.middle[...] + parts.far[...])


def sweep_kernel(sizes, iteration, names_in, names_out, *refs):
    rows, techs, nodes = sizes.rows, sizes.techs, sizes.nodes
    slots, regions, lines, units = sizes.slots, sizes.regions, sizes.lines, sizes.units
    second = iteration == 1
    last = iteration == ITERS - 1
    given = Bag(**dict(zip(names_in, refs[: len(names_in)])))
    gives = Bag(**dict(zip(names_out, refs[len(names_in) :])))
    own = lax.axis_index("region")
    hour_index = lax.axis_index("hours")
    gathered = given.gathered

    at = places(sizes)
    fixed = given.available.at[techs + 1]
    small = given.dispatch.at[techs]
    sums = total_of(given)
    squares = jnp.sum(sums[techs : techs + 2], axis=1, keepdims=True)
    old_weight = jnp.ones((1, 1), jnp.float32) if second else small[at.weight : at.weight + 1, :1]
    weight = jnp.sqrt(
        old_weight * jnp.sqrt((squares[1:2] + EPSILON) / (squares[0:1] + EPSILON))
    )
    primal_step = 0.5 / weight
    if second:
        first = sums_rows(sizes)
        col_weight, cost = sums[first : first + techs], sums[first + techs : first + 2 * techs]
        negative = sums[techs + 2 : techs + 3]
        capacity = jnp.maximum(-cost / col_weight, 0.0)
        first_bar = 2.0 * capacity
    else:
        col_weight = given.cap_duals[techs, :techs, :]
        cost = given.cap_duals[techs, techs : 2 * techs, :]
        capacity = small[:techs, :]
        negative = small[at.negative : at.negative + 1, :]
    capacity_new = jnp.maximum(capacity - (cost - sums[:techs]) / (weight * col_weight), 0.0)
    capacity_bar = 2.0 * capacity_new - capacity

    prices_all = jnp.concatenate([gathered[region, :rows, :] for region in range(regions)], axis=1)
    prices = gathered[own, :rows, :]
    maps_local = given.maps_local[...]
    slope_local = dot3(prices, maps_local, False)
    slope_cross = dot3(prices_all, given.maps_cross[...], False)

    energy = read_lanes(fixed, at.energy, units)
    row_id = lax.broadcasted_iota(jnp.int32, (rows, units), 0)
    next_row, prev_row = neighbour_rows(sizes, given, hour_index)
    store_duals = given.store_duals[...]
    next_duals = jnp.where(row_id == rows - 1, next_row, pltpu.roll(store_duals, rows - 1, 0))
    if second:
        charge = jnp.zeros((rows, units), jnp.float32)
        charge_before = jnp.zeros((1, units), jnp.float32)
    else:
        charge = given.charge[...]
        charge_before = read_lanes(small, at.before, units)
    charge_new = jnp.clip(charge - primal_step * (store_duals - next_duals), 0.0, energy)
    gives.charge[...] = charge_new

    primal_row = jnp.zeros((1, LANES), jnp.float32)
    bars = []
    local, total_flows = lines + units, lines + units + regions * slots
    local_limits = read_lanes(fixed, at.limits, local)
    cross_limits = given.flows[rows : rows + 1, local:]
    for bound, slope, low, high in (
        (local_limits[:, :lines], slope_local[:, :lines], 0, lines),
        (local_limits[:, lines:], slope_local[:, lines:] + store_duals, lines, local),
        (cross_limits, slope_cross, local, total_flows),
    ):
        old = given.flows[:rows, low:high]
        new = jnp.clip(old - primal_step * slope, -bound, bound)
        bars.append(2.0 * new - old)
        if not last:
            gives.flows[:rows, low:high] = new
            change = row_sum((new - old) ** 2)
            if low == local:
                slot = lax.broadcasted_iota(jnp.int32, change.shape, 1)
                change = jnp.where(slot // slots == own, change, 0.0)
            primal_row = primal_row + fold_lanes(change)
    maps_own = given.maps_cross[pl.ds(pl.multiple_of(own * nodes, nodes), nodes), :]
    balance = dot3(jnp.concatenate(bars[:2], axis=1), maps_local, True) - given.available[techs]
    balance = balance + dot3(bars[2], maps_own, True)

    gen_cost = fixed[:techs, :]
    half_weight = weight / 2.0
    primal_acc = jnp.zeros((rows, nodes), jnp.float32)
    dual_acc = jnp.zeros((rows, nodes), jnp.float32)
    for tech in range(techs):
        slope = gen_cost[tech : tech + 1] + prices
        dispatch = given.dispatch[tech]
        avail = given.available[tech]
        if second:
            duals = jnp.maximum(0.5 * (2.0 * dispatch - avail * first_bar[tech : tech + 1]), 0.0)
        else:
            duals = given.cap_duals[tech]
        dispatch_new = jnp.maximum(dispatch - primal_step * (slope + duals), 0.0)
        dispatch_bar = 2.0 * dispatch_new - dispatch
        balance = balance + dispatch_bar
        if last:
            gives.dispatch[pl.ds(tech, rows, stride=techs), :] = dispatch_new
            continue
        gives.dispatch[tech] = dispatch_new
        cap_rows = dispatch_bar - avail * capacity_bar[tech : tech + 1]
        primal_acc = primal_acc + (dispatch_new - dispatch) ** 2
        duals_new = jnp.maximum(duals + half_weight * cap_rows, 0.0)
        dual_acc = dual_acc + (duals_new - duals) ** 2
        gives.cap_duals[tech] = duals_new
        gives.sums[tech : tech + 1, :] = row_sum(avail * duals_new)

    step_up = weight / (techs + 8.0) * balance
    if last:
        gives.prices[...] = prices + step_up
        owned = fixed[at.owned : at.owned + 1, : gives.capacity.shape[1]].astype(jnp.int32)
        tech_hot, node_hot = owned_one_hots(owned, techs, nodes)
        chosen = dot3(capacity_new, node_hot, False)
        gives.capacity[...] = row_sum(jnp.where(tech_hot, chosen, 0.0))
        gives.negative[...] = negative
        return
    gives.prices[...] = prices + step_up
    gives.flows[rows : rows + 1, local:] = cross_limits
    gives.cap_duals[techs, :techs, :] = col_weight
    gives.cap_duals[techs, techs : 2 * techs, :] = cost
    small_new = gives.dispatch.at[techs]
    small_new[:techs, :] = capacity_new
    small_new[at.weight : at.weight + 1, :] = jnp.broadcast_to(weight, (1, LANES))
    small_new[at.negative : at.negative + 1, :] = negative
    charge_bar = 2.0 * charge_new - charge
    before_new = jnp.clip(charge_before - primal_step * (prev_row - store_duals[0:1]), 0.0, energy)
    write_lanes(small_new, at.before, before_new)
    before_bar = 2.0 * before_new - charge_before
    shifted_bar = jnp.where(row_id == 0, before_bar, pltpu.roll(charge_bar, 1, 0))
    store_step = weight / 3.0 * (charge_bar - shifted_bar + bars[1])
    store_new = store_duals + store_step
    gives.store_duals[...] = store_new
    primal_row = primal_row + row_sum(primal_acc) + fold_lanes(row_sum((charge_new - charge) ** 2))
    primal_row = primal_row + jnp.where(
        hour_index == 0, row_sum((capacity_new - capacity) ** 2), 0.0
    )
    dual_row = row_sum(dual_acc + step_up * step_up) + fold_lanes(row_sum(store_step * store_step))
    squares = jnp.concatenate(
        [primal_row, dual_row, jnp.zeros((SQUARES - 2, LANES), jnp.float32)], axis=0
    )
    gives.sums[techs : techs + SQUARES, :] = squares
    write_halo(sizes, gives.sums, store_new)


def call(kernel, given, outs, flops=0, left=(), scratch=(), limit=VMEM_BYTES):
    names_in, names_out = tuple(vars(given)), tuple(vars(outs))
    values = pl.pallas_call(
        functools.partial(kernel, names_in, names_out),
        out_shape=tuple(vars(outs).values()),
        in_specs=[
            pl.BlockSpec(memory_space=pl.ANY if i in left else pltpu.VMEM)
            for i in range(len(names_in))
        ],
        out_specs=[pl.BlockSpec(memory_space=pltpu.VMEM)] * len(names_out),
        scratch_shapes=scratch,
        cost_estimate=pl.CostEstimate(flops=flops, bytes_accessed=4 * flops, transcendentals=0),
        compiler_params=pltpu.CompilerParams(vmem_limit_bytes=limit),
    )(*vars(given).values())
    return Bag(**dict(zip(names_out, values)))


def swap(value, hour_bit, region_bit):
    hours, regions = lax.axis_size("hours"), lax.axis_size("region")
    pairs = [
        (hour * regions + region, (hour ^ hour_bit) * regions + (region ^ region_bit))
        for hour in range(hours)
        for region in range(regions)
    ]
    return lax.ppermute(value, ("hours", "region"), pairs)


def shifted(value, steps):
    count = lax.axis_size("hours")
    return lax.ppermute(value, "hours", [(i, (i + steps) % count) for i in range(count)])


def both_regions(block):
    if lax.axis_size("region") != 2:
        return lax.all_gather(block, "region")
    return in_order(block, swap(block, 0, 1))


def in_order(block, other):
    return jnp.where(
        lax.axis_index("region") == 0, jnp.stack([block, other]), jnp.stack([other, block])
    )


def exchange(sizes, prices, sums):
    hours, regions = lax.axis_size("hours"), lax.axis_size("region")
    techs, span = sizes.techs, sizes.units // LANES
    halo = halo_at(sizes)
    if regions != 2 or hours != 16:
        gathered = lax.all_gather(prices, "region")
        totals = lax.psum(sums, "hours")
        totals = totals.at[techs:halo].set(lax.psum(totals[techs:halo], "region"))
        next_row = shifted(sums[halo : halo + span], -1)
        prev_row = shifted(sums[halo + span : halo + 2 * span], 1)
        return gathered, Bag(totals=totals, next_row=next_row, prev_row=prev_row)

    def merged(mine, yours, mine_first):
        last = halo + span
        edges = [
            jnp.where(mine_first, mine[halo:last], yours[halo:last]),
            jnp.where(mine_first, yours[last : last + span], mine[last : last + span]),
        ]
        total = mine + yours
        return jnp.concatenate([total[:halo], *edges, total[last + span :]], axis=0)

    hour = lax.axis_index("hours")
    partner = swap(sums, 1, 0)
    chip = merged(sums, partner, hour % 2 == 0)
    across = swap(chip, 2 + 1, 0)
    diagonal = swap(chip[techs:halo], 2 + 1, 1)
    beside = swap(jnp.concatenate([prices, chip[techs:halo]], axis=0), 0, 1)
    other, squares = beside[: sizes.rows], beside[sizes.rows :]
    slab = merged(chip, across, hour // 2 % 2 == 0)
    slab = slab.at[techs:halo].add(squares + diagonal)
    near, middle, far = [swap(slab, 4 * step + 1, 0) for step in (1, 2, 3)]
    parts = Bag(slab=slab, near=near, middle=middle, far=far, partner=partner, across=across)
    return in_order(prices, other), parts


def shape(*dims, dtype=jnp.float32):
    return jax.ShapeDtypeStruct(dims, dtype)


def corrected(sizes, state, prices, sums, parts):
    techs = sizes.techs
    totals = total_of(parts)
    first = sums_rows(sizes)
    col_weight, cost = totals[first : first + techs], totals[first + techs :]
    capacity = jnp.maximum(-cost / col_weight, 0.0)
    taken = state.dispatch[:techs]
    rows_of = 2.0 * taken - state.available[:techs] * (2.0 * capacity)[:, None, :]
    duals = jnp.maximum(0.5 * rows_of, 0.0)
    own = jnp.where(lax.axis_index("hours") == 0, jnp.sum(capacity**2, axis=0), 0.0)
    fixed = sums.at[:techs].set(jnp.sum(state.available[:techs] * duals, axis=1))
    fixed = fixed.at[techs].add(own)
    fixed = fixed.at[techs + 1].add(jnp.sum(duals**2 - taken**2, axis=(0, 1)))
    return exchange(sizes, prices, fixed)[1]


def run(args, exact):
    rows, techs, nodes = args.availability.shape
    hours, regions = lax.axis_size("hours"), lax.axis_size("region")
    slots, owned = args.cross_limit.shape[1], args.cap_cost.shape[1]
    units, lines = args.store_node.shape[0], args.line_limit.shape[0]
    sizes = Bag(
        rows=rows, techs=techs, nodes=nodes, regions=regions, slots=slots, lines=lines, units=units
    )
    cross = regions * slots

    gathered = both_regions(
        call(
            lambda names_in, names_out, *refs: first_kernel(sizes, refs[:4], *refs[4:]),
            Bag(
                price=args.price_start,
                ends=args.cross_ends[:, 0],
                limit=args.cross_limit,
                pairs=args.pair_counts,
            ),
            Bag(block=shape(rows + 8 * (cross // LANES), nodes)),
            left=(0, 1, 2, 3),
            scratch=[
                pltpu.VMEM((2, slots), jnp.int32),
                pltpu.VMEM((1, slots), jnp.float32),
                pltpu.VMEM((1, regions), jnp.int32),
                pltpu.SemaphoreType.DMA((4,)),
            ],
            limit=None,
        ).block
    )
    state = call(
        functools.partial(start_kernel, sizes),
        Bag(
            availability=args.availability.reshape(rows * techs, nodes),
            price=args.price_start,
            demand=args.demand,
            gen_cost=args.gen_cost,
            cap_cost=args.cap_cost,
            owner=args.owner_map.reshape(hours, owned),
            line_ends=args.line_ends,
            line_limit=args.line_limit[None],
            store_node=args.store_node[None],
            store_power=args.store_power[None],
            store_energy=args.store_energy[None],
        ),
        Bag(
            available=shape(techs + 2, rows, nodes),
            maps_local=shape(nodes, lines + units, dtype=jnp.bfloat16),
            flows_local=shape(rows, lines + units),
            store_duals=shape(rows, units),
            dispatch=shape(techs + 1, rows, nodes),
            balance=shape(rows, nodes),
            sums=shape(sums_rows(sizes) + 2 * techs, nodes),
        ),
        flops=10**6,
        left=(0,),
        scratch=[pltpu.VMEM((rows * techs, nodes), jnp.float32), pltpu.SemaphoreType.DMA],
    )
    closed = call(
        lambda names_in, names_out, *refs: close_kernel(sizes, *refs),
        Bag(
            gathered=gathered,
            flows_local=state.flows_local,
            balance=state.balance,
            sums=state.sums,
        ),
        Bag(
            maps=shape(regions * nodes, cross, dtype=jnp.bfloat16),
            flows=shape(rows + 8, lines + units + cross),
            prices=shape(rows, nodes),
            sums=shape(*state.sums.shape),
        ),
    )
    del state.sums, state.balance, state.flows_local
    state.maps_cross, state.flows = closed.maps, closed.flows
    gathered, parts = exchange(sizes, closed.prices, closed.sums)
    if exact:
        parts = corrected(sizes, state, closed.prices, closed.sums, parts)
    return sweeps(sizes, owned, state, gathered, parts)


def sweeps(sizes, owned, state, gathered, parts):
    rows, techs, nodes, lines, units = (
        sizes.rows,
        sizes.techs,
        sizes.nodes,
        sizes.lines,
        sizes.units,
    )
    state = Bag(**vars(state))
    for iteration in range(1, ITERS):
        given = Bag(**vars(state), **vars(parts), gathered=gathered)
        if iteration < ITERS - 1:
            outs = Bag(
                dispatch=shape(techs + 1, rows, nodes),
                cap_duals=shape(techs + 1, rows, nodes),
                flows=shape(rows + 8, lines + units + sizes.regions * sizes.slots),
                store_duals=shape(rows, units),
                charge=shape(rows, units),
                prices=shape(rows, nodes),
                sums=shape(sums_rows(sizes), nodes),
            )
        else:
            outs = Bag(
                dispatch=shape(rows * techs, nodes),
                capacity=shape(1, owned),
                prices=shape(rows, nodes),
                charge=shape(rows, units),
                negative=shape(1, LANES),
            )
        results = call(functools.partial(sweep_kernel, sizes, iteration), given, outs)
        if iteration < ITERS - 1:
            gathered, parts = exchange(sizes, results.prices, results.sums)
            del results.prices, results.sums
            vars(state).update(vars(results))
    dispatch = results.dispatch.reshape(rows, techs, nodes)
    outputs = (dispatch, results.capacity, results.prices, results.charge)
    return outputs, results.negative[0, 0]


def body(
    availability,
    demand,
    gen_cost,
    cap_cost,
    owner_map,
    line_ends,
    line_limit,
    cross_ends,
    cross_limit,
    pair_counts,
    store_node,
    store_energy,
    store_power,
    price_start,
):
    args = Bag(**locals())
    outputs, negative = run(args, False)
    return lax.cond(negative > 0.0, lambda: run(args, True)[0], lambda: outputs)


def solution(mesh):
    placed = (
        P("hours", None, "region"),
        P("hours", "region"),
        P(None, "region"),
        P("region", "hours"),
        P("region", None),
        P(None, "region"),
        P("region"),
        P(None, "region", None),
        P("region", None),
        P("region", None),
        P("region"),
        P("region"),
        P("region"),
        P("hours", "region"),
    )
    return jax.shard_map(
        body,
        mesh=mesh,
        in_specs=placed,
        out_specs=(
            P("hours", None, "region"),
            P("region", "hours"),
            P("hours", "region"),
            P("hours", "region"),
        ),
        check_vma=False,
    )
```

```python
import functools
from types import SimpleNamespace as Bag

import jax
import jax.numpy as jnp
from jax import lax
from jax.experimental import pallas as pl
from jax.experimental.pallas import tpu as pltpu
from jax.sharding import PartitionSpec as P

ITERS = 4
EPSILON = 1e-06
LANES = 128
VMEM_BYTES = 24 * 1024 * 1024
SQUARES = 3


def split3(value):
    high = value.astype(jnp.bfloat16)
    rest = value - high.astype(jnp.float32)
    middle = rest.astype(jnp.bfloat16)
    low = (rest - middle.astype(jnp.float32)).astype(jnp.bfloat16)
    return jnp.concatenate([high, middle, low], axis=0)


def dot3(value, matrix, transposed):
    rows = value.shape[0]
    contract = ((1,), (1 if transposed else 0,))
    product = lax.dot_general(
        split3(value), matrix, (contract, ((), ())), preferred_element_type=jnp.float32
    )
    return product[:rows] + product[rows : 2 * rows] + product[2 * rows :]


def row_sum(value):
    return jnp.sum(value, axis=0, keepdims=True)


def fold_lanes(row):
    total = row[:, :LANES]
    for start in range(LANES, row.shape[1], LANES):
        total = total + row[:, start : start + LANES]
    return total


def owned_one_hots(owned, tech_count, node_count):
    shape_t = (tech_count, owned.shape[1])
    shape_n = (node_count, owned.shape[1])
    tech = lax.broadcasted_iota(jnp.int32, shape_t, 0) == owned // node_count
    node = lax.broadcasted_iota(jnp.int32, shape_n, 0) == owned % node_count
    return tech, node.astype(jnp.float32).astype(jnp.bfloat16)


def incidence(start, end, count):
    node = lax.broadcasted_iota(jnp.int32, (count, start.shape[1]), 0)
    maps = (node == end).astype(jnp.float32) - (node == start).astype(jnp.float32)
    return maps.astype(jnp.bfloat16)


def halo_at(sizes):
    return sizes.techs + SQUARES


def sums_rows(sizes):
    return (halo_at(sizes) + 2 * sizes.units // LANES + 7) // 8 * 8


def write_halo(sizes, sums_ref, store_new):
    halo, span, rows = halo_at(sizes), sizes.units // LANES, sizes.rows
    write_lanes(sums_ref, halo, store_new[:1])
    write_lanes(sums_ref, halo + span, store_new[rows - 1 :])
    used, end = halo + 2 * span, sums_rows(sizes)
    if used < end:
        sums_ref[used:end, :] = jnp.zeros((end - used, LANES), jnp.float32)


def write_lanes(ref, start, row):
    for i in range(row.shape[1] // LANES):
        ref[start + i : start + i + 1, :] = row[:, i * LANES : (i + 1) * LANES]


def read_lanes(ref, start, length):
    return jnp.concatenate(
        [ref[start + i : start + i + 1, :] for i in range(length // LANES)], axis=1
    )


def places(sizes):
    span = sizes.units // LANES
    limits = sizes.techs
    energy = limits + (sizes.lines + sizes.units) // LANES
    return Bag(
        limits=limits,
        energy=energy,
        owned=energy + span,
        weight=sizes.techs,
        before=sizes.techs + 1,
        negative=sizes.techs + 1 + span,
    )


def first_kernel(sizes, sources, block_ref, ends_ref, limit_ref, pairs_ref, sems):
    rows = sizes.rows
    targets = (block_ref.at[pl.ds(0, rows)], ends_ref, limit_ref, pairs_ref)
    copies = [
        pltpu.make_async_copy(source, target, sems.at[i])
        for i, (source, target) in enumerate(zip(sources, targets))
    ]
    for copy in copies:
        copy.start()
    nodes, slots, regions = sizes.nodes, sizes.slots, sizes.regions
    own = lax.axis_index("region")
    width = slots // regions
    slot = lax.broadcasted_iota(jnp.int32, (1, slots), 1)
    pair = slot // width
    for copy in copies[1:]:
        copy.wait()
    in_use = jnp.zeros((1, slots), jnp.int32)
    for target in range(regions):
        in_use = jnp.where(pair == target, pairs_ref[0:1, target : target + 1], in_use)
    place = lax.broadcasted_iota(jnp.int32, (slots, regions * slots), 1) == (
        own * slots + lax.broadcasted_iota(jnp.int32, (slots, regions * slots), 0)
    )
    place = place.astype(jnp.float32).astype(jnp.bfloat16)
    bound = jnp.where(slot % width < in_use, limit_ref[...], 0.0)
    start = (ends_ref[0:1, :] + own * nodes).astype(jnp.float32)
    end = (ends_ref[1:2, :] + pair * nodes).astype(jnp.float32)
    rest = jnp.zeros((13, slots), jnp.float32)
    info = dot3(jnp.concatenate([start, end, bound, rest], axis=0), place, False)
    for chunk in range(regions * slots // LANES):
        block_ref[rows + 8 * chunk : rows + 8 * chunk + 8, :] = info[
            :8, chunk * LANES : (chunk + 1) * LANES
        ]
    copies[0].wait()


def start_kernel(sizes, names_in, names_out, *refs):
    given = Bag(**dict(zip(names_in, refs[: len(names_in)])))
    gives = Bag(**dict(zip(names_out, refs[len(names_in) : -2])))
    availability, sem = refs[-2:]
    copy = pltpu.make_async_copy(given.availability, availability, sem)
    copy.start()
    rows, techs, nodes, lines = sizes.rows, sizes.techs, sizes.nodes, sizes.lines
    at = places(sizes)
    fixed = gives.available.at[techs + 1]
    gives.available[techs] = given.demand[...]
    fixed[:techs, :] = given.gen_cost[...]
    write_lanes(fixed, at.energy, given.store_energy[...])
    owned = given.owner[pl.ds(lax.axis_index("hours"), 1), :]
    fixed[at.owned : at.owned + 1, : owned.shape[1]] = owned.astype(jnp.float32)
    line_ends, stores = given.line_ends[...], given.store_node[...]
    start = jnp.concatenate([line_ends[0:1], jnp.full_like(stores, -1)], axis=1)
    end = jnp.concatenate([line_ends[1:2], stores], axis=1)
    maps = incidence(start, end, nodes)
    limits = jnp.concatenate([given.line_limit[...], given.store_power[...]], axis=1)
    gives.maps_local[...] = maps
    write_lanes(fixed, at.limits, limits)
    prices = given.price[...]
    flows = jnp.clip(-0.5 * dot3(prices, maps, False), -limits, limits)
    gives.flows_local[...] = flows
    store_new = (1.0 / 3.0) * (2.0 * flows[:, lines:])
    gives.store_duals[...] = store_new
    primal_row = fold_lanes(row_sum(flows * flows))
    dual_row = fold_lanes(row_sum(store_new * store_new))
    balance = dot3(2.0 * flows, maps, True) - given.demand[...]
    gen_cost = given.gen_cost[...]
    copy.wait()
    acc = jnp.zeros((rows, nodes), jnp.float32)
    weights = jnp.zeros((techs, nodes), jnp.float32)
    for hour in range(rows):
        weights = weights + availability[hour * techs : (hour + 1) * techs, :]
    for tech in range(techs):
        avail = availability[pl.ds(tech, rows, stride=techs), :]
        gives.available[tech] = avail
        dispatch = jnp.maximum(-0.5 * (gen_cost[tech : tech + 1] + prices), 0.0)
        gives.dispatch[tech] = dispatch
        dispatch_bar = 2.0 * dispatch
        balance = balance + dispatch_bar
        duals = jnp.maximum(0.5 * dispatch_bar, 0.0)
        acc = acc + dispatch * dispatch
        gives.sums[tech : tech + 1, :] = row_sum(avail * duals)
    gives.balance[...] = balance
    squares = row_sum(acc)
    cost = given.cap_cost[...]
    negative = jnp.sum((cost < 0.0).astype(jnp.float32), axis=1, keepdims=True)
    write_halo(sizes, gives.sums, store_new)
    gives.sums[techs : techs + SQUARES, :] = jnp.concatenate(
        [primal_row + squares, dual_row + squares, jnp.broadcast_to(negative, (1, LANES))], axis=0
    )
    tech_hot, node_hot = owned_one_hots(owned, techs, nodes)
    first = sums_rows(sizes)
    gives.sums[first : first + techs, :] = weights
    gives.sums[first + techs : first + 2 * techs, :] = dot3(
        jnp.where(tech_hot, cost, 0.0), node_hot, True
    )


def close_kernel(
    sizes,
    gathered,
    local_ref,
    balance_ref,
    sums_in_ref,
    maps_ref,
    flows_ref,
    prices_ref,
    sums_ref,
):
    rows, techs, nodes = sizes.rows, sizes.techs, sizes.nodes
    slots, regions = sizes.slots, sizes.regions
    own = lax.axis_index("region")
    chunks = []
    for chunk in range(regions * slots // LANES):
        at = slice(rows + 8 * chunk, rows + 8 * chunk + 8)
        part = gathered[0, at, :]
        for region in range(1, regions):
            part = part + gathered[region, at, :]
        chunks.append(part)
    info = jnp.concatenate(chunks, axis=1) if len(chunks) > 1 else chunks[0]
    maps_ref[...] = incidence(
        info[0:1].astype(jnp.int32), info[1:2].astype(jnp.int32), regions * nodes
    )
    limits = info[2:3]
    prices_all = jnp.concatenate([gathered[region, :rows, :] for region in range(regions)], axis=1)
    flows = jnp.clip(-0.5 * dot3(prices_all, maps_ref[...], False), -limits, limits)
    local = local_ref.shape[1]
    flows_ref[:rows, :local] = local_ref[...]
    flows_ref[:rows, local:] = flows
    flows_ref[rows : rows + 1, local:] = limits
    maps_own = maps_ref[pl.ds(pl.multiple_of(own * nodes, nodes), nodes), :]
    balance = balance_ref[...] + dot3(2.0 * flows, maps_own, True)
    step_up = (1.0 / (techs + 8.0)) * balance
    prices_ref[...] = gathered[own, :rows, :] + step_up
    change = row_sum(flows * flows)
    slot = lax.broadcasted_iota(jnp.int32, change.shape, 1)
    primal = fold_lanes(jnp.where(slot // slots == own, change, 0.0))
    more = jnp.concatenate(
        [primal, row_sum(step_up * step_up), jnp.zeros((SQUARES - 2, LANES), jnp.float32)], axis=0
    )
    sums_ref[...] = sums_in_ref[...]
    squares = sums_in_ref[techs : techs + SQUARES, :] + more
    sums_ref[techs : techs + SQUARES, :] = squares


def neighbour_rows(sizes, given, hour_index):
    units = sizes.units
    if hasattr(given, "totals"):
        return read_lanes(given.next_row, 0, units), read_lanes(given.prev_row, 0, units)
    first = halo_at(sizes)
    last = first + units // LANES
    core, x_place, odd = hour_index % 2, hour_index // 2 % 2, hour_index // 4 % 2
    next_row = jnp.where(
        odd == 0, read_lanes(given.near, first, units), read_lanes(given.far, first, units)
    )
    prev_row = jnp.where(
        odd == 0, read_lanes(given.far, last, units), read_lanes(given.near, last, units)
    )
    next_row = jnp.where(x_place == 0, read_lanes(given.across, first, units), next_row)
    prev_row = jnp.where(x_place == 0, prev_row, read_lanes(given.across, last, units))
    next_row = jnp.where(core == 0, read_lanes(given.partner, first, units), next_row)
    prev_row = jnp.where(core == 0, prev_row, read_lanes(given.partner, last, units))
    return next_row, prev_row


def total_of(parts):
    if hasattr(parts, "totals"):
        return parts.totals[...]
    return (parts.slab[...] + parts.near[...]) + (parts.middle[...] + parts.far[...])


def sweep_kernel(sizes, iteration, names_in, names_out, *refs):
    rows, techs, nodes = sizes.rows, sizes.techs, sizes.nodes
    slots, regions, lines, units = sizes.slots, sizes.regions, sizes.lines, sizes.units
    second = iteration == 1
    last = iteration == ITERS - 1
    given = Bag(**dict(zip(names_in, refs[: len(names_in)])))
    gives = Bag(**dict(zip(names_out, refs[len(names_in) :])))
    own = lax.axis_index("region")
    hour_index = lax.axis_index("hours")
    gathered = given.gathered

    at = places(sizes)
    fixed = given.available.at[techs + 1]
    small = given.dispatch.at[techs]
    sums = total_of(given)
    squares = jnp.sum(sums[techs : techs + 2], axis=1, keepdims=True)
    old_weight = jnp.ones((1, 1), jnp.float32) if second else small[at.weight : at.weight + 1, :1]
    weight = jnp.sqrt(
        old_weight * jnp.sqrt((squares[1:2] + EPSILON) / (squares[0:1] + EPSILON))
    )
    primal_step = 0.5 / weight
    if second:
        first = sums_rows(sizes)
        col_weight, cost = sums[first : first + techs], sums[first + techs : first + 2 * techs]
        negative = sums[techs + 2 : techs + 3]
        capacity = jnp.maximum(-cost / col_weight, 0.0)
        first_bar = 2.0 * capacity
    else:
        col_weight = given.cap_duals[techs, :techs, :]
        cost = given.cap_duals[techs, techs : 2 * techs, :]
        capacity = small[:techs, :]
        negative = small[at.negative : at.negative + 1, :]
    capacity_new = jnp.maximum(capacity - (cost - sums[:techs]) / (weight * col_weight), 0.0)
    capacity_bar = 2.0 * capacity_new - capacity

    prices_all = jnp.concatenate([gathered[region, :rows, :] for region in range(regions)], axis=1)
    prices = gathered[own, :rows, :]
    maps_local = given.maps_local[...]
    slope_local = dot3(prices, maps_local, False)
    slope_cross = dot3(prices_all, given.maps_cross[...], False)

    energy = read_lanes(fixed, at.energy, units)
    row_id = lax.broadcasted_iota(jnp.int32, (rows, units), 0)
    next_row, prev_row = neighbour_rows(sizes, given, hour_index)
    store_duals = given.store_duals[...]
    next_duals = jnp.where(row_id == rows - 1, next_row, pltpu.roll(store_duals, rows - 1, 0))
    if second:
        charge = jnp.zeros((rows, units), jnp.float32)
        charge_before = jnp.zeros((1, units), jnp.float32)
    else:
        charge = given.charge[...]
        charge_before = read_lanes(small, at.before, units)
    charge_new = jnp.clip(charge - primal_step * (store_duals - next_duals), 0.0, energy)
    gives.charge[...] = charge_new

    primal_row = jnp.zeros((1, LANES), jnp.float32)
    bars = []
    local, total_flows = lines + units, lines + units + regions * slots
    local_limits = read_lanes(fixed, at.limits, local)
    cross_limits = given.flows[rows : rows + 1, local:]
    for bound, slope, low, high in (
        (local_limits[:, :lines], slope_local[:, :lines], 0, lines),
        (local_limits[:, lines:], slope_local[:, lines:] + store_duals, lines, local),
        (cross_limits, slope_cross, local, total_flows),
    ):
        old = given.flows[:rows, low:high]
        new = jnp.clip(old - primal_step * slope, -bound, bound)
        bars.append(2.0 * new - old)
        if not last:
            gives.flows[:rows, low:high] = new
            change = row_sum((new - old) ** 2)
            if low == local:
                slot = lax.broadcasted_iota(jnp.int32, change.shape, 1)
                change = jnp.where(slot // slots == own, change, 0.0)
            primal_row = primal_row + fold_lanes(change)
    maps_own = given.maps_cross[pl.ds(pl.multiple_of(own * nodes, nodes), nodes), :]
    balance = dot3(jnp.concatenate(bars[:2], axis=1), maps_local, True) - given.available[techs]
    balance = balance + dot3(bars[2], maps_own, True)

    gen_cost = fixed[:techs, :]
    half_weight = weight / 2.0
    primal_acc = jnp.zeros((rows, nodes), jnp.float32)
    dual_acc = jnp.zeros((rows, nodes), jnp.float32)
    for tech in range(techs):
        slope = gen_cost[tech : tech + 1] + prices
        dispatch = given.dispatch[tech]
        avail = given.available[tech]
        if second:
            duals = jnp.maximum(0.5 * (2.0 * dispatch - avail * first_bar[tech : tech + 1]), 0.0)
        else:
            duals = given.cap_duals[tech]
        dispatch_new = jnp.maximum(dispatch - primal_step * (slope + duals), 0.0)
        dispatch_bar = 2.0 * dispatch_new - dispatch
        balance = balance + dispatch_bar
        if last:
            gives.dispatch[pl.ds(tech, rows, stride=techs), :] = dispatch_new
            continue
        gives.dispatch[tech] = dispatch_new
        cap_rows = dispatch_bar - avail * capacity_bar[tech : tech + 1]
        primal_acc = primal_acc + (dispatch_new - dispatch) ** 2
        duals_new = jnp.maximum(duals + half_weight * cap_rows, 0.0)
        dual_acc = dual_acc + (duals_new - duals) ** 2
        gives.cap_duals[tech] = duals_new
        gives.sums[tech : tech + 1, :] = row_sum(avail * duals_new)

    step_up = weight / (techs + 8.0) * balance
    if last:
        gives.prices[...] = prices + step_up
        owned = fixed[at.owned : at.owned + 1, : gives.capacity.shape[1]].astype(jnp.int32)
        tech_hot, node_hot = owned_one_hots(owned, techs, nodes)
        chosen = dot3(capacity_new, node_hot, False)
        gives.capacity[...] = row_sum(jnp.where(tech_hot, chosen, 0.0))
        gives.negative[...] = negative
        return
    gives.prices[...] = prices + step_up
    gives.flows[rows : rows + 1, local:] = cross_limits
    gives.cap_duals[techs, :techs, :] = col_weight
    gives.cap_duals[techs, techs : 2 * techs, :] = cost
    small_new = gives.dispatch.at[techs]
    small_new[:techs, :] = capacity_new
    small_new[at.weight : at.weight + 1, :] = jnp.broadcast_to(weight, (1, LANES))
    small_new[at.negative : at.negative + 1, :] = negative
    charge_bar = 2.0 * charge_new - charge
    before_new = jnp.clip(charge_before - primal_step * (prev_row - store_duals[0:1]), 0.0, energy)
    write_lanes(small_new, at.before, before_new)
    before_bar = 2.0 * before_new - charge_before
    shifted_bar = jnp.where(row_id == 0, before_bar, pltpu.roll(charge_bar, 1, 0))
    store_step = weight / 3.0 * (charge_bar - shifted_bar + bars[1])
    store_new = store_duals + store_step
    gives.store_duals[...] = store_new
    primal_row = primal_row + row_sum(primal_acc) + fold_lanes(row_sum((charge_new - charge) ** 2))
    primal_row = primal_row + jnp.where(
        hour_index == 0, row_sum((capacity_new - capacity) ** 2), 0.0
    )
    dual_row = row_sum(dual_acc + step_up * step_up) + fold_lanes(row_sum(store_step * store_step))
    squares = jnp.concatenate(
        [primal_row, dual_row, jnp.zeros((SQUARES - 2, LANES), jnp.float32)], axis=0
    )
    gives.sums[techs : techs + SQUARES, :] = squares
    write_halo(sizes, gives.sums, store_new)


def call(kernel, given, outs, flops=0, left=(), scratch=(), limit=VMEM_BYTES):
    names_in, names_out = tuple(vars(given)), tuple(vars(outs))
    values = pl.pallas_call(
        functools.partial(kernel, names_in, names_out),
        out_shape=tuple(vars(outs).values()),
        in_specs=[
            pl.BlockSpec(memory_space=pl.ANY if i in left else pltpu.VMEM)
            for i in range(len(names_in))
        ],
        out_specs=[pl.BlockSpec(memory_space=pltpu.VMEM)] * len(names_out),
        scratch_shapes=scratch,
        cost_estimate=pl.CostEstimate(flops=flops, bytes_accessed=4 * flops, transcendentals=0),
        compiler_params=pltpu.CompilerParams(vmem_limit_bytes=limit),
    )(*vars(given).values())
    return Bag(**dict(zip(names_out, values)))


def swap(value, hour_bit, region_bit):
    hours, regions = lax.axis_size("hours"), lax.axis_size("region")
    pairs = [
        (hour * regions + region, (hour ^ hour_bit) * regions + (region ^ region_bit))
        for hour in range(hours)
        for region in range(regions)
    ]
    return lax.ppermute(value, ("hours", "region"), pairs)


def shifted(value, steps):
    count = lax.axis_size("hours")
    return lax.ppermute(value, "hours", [(i, (i + steps) % count) for i in range(count)])


def both_regions(block):
    if lax.axis_size("region") != 2:
        return lax.all_gather(block, "region")
    return in_order(block, swap(block, 0, 1))


def in_order(block, other):
    return jnp.where(
        lax.axis_index("region") == 0, jnp.stack([block, other]), jnp.stack([other, block])
    )


def exchange(sizes, prices, sums):
    hours, regions = lax.axis_size("hours"), lax.axis_size("region")
    techs, span = sizes.techs, sizes.units // LANES
    halo = halo_at(sizes)
    if regions != 2 or hours != 16:
        gathered = lax.all_gather(prices, "region")
        totals = lax.psum(sums, "hours")
        totals = totals.at[techs:halo].set(lax.psum(totals[techs:halo], "region"))
        next_row = shifted(sums[halo : halo + span], -1)
        prev_row = shifted(sums[halo + span : halo + 2 * span], 1)
        return gathered, Bag(totals=totals, next_row=next_row, prev_row=prev_row)

    def merged(mine, yours, mine_first):
        last = halo + span
        edges = [
            jnp.where(mine_first, mine[halo:last], yours[halo:last]),
            jnp.where(mine_first, yours[last : last + span], mine[last : last + span]),
        ]
        total = mine + yours
        return jnp.concatenate([total[:halo], *edges, total[last + span :]], axis=0)

    hour = lax.axis_index("hours")
    partner = swap(sums, 1, 0)
    chip = merged(sums, partner, hour % 2 == 0)
    across = swap(chip, 2 + 1, 0)
    diagonal = swap(chip[techs:halo], 2 + 1, 1)
    beside = swap(jnp.concatenate([prices, chip[techs:halo]], axis=0), 0, 1)
    other, squares = beside[: sizes.rows], beside[sizes.rows :]
    slab = merged(chip, across, hour // 2 % 2 == 0)
    slab = slab + jnp.pad(squares + diagonal, ((techs, slab.shape[0] - halo), (0, 0)))
    near, middle, far = [swap(slab, 4 * step + 1, 0) for step in (1, 2, 3)]
    parts = Bag(slab=slab, near=near, middle=middle, far=far, partner=partner, across=across)
    return in_order(prices, other), parts


def shape(*dims, dtype=jnp.float32):
    return jax.ShapeDtypeStruct(dims, dtype)


def corrected(sizes, state, prices, sums, parts):
    techs = sizes.techs
    totals = total_of(parts)
    first = sums_rows(sizes)
    col_weight, cost = totals[first : first + techs], totals[first + techs :]
    capacity = jnp.maximum(-cost / col_weight, 0.0)
    taken = state.dispatch[:techs]
    rows_of = 2.0 * taken - state.available[:techs] * (2.0 * capacity)[:, None, :]
    duals = jnp.maximum(0.5 * rows_of, 0.0)
    own = jnp.where(lax.axis_index("hours") == 0, jnp.sum(capacity**2, axis=0), 0.0)
    fixed = sums.at[:techs].set(jnp.sum(state.available[:techs] * duals, axis=1))
    fixed = fixed.at[techs].add(own)
    fixed = fixed.at[techs + 1].add(jnp.sum(duals**2 - taken**2, axis=(0, 1)))
    return exchange(sizes, prices, fixed)[1]


def run(args, exact):
    rows, techs, nodes = args.availability.shape
    hours, regions = lax.axis_size("hours"), lax.axis_size("region")
    slots, owned = args.cross_limit.shape[1], args.cap_cost.shape[1]
    units, lines = args.store_node.shape[0], args.line_limit.shape[0]
    sizes = Bag(
        rows=rows, techs=techs, nodes=nodes, regions=regions, slots=slots, lines=lines, units=units
    )
    cross = regions * slots

    gathered = both_regions(
        call(
            lambda names_in, names_out, *refs: first_kernel(sizes, refs[:4], *refs[4:]),
            Bag(
                price=args.price_start,
                ends=args.cross_ends[:, 0],
                limit=args.cross_limit,
                pairs=args.pair_counts,
            ),
            Bag(block=shape(rows + 8 * (cross // LANES), nodes)),
            left=(0, 1, 2, 3),
            scratch=[
                pltpu.VMEM((2, slots), jnp.int32),
                pltpu.VMEM((1, slots), jnp.float32),
                pltpu.VMEM((1, regions), jnp.int32),
                pltpu.SemaphoreType.DMA((4,)),
            ],
            limit=None,
        ).block
    )
    state = call(
        functools.partial(start_kernel, sizes),
        Bag(
            availability=args.availability.reshape(rows * techs, nodes),
            price=args.price_start,
            demand=args.demand,
            gen_cost=args.gen_cost,
            cap_cost=args.cap_cost,
            owner=args.owner_map.reshape(hours, owned),
            line_ends=args.line_ends,
            line_limit=args.line_limit[None],
            store_node=args.store_node[None],
            store_power=args.store_power[None],
            store_energy=args.store_energy[None],
        ),
        Bag(
            available=shape(techs + 2, rows, nodes),
            maps_local=shape(nodes, lines + units, dtype=jnp.bfloat16),
            flows_local=shape(rows, lines + units),
            store_duals=shape(rows, units),
            dispatch=shape(techs + 1, rows, nodes),
            balance=shape(rows, nodes),
            sums=shape(sums_rows(sizes) + 2 * techs, nodes),
        ),
        flops=10**6,
        left=(0,),
        scratch=[pltpu.VMEM((rows * techs, nodes), jnp.float32), pltpu.SemaphoreType.DMA],
    )
    closed = call(
        lambda names_in, names_out, *refs: close_kernel(sizes, *refs),
        Bag(
            gathered=gathered,
            flows_local=state.flows_local,
            balance=state.balance,
            sums=state.sums,
        ),
        Bag(
            maps=shape(regions * nodes, cross, dtype=jnp.bfloat16),
            flows=shape(rows + 8, lines + units + cross),
            prices=shape(rows, nodes),
            sums=shape(*state.sums.shape),
        ),
    )
    del state.sums, state.balance, state.flows_local
    state.maps_cross, state.flows = closed.maps, closed.flows
    gathered, parts = exchange(sizes, closed.prices, closed.sums)
    if exact:
        parts = corrected(sizes, state, closed.prices, closed.sums, parts)
    return sweeps(sizes, owned, state, gathered, parts)


def sweeps(sizes, owned, state, gathered, parts):
    rows, techs, nodes, lines, units = (
        sizes.rows,
        sizes.techs,
        sizes.nodes,
        sizes.lines,
        sizes.units,
    )
    state = Bag(**vars(state))
    for iteration in range(1, ITERS):
        given = Bag(**vars(state), **vars(parts), gathered=gathered)
        if iteration < ITERS - 1:
            outs = Bag(
                dispatch=shape(techs + 1, rows, nodes),
                cap_duals=shape(techs + 1, rows, nodes),
                flows=shape(rows + 8, lines + units + sizes.regions * sizes.slots),
                store_duals=shape(rows, units),
                charge=shape(rows, units),
                prices=shape(rows, nodes),
                sums=shape(sums_rows(sizes), nodes),
            )
        else:
            outs = Bag(
                dispatch=shape(rows * techs, nodes),
                capacity=shape(1, owned),
                prices=shape(rows, nodes),
                charge=shape(rows, units),
                negative=shape(1, LANES),
            )
        results = call(functools.partial(sweep_kernel, sizes, iteration), given, outs)
        if iteration < ITERS - 1:
            gathered, parts = exchange(sizes, results.prices, results.sums)
            del results.prices, results.sums
            vars(state).update(vars(results))
    dispatch = results.dispatch.reshape(rows, techs, nodes)
    outputs = (dispatch, results.capacity, results.prices, results.charge)
    return outputs, results.negative[0, 0]


def body(
    availability,
    demand,
    gen_cost,
    cap_cost,
    owner_map,
    line_ends,
    line_limit,
    cross_ends,
    cross_limit,
    pair_counts,
    store_node,
    store_energy,
    store_power,
    price_start,
):
    args = Bag(**locals())
    outputs, negative = run(args, False)
    return lax.cond(negative > 0.0, lambda: run(args, True)[0], lambda: outputs)


def solution(mesh):
    placed = (
        P("hours", None, "region"),
        P("hours", "region"),
        P(None, "region"),
        P("region", "hours"),
        P("region", None),
        P(None, "region"),
        P("region"),
        P(None, "region", None),
        P("region", None),
        P("region", None),
        P("region"),
        P("region"),
        P("region"),
        P("hours", "region"),
    )
    return jax.shard_map(
        body,
        mesh=mesh,
        in_specs=placed,
        out_specs=(
            P("hours", None, "region"),
            P("region", "hours"),
            P("hours", "region"),
            P("hours", "region"),
        ),
        check_vma=False,
    )
```

```python
import functools
from types import SimpleNamespace as Bag

import jax
import jax.numpy as jnp
from jax import lax
from jax.experimental import pallas as pl
from jax.experimental.pallas import tpu as pltpu
from jax.sharding import PartitionSpec as P

ITERS = 4
EPSILON = 1e-06
LANES = 128
VMEM_BYTES = 24 * 1024 * 1024
SQUARES = 3


def split3(value):
    high = value.astype(jnp.bfloat16)
    rest = value - high.astype(jnp.float32)
    middle = rest.astype(jnp.bfloat16)
    low = (rest - middle.astype(jnp.float32)).astype(jnp.bfloat16)
    return jnp.concatenate([high, middle, low], axis=0)


def dot3(value, matrix, transposed):
    rows = value.shape[0]
    contract = ((1,), (1 if transposed else 0,))
    product = lax.dot_general(
        split3(value), matrix, (contract, ((), ())), preferred_element_type=jnp.float32
    )
    return product[:rows] + product[rows : 2 * rows] + product[2 * rows :]


def row_sum(value):
    return jnp.sum(value, axis=0, keepdims=True)


def fold_lanes(row):
    total = row[:, :LANES]
    for start in range(LANES, row.shape[1], LANES):
        total = total + row[:, start : start + LANES]
    return total


def owned_one_hots(owned, tech_count, node_count):
    shape_t = (tech_count, owned.shape[1])
    shape_n = (node_count, owned.shape[1])
    tech = lax.broadcasted_iota(jnp.int32, shape_t, 0) == owned // node_count
    node = lax.broadcasted_iota(jnp.int32, shape_n, 0) == owned % node_count
    return tech, node.astype(jnp.float32).astype(jnp.bfloat16)


def incidence(start, end, count):
    node = lax.broadcasted_iota(jnp.int32, (count, start.shape[1]), 0)
    maps = (node == end).astype(jnp.float32) - (node == start).astype(jnp.float32)
    return maps.astype(jnp.bfloat16)


def halo_at(sizes):
    return sizes.techs + SQUARES


def sums_rows(sizes):
    return (halo_at(sizes) + 2 * sizes.units // LANES + 7) // 8 * 8


def write_halo(sizes, sums_ref, store_new):
    halo, span, rows = halo_at(sizes), sizes.units // LANES, sizes.rows
    write_lanes(sums_ref, halo, store_new[:1])
    write_lanes(sums_ref, halo + span, store_new[rows - 1 :])
    used, end = halo + 2 * span, sums_rows(sizes)
    if used < end:
        sums_ref[used:end, :] = jnp.zeros((end - used, LANES), jnp.float32)


def write_lanes(ref, start, row):
    for i in range(row.shape[1] // LANES):
        ref[start + i : start + i + 1, :] = row[:, i * LANES : (i + 1) * LANES]


def read_lanes(ref, start, length):
    return jnp.concatenate(
        [ref[start + i : start + i + 1, :] for i in range(length // LANES)], axis=1
    )


def places(sizes):
    span = sizes.units // LANES
    limits = sizes.techs
    energy = limits + (sizes.lines + sizes.units) // LANES
    return Bag(
        limits=limits,
        energy=energy,
        owned=energy + span,
        weight=sizes.techs,
        before=sizes.techs + 1,
        negative=sizes.techs + 1 + span,
    )


def first_kernel(sizes, sources, block_ref, ends_ref, limit_ref, pairs_ref, sems):
    rows = sizes.rows
    targets = (block_ref.at[pl.ds(0, rows)], ends_ref, limit_ref, pairs_ref)
    copies = [
        pltpu.make_async_copy(source, target, sems.at[i])
        for i, (source, target) in enumerate(zip(sources, targets))
    ]
    for copy in copies:
        copy.start()
    nodes, slots, regions = sizes.nodes, sizes.slots, sizes.regions
    own = lax.axis_index("region")
    width = slots // regions
    slot = lax.broadcasted_iota(jnp.int32, (1, slots), 1)
    pair = slot // width
    for copy in copies[1:]:
        copy.wait()
    in_use = jnp.zeros((1, slots), jnp.int32)
    for target in range(regions):
        in_use = jnp.where(pair == target, pairs_ref[0:1, target : target + 1], in_use)
    bound = jnp.where(slot % width < in_use, limit_ref[...], 0.0)
    start = (ends_ref[0:1, :] + own * nodes).astype(jnp.float32)
    end = (ends_ref[1:2, :] + pair * nodes).astype(jnp.float32)
    block_ref[rows:, :] = jnp.zeros((block_ref.shape[0] - rows, LANES), jnp.float32)
    width = min(slots, LANES)
    for chunk in range(slots // width):
        at = rows + 8 * chunk
        for i, row in enumerate((start, end, bound)):
            block_ref[at + i : at + i + 1, :width] = row[:, chunk * width : (chunk + 1) * width]
    copies[0].wait()


def start_kernel(sizes, names_in, names_out, *refs):
    given = Bag(**dict(zip(names_in, refs[: len(names_in)])))
    gives = Bag(**dict(zip(names_out, refs[len(names_in) : -2])))
    availability, sem = refs[-2:]
    copy = pltpu.make_async_copy(given.availability, availability, sem)
    copy.start()
    rows, techs, nodes, lines = sizes.rows, sizes.techs, sizes.nodes, sizes.lines
    at = places(sizes)
    fixed = gives.available.at[techs + 1]
    gives.available[techs] = given.demand[...]
    fixed[:techs, :] = given.gen_cost[...]
    write_lanes(fixed, at.energy, given.store_energy[...])
    owned = given.owner[pl.ds(lax.axis_index("hours"), 1), :]
    fixed[at.owned : at.owned + 1, : owned.shape[1]] = owned.astype(jnp.float32)
    line_ends, stores = given.line_ends[...], given.store_node[...]
    start = jnp.concatenate([line_ends[0:1], jnp.full_like(stores, -1)], axis=1)
    end = jnp.concatenate([line_ends[1:2], stores], axis=1)
    maps = incidence(start, end, nodes)
    limits = jnp.concatenate([given.line_limit[...], given.store_power[...]], axis=1)
    gives.maps_local[...] = maps
    write_lanes(fixed, at.limits, limits)
    prices = given.price[...]
    flows = jnp.clip(-0.5 * dot3(prices, maps, False), -limits, limits)
    gives.flows_local[...] = flows
    store_new = (1.0 / 3.0) * (2.0 * flows[:, lines:])
    gives.store_duals[...] = store_new
    primal_row = fold_lanes(row_sum(flows * flows))
    dual_row = fold_lanes(row_sum(store_new * store_new))
    balance = dot3(2.0 * flows, maps, True) - given.demand[...]
    gen_cost = given.gen_cost[...]
    copy.wait()
    acc = jnp.zeros((rows, nodes), jnp.float32)
    weights = jnp.zeros((techs, nodes), jnp.float32)
    for hour in range(rows):
        weights = weights + availability[hour * techs : (hour + 1) * techs, :]
    for tech in range(techs):
        avail = availability[pl.ds(tech, rows, stride=techs), :]
        gives.available[tech] = avail
        dispatch = jnp.maximum(-0.5 * (gen_cost[tech : tech + 1] + prices), 0.0)
        gives.dispatch[tech] = dispatch
        dispatch_bar = 2.0 * dispatch
        balance = balance + dispatch_bar
        duals = jnp.maximum(0.5 * dispatch_bar, 0.0)
        acc = acc + dispatch * dispatch
        gives.sums[tech : tech + 1, :] = row_sum(avail * duals)
    gives.balance[...] = balance
    squares = row_sum(acc)
    cost = given.cap_cost[...]
    negative = jnp.sum((cost < 0.0).astype(jnp.float32), axis=1, keepdims=True)
    write_halo(sizes, gives.sums, store_new)
    gives.sums[techs : techs + SQUARES, :] = jnp.concatenate(
        [primal_row + squares, dual_row + squares, jnp.broadcast_to(negative, (1, LANES))], axis=0
    )
    tech_hot, node_hot = owned_one_hots(owned, techs, nodes)
    first = sums_rows(sizes)
    gives.sums[first : first + techs, :] = weights
    gives.sums[first + techs : first + 2 * techs, :] = dot3(
        jnp.where(tech_hot, cost, 0.0), node_hot, True
    )


def close_kernel(
    sizes,
    gathered,
    local_ref,
    balance_ref,
    sums_in_ref,
    maps_ref,
    flows_ref,
    prices_ref,
    sums_ref,
):
    rows, techs, nodes = sizes.rows, sizes.techs, sizes.nodes
    slots, regions = sizes.slots, sizes.regions
    own = lax.axis_index("region")
    width = min(slots, LANES)
    info = jnp.concatenate(
        [
            gathered[region, rows + 8 * chunk : rows + 8 * chunk + 8, :width]
            for region in range(regions)
            for chunk in range(slots // width)
        ],
        axis=1,
    )
    maps_ref[...] = incidence(
        info[0:1].astype(jnp.int32), info[1:2].astype(jnp.int32), regions * nodes
    )
    limits = info[2:3]
    prices_all = jnp.concatenate([gathered[region, :rows, :] for region in range(regions)], axis=1)
    flows = jnp.clip(-0.5 * dot3(prices_all, maps_ref[...], False), -limits, limits)
    local = local_ref.shape[1]
    flows_ref[:rows, :local] = local_ref[...]
    flows_ref[:rows, local:] = flows
    flows_ref[rows:, local:] = info
    maps_own = maps_ref[pl.ds(pl.multiple_of(own * nodes, nodes), nodes), :]
    balance = balance_ref[...] + dot3(2.0 * flows, maps_own, True)
    step_up = (1.0 / (techs + 8.0)) * balance
    prices_ref[...] = gathered[own, :rows, :] + step_up
    change = row_sum(flows * flows)
    slot = lax.broadcasted_iota(jnp.int32, change.shape, 1)
    primal = fold_lanes(jnp.where(slot // slots == own, change, 0.0))
    more = jnp.concatenate(
        [primal, row_sum(step_up * step_up), jnp.zeros((SQUARES - 2, LANES), jnp.float32)], axis=0
    )
    sums_ref[...] = sums_in_ref[...]
    squares = sums_in_ref[techs : techs + SQUARES, :] + more
    sums_ref[techs : techs + SQUARES, :] = squares


def neighbour_rows(sizes, given, hour_index):
    units = sizes.units
    if hasattr(given, "totals"):
        return read_lanes(given.next_row, 0, units), read_lanes(given.prev_row, 0, units)
    first = halo_at(sizes)
    last = first + units // LANES
    core, x_place, odd = hour_index % 2, hour_index // 2 % 2, hour_index // 4 % 2
    next_row = jnp.where(
        odd == 0, read_lanes(given.near, first, units), read_lanes(given.far, first, units)
    )
    prev_row = jnp.where(
        odd == 0, read_lanes(given.far, last, units), read_lanes(given.near, last, units)
    )
    next_row = jnp.where(x_place == 0, read_lanes(given.across, first, units), next_row)
    prev_row = jnp.where(x_place == 0, prev_row, read_lanes(given.across, last, units))
    next_row = jnp.where(core == 0, read_lanes(given.partner, first, units), next_row)
    prev_row = jnp.where(core == 0, prev_row, read_lanes(given.partner, last, units))
    return next_row, prev_row


def total_of(parts):
    if hasattr(parts, "totals"):
        return parts.totals[...]
    return (parts.slab[...] + parts.near[...]) + (parts.middle[...] + parts.far[...])


def sweep_kernel(sizes, iteration, names_in, names_out, *refs):
    rows, techs, nodes = sizes.rows, sizes.techs, sizes.nodes
    slots, regions, lines, units = sizes.slots, sizes.regions, sizes.lines, sizes.units
    second = iteration == 1
    last = iteration == ITERS - 1
    given = Bag(**dict(zip(names_in, refs[: len(names_in)])))
    gives = Bag(**dict(zip(names_out, refs[len(names_in) :])))
    own = lax.axis_index("region")
    hour_index = lax.axis_index("hours")
    gathered = given.gathered

    at = places(sizes)
    fixed = given.available.at[techs + 1]
    small = given.dispatch.at[techs]
    sums = total_of(given)
    squares = jnp.sum(sums[techs : techs + 2], axis=1, keepdims=True)
    old_weight = jnp.ones((1, 1), jnp.float32) if second else small[at.weight : at.weight + 1, :1]
    weight = jnp.sqrt(
        old_weight * jnp.sqrt((squares[1:2] + EPSILON) / (squares[0:1] + EPSILON))
    )
    primal_step = 0.5 / weight
    if second:
        first = sums_rows(sizes)
        col_weight, cost = sums[first : first + techs], sums[first + techs : first + 2 * techs]
        negative = sums[techs + 2 : techs + 3]
        capacity = jnp.maximum(-cost / col_weight, 0.0)
        first_bar = 2.0 * capacity
    else:
        col_weight = given.cap_duals[techs, :techs, :]
        cost = given.cap_duals[techs, techs : 2 * techs, :]
        capacity = small[:techs, :]
        negative = small[at.negative : at.negative + 1, :]
    capacity_new = jnp.maximum(capacity - (cost - sums[:techs]) / (weight * col_weight), 0.0)
    capacity_bar = 2.0 * capacity_new - capacity

    prices_all = jnp.concatenate([gathered[region, :rows, :] for region in range(regions)], axis=1)
    prices = gathered[own, :rows, :]
    maps_local = given.maps_local[...]
    slope_local = dot3(prices, maps_local, False)
    slope_cross = dot3(prices_all, given.maps_cross[...], False)

    energy = read_lanes(fixed, at.energy, units)
    row_id = lax.broadcasted_iota(jnp.int32, (rows, units), 0)
    next_row, prev_row = neighbour_rows(sizes, given, hour_index)
    store_duals = given.store_duals[...]
    next_duals = jnp.where(row_id == rows - 1, next_row, pltpu.roll(store_duals, rows - 1, 0))
    if second:
        charge = jnp.zeros((rows, units), jnp.float32)
        charge_before = jnp.zeros((1, units), jnp.float32)
    else:
        charge = given.charge[...]
        charge_before = read_lanes(small, at.before, units)
    charge_new = jnp.clip(charge - primal_step * (store_duals - next_duals), 0.0, energy)
    gives.charge[...] = charge_new

    primal_row = jnp.zeros((1, LANES), jnp.float32)
    bars = []
    local, total_flows = lines + units, lines + units + regions * slots
    local_limits = read_lanes(fixed, at.limits, local)
    cross_limits = given.flows[rows + 2 : rows + 3, local:]
    for bound, slope, low, high in (
        (local_limits[:, :lines], slope_local[:, :lines], 0, lines),
        (local_limits[:, lines:], slope_local[:, lines:] + store_duals, lines, local),
        (cross_limits, slope_cross, local, total_flows),
    ):
        old = given.flows[:rows, low:high]
        new = jnp.clip(old - primal_step * slope, -bound, bound)
        bars.append(2.0 * new - old)
        if not last:
            gives.flows[:rows, low:high] = new
            change = row_sum((new - old) ** 2)
            if low == local:
                slot = lax.broadcasted_iota(jnp.int32, change.shape, 1)
                change = jnp.where(slot // slots == own, change, 0.0)
            primal_row = primal_row + fold_lanes(change)
    maps_own = given.maps_cross[pl.ds(pl.multiple_of(own * nodes, nodes), nodes), :]
    balance = dot3(jnp.concatenate(bars[:2], axis=1), maps_local, True) - given.available[techs]
    balance = balance + dot3(bars[2], maps_own, True)

    gen_cost = fixed[:techs, :]
    half_weight = weight / 2.0
    primal_acc = jnp.zeros((rows, nodes), jnp.float32)
    dual_acc = jnp.zeros((rows, nodes), jnp.float32)
    for tech in range(techs):
        slope = gen_cost[tech : tech + 1] + prices
        dispatch = given.dispatch[tech]
        avail = given.available[tech]
        if second:
            duals = jnp.maximum(0.5 * (2.0 * dispatch - avail * first_bar[tech : tech + 1]), 0.0)
        else:
            duals = given.cap_duals[tech]
        dispatch_new = jnp.maximum(dispatch - primal_step * (slope + duals), 0.0)
        dispatch_bar = 2.0 * dispatch_new - dispatch
        balance = balance + dispatch_bar
        if last:
            gives.dispatch[pl.ds(tech, rows, stride=techs), :] = dispatch_new
            continue
        gives.dispatch[tech] = dispatch_new
        cap_rows = dispatch_bar - avail * capacity_bar[tech : tech + 1]
        primal_acc = primal_acc + (dispatch_new - dispatch) ** 2
        duals_new = jnp.maximum(duals + half_weight * cap_rows, 0.0)
        dual_acc = dual_acc + (duals_new - duals) ** 2
        gives.cap_duals[tech] = duals_new
        gives.sums[tech : tech + 1, :] = row_sum(avail * duals_new)

    step_up = weight / (techs + 8.0) * balance
    if last:
        gives.prices[...] = prices + step_up
        owned = fixed[at.owned : at.owned + 1, : gives.capacity.shape[1]].astype(jnp.int32)
        tech_hot, node_hot = owned_one_hots(owned, techs, nodes)
        chosen = dot3(capacity_new, node_hot, False)
        gives.capacity[...] = row_sum(jnp.where(tech_hot, chosen, 0.0))
        gives.negative[...] = negative
        gives.kept[:rows, :] = fixed[...]
        gives.kept[rows : rows + techs, :] = col_weight
        gives.kept[rows + techs : rows + 2 * techs, :] = cost
        for chunk in range(regions * slots // LANES):
            low = local + chunk * LANES
            first = rows + 2 * techs + 8 * chunk
            gives.kept[first : first + 8, :] = given.flows[rows:, low : low + LANES]
        return
    gives.prices[...] = prices + step_up
    gives.flows[rows:, local:] = given.flows[rows:, local:]
    gives.cap_duals[techs, :techs, :] = col_weight
    gives.cap_duals[techs, techs : 2 * techs, :] = cost
    small_new = gives.dispatch.at[techs]
    small_new[:techs, :] = capacity_new
    small_new[at.weight : at.weight + 1, :] = jnp.broadcast_to(weight, (1, LANES))
    small_new[at.negative : at.negative + 1, :] = negative
    charge_bar = 2.0 * charge_new - charge
    before_new = jnp.clip(charge_before - primal_step * (prev_row - store_duals[0:1]), 0.0, energy)
    write_lanes(small_new, at.before, before_new)
    before_bar = 2.0 * before_new - charge_before
    shifted_bar = jnp.where(row_id == 0, before_bar, pltpu.roll(charge_bar, 1, 0))
    store_step = weight / 3.0 * (charge_bar - shifted_bar + bars[1])
    store_new = store_duals + store_step
    gives.store_duals[...] = store_new
    primal_row = primal_row + row_sum(primal_acc) + fold_lanes(row_sum((charge_new - charge) ** 2))
    primal_row = primal_row + jnp.where(
        hour_index == 0, row_sum((capacity_new - capacity) ** 2), 0.0
    )
    dual_row = row_sum(dual_acc + step_up * step_up) + fold_lanes(row_sum(store_step * store_step))
    squares = jnp.concatenate(
        [primal_row, dual_row, jnp.zeros((SQUARES - 2, LANES), jnp.float32)], axis=0
    )
    gives.sums[techs : techs + SQUARES, :] = squares
    write_halo(sizes, gives.sums, store_new)


def call(kernel, given, outs, flops=0, left=(), scratch=(), limit=VMEM_BYTES):
    names_in, names_out = tuple(vars(given)), tuple(vars(outs))
    values = pl.pallas_call(
        functools.partial(kernel, names_in, names_out),
        out_shape=tuple(vars(outs).values()),
        in_specs=[
            pl.BlockSpec(memory_space=pl.ANY if i in left else pltpu.VMEM)
            for i in range(len(names_in))
        ],
        out_specs=[pl.BlockSpec(memory_space=pltpu.VMEM)] * len(names_out),
        scratch_shapes=scratch,
        cost_estimate=pl.CostEstimate(flops=flops, bytes_accessed=4 * flops, transcendentals=0),
        compiler_params=pltpu.CompilerParams(vmem_limit_bytes=limit),
    )(*vars(given).values())
    return Bag(**dict(zip(names_out, values)))


def swap(value, hour_bit, region_bit):
    hours, regions = lax.axis_size("hours"), lax.axis_size("region")
    pairs = [
        (hour * regions + region, (hour ^ hour_bit) * regions + (region ^ region_bit))
        for hour in range(hours)
        for region in range(regions)
    ]
    return lax.ppermute(value, ("hours", "region"), pairs)


def shifted(value, steps):
    count = lax.axis_size("hours")
    return lax.ppermute(value, "hours", [(i, (i + steps) % count) for i in range(count)])


def both_regions(block):
    if lax.axis_size("region") != 2:
        return lax.all_gather(block, "region")
    return in_order(block, swap(block, 0, 1))


def in_order(block, other):
    return jnp.where(
        lax.axis_index("region") == 0, jnp.stack([block, other]), jnp.stack([other, block])
    )


def exchange(sizes, prices, sums):
    hours, regions = lax.axis_size("hours"), lax.axis_size("region")
    techs, span = sizes.techs, sizes.units // LANES
    halo = halo_at(sizes)
    if regions != 2 or hours != 16:
        gathered = lax.all_gather(prices, "region")
        totals = lax.psum(sums, "hours")
        totals = totals.at[techs:halo].set(lax.psum(totals[techs:halo], "region"))
        next_row = shifted(sums[halo : halo + span], -1)
        prev_row = shifted(sums[halo + span : halo + 2 * span], 1)
        return gathered, Bag(totals=totals, next_row=next_row, prev_row=prev_row)

    def merged(mine, yours, mine_first):
        last = halo + span
        edges = [
            jnp.where(mine_first, mine[halo:last], yours[halo:last]),
            jnp.where(mine_first, yours[last : last + span], mine[last : last + span]),
        ]
        total = mine + yours
        return jnp.concatenate([total[:halo], *edges, total[last + span :]], axis=0)

    hour = lax.axis_index("hours")
    partner = swap(sums, 1, 0)
    chip = merged(sums, partner, hour % 2 == 0)
    across = swap(chip, 2 + 1, 0)
    diagonal = swap(chip[techs:halo], 2 + 1, 1)
    beside = swap(jnp.concatenate([prices, chip[techs:halo]], axis=0), 0, 1)
    other, squares = beside[: sizes.rows], beside[sizes.rows :]
    slab = merged(chip, across, hour // 2 % 2 == 0)
    slab = slab + jnp.pad(squares + diagonal, ((techs, slab.shape[0] - halo), (0, 0)))
    near, middle, far = [swap(slab, 4 * step + 1, 0) for step in (1, 2, 3)]
    parts = Bag(slab=slab, near=near, middle=middle, far=far, partner=partner, across=across)
    return in_order(prices, other), parts


def shape(*dims, dtype=jnp.float32):
    return jax.ShapeDtypeStruct(dims, dtype)


def restarted(sizes, kept, args):
    rows, techs, nodes, lines = sizes.rows, sizes.techs, sizes.nodes, sizes.lines
    local, cross = lines + sizes.units, sizes.regions * sizes.slots
    at, own = places(sizes), lax.axis_index("region")
    first_hour = lax.axis_index("hours") == 0
    price_start = args.price_start
    available = args.availability.transpose(1, 0, 2)
    fixed, last = kept[:rows], rows + 2 * techs
    col_weight, cost = kept[rows : rows + techs], kept[rows + techs : last]
    info = kept[last:].reshape(-1, 8, LANES).transpose(1, 0, 2).reshape(8, cross)
    local_limits = fixed[at.limits : at.energy].reshape(1, local)
    cross_limits = info[2:3]
    ends = info[:2].astype(jnp.int32)
    maps_cross_low = incidence(ends[:1], ends[1:], sizes.regions * nodes)
    stores = args.store_node[None]
    maps_local_low = incidence(
        jnp.concatenate([args.line_ends[:1], jnp.full_like(stores, -1)], axis=1),
        jnp.concatenate([args.line_ends[1:], stores], axis=1),
        nodes,
    )
    maps_local = maps_local_low.astype(jnp.float32)
    maps_cross = maps_cross_low.astype(jnp.float32)
    maps_own = lax.dynamic_slice_in_dim(maps_cross, own * nodes, nodes)
    prices_all = jnp.concatenate(list(both_regions(price_start)), axis=1)
    highest = lax.Precision.HIGHEST

    capacity = jnp.maximum(-cost / col_weight, 0.0)
    slopes = fixed[:techs][:, None, :] + price_start[None]
    dispatch = jnp.maximum(-0.5 * slopes, 0.0)
    slope = jnp.dot(price_start, maps_local, precision=highest)
    flows_local = jnp.clip(-0.5 * slope, -local_limits, local_limits)
    slope = jnp.dot(prices_all, maps_cross, precision=highest)
    flows_cross = jnp.clip(-0.5 * slope, -cross_limits, cross_limits)
    balance = (
        jnp.sum(2.0 * dispatch, axis=0)
        + jnp.dot(2.0 * flows_local, maps_local.T, precision=highest)
        + jnp.dot(2.0 * flows_cross, maps_own.T, precision=highest)
        - args.demand
    )
    step_up = balance / (techs + 8.0)
    duals = jnp.maximum(0.5 * (2.0 * dispatch - available * (2.0 * capacity)[:, None, :]), 0.0)
    store_duals = 2.0 * flows_local[:, lines:] / 3.0
    slot = lax.broadcasted_iota(jnp.int32, (1, cross), 1) // sizes.slots
    primal = (
        jnp.sum(dispatch**2)
        + jnp.sum(flows_local**2)
        + jnp.sum(jnp.where(slot == own, flows_cross**2, 0.0))
        + jnp.where(first_hour, jnp.sum(capacity**2), 0.0)
    )
    dual = jnp.sum(step_up**2) + jnp.sum(duals**2) + jnp.sum(store_duals**2)
    rows_of = [
        jnp.sum(available * duals, axis=1),
        jnp.zeros((SQUARES, nodes)).at[0, 0].set(primal).at[1, 0].set(dual),
        store_duals[:1].reshape(-1, LANES),
        store_duals[rows - 1 :].reshape(-1, LANES),
    ]
    used = halo_at(sizes) + 2 * sizes.units // LANES
    rows_of.append(jnp.zeros((sums_rows(sizes) - used, nodes)))
    rows_of += [jnp.where(first_hour, part, 0.0) for part in (col_weight, cost)]
    gathered, parts = exchange(sizes, price_start + step_up, jnp.concatenate(rows_of, axis=0))
    flows = jnp.concatenate([flows_local, flows_cross], axis=1)
    spare = jnp.concatenate([jnp.zeros((8, local)), info], axis=1)
    state = Bag(
        available=jnp.concatenate([available, args.demand[None], fixed[None]], axis=0),
        maps_local=maps_local_low,
        maps_cross=maps_cross_low,
        store_duals=store_duals,
        dispatch=jnp.concatenate([dispatch, jnp.zeros((1, rows, nodes))], axis=0),
        flows=jnp.concatenate([flows, spare], axis=0),
    )
    return state, gathered, parts


def run(args):
    rows, techs, nodes = args.availability.shape
    hours, regions = lax.axis_size("hours"), lax.axis_size("region")
    slots, owned = args.cross_limit.shape[1], args.cap_cost.shape[1]
    units, lines = args.store_node.shape[0], args.line_limit.shape[0]
    sizes = Bag(
        rows=rows, techs=techs, nodes=nodes, regions=regions, slots=slots, lines=lines, units=units
    )
    cross = regions * slots

    gathered = both_regions(
        call(
            lambda names_in, names_out, *refs: first_kernel(sizes, refs[:4], *refs[4:]),
            Bag(
                price=args.price_start,
                ends=args.cross_ends[:, 0],
                limit=args.cross_limit,
                pairs=args.pair_counts,
            ),
            Bag(block=shape(rows + 8 * max(1, slots // LANES), nodes)),
            left=(0, 1, 2, 3),
            scratch=[
                pltpu.VMEM((2, slots), jnp.int32),
                pltpu.VMEM((1, slots), jnp.float32),
                pltpu.VMEM((1, regions), jnp.int32),
                pltpu.SemaphoreType.DMA((4,)),
            ],
            limit=None,
        ).block
    )
    state = call(
        functools.partial(start_kernel, sizes),
        Bag(
            availability=args.availability.reshape(rows * techs, nodes),
            price=args.price_start,
            demand=args.demand,
            gen_cost=args.gen_cost,
            cap_cost=args.cap_cost,
            owner=args.owner_map.reshape(hours, owned),
            line_ends=args.line_ends,
            line_limit=args.line_limit[None],
            store_node=args.store_node[None],
            store_power=args.store_power[None],
            store_energy=args.store_energy[None],
        ),
        Bag(
            available=shape(techs + 2, rows, nodes),
            maps_local=shape(nodes, lines + units, dtype=jnp.bfloat16),
            flows_local=shape(rows, lines + units),
            store_duals=shape(rows, units),
            dispatch=shape(techs + 1, rows, nodes),
            balance=shape(rows, nodes),
            sums=shape(sums_rows(sizes) + 2 * techs, nodes),
        ),
        flops=10**6,
        left=(0,),
        scratch=[pltpu.VMEM((rows * techs, nodes), jnp.float32), pltpu.SemaphoreType.DMA],
    )
    closed = call(
        lambda names_in, names_out, *refs: close_kernel(sizes, *refs),
        Bag(
            gathered=gathered,
            flows_local=state.flows_local,
            balance=state.balance,
            sums=state.sums,
        ),
        Bag(
            maps=shape(regions * nodes, cross, dtype=jnp.bfloat16),
            flows=shape(rows + 8, lines + units + cross),
            prices=shape(rows, nodes),
            sums=shape(*state.sums.shape),
        ),
    )
    del state.sums, state.balance, state.flows_local
    state.maps_cross, state.flows = closed.maps, closed.flows
    gathered, parts = exchange(sizes, closed.prices, closed.sums)
    outputs, negative, kept = sweeps(sizes, owned, state, gathered, parts)

    def again():
        return sweeps(sizes, owned, *restarted(sizes, kept, args))[0]

    return lax.cond(negative > 0.0, again, lambda: outputs)


def sweeps(sizes, owned, state, gathered, parts):
    rows, techs, nodes, lines, units = (
        sizes.rows,
        sizes.techs,
        sizes.nodes,
        sizes.lines,
        sizes.units,
    )
    state = Bag(**vars(state))
    for iteration in range(1, ITERS):
        given = Bag(**vars(state), **vars(parts), gathered=gathered)
        if iteration < ITERS - 1:
            outs = Bag(
                dispatch=shape(techs + 1, rows, nodes),
                cap_duals=shape(techs + 1, rows, nodes),
                flows=shape(rows + 8, lines + units + sizes.regions * sizes.slots),
                store_duals=shape(rows, units),
                charge=shape(rows, units),
                prices=shape(rows, nodes),
                sums=shape(sums_rows(sizes), nodes),
            )
        else:
            outs = Bag(
                dispatch=shape(rows * techs, nodes),
                capacity=shape(1, owned),
                prices=shape(rows, nodes),
                charge=shape(rows, units),
                negative=shape(1, LANES),
                kept=shape(rows + 2 * techs + 8 * (sizes.regions * sizes.slots // LANES), LANES),
            )
        results = call(functools.partial(sweep_kernel, sizes, iteration), given, outs)
        if iteration < ITERS - 1:
            gathered, parts = exchange(sizes, results.prices, results.sums)
            del results.prices, results.sums
            vars(state).update(vars(results))
    dispatch = results.dispatch.reshape(rows, techs, nodes)
    outputs = (dispatch, results.capacity, results.prices, results.charge)
    return outputs, results.negative[0, 0], results.kept


def body(
    availability,
    demand,
    gen_cost,
    cap_cost,
    owner_map,
    line_ends,
    line_limit,
    cross_ends,
    cross_limit,
    pair_counts,
    store_node,
    store_energy,
    store_power,
    price_start,
):
    args = Bag(**locals())
    return run(args)


def solution(mesh):
    placed = (
        P("hours", None, "region"),
        P("hours", "region"),
        P(None, "region"),
        P("region", "hours"),
        P("region", None),
        P(None, "region"),
        P("region"),
        P(None, "region", None),
        P("region", None),
        P("region", None),
        P("region"),
        P("region"),
        P("region"),
        P("hours", "region"),
    )
    return jax.shard_map(
        body,
        mesh=mesh,
        in_specs=placed,
        out_specs=(
            P("hours", None, "region"),
            P("region", "hours"),
            P("hours", "region"),
            P("hours", "region"),
        ),
        check_vma=False,
    )
```

```python
import functools
from types import SimpleNamespace as Bag

import jax
import jax.numpy as jnp
from jax import lax
from jax.experimental import pallas as pl
from jax.experimental.pallas import tpu as pltpu
from jax.sharding import PartitionSpec as P

ITERS = 4
EPSILON = 1e-06
LANES = 128
VMEM_BYTES = 24 * 1024 * 1024
SQUARES = 3


def split3(value):
    high = value.astype(jnp.bfloat16)
    rest = value - high.astype(jnp.float32)
    middle = rest.astype(jnp.bfloat16)
    low = (rest - middle.astype(jnp.float32)).astype(jnp.bfloat16)
    return jnp.concatenate([high, middle, low], axis=0)


def dot3(value, matrix, transposed):
    rows = value.shape[0]
    contract = ((1,), (1 if transposed else 0,))
    product = lax.dot_general(
        split3(value), matrix, (contract, ((), ())), preferred_element_type=jnp.float32
    )
    return product[:rows] + product[rows : 2 * rows] + product[2 * rows :]


def row_sum(value):
    return jnp.sum(value, axis=0, keepdims=True)


def fold_lanes(row):
    total = row[:, :LANES]
    for start in range(LANES, row.shape[1], LANES):
        total = total + row[:, start : start + LANES]
    return total


def owned_one_hots(owned, tech_count, node_count):
    shape_t = (tech_count, owned.shape[1])
    shape_n = (node_count, owned.shape[1])
    tech = lax.broadcasted_iota(jnp.int32, shape_t, 0) == owned // node_count
    node = lax.broadcasted_iota(jnp.int32, shape_n, 0) == owned % node_count
    return tech, node.astype(jnp.float32).astype(jnp.bfloat16)


def incidence(start, end, count):
    node = lax.broadcasted_iota(jnp.int32, (count, start.shape[1]), 0)
    maps = (node == end).astype(jnp.float32) - (node == start).astype(jnp.float32)
    return maps.astype(jnp.bfloat16)


def halo_at(sizes):
    return sizes.techs + SQUARES


def sums_rows(sizes):
    return (halo_at(sizes) + 2 * sizes.units // LANES + 7) // 8 * 8


def write_halo(sizes, sums_ref, store_new):
    halo, span, rows = halo_at(sizes), sizes.units // LANES, sizes.rows
    write_lanes(sums_ref, halo, store_new[:1])
    write_lanes(sums_ref, halo + span, store_new[rows - 1 :])
    used, end = halo + 2 * span, sums_rows(sizes)
    if used < end:
        sums_ref[used:end, :] = jnp.zeros((end - used, LANES), jnp.float32)


def write_lanes(ref, start, row):
    for i in range(row.shape[1] // LANES):
        ref[start + i : start + i + 1, :] = row[:, i * LANES : (i + 1) * LANES]


def read_lanes(ref, start, length):
    return jnp.concatenate(
        [ref[start + i : start + i + 1, :] for i in range(length // LANES)], axis=1
    )


def places(sizes):
    span = sizes.units // LANES
    limits = sizes.techs
    energy = limits + (sizes.lines + sizes.units) // LANES
    return Bag(
        limits=limits,
        energy=energy,
        owned=energy + span,
        weight=sizes.techs,
        before=sizes.techs + 1,
        negative=sizes.techs + 1 + span,
    )


def first_kernel(sizes, names_in, names_out, *refs):
    rows, count = sizes.rows, len(names_in)
    sources, (block_ref, *outs) = refs[:count], refs[count : count + len(names_out)]
    ends_ref, limit_ref, pairs_ref, sems = refs[count + len(names_out) :]
    targets = (block_ref.at[pl.ds(0, rows)], ends_ref, limit_ref, pairs_ref, *outs)
    copies = [
        pltpu.make_async_copy(source, target, sems.at[i])
        for i, (source, target) in enumerate(zip(sources, targets))
    ]
    for copy in copies:
        copy.start()
    nodes, slots, regions = sizes.nodes, sizes.slots, sizes.regions
    own = lax.axis_index("region")
    width = slots // regions
    slot = lax.broadcasted_iota(jnp.int32, (1, slots), 1)
    pair = slot // width
    for copy in copies[1:4]:
        copy.wait()
    in_use = jnp.zeros((1, slots), jnp.int32)
    for target in range(regions):
        in_use = jnp.where(pair == target, pairs_ref[0:1, target : target + 1], in_use)
    bound = jnp.where(slot % width < in_use, limit_ref[...], 0.0)
    start = (ends_ref[0:1, :] + own * nodes).astype(jnp.float32)
    end = (ends_ref[1:2, :] + pair * nodes).astype(jnp.float32)
    block_ref[rows:, :] = jnp.zeros((block_ref.shape[0] - rows, LANES), jnp.float32)
    width = min(slots, LANES)
    for chunk in range(slots // width):
        at = rows + 8 * chunk
        for i, row in enumerate((start, end, bound)):
            block_ref[at + i : at + i + 1, :width] = row[:, chunk * width : (chunk + 1) * width]
    copies[0].wait()
    for copy in copies[4:]:
        copy.wait()


def start_kernel(sizes, names_in, names_out, *refs):
    given = Bag(**dict(zip(names_in, refs[: len(names_in)])))
    gives = Bag(**dict(zip(names_out, refs[len(names_in) : -2])))
    availability, sem = refs[-2:]
    copy = pltpu.make_async_copy(given.availability, availability, sem)
    copy.start()
    rows, techs, nodes, lines = sizes.rows, sizes.techs, sizes.nodes, sizes.lines
    at = places(sizes)
    fixed = gives.available.at[techs + 1]
    gives.available[techs] = given.demand[...]
    fixed[:techs, :] = given.gen_cost[...]
    write_lanes(fixed, at.energy, given.store_energy[...])
    owned = given.owner[pl.ds(lax.axis_index("hours"), 1), :]
    fixed[at.owned : at.owned + 1, : owned.shape[1]] = owned.astype(jnp.float32)
    line_ends, stores = given.line_ends[...], given.store_node[...]
    start = jnp.concatenate([line_ends[0:1], jnp.full_like(stores, -1)], axis=1)
    end = jnp.concatenate([line_ends[1:2], stores], axis=1)
    maps = incidence(start, end, nodes)
    limits = jnp.concatenate([given.line_limit[...], given.store_power[...]], axis=1)
    gives.maps_local[...] = maps
    write_lanes(fixed, at.limits, limits)
    prices = given.price[...]
    flows = jnp.clip(-0.5 * dot3(prices, maps, False), -limits, limits)
    gives.flows_local[...] = flows
    store_new = (1.0 / 3.0) * (2.0 * flows[:, lines:])
    gives.store_duals[...] = store_new
    primal_row = fold_lanes(row_sum(flows * flows))
    dual_row = fold_lanes(row_sum(store_new * store_new))
    balance = dot3(2.0 * flows, maps, True) - given.demand[...]
    gen_cost = given.gen_cost[...]
    copy.wait()
    acc = jnp.zeros((rows, nodes), jnp.float32)
    weights = jnp.zeros((techs, nodes), jnp.float32)
    for hour in range(rows):
        weights = weights + availability[hour * techs : (hour + 1) * techs, :]
    for tech in range(techs):
        avail = availability[pl.ds(tech, rows, stride=techs), :]
        gives.available[tech] = avail
        dispatch = jnp.maximum(-0.5 * (gen_cost[tech : tech + 1] + prices), 0.0)
        gives.dispatch[tech] = dispatch
        dispatch_bar = 2.0 * dispatch
        balance = balance + dispatch_bar
        duals = jnp.maximum(0.5 * dispatch_bar, 0.0)
        acc = acc + dispatch * dispatch
        gives.sums[tech : tech + 1, :] = row_sum(avail * duals)
    gives.balance[...] = balance
    squares = row_sum(acc)
    cost = given.cap_cost[...]
    negative = jnp.sum((cost < 0.0).astype(jnp.float32), axis=1, keepdims=True)
    write_halo(sizes, gives.sums, store_new)
    gives.sums[techs : techs + SQUARES, :] = jnp.concatenate(
        [primal_row + squares, dual_row + squares, jnp.broadcast_to(negative, (1, LANES))], axis=0
    )
    tech_hot, node_hot = owned_one_hots(owned, techs, nodes)
    first = sums_rows(sizes)
    gives.sums[first : first + techs, :] = weights
    gives.sums[first + techs : first + 2 * techs, :] = dot3(
        jnp.where(tech_hot, cost, 0.0), node_hot, True
    )


def close_kernel(
    sizes,
    gathered,
    local_ref,
    balance_ref,
    sums_in_ref,
    maps_ref,
    flows_ref,
    block_ref,
):
    rows, techs, nodes = sizes.rows, sizes.techs, sizes.nodes
    slots, regions = sizes.slots, sizes.regions
    own = lax.axis_index("region")
    width = min(slots, LANES)
    info = jnp.concatenate(
        [
            gathered[region, rows + 8 * chunk : rows + 8 * chunk + 8, :width]
            for region in range(regions)
            for chunk in range(slots // width)
        ],
        axis=1,
    )
    maps_ref[...] = incidence(
        info[0:1].astype(jnp.int32), info[1:2].astype(jnp.int32), regions * nodes
    )
    limits = info[2:3]
    prices_all = jnp.concatenate([gathered[region, :rows, :] for region in range(regions)], axis=1)
    flows = jnp.clip(-0.5 * dot3(prices_all, maps_ref[...], False), -limits, limits)
    local = local_ref.shape[1]
    flows_ref[:rows, :local] = local_ref[...]
    flows_ref[:rows, local:] = flows
    flows_ref[rows:, local:] = info
    maps_own = maps_ref[pl.ds(pl.multiple_of(own * nodes, nodes), nodes), :]
    balance = balance_ref[...] + dot3(2.0 * flows, maps_own, True)
    step_up = (1.0 / (techs + 8.0)) * balance
    block_ref[:rows, :] = gathered[own, :rows, :] + step_up
    change = row_sum(flows * flows)
    slot = lax.broadcasted_iota(jnp.int32, change.shape, 1)
    primal = fold_lanes(jnp.where(slot // slots == own, change, 0.0))
    more = jnp.concatenate(
        [primal, row_sum(step_up * step_up), jnp.zeros((SQUARES - 2, LANES), jnp.float32)], axis=0
    )
    block_ref[rows:, :] = sums_in_ref[...]
    block_ref[rows + techs : rows + techs + SQUARES, :] = (
        sums_in_ref[techs : techs + SQUARES, :] + more
    )


def neighbour_rows(sizes, given, hour_index):
    units = sizes.units
    if hasattr(given, "totals"):
        return read_lanes(given.next_row, 0, units), read_lanes(given.prev_row, 0, units)
    first = halo_at(sizes)
    last = first + units // LANES
    core, x_place, odd = hour_index % 2, hour_index // 2 % 2, hour_index // 4 % 2
    next_row = jnp.where(
        odd == 0, read_lanes(given.near, first, units), read_lanes(given.far, first, units)
    )
    prev_row = jnp.where(
        odd == 0, read_lanes(given.far, last, units), read_lanes(given.near, last, units)
    )
    next_row = jnp.where(x_place == 0, read_lanes(given.across, first, units), next_row)
    prev_row = jnp.where(x_place == 0, prev_row, read_lanes(given.across, last, units))
    next_row = jnp.where(core == 0, read_lanes(given.partner, first, units), next_row)
    prev_row = jnp.where(core == 0, prev_row, read_lanes(given.partner, last, units))
    return next_row, prev_row


def total_of(parts):
    if hasattr(parts, "totals"):
        return parts.totals[...]
    return (parts.slab[...] + parts.near[...]) + (parts.middle[...] + parts.far[...])


def sweep_kernel(sizes, iteration, names_in, names_out, *refs):
    rows, techs, nodes = sizes.rows, sizes.techs, sizes.nodes
    slots, regions, lines, units = sizes.slots, sizes.regions, sizes.lines, sizes.units
    second = iteration == 1
    last = iteration == ITERS - 1
    given = Bag(**dict(zip(names_in, refs[: len(names_in)])))
    gives = Bag(**dict(zip(names_out, refs[len(names_in) :])))
    own = lax.axis_index("region")
    hour_index = lax.axis_index("hours")
    gathered = given.gathered

    at = places(sizes)
    fixed = given.available.at[techs + 1]
    small = given.dispatch.at[techs]
    out_sums = None if last else gives.block.at[pl.ds(rows, sums_rows(sizes))]
    sums = total_of(given)
    squares = jnp.sum(sums[techs : techs + 2], axis=1, keepdims=True)
    old_weight = jnp.ones((1, 1), jnp.float32) if second else small[at.weight : at.weight + 1, :1]
    weight = jnp.sqrt(
        old_weight * jnp.sqrt((squares[1:2] + EPSILON) / (squares[0:1] + EPSILON))
    )
    primal_step = 0.5 / weight
    if second:
        first = sums_rows(sizes)
        col_weight, cost = sums[first : first + techs], sums[first + techs : first + 2 * techs]
        negative = sums[techs + 2 : techs + 3]
        capacity = jnp.maximum(-cost / col_weight, 0.0)
        first_bar = 2.0 * capacity
    else:
        col_weight = given.cap_duals[techs, :techs, :]
        cost = given.cap_duals[techs, techs : 2 * techs, :]
        capacity = small[:techs, :]
        negative = small[at.negative : at.negative + 1, :]
    capacity_new = jnp.maximum(capacity - (cost - sums[:techs]) / (weight * col_weight), 0.0)
    capacity_bar = 2.0 * capacity_new - capacity

    prices_all = jnp.concatenate([gathered[region, :rows, :] for region in range(regions)], axis=1)
    prices = gathered[own, :rows, :]
    maps_local = given.maps_local[...]
    slope_local = dot3(prices, maps_local, False)
    slope_cross = dot3(prices_all, given.maps_cross[...], False)

    energy = read_lanes(fixed, at.energy, units)
    row_id = lax.broadcasted_iota(jnp.int32, (rows, units), 0)
    next_row, prev_row = neighbour_rows(sizes, given, hour_index)
    store_duals = given.store_duals[...]
    next_duals = jnp.where(row_id == rows - 1, next_row, pltpu.roll(store_duals, rows - 1, 0))
    if second:
        charge = jnp.zeros((rows, units), jnp.float32)
        charge_before = jnp.zeros((1, units), jnp.float32)
    else:
        charge = given.charge[...]
        charge_before = read_lanes(small, at.before, units)
    charge_new = jnp.clip(charge - primal_step * (store_duals - next_duals), 0.0, energy)
    gives.charge[...] = charge_new

    primal_row = jnp.zeros((1, LANES), jnp.float32)
    bars = []
    local, total_flows = lines + units, lines + units + regions * slots
    local_limits = read_lanes(fixed, at.limits, local)
    cross_limits = given.flows[rows + 2 : rows + 3, local:]
    for bound, slope, low, high in (
        (local_limits[:, :lines], slope_local[:, :lines], 0, lines),
        (local_limits[:, lines:], slope_local[:, lines:] + store_duals, lines, local),
        (cross_limits, slope_cross, local, total_flows),
    ):
        old = given.flows[:rows, low:high]
        new = jnp.clip(old - primal_step * slope, -bound, bound)
        bars.append(2.0 * new - old)
        if not last:
            gives.flows[:rows, low:high] = new
            change = row_sum((new - old) ** 2)
            if low == local:
                slot = lax.broadcasted_iota(jnp.int32, change.shape, 1)
                change = jnp.where(slot // slots == own, change, 0.0)
            primal_row = primal_row + fold_lanes(change)
    maps_own = given.maps_cross[pl.ds(pl.multiple_of(own * nodes, nodes), nodes), :]
    balance = dot3(jnp.concatenate(bars[:2], axis=1), maps_local, True) - given.available[techs]
    balance = balance + dot3(bars[2], maps_own, True)

    gen_cost = fixed[:techs, :]
    half_weight = weight / 2.0
    primal_acc = jnp.zeros((rows, nodes), jnp.float32)
    dual_acc = jnp.zeros((rows, nodes), jnp.float32)
    for tech in range(techs):
        slope = gen_cost[tech : tech + 1] + prices
        dispatch = given.dispatch[tech]
        avail = given.available[tech]
        if second:
            duals = jnp.maximum(0.5 * (2.0 * dispatch - avail * first_bar[tech : tech + 1]), 0.0)
        else:
            duals = given.cap_duals[tech]
        dispatch_new = jnp.maximum(dispatch - primal_step * (slope + duals), 0.0)
        dispatch_bar = 2.0 * dispatch_new - dispatch
        balance = balance + dispatch_bar
        if last:
            gives.dispatch[pl.ds(tech, rows, stride=techs), :] = dispatch_new
            continue
        gives.dispatch[tech] = dispatch_new
        cap_rows = dispatch_bar - avail * capacity_bar[tech : tech + 1]
        primal_acc = primal_acc + (dispatch_new - dispatch) ** 2
        duals_new = jnp.maximum(duals + half_weight * cap_rows, 0.0)
        dual_acc = dual_acc + (duals_new - duals) ** 2
        gives.cap_duals[tech] = duals_new
        out_sums[tech : tech + 1, :] = row_sum(avail * duals_new)

    step_up = weight / (techs + 8.0) * balance
    if last:
        gives.prices[...] = prices + step_up
        owned = fixed[at.owned : at.owned + 1, : gives.capacity.shape[1]].astype(jnp.int32)
        tech_hot, node_hot = owned_one_hots(owned, techs, nodes)
        chosen = dot3(capacity_new, node_hot, False)
        gives.capacity[...] = row_sum(jnp.where(tech_hot, chosen, 0.0))
        gives.negative[...] = negative
        gives.kept[:rows, :] = fixed[...]
        gives.kept[rows : rows + techs, :] = col_weight
        gives.kept[rows + techs : rows + 2 * techs, :] = cost
        for chunk in range(regions * slots // LANES):
            low = local + chunk * LANES
            first = rows + 2 * techs + 8 * chunk
            gives.kept[first : first + 8, :] = given.flows[rows:, low : low + LANES]
        return
    gives.block[:rows, :] = prices + step_up
    gives.flows[rows:, local:] = given.flows[rows:, local:]
    gives.cap_duals[techs, :techs, :] = col_weight
    gives.cap_duals[techs, techs : 2 * techs, :] = cost
    small_new = gives.dispatch.at[techs]
    small_new[:techs, :] = capacity_new
    small_new[at.weight : at.weight + 1, :] = jnp.broadcast_to(weight, (1, LANES))
    small_new[at.negative : at.negative + 1, :] = negative
    charge_bar = 2.0 * charge_new - charge
    before_new = jnp.clip(charge_before - primal_step * (prev_row - store_duals[0:1]), 0.0, energy)
    write_lanes(small_new, at.before, before_new)
    before_bar = 2.0 * before_new - charge_before
    shifted_bar = jnp.where(row_id == 0, before_bar, pltpu.roll(charge_bar, 1, 0))
    store_step = weight / 3.0 * (charge_bar - shifted_bar + bars[1])
    store_new = store_duals + store_step
    gives.store_duals[...] = store_new
    primal_row = primal_row + row_sum(primal_acc) + fold_lanes(row_sum((charge_new - charge) ** 2))
    primal_row = primal_row + jnp.where(
        hour_index == 0, row_sum((capacity_new - capacity) ** 2), 0.0
    )
    dual_row = row_sum(dual_acc + step_up * step_up) + fold_lanes(row_sum(store_step * store_step))
    squares = jnp.concatenate(
        [primal_row, dual_row, jnp.zeros((SQUARES - 2, LANES), jnp.float32)], axis=0
    )
    out_sums[techs : techs + SQUARES, :] = squares
    write_halo(sizes, out_sums, store_new)


def call(kernel, given, outs, flops=0, left=(), scratch=(), limit=VMEM_BYTES):
    names_in, names_out = tuple(vars(given)), tuple(vars(outs))
    values = pl.pallas_call(
        functools.partial(kernel, names_in, names_out),
        out_shape=tuple(vars(outs).values()),
        in_specs=[
            pl.BlockSpec(memory_space=pl.ANY if i in left else pltpu.VMEM)
            for i in range(len(names_in))
        ],
        out_specs=[pl.BlockSpec(memory_space=pltpu.VMEM)] * len(names_out),
        scratch_shapes=scratch,
        cost_estimate=pl.CostEstimate(flops=flops, bytes_accessed=4 * flops, transcendentals=0),
        compiler_params=pltpu.CompilerParams(vmem_limit_bytes=limit),
    )(*vars(given).values())
    return Bag(**dict(zip(names_out, values)))


def swap(value, hour_bit, region_bit):
    hours, regions = lax.axis_size("hours"), lax.axis_size("region")
    pairs = [
        (hour * regions + region, (hour ^ hour_bit) * regions + (region ^ region_bit))
        for hour in range(hours)
        for region in range(regions)
    ]
    return lax.ppermute(value, ("hours", "region"), pairs)


def shifted(value, steps):
    count = lax.axis_size("hours")
    return lax.ppermute(value, "hours", [(i, (i + steps) % count) for i in range(count)])


def both_regions(block):
    if lax.axis_size("region") != 2:
        return lax.all_gather(block, "region")
    return in_order(block, swap(block, 0, 1))


def in_order(block, other):
    return jnp.where(
        lax.axis_index("region") == 0, jnp.stack([block, other]), jnp.stack([other, block])
    )


def exchange(sizes, block):
    hours, regions = lax.axis_size("hours"), lax.axis_size("region")
    techs, span = sizes.techs, sizes.units // LANES
    halo = halo_at(sizes)
    prices, sums = block[: sizes.rows], block[sizes.rows :]
    if regions != 2 or hours != 16:
        gathered = lax.all_gather(prices, "region")
        totals = lax.psum(sums, "hours")
        totals = totals.at[techs:halo].set(lax.psum(totals[techs:halo], "region"))
        next_row = shifted(sums[halo : halo + span], -1)
        prev_row = shifted(sums[halo + span : halo + 2 * span], 1)
        return gathered, Bag(totals=totals, next_row=next_row, prev_row=prev_row)

    def merged(mine, yours, mine_first):
        last = halo + span
        edges = [
            jnp.where(mine_first, mine[halo:last], yours[halo:last]),
            jnp.where(mine_first, yours[last : last + span], mine[last : last + span]),
        ]
        total = mine + yours
        return jnp.concatenate([total[:halo], *edges, total[last + span :]], axis=0)

    hour = lax.axis_index("hours")
    beside_core = swap(block, 1, 0)
    partner_prices, partner = beside_core[: sizes.rows], beside_core[sizes.rows :]
    chip = merged(sums, partner, hour % 2 == 0)
    across = swap(chip, 2 + 1, 0)
    diagonal = swap(chip[techs:halo], 2 + 1, 1)
    beside = swap(jnp.concatenate([partner_prices, chip[techs:halo]], axis=0), 1, 1)
    other, squares = beside[: sizes.rows], beside[sizes.rows :]
    slab = merged(chip, across, hour // 2 % 2 == 0)
    slab = slab + jnp.pad(squares + diagonal, ((techs, slab.shape[0] - halo), (0, 0)))
    near, middle, far = [swap(slab, 4 * step + 1, 0) for step in (1, 2, 3)]
    parts = Bag(slab=slab, near=near, middle=middle, far=far, partner=partner, across=across)
    return in_order(prices, other), parts


def shape(*dims, dtype=jnp.float32):
    return jax.ShapeDtypeStruct(dims, dtype)


def restarted(sizes, kept, args):
    rows, techs, nodes, lines = sizes.rows, sizes.techs, sizes.nodes, sizes.lines
    local, cross = lines + sizes.units, sizes.regions * sizes.slots
    at, own = places(sizes), lax.axis_index("region")
    first_hour = lax.axis_index("hours") == 0
    price_start = args.price_start
    available = args.availability.transpose(1, 0, 2)
    fixed, last = kept[:rows], rows + 2 * techs
    col_weight, cost = kept[rows : rows + techs], kept[rows + techs : last]
    info = kept[last:].reshape(-1, 8, LANES).transpose(1, 0, 2).reshape(8, cross)
    local_limits = fixed[at.limits : at.energy].reshape(1, local)
    cross_limits = info[2:3]
    ends = info[:2].astype(jnp.int32)
    maps_cross_low = incidence(ends[:1], ends[1:], sizes.regions * nodes)
    stores = args.store_node[None]
    maps_local_low = incidence(
        jnp.concatenate([args.line_ends[:1], jnp.full_like(stores, -1)], axis=1),
        jnp.concatenate([args.line_ends[1:], stores], axis=1),
        nodes,
    )
    maps_local = maps_local_low.astype(jnp.float32)
    maps_cross = maps_cross_low.astype(jnp.float32)
    maps_own = lax.dynamic_slice_in_dim(maps_cross, own * nodes, nodes)
    prices_all = jnp.concatenate(list(both_regions(price_start)), axis=1)
    highest = lax.Precision.HIGHEST

    capacity = jnp.maximum(-cost / col_weight, 0.0)
    slopes = fixed[:techs][:, None, :] + price_start[None]
    dispatch = jnp.maximum(-0.5 * slopes, 0.0)
    slope = jnp.dot(price_start, maps_local, precision=highest)
    flows_local = jnp.clip(-0.5 * slope, -local_limits, local_limits)
    slope = jnp.dot(prices_all, maps_cross, precision=highest)
    flows_cross = jnp.clip(-0.5 * slope, -cross_limits, cross_limits)
    balance = (
        jnp.sum(2.0 * dispatch, axis=0)
        + jnp.dot(2.0 * flows_local, maps_local.T, precision=highest)
        + jnp.dot(2.0 * flows_cross, maps_own.T, precision=highest)
        - args.demand
    )
    step_up = balance / (techs + 8.0)
    duals = jnp.maximum(0.5 * (2.0 * dispatch - available * (2.0 * capacity)[:, None, :]), 0.0)
    store_duals = 2.0 * flows_local[:, lines:] / 3.0
    slot = lax.broadcasted_iota(jnp.int32, (1, cross), 1) // sizes.slots
    primal = (
        jnp.sum(dispatch**2)
        + jnp.sum(flows_local**2)
        + jnp.sum(jnp.where(slot == own, flows_cross**2, 0.0))
        + jnp.where(first_hour, jnp.sum(capacity**2), 0.0)
    )
    dual = jnp.sum(step_up**2) + jnp.sum(duals**2) + jnp.sum(store_duals**2)
    rows_of = [
        jnp.sum(available * duals, axis=1),
        jnp.zeros((SQUARES, nodes)).at[0, 0].set(primal).at[1, 0].set(dual),
        store_duals[:1].reshape(-1, LANES),
        store_duals[rows - 1 :].reshape(-1, LANES),
    ]
    used = halo_at(sizes) + 2 * sizes.units // LANES
    rows_of.append(jnp.zeros((sums_rows(sizes) - used, nodes)))
    rows_of += [jnp.where(first_hour, part, 0.0) for part in (col_weight, cost)]
    block = jnp.concatenate([price_start + step_up, *rows_of], axis=0)
    gathered, parts = exchange(sizes, block)
    flows = jnp.concatenate([flows_local, flows_cross], axis=1)
    spare = jnp.concatenate([jnp.zeros((8, local)), info], axis=1)
    state = Bag(
        available=jnp.concatenate([available, args.demand[None], fixed[None]], axis=0),
        maps_local=maps_local_low,
        maps_cross=maps_cross_low,
        store_duals=store_duals,
        dispatch=jnp.concatenate([dispatch, jnp.zeros((1, rows, nodes))], axis=0),
        flows=jnp.concatenate([flows, spare], axis=0),
    )
    return state, gathered, parts


def run(args):
    rows, techs, nodes = args.availability.shape
    hours, regions = lax.axis_size("hours"), lax.axis_size("region")
    slots, owned = args.cross_limit.shape[1], args.cap_cost.shape[1]
    units, lines = args.store_node.shape[0], args.line_limit.shape[0]
    sizes = Bag(
        rows=rows, techs=techs, nodes=nodes, regions=regions, slots=slots, lines=lines, units=units
    )
    cross = regions * slots

    small = Bag(
        demand=args.demand,
        gen_cost=args.gen_cost,
        cap_cost=args.cap_cost,
        owner=args.owner_map.reshape(hours, owned),
        line_ends=args.line_ends,
        line_limit=args.line_limit[None],
        store_node=args.store_node[None],
        store_power=args.store_power[None],
        store_energy=args.store_energy[None],
    )
    given = Bag(
        price=args.price_start,
        ends=args.cross_ends[:, 0],
        limit=args.cross_limit,
        pairs=args.pair_counts,
        **vars(small),
    )
    first = call(
        functools.partial(first_kernel, sizes),
        given,
        Bag(
            block=shape(rows + 8 * max(1, slots // LANES), nodes),
            **{name: shape(*value.shape, dtype=value.dtype) for name, value in vars(small).items()},
        ),
        left=range(len(vars(given))),
        scratch=[
            pltpu.VMEM((2, slots), jnp.int32),
            pltpu.VMEM((1, slots), jnp.float32),
            pltpu.VMEM((1, regions), jnp.int32),
            pltpu.SemaphoreType.DMA((len(vars(given)),)),
        ],
        limit=None,
    )
    block = first.block
    del first.block
    gathered = both_regions(block)
    state = call(
        functools.partial(start_kernel, sizes),
        Bag(
            availability=args.availability.reshape(rows * techs, nodes),
            price=block[:rows],
            **vars(first),
        ),
        Bag(
            available=shape(techs + 2, rows, nodes),
            maps_local=shape(nodes, lines + units, dtype=jnp.bfloat16),
            flows_local=shape(rows, lines + units),
            store_duals=shape(rows, units),
            dispatch=shape(techs + 1, rows, nodes),
            balance=shape(rows, nodes),
            sums=shape(sums_rows(sizes) + 2 * techs, nodes),
        ),
        flops=10**6,
        left=(0,),
        scratch=[pltpu.VMEM((rows * techs, nodes), jnp.float32), pltpu.SemaphoreType.DMA],
    )
    closed = call(
        lambda names_in, names_out, *refs: close_kernel(sizes, *refs),
        Bag(
            gathered=gathered,
            flows_local=state.flows_local,
            balance=state.balance,
            sums=state.sums,
        ),
        Bag(
            maps=shape(regions * nodes, cross, dtype=jnp.bfloat16),
            flows=shape(rows + 8, lines + units + cross),
            block=shape(rows + state.sums.shape[0], nodes),
        ),
    )
    del state.sums, state.balance, state.flows_local
    state.maps_cross, state.flows = closed.maps, closed.flows
    gathered, parts = exchange(sizes, closed.block)
    outputs, negative, kept = sweeps(sizes, owned, state, gathered, parts)

    def again():
        return sweeps(sizes, owned, *restarted(sizes, kept, args))[0]

    return lax.cond(negative > 0.0, again, lambda: outputs)


def sweeps(sizes, owned, state, gathered, parts):
    rows, techs, nodes, lines, units = (
        sizes.rows,
        sizes.techs,
        sizes.nodes,
        sizes.lines,
        sizes.units,
    )
    state = Bag(**vars(state))
    for iteration in range(1, ITERS):
        given = Bag(**vars(state), **vars(parts), gathered=gathered)
        if iteration < ITERS - 1:
            outs = Bag(
                dispatch=shape(techs + 1, rows, nodes),
                cap_duals=shape(techs + 1, rows, nodes),
                flows=shape(rows + 8, lines + units + sizes.regions * sizes.slots),
                store_duals=shape(rows, units),
                charge=shape(rows, units),
                block=shape(rows + sums_rows(sizes), nodes),
            )
        else:
            outs = Bag(
                dispatch=shape(rows * techs, nodes),
                capacity=shape(1, owned),
                prices=shape(rows, nodes),
                charge=shape(rows, units),
                negative=shape(1, LANES),
                kept=shape(rows + 2 * techs + 8 * (sizes.regions * sizes.slots // LANES), LANES),
            )
        results = call(functools.partial(sweep_kernel, sizes, iteration), given, outs)
        if iteration < ITERS - 1:
            gathered, parts = exchange(sizes, results.block)
            del results.block
            vars(state).update(vars(results))
    dispatch = results.dispatch.reshape(rows, techs, nodes)
    outputs = (dispatch, results.capacity, results.prices, results.charge)
    return outputs, results.negative[0, 0], results.kept


def body(
    availability,
    demand,
    gen_cost,
    cap_cost,
    owner_map,
    line_ends,
    line_limit,
    cross_ends,
    cross_limit,
    pair_counts,
    store_node,
    store_energy,
    store_power,
    price_start,
):
    args = Bag(**locals())
    return run(args)


def solution(mesh):
    placed = (
        P("hours", None, "region"),
        P("hours", "region"),
        P(None, "region"),
        P("region", "hours"),
        P("region", None),
        P(None, "region"),
        P("region"),
        P(None, "region", None),
        P("region", None),
        P("region", None),
        P("region"),
        P("region"),
        P("region"),
        P("hours", "region"),
    )
    return jax.shard_map(
        body,
        mesh=mesh,
        in_specs=placed,
        out_specs=(
            P("hours", None, "region"),
            P("region", "hours"),
            P("hours", "region"),
            P("hours", "region"),
        ),
        check_vma=False,
    )
```

```python
import functools
from types import SimpleNamespace as Bag

import jax
import jax.numpy as jnp
from jax import lax
from jax.experimental import pallas as pl
from jax.experimental.pallas import tpu as pltpu
from jax.sharding import PartitionSpec as P

ITERS = 4
EPSILON = 1e-06
LANES = 128
VMEM_BYTES = 24 * 1024 * 1024
SQUARES = 3


def split3(value):
    high = value.astype(jnp.bfloat16)
    rest = value - high.astype(jnp.float32)
    middle = rest.astype(jnp.bfloat16)
    low = (rest - middle.astype(jnp.float32)).astype(jnp.bfloat16)
    return jnp.concatenate([high, middle, low], axis=0)


def dot3(value, matrix, transposed):
    rows = value.shape[0]
    contract = ((1,), (1 if transposed else 0,))
    product = lax.dot_general(
        split3(value), matrix, (contract, ((), ())), preferred_element_type=jnp.float32
    )
    return product[:rows] + product[rows : 2 * rows] + product[2 * rows :]


def row_sum(value):
    return jnp.sum(value, axis=0, keepdims=True)


def fold_lanes(row):
    total = row[:, :LANES]
    for start in range(LANES, row.shape[1], LANES):
        total = total + row[:, start : start + LANES]
    return total


def owned_one_hots(owned, tech_count, node_count):
    shape_t = (tech_count, owned.shape[1])
    shape_n = (node_count, owned.shape[1])
    tech = lax.broadcasted_iota(jnp.int32, shape_t, 0) == owned // node_count
    node = lax.broadcasted_iota(jnp.int32, shape_n, 0) == owned % node_count
    return tech, node.astype(jnp.float32).astype(jnp.bfloat16)


def incidence(start, end, count):
    node = lax.broadcasted_iota(jnp.int32, (count, start.shape[1]), 0)
    maps = (node == end).astype(jnp.float32) - (node == start).astype(jnp.float32)
    return maps.astype(jnp.bfloat16)


def halo_at(sizes):
    return sizes.techs + SQUARES


def sums_rows(sizes):
    return (halo_at(sizes) + 2 * sizes.units // LANES + 7) // 8 * 8


def write_halo(sizes, sums_ref, store_new):
    halo, span, rows = halo_at(sizes), sizes.units // LANES, sizes.rows
    write_lanes(sums_ref, halo, store_new[:1])
    write_lanes(sums_ref, halo + span, store_new[rows - 1 :])
    used, end = halo + 2 * span, sums_rows(sizes)
    if used < end:
        sums_ref[used:end, :] = jnp.zeros((end - used, LANES), jnp.float32)


def write_lanes(ref, start, row):
    for i in range(row.shape[1] // LANES):
        ref[start + i : start + i + 1, :] = row[:, i * LANES : (i + 1) * LANES]


def read_lanes(ref, start, length):
    return jnp.concatenate(
        [ref[start + i : start + i + 1, :] for i in range(length // LANES)], axis=1
    )


def places(sizes):
    span = sizes.units // LANES
    limits = sizes.techs
    energy = limits + (sizes.lines + sizes.units) // LANES
    return Bag(
        limits=limits,
        energy=energy,
        owned=energy + span,
        weight=sizes.techs,
        before=sizes.techs + 1,
        negative=sizes.techs + 1 + span,
    )


def first_kernel(sizes, sources, block_ref, ends_ref, limit_ref, pairs_ref, sems):
    rows = sizes.rows
    targets = (block_ref.at[pl.ds(0, rows)], ends_ref, limit_ref, pairs_ref)
    copies = [
        pltpu.make_async_copy(source, target, sems.at[i])
        for i, (source, target) in enumerate(zip(sources, targets))
    ]
    for copy in copies:
        copy.start()
    nodes, slots, regions = sizes.nodes, sizes.slots, sizes.regions
    own = lax.axis_index("region")
    width = slots // regions
    slot = lax.broadcasted_iota(jnp.int32, (1, slots), 1)
    pair = slot // width
    for copy in copies[1:]:
        copy.wait()
    in_use = jnp.zeros((1, slots), jnp.int32)
    for target in range(regions):
        in_use = jnp.where(pair == target, pairs_ref[0:1, target : target + 1], in_use)
    bound = jnp.where(slot % width < in_use, limit_ref[...], 0.0)
    start = (ends_ref[0:1, :] + own * nodes).astype(jnp.float32)
    end = (ends_ref[1:2, :] + pair * nodes).astype(jnp.float32)
    block_ref[rows:, :] = jnp.zeros((block_ref.shape[0] - rows, LANES), jnp.float32)
    width = min(slots, LANES)
    for chunk in range(slots // width):
        at = rows + 8 * chunk
        for i, row in enumerate((start, end, bound)):
            block_ref[at + i : at + i + 1, :width] = row[:, chunk * width : (chunk + 1) * width]
    copies[0].wait()


def start_kernel(sizes, names_in, names_out, *refs):
    given = Bag(**dict(zip(names_in, refs[: len(names_in)])))
    gives = Bag(**dict(zip(names_out, refs[len(names_in) : -2])))
    availability, sem = refs[-2:]
    copy = pltpu.make_async_copy(given.availability, availability, sem)
    copy.start()
    rows, techs, nodes, lines = sizes.rows, sizes.techs, sizes.nodes, sizes.lines
    at = places(sizes)
    fixed = gives.available.at[techs + 1]
    gives.available[techs] = given.demand[...]
    fixed[:techs, :] = given.gen_cost[...]
    write_lanes(fixed, at.energy, given.store_energy[...])
    owned = given.owner[pl.ds(lax.axis_index("hours"), 1), :]
    fixed[at.owned : at.owned + 1, : owned.shape[1]] = owned.astype(jnp.float32)
    line_ends, stores = given.line_ends[...], given.store_node[...]
    start = jnp.concatenate([line_ends[0:1], jnp.full_like(stores, -1)], axis=1)
    end = jnp.concatenate([line_ends[1:2], stores], axis=1)
    maps = incidence(start, end, nodes)
    limits = jnp.concatenate([given.line_limit[...], given.store_power[...]], axis=1)
    gives.maps_local[...] = maps
    write_lanes(fixed, at.limits, limits)
    prices = given.price[...]
    flows = jnp.clip(-0.5 * dot3(prices, maps, False), -limits, limits)
    gives.flows_local[...] = flows
    store_new = (1.0 / 3.0) * (2.0 * flows[:, lines:])
    gives.store_duals[...] = store_new
    primal_row = fold_lanes(row_sum(flows * flows))
    dual_row = fold_lanes(row_sum(store_new * store_new))
    balance = dot3(2.0 * flows, maps, True) - given.demand[...]
    gen_cost = given.gen_cost[...]
    copy.wait()
    acc = jnp.zeros((rows, nodes), jnp.float32)
    weights = jnp.zeros((techs, nodes), jnp.float32)
    for hour in range(rows):
        weights = weights + availability[hour * techs : (hour + 1) * techs, :]
    for tech in range(techs):
        avail = availability[pl.ds(tech, rows, stride=techs), :]
        gives.available[tech] = avail
        dispatch = jnp.maximum(-0.5 * (gen_cost[tech : tech + 1] + prices), 0.0)
        gives.dispatch[tech] = dispatch
        dispatch_bar = 2.0 * dispatch
        balance = balance + dispatch_bar
        duals = jnp.maximum(0.5 * dispatch_bar, 0.0)
        acc = acc + dispatch * dispatch
        gives.sums[tech : tech + 1, :] = row_sum(avail * duals)
    gives.balance[...] = balance
    squares = row_sum(acc)
    cost = given.cap_cost[...]
    negative = jnp.sum((cost < 0.0).astype(jnp.float32), axis=1, keepdims=True)
    write_halo(sizes, gives.sums, store_new)
    gives.sums[techs : techs + SQUARES, :] = jnp.concatenate(
        [primal_row + squares, dual_row + squares, jnp.broadcast_to(negative, (1, LANES))], axis=0
    )
    tech_hot, node_hot = owned_one_hots(owned, techs, nodes)
    first = sums_rows(sizes)
    gives.sums[first : first + techs, :] = weights
    gives.sums[first + techs : first + 2 * techs, :] = dot3(
        jnp.where(tech_hot, cost, 0.0), node_hot, True
    )


def close_kernel(
    sizes,
    gathered,
    local_ref,
    balance_ref,
    sums_in_ref,
    maps_ref,
    flows_ref,
    block_ref,
):
    rows, techs, nodes = sizes.rows, sizes.techs, sizes.nodes
    slots, regions = sizes.slots, sizes.regions
    own = lax.axis_index("region")
    width = min(slots, LANES)
    info = jnp.concatenate(
        [
            gathered[region, rows + 8 * chunk : rows + 8 * chunk + 8, :width]
            for region in range(regions)
            for chunk in range(slots // width)
        ],
        axis=1,
    )
    maps_ref[...] = incidence(
        info[0:1].astype(jnp.int32), info[1:2].astype(jnp.int32), regions * nodes
    )
    limits = info[2:3]
    prices_all = jnp.concatenate([gathered[region, :rows, :] for region in range(regions)], axis=1)
    flows = jnp.clip(-0.5 * dot3(prices_all, maps_ref[...], False), -limits, limits)
    local = local_ref.shape[1]
    flows_ref[:rows, :local] = local_ref[...]
    flows_ref[:rows, local:] = flows
    flows_ref[rows:, local:] = info
    maps_own = maps_ref[pl.ds(pl.multiple_of(own * nodes, nodes), nodes), :]
    balance = balance_ref[...] + dot3(2.0 * flows, maps_own, True)
    step_up = (1.0 / (techs + 8.0)) * balance
    block_ref[:rows, :] = gathered[own, :rows, :] + step_up
    change = row_sum(flows * flows)
    slot = lax.broadcasted_iota(jnp.int32, change.shape, 1)
    primal = fold_lanes(jnp.where(slot // slots == own, change, 0.0))
    more = jnp.concatenate(
        [primal, row_sum(step_up * step_up), jnp.zeros((SQUARES - 2, LANES), jnp.float32)], axis=0
    )
    block_ref[rows:, :] = sums_in_ref[...]
    block_ref[rows + techs : rows + techs + SQUARES, :] = (
        sums_in_ref[techs : techs + SQUARES, :] + more
    )


def neighbour_rows(sizes, given, hour_index):
    units = sizes.units
    if hasattr(given, "totals"):
        return read_lanes(given.next_row, 0, units), read_lanes(given.prev_row, 0, units)
    first = halo_at(sizes)
    last = first + units // LANES
    core, x_place, odd = hour_index % 2, hour_index // 2 % 2, hour_index // 4 % 2
    next_row = jnp.where(
        odd == 0, read_lanes(given.near, first, units), read_lanes(given.far, first, units)
    )
    prev_row = jnp.where(
        odd == 0, read_lanes(given.far, last, units), read_lanes(given.near, last, units)
    )
    next_row = jnp.where(x_place == 0, read_lanes(given.across, first, units), next_row)
    prev_row = jnp.where(x_place == 0, prev_row, read_lanes(given.across, last, units))
    next_row = jnp.where(core == 0, read_lanes(given.partner, first, units), next_row)
    prev_row = jnp.where(core == 0, prev_row, read_lanes(given.partner, last, units))
    return next_row, prev_row


def total_of(parts):
    if hasattr(parts, "totals"):
        return parts.totals[...]
    return (parts.slab[...] + parts.near[...]) + (parts.middle[...] + parts.far[...])


def sweep_kernel(sizes, iteration, names_in, names_out, *refs):
    rows, techs, nodes = sizes.rows, sizes.techs, sizes.nodes
    slots, regions, lines, units = sizes.slots, sizes.regions, sizes.lines, sizes.units
    second = iteration == 1
    last = iteration == ITERS - 1
    given = Bag(**dict(zip(names_in, refs[: len(names_in)])))
    gives = Bag(**dict(zip(names_out, refs[len(names_in) :])))
    if last:
        staged, sem = refs[-2:]
    own = lax.axis_index("region")
    hour_index = lax.axis_index("hours")
    gathered = given.gathered

    at = places(sizes)
    fixed = given.available.at[techs + 1]
    small = given.dispatch.at[techs]
    out_sums = None if last else gives.block.at[pl.ds(rows, sums_rows(sizes))]
    sums = total_of(given)
    squares = jnp.sum(sums[techs : techs + 2], axis=1, keepdims=True)
    old_weight = jnp.ones((1, 1), jnp.float32) if second else small[at.weight : at.weight + 1, :1]
    weight = jnp.sqrt(
        old_weight * jnp.sqrt((squares[1:2] + EPSILON) / (squares[0:1] + EPSILON))
    )
    primal_step = 0.5 / weight
    if second:
        first = sums_rows(sizes)
        col_weight, cost = sums[first : first + techs], sums[first + techs : first + 2 * techs]
        negative = sums[techs + 2 : techs + 3]
        capacity = jnp.maximum(-cost / col_weight, 0.0)
        first_bar = 2.0 * capacity
    else:
        col_weight = given.cap_duals[techs, :techs, :]
        cost = given.cap_duals[techs, techs : 2 * techs, :]
        capacity = small[:techs, :]
        negative = small[at.negative : at.negative + 1, :]
    capacity_new = jnp.maximum(capacity - (cost - sums[:techs]) / (weight * col_weight), 0.0)
    capacity_bar = 2.0 * capacity_new - capacity

    prices_all = jnp.concatenate([gathered[region, :rows, :] for region in range(regions)], axis=1)
    prices = gathered[own, :rows, :]
    gen_cost = fixed[:techs, :]
    half_weight = weight / 2.0
    primal_acc = jnp.zeros((rows, nodes), jnp.float32)
    dual_acc = jnp.zeros((rows, nodes), jnp.float32)
    supply = jnp.zeros((rows, nodes), jnp.float32)
    for tech in range(techs):
        slope = gen_cost[tech : tech + 1] + prices
        dispatch = given.dispatch[tech]
        avail = given.available[tech]
        if second:
            duals = jnp.maximum(0.5 * (2.0 * dispatch - avail * first_bar[tech : tech + 1]), 0.0)
        else:
            duals = given.cap_duals[tech]
        dispatch_new = jnp.maximum(dispatch - primal_step * (slope + duals), 0.0)
        dispatch_bar = 2.0 * dispatch_new - dispatch
        supply = supply + dispatch_bar
        if last:
            staged[pl.ds(tech, rows, stride=techs), :] = dispatch_new
            continue
        gives.dispatch[tech] = dispatch_new
        cap_rows = dispatch_bar - avail * capacity_bar[tech : tech + 1]
        primal_acc = primal_acc + (dispatch_new - dispatch) ** 2
        duals_new = jnp.maximum(duals + half_weight * cap_rows, 0.0)
        dual_acc = dual_acc + (duals_new - duals) ** 2
        gives.cap_duals[tech] = duals_new
        out_sums[tech : tech + 1, :] = row_sum(avail * duals_new)
    if last:
        copy = pltpu.make_async_copy(staged, gives.dispatch, sem)
        copy.start()

    maps_local = given.maps_local[...]
    slope_local = dot3(prices, maps_local, False)
    slope_cross = dot3(prices_all, given.maps_cross[...], False)

    energy = read_lanes(fixed, at.energy, units)
    row_id = lax.broadcasted_iota(jnp.int32, (rows, units), 0)
    next_row, prev_row = neighbour_rows(sizes, given, hour_index)
    store_duals = given.store_duals[...]
    next_duals = jnp.where(row_id == rows - 1, next_row, pltpu.roll(store_duals, rows - 1, 0))
    if second:
        charge = jnp.zeros((rows, units), jnp.float32)
        charge_before = jnp.zeros((1, units), jnp.float32)
    else:
        charge = given.charge[...]
        charge_before = read_lanes(small, at.before, units)
    charge_new = jnp.clip(charge - primal_step * (store_duals - next_duals), 0.0, energy)
    gives.charge[...] = charge_new

    primal_row = jnp.zeros((1, LANES), jnp.float32)
    bars = []
    local, total_flows = lines + units, lines + units + regions * slots
    local_limits = read_lanes(fixed, at.limits, local)
    cross_limits = given.flows[rows + 2 : rows + 3, local:]
    for bound, slope, low, high in (
        (local_limits[:, :lines], slope_local[:, :lines], 0, lines),
        (local_limits[:, lines:], slope_local[:, lines:] + store_duals, lines, local),
        (cross_limits, slope_cross, local, total_flows),
    ):
        old = given.flows[:rows, low:high]
        new = jnp.clip(old - primal_step * slope, -bound, bound)
        bars.append(2.0 * new - old)
        if not last:
            gives.flows[:rows, low:high] = new
            change = row_sum((new - old) ** 2)
            if low == local:
                slot = lax.broadcasted_iota(jnp.int32, change.shape, 1)
                change = jnp.where(slot // slots == own, change, 0.0)
            primal_row = primal_row + fold_lanes(change)
    maps_own = given.maps_cross[pl.ds(pl.multiple_of(own * nodes, nodes), nodes), :]
    balance = dot3(jnp.concatenate(bars[:2], axis=1), maps_local, True) - given.available[techs]
    balance = balance + supply + dot3(bars[2], maps_own, True)

    step_up = weight / (techs + 8.0) * balance
    if last:
        gives.prices[...] = prices + step_up
        owned = fixed[at.owned : at.owned + 1, : gives.capacity.shape[1]].astype(jnp.int32)
        tech_hot, node_hot = owned_one_hots(owned, techs, nodes)
        chosen = dot3(capacity_new, node_hot, False)
        gives.capacity[...] = row_sum(jnp.where(tech_hot, chosen, 0.0))
        gives.negative[...] = negative
        gives.kept[:rows, :] = fixed[...]
        gives.kept[rows : rows + techs, :] = col_weight
        gives.kept[rows + techs : rows + 2 * techs, :] = cost
        for chunk in range(regions * slots // LANES):
            low = local + chunk * LANES
            first = rows + 2 * techs + 8 * chunk
            gives.kept[first : first + 8, :] = given.flows[rows:, low : low + LANES]
        copy.wait()
        return
    gives.block[:rows, :] = prices + step_up
    gives.flows[rows:, local:] = given.flows[rows:, local:]
    gives.cap_duals[techs, :techs, :] = col_weight
    gives.cap_duals[techs, techs : 2 * techs, :] = cost
    small_new = gives.dispatch.at[techs]
    small_new[:techs, :] = capacity_new
    small_new[at.weight : at.weight + 1, :] = jnp.broadcast_to(weight, (1, LANES))
    small_new[at.negative : at.negative + 1, :] = negative
    charge_bar = 2.0 * charge_new - charge
    before_new = jnp.clip(charge_before - primal_step * (prev_row - store_duals[0:1]), 0.0, energy)
    write_lanes(small_new, at.before, before_new)
    before_bar = 2.0 * before_new - charge_before
    shifted_bar = jnp.where(row_id == 0, before_bar, pltpu.roll(charge_bar, 1, 0))
    store_step = weight / 3.0 * (charge_bar - shifted_bar + bars[1])
    store_new = store_duals + store_step
    gives.store_duals[...] = store_new
    primal_row = primal_row + row_sum(primal_acc) + fold_lanes(row_sum((charge_new - charge) ** 2))
    primal_row = primal_row + jnp.where(
        hour_index == 0, row_sum((capacity_new - capacity) ** 2), 0.0
    )
    dual_row = row_sum(dual_acc + step_up * step_up) + fold_lanes(row_sum(store_step * store_step))
    squares = jnp.concatenate(
        [primal_row, dual_row, jnp.zeros((SQUARES - 2, LANES), jnp.float32)], axis=0
    )
    out_sums[techs : techs + SQUARES, :] = squares
    write_halo(sizes, out_sums, store_new)


def call(kernel, given, outs, flops=0, left=(), scratch=(), limit=VMEM_BYTES, copied=0):
    names_in, names_out = tuple(vars(given)), tuple(vars(outs))
    values = pl.pallas_call(
        functools.partial(kernel, names_in, names_out),
        out_shape=tuple(vars(outs).values()),
        in_specs=[
            pl.BlockSpec(memory_space=pl.ANY if i in left else pltpu.VMEM)
            for i in range(len(names_in))
        ],
        out_specs=[
            pl.BlockSpec(memory_space=pl.ANY if i < copied else pltpu.VMEM)
            for i in range(len(names_out))
        ],
        scratch_shapes=scratch,
        cost_estimate=pl.CostEstimate(flops=flops, bytes_accessed=4 * flops, transcendentals=0),
        compiler_params=pltpu.CompilerParams(vmem_limit_bytes=limit),
    )(*vars(given).values())
    return Bag(**dict(zip(names_out, values)))


def swap(value, hour_bit, region_bit):
    hours, regions = lax.axis_size("hours"), lax.axis_size("region")
    pairs = [
        (hour * regions + region, (hour ^ hour_bit) * regions + (region ^ region_bit))
        for hour in range(hours)
        for region in range(regions)
    ]
    return lax.ppermute(value, ("hours", "region"), pairs)


def shifted(value, steps):
    count = lax.axis_size("hours")
    return lax.ppermute(value, "hours", [(i, (i + steps) % count) for i in range(count)])


def both_regions(block):
    if lax.axis_size("region") != 2:
        return lax.all_gather(block, "region")
    return in_order(block, swap(block, 0, 1))


def in_order(block, other):
    return jnp.where(
        lax.axis_index("region") == 0, jnp.stack([block, other]), jnp.stack([other, block])
    )


def exchange(sizes, block):
    hours, regions = lax.axis_size("hours"), lax.axis_size("region")
    techs, span = sizes.techs, sizes.units // LANES
    halo = halo_at(sizes)
    prices, sums = block[: sizes.rows], block[sizes.rows :]
    if regions != 2 or hours != 16:
        gathered = lax.all_gather(prices, "region")
        totals = lax.psum(sums, "hours")
        totals = totals.at[techs:halo].set(lax.psum(totals[techs:halo], "region"))
        next_row = shifted(sums[halo : halo + span], -1)
        prev_row = shifted(sums[halo + span : halo + 2 * span], 1)
        return gathered, Bag(totals=totals, next_row=next_row, prev_row=prev_row)

    def merged(mine, yours, mine_first):
        last = halo + span
        edges = [
            jnp.where(mine_first, mine[halo:last], yours[halo:last]),
            jnp.where(mine_first, yours[last : last + span], mine[last : last + span]),
        ]
        total = mine + yours
        return jnp.concatenate([total[:halo], *edges, total[last + span :]], axis=0)

    hour = lax.axis_index("hours")
    beside_core = swap(block, 1, 0)
    partner_prices, partner = beside_core[: sizes.rows], beside_core[sizes.rows :]
    chip = merged(sums, partner, hour % 2 == 0)
    across = swap(chip, 2 + 1, 0)
    diagonal = swap(chip[techs:halo], 2 + 1, 1)
    beside = swap(jnp.concatenate([partner_prices, chip[techs:halo]], axis=0), 1, 1)
    other, squares = beside[: sizes.rows], beside[sizes.rows :]
    slab = merged(chip, across, hour // 2 % 2 == 0)
    slab = slab + jnp.pad(squares + diagonal, ((techs, slab.shape[0] - halo), (0, 0)))
    near, middle, far = [swap(slab, 4 * step + 1, 0) for step in (1, 2, 3)]
    parts = Bag(slab=slab, near=near, middle=middle, far=far, partner=partner, across=across)
    return in_order(prices, other), parts


def shape(*dims, dtype=jnp.float32):
    return jax.ShapeDtypeStruct(dims, dtype)


def restarted(sizes, kept, args):
    rows, techs, nodes, lines = sizes.rows, sizes.techs, sizes.nodes, sizes.lines
    local, cross = lines + sizes.units, sizes.regions * sizes.slots
    at, own = places(sizes), lax.axis_index("region")
    first_hour = lax.axis_index("hours") == 0
    price_start = args.price_start
    available = args.availability.transpose(1, 0, 2)
    fixed, last = kept[:rows], rows + 2 * techs
    col_weight, cost = kept[rows : rows + techs], kept[rows + techs : last]
    info = kept[last:].reshape(-1, 8, LANES).transpose(1, 0, 2).reshape(8, cross)
    local_limits = fixed[at.limits : at.energy].reshape(1, local)
    cross_limits = info[2:3]
    ends = info[:2].astype(jnp.int32)
    maps_cross_low = incidence(ends[:1], ends[1:], sizes.regions * nodes)
    stores = args.store_node[None]
    maps_local_low = incidence(
        jnp.concatenate([args.line_ends[:1], jnp.full_like(stores, -1)], axis=1),
        jnp.concatenate([args.line_ends[1:], stores], axis=1),
        nodes,
    )
    maps_local = maps_local_low.astype(jnp.float32)
    maps_cross = maps_cross_low.astype(jnp.float32)
    maps_own = lax.dynamic_slice_in_dim(maps_cross, own * nodes, nodes)
    prices_all = jnp.concatenate(list(both_regions(price_start)), axis=1)
    highest = lax.Precision.HIGHEST

    capacity = jnp.maximum(-cost / col_weight, 0.0)
    slopes = fixed[:techs][:, None, :] + price_start[None]
    dispatch = jnp.maximum(-0.5 * slopes, 0.0)
    slope = jnp.dot(price_start, maps_local, precision=highest)
    flows_local = jnp.clip(-0.5 * slope, -local_limits, local_limits)
    slope = jnp.dot(prices_all, maps_cross, precision=highest)
    flows_cross = jnp.clip(-0.5 * slope, -cross_limits, cross_limits)
    balance = (
        jnp.sum(2.0 * dispatch, axis=0)
        + jnp.dot(2.0 * flows_local, maps_local.T, precision=highest)
        + jnp.dot(2.0 * flows_cross, maps_own.T, precision=highest)
        - args.demand
    )
    step_up = balance / (techs + 8.0)
    duals = jnp.maximum(0.5 * (2.0 * dispatch - available * (2.0 * capacity)[:, None, :]), 0.0)
    store_duals = 2.0 * flows_local[:, lines:] / 3.0
    slot = lax.broadcasted_iota(jnp.int32, (1, cross), 1) // sizes.slots
    primal = (
        jnp.sum(dispatch**2)
        + jnp.sum(flows_local**2)
        + jnp.sum(jnp.where(slot == own, flows_cross**2, 0.0))
        + jnp.where(first_hour, jnp.sum(capacity**2), 0.0)
    )
    dual = jnp.sum(step_up**2) + jnp.sum(duals**2) + jnp.sum(store_duals**2)
    rows_of = [
        jnp.sum(available * duals, axis=1),
        jnp.zeros((SQUARES, nodes)).at[0, 0].set(primal).at[1, 0].set(dual),
        store_duals[:1].reshape(-1, LANES),
        store_duals[rows - 1 :].reshape(-1, LANES),
    ]
    used = halo_at(sizes) + 2 * sizes.units // LANES
    rows_of.append(jnp.zeros((sums_rows(sizes) - used, nodes)))
    rows_of += [jnp.where(first_hour, part, 0.0) for part in (col_weight, cost)]
    block = jnp.concatenate([price_start + step_up, *rows_of], axis=0)
    gathered, parts = exchange(sizes, block)
    flows = jnp.concatenate([flows_local, flows_cross], axis=1)
    spare = jnp.concatenate([jnp.zeros((8, local)), info], axis=1)
    state = Bag(
        available=jnp.concatenate([available, args.demand[None], fixed[None]], axis=0),
        maps_local=maps_local_low,
        maps_cross=maps_cross_low,
        store_duals=store_duals,
        dispatch=jnp.concatenate([dispatch, jnp.zeros((1, rows, nodes))], axis=0),
        flows=jnp.concatenate([flows, spare], axis=0),
    )
    return state, gathered, parts


def run(args):
    rows, techs, nodes = args.availability.shape
    hours, regions = lax.axis_size("hours"), lax.axis_size("region")
    slots, owned = args.cross_limit.shape[1], args.cap_cost.shape[1]
    units, lines = args.store_node.shape[0], args.line_limit.shape[0]
    sizes = Bag(
        rows=rows, techs=techs, nodes=nodes, regions=regions, slots=slots, lines=lines, units=units
    )
    cross = regions * slots

    gathered = both_regions(
        call(
            lambda names_in, names_out, *refs: first_kernel(sizes, refs[:4], *refs[4:]),
            Bag(
                price=args.price_start,
                ends=args.cross_ends[:, 0],
                limit=args.cross_limit,
                pairs=args.pair_counts,
            ),
            Bag(block=shape(rows + 8 * max(1, slots // LANES), nodes)),
            left=(0, 1, 2, 3),
            scratch=[
                pltpu.VMEM((2, slots), jnp.int32),
                pltpu.VMEM((1, slots), jnp.float32),
                pltpu.VMEM((1, regions), jnp.int32),
                pltpu.SemaphoreType.DMA((4,)),
            ],
            limit=None,
        ).block
    )
    state = call(
        functools.partial(start_kernel, sizes),
        Bag(
            availability=args.availability.reshape(rows * techs, nodes),
            price=args.price_start,
            demand=args.demand,
            gen_cost=args.gen_cost,
            cap_cost=args.cap_cost,
            owner=args.owner_map.reshape(hours, owned),
            line_ends=args.line_ends,
            line_limit=args.line_limit[None],
            store_node=args.store_node[None],
            store_power=args.store_power[None],
            store_energy=args.store_energy[None],
        ),
        Bag(
            available=shape(techs + 2, rows, nodes),
            maps_local=shape(nodes, lines + units, dtype=jnp.bfloat16),
            flows_local=shape(rows, lines + units),
            store_duals=shape(rows, units),
            dispatch=shape(techs + 1, rows, nodes),
            balance=shape(rows, nodes),
            sums=shape(sums_rows(sizes) + 2 * techs, nodes),
        ),
        flops=10**6,
        left=(0,),
        scratch=[pltpu.VMEM((rows * techs, nodes), jnp.float32), pltpu.SemaphoreType.DMA],
    )
    closed = call(
        lambda names_in, names_out, *refs: close_kernel(sizes, *refs),
        Bag(
            gathered=gathered,
            flows_local=state.flows_local,
            balance=state.balance,
            sums=state.sums,
        ),
        Bag(
            maps=shape(regions * nodes, cross, dtype=jnp.bfloat16),
            flows=shape(rows + 8, lines + units + cross),
            block=shape(rows + state.sums.shape[0], nodes),
        ),
    )
    del state.sums, state.balance, state.flows_local
    state.maps_cross, state.flows = closed.maps, closed.flows
    gathered, parts = exchange(sizes, closed.block)
    outputs, negative, kept = sweeps(sizes, owned, state, gathered, parts)

    def again():
        return sweeps(sizes, owned, *restarted(sizes, kept, args))[0]

    return lax.cond(negative > 0.0, again, lambda: outputs)


def sweeps(sizes, owned, state, gathered, parts):
    rows, techs, nodes, lines, units = (
        sizes.rows,
        sizes.techs,
        sizes.nodes,
        sizes.lines,
        sizes.units,
    )
    state = Bag(**vars(state))
    for iteration in range(1, ITERS):
        given = Bag(**vars(state), **vars(parts), gathered=gathered)
        if iteration < ITERS - 1:
            outs = Bag(
                dispatch=shape(techs + 1, rows, nodes),
                cap_duals=shape(techs + 1, rows, nodes),
                flows=shape(rows + 8, lines + units + sizes.regions * sizes.slots),
                store_duals=shape(rows, units),
                charge=shape(rows, units),
                block=shape(rows + sums_rows(sizes), nodes),
            )
        else:
            outs = Bag(
                dispatch=shape(rows * techs, nodes),
                capacity=shape(1, owned),
                prices=shape(rows, nodes),
                charge=shape(rows, units),
                negative=shape(1, LANES),
                kept=shape(rows + 2 * techs + 8 * (sizes.regions * sizes.slots // LANES), LANES),
            )
        final = iteration == ITERS - 1
        results = call(
            functools.partial(sweep_kernel, sizes, iteration),
            given,
            outs,
            copied=int(final),
            scratch=[pltpu.VMEM(outs.dispatch.shape, jnp.float32), pltpu.SemaphoreType.DMA]
            if final
            else [],
        )
        if iteration < ITERS - 1:
            gathered, parts = exchange(sizes, results.block)
            del results.block
            vars(state).update(vars(results))
    dispatch = results.dispatch.reshape(rows, techs, nodes)
    outputs = (dispatch, results.capacity, results.prices, results.charge)
    return outputs, results.negative[0, 0], results.kept


def body(
    availability,
    demand,
    gen_cost,
    cap_cost,
    owner_map,
    line_ends,
    line_limit,
    cross_ends,
    cross_limit,
    pair_counts,
    store_node,
    store_energy,
    store_power,
    price_start,
):
    args = Bag(**locals())
    return run(args)


def solution(mesh):
    placed = (
        P("hours", None, "region"),
        P("hours", "region"),
        P(None, "region"),
        P("region", "hours"),
        P("region", None),
        P(None, "region"),
        P("region"),
        P(None, "region", None),
        P("region", None),
        P("region", None),
        P("region"),
        P("region"),
        P("region"),
        P("hours", "region"),
    )
    return jax.shard_map(
        body,
        mesh=mesh,
        in_specs=placed,
        out_specs=(
            P("hours", None, "region"),
            P("region", "hours"),
            P("hours", "region"),
            P("hours", "region"),
        ),
        check_vma=False,
    )
```

```python
import functools
from types import SimpleNamespace as Bag

import jax
import jax.numpy as jnp
from jax import lax
from jax.experimental import pallas as pl
from jax.experimental.pallas import tpu as pltpu
from jax.sharding import PartitionSpec as P

ITERS = 4
EPSILON = 1e-06
LANES = 128
VMEM_BYTES = 24 * 1024 * 1024
SQUARES = 3


def split3(value):
    high = value.astype(jnp.bfloat16)
    rest = value - high.astype(jnp.float32)
    middle = rest.astype(jnp.bfloat16)
    low = (rest - middle.astype(jnp.float32)).astype(jnp.bfloat16)
    return jnp.concatenate([high, middle, low], axis=0)


def dot3(value, matrix, transposed):
    rows = value.shape[0]
    contract = ((1,), (1 if transposed else 0,))
    product = lax.dot_general(
        split3(value), matrix, (contract, ((), ())), preferred_element_type=jnp.float32
    )
    return product[:rows] + product[rows : 2 * rows] + product[2 * rows :]


def row_sum(value):
    return jnp.sum(value, axis=0, keepdims=True)


def fold_lanes(row):
    total = row[:, :LANES]
    for start in range(LANES, row.shape[1], LANES):
        total = total + row[:, start : start + LANES]
    return total


def owned_one_hots(owned, tech_count, node_count):
    shape_t = (tech_count, owned.shape[1])
    shape_n = (node_count, owned.shape[1])
    tech = lax.broadcasted_iota(jnp.int32, shape_t, 0) == owned // node_count
    node = lax.broadcasted_iota(jnp.int32, shape_n, 0) == owned % node_count
    return tech, node.astype(jnp.float32).astype(jnp.bfloat16)


def incidence(start, end, count):
    node = lax.broadcasted_iota(jnp.int32, (count, start.shape[1]), 0)
    maps = (node == end).astype(jnp.float32) - (node == start).astype(jnp.float32)
    return maps.astype(jnp.bfloat16)


def halo_at(sizes):
    return sizes.techs + SQUARES


def sums_rows(sizes):
    return (halo_at(sizes) + 2 * sizes.units // LANES + 7) // 8 * 8


def write_halo(sizes, sums_ref, store_new):
    halo, span, rows = halo_at(sizes), sizes.units // LANES, sizes.rows
    write_lanes(sums_ref, halo, store_new[:1])
    write_lanes(sums_ref, halo + span, store_new[rows - 1 :])
    used, end = halo + 2 * span, sums_rows(sizes)
    if used < end:
        sums_ref[used:end, :] = jnp.zeros((end - used, LANES), jnp.float32)


def write_lanes(ref, start, row):
    for i in range(row.shape[1] // LANES):
        ref[start + i : start + i + 1, :] = row[:, i * LANES : (i + 1) * LANES]


def read_lanes(ref, start, length):
    return jnp.concatenate(
        [ref[start + i : start + i + 1, :] for i in range(length // LANES)], axis=1
    )


def places(sizes):
    span = sizes.units // LANES
    limits = sizes.techs
    energy = limits + (sizes.lines + sizes.units) // LANES
    return Bag(
        limits=limits,
        energy=energy,
        owned=energy + span,
        weight=sizes.techs,
        before=sizes.techs + 1,
        negative=sizes.techs + 1 + span,
    )


def first_kernel(sizes, sources, block_ref, ends_ref, limit_ref, pairs_ref, sems):
    rows = sizes.rows
    targets = (block_ref.at[pl.ds(0, rows)], ends_ref, limit_ref, pairs_ref)
    copies = [
        pltpu.make_async_copy(source, target, sems.at[i])
        for i, (source, target) in enumerate(zip(sources, targets))
    ]
    for copy in copies:
        copy.start()
    nodes, slots, regions = sizes.nodes, sizes.slots, sizes.regions
    own = lax.axis_index("region")
    width = slots // regions
    slot = lax.broadcasted_iota(jnp.int32, (1, slots), 1)
    pair = slot // width
    for copy in copies[1:]:
        copy.wait()
    in_use = jnp.zeros((1, slots), jnp.int32)
    for target in range(regions):
        in_use = jnp.where(pair == target, pairs_ref[0:1, target : target + 1], in_use)
    bound = jnp.where(slot % width < in_use, limit_ref[...], 0.0)
    start = (ends_ref[0:1, :] + own * nodes).astype(jnp.float32)
    end = (ends_ref[1:2, :] + pair * nodes).astype(jnp.float32)
    block_ref[rows:, :] = jnp.zeros((block_ref.shape[0] - rows, LANES), jnp.float32)
    width = min(slots, LANES)
    for chunk in range(slots // width):
        at = rows + 8 * chunk
        for i, row in enumerate((start, end, bound)):
            block_ref[at + i : at + i + 1, :width] = row[:, chunk * width : (chunk + 1) * width]
    copies[0].wait()


def start_kernel(sizes, names_in, names_out, *refs):
    given = Bag(**dict(zip(names_in, refs[: len(names_in)])))
    gives = Bag(**dict(zip(names_out, refs[len(names_in) : -2])))
    availability, sem = refs[-2:]
    copy = pltpu.make_async_copy(given.availability, availability, sem)
    copy.start()
    rows, techs, nodes, lines = sizes.rows, sizes.techs, sizes.nodes, sizes.lines
    at = places(sizes)
    fixed = gives.available.at[techs + 1]
    gives.available[techs] = given.demand[...]
    fixed[:techs, :] = given.gen_cost[...]
    write_lanes(fixed, at.energy, given.store_energy[...])
    owned = given.owner[pl.ds(lax.axis_index("hours"), 1), :]
    fixed[at.owned : at.owned + 1, : owned.shape[1]] = owned.astype(jnp.float32)
    line_ends, stores = given.line_ends[...], given.store_node[...]
    start = jnp.concatenate([line_ends[0:1], jnp.full_like(stores, -1)], axis=1)
    end = jnp.concatenate([line_ends[1:2], stores], axis=1)
    maps = incidence(start, end, nodes)
    limits = jnp.concatenate([given.line_limit[...], given.store_power[...]], axis=1)
    gives.maps_local[...] = maps
    write_lanes(fixed, at.limits, limits)
    prices = given.price[...]
    flows = jnp.clip(-0.5 * dot3(prices, maps, False), -limits, limits)
    gives.flows_local[...] = flows
    store_new = (1.0 / 3.0) * (2.0 * flows[:, lines:])
    gives.store_duals[...] = store_new
    primal_row = fold_lanes(row_sum(flows * flows))
    dual_row = fold_lanes(row_sum(store_new * store_new))
    balance = dot3(2.0 * flows, maps, True) - given.demand[...]
    gen_cost = given.gen_cost[...]
    copy.wait()
    acc = jnp.zeros((rows, nodes), jnp.float32)
    weights = jnp.zeros((techs, nodes), jnp.float32)
    for hour in range(rows):
        weights = weights + availability[hour * techs : (hour + 1) * techs, :]
    for tech in range(techs):
        avail = availability[pl.ds(tech, rows, stride=techs), :]
        gives.available[tech] = avail
        dispatch = jnp.maximum(-0.5 * (gen_cost[tech : tech + 1] + prices), 0.0)
        gives.dispatch[tech] = dispatch
        dispatch_bar = 2.0 * dispatch
        balance = balance + dispatch_bar
        duals = jnp.maximum(0.5 * dispatch_bar, 0.0)
        acc = acc + dispatch * dispatch
        gives.sums[tech : tech + 1, :] = row_sum(avail * duals)
    gives.balance[...] = balance
    squares = row_sum(acc)
    cost = given.cap_cost[...]
    negative = jnp.sum((cost < 0.0).astype(jnp.float32), axis=1, keepdims=True)
    write_halo(sizes, gives.sums, store_new)
    gives.sums[techs : techs + SQUARES, :] = jnp.concatenate(
        [primal_row + squares, dual_row + squares, jnp.broadcast_to(negative, (1, LANES))], axis=0
    )
    tech_hot, node_hot = owned_one_hots(owned, techs, nodes)
    first = sums_rows(sizes)
    gives.sums[first : first + techs, :] = weights
    gives.sums[first + techs : first + 2 * techs, :] = dot3(
        jnp.where(tech_hot, cost, 0.0), node_hot, True
    )


def close_kernel(
    sizes,
    gathered,
    local_ref,
    balance_ref,
    sums_in_ref,
    maps_ref,
    flows_ref,
    block_ref,
):
    rows, techs, nodes = sizes.rows, sizes.techs, sizes.nodes
    slots, regions = sizes.slots, sizes.regions
    own = lax.axis_index("region")
    width = min(slots, LANES)
    info = jnp.concatenate(
        [
            gathered[region, rows + 8 * chunk : rows + 8 * chunk + 8, :width]
            for region in range(regions)
            for chunk in range(slots // width)
        ],
        axis=1,
    )
    maps_ref[...] = incidence(
        info[0:1].astype(jnp.int32), info[1:2].astype(jnp.int32), regions * nodes
    )
    limits = info[2:3]
    prices_all = jnp.concatenate([gathered[region, :rows, :] for region in range(regions)], axis=1)
    flows = jnp.clip(-0.5 * dot3(prices_all, maps_ref[...], False), -limits, limits)
    local = local_ref.shape[1]
    flows_ref[:rows, :local] = local_ref[...]
    flows_ref[:rows, local:] = flows
    flows_ref[rows:, local:] = info
    maps_own = maps_ref[pl.ds(pl.multiple_of(own * nodes, nodes), nodes), :]
    balance = balance_ref[...] + dot3(2.0 * flows, maps_own, True)
    step_up = (1.0 / (techs + 8.0)) * balance
    block_ref[:rows, :] = gathered[own, :rows, :] + step_up
    change = row_sum(flows * flows)
    slot = lax.broadcasted_iota(jnp.int32, change.shape, 1)
    primal = fold_lanes(jnp.where(slot // slots == own, change, 0.0))
    more = jnp.concatenate(
        [primal, row_sum(step_up * step_up), jnp.zeros((SQUARES - 2, LANES), jnp.float32)], axis=0
    )
    block_ref[rows:, :] = sums_in_ref[...]
    block_ref[rows + techs : rows + techs + SQUARES, :] = (
        sums_in_ref[techs : techs + SQUARES, :] + more
    )


def neighbour_rows(sizes, given, hour_index):
    units = sizes.units
    if hasattr(given, "totals"):
        return read_lanes(given.next_row, 0, units), read_lanes(given.prev_row, 0, units)
    first = halo_at(sizes)
    last = first + units // LANES
    core, x_place, odd = hour_index % 2, hour_index // 2 % 2, hour_index // 4 % 2
    next_row = jnp.where(
        odd == 0, read_lanes(given.near, first, units), read_lanes(given.far, first, units)
    )
    prev_row = jnp.where(
        odd == 0, read_lanes(given.far, last, units), read_lanes(given.near, last, units)
    )
    next_row = jnp.where(x_place == 0, read_lanes(given.across, first, units), next_row)
    prev_row = jnp.where(x_place == 0, prev_row, read_lanes(given.across, last, units))
    next_row = jnp.where(core == 0, read_lanes(given.partner, first, units), next_row)
    prev_row = jnp.where(core == 0, prev_row, read_lanes(given.partner, last, units))
    return next_row, prev_row


def total_of(parts):
    if hasattr(parts, "totals"):
        return parts.totals[...]
    return (parts.slab[...] + parts.near[...]) + (parts.middle[...] + parts.far[...])


def sweep_kernel(sizes, iteration, names_in, names_out, *refs):
    rows, techs, nodes = sizes.rows, sizes.techs, sizes.nodes
    slots, regions, lines, units = sizes.slots, sizes.regions, sizes.lines, sizes.units
    second = iteration == 1
    last = iteration == ITERS - 1
    given = Bag(**dict(zip(names_in, refs[: len(names_in)])))
    gives = Bag(**dict(zip(names_out, refs[len(names_in) :])))
    if last:
        staged, staged_charge, sems = refs[-3:]
    own = lax.axis_index("region")
    hour_index = lax.axis_index("hours")
    gathered = given.gathered

    at = places(sizes)
    fixed = given.available.at[techs + 1]
    small = given.dispatch.at[techs]
    out_sums = None if last else gives.block.at[pl.ds(rows, sums_rows(sizes))]
    sums = total_of(given)
    squares = jnp.sum(sums[techs : techs + 2], axis=1, keepdims=True)
    old_weight = jnp.ones((1, 1), jnp.float32) if second else small[at.weight : at.weight + 1, :1]
    weight = jnp.sqrt(
        old_weight * jnp.sqrt((squares[1:2] + EPSILON) / (squares[0:1] + EPSILON))
    )
    primal_step = 0.5 / weight
    if second:
        first = sums_rows(sizes)
        col_weight, cost = sums[first : first + techs], sums[first + techs : first + 2 * techs]
        negative = sums[techs + 2 : techs + 3]
        capacity = jnp.maximum(-cost / col_weight, 0.0)
        first_bar = 2.0 * capacity
    else:
        col_weight = given.cap_duals[techs, :techs, :]
        cost = given.cap_duals[techs, techs : 2 * techs, :]
        capacity = small[:techs, :]
        negative = small[at.negative : at.negative + 1, :]
    capacity_new = jnp.maximum(capacity - (cost - sums[:techs]) / (weight * col_weight), 0.0)
    capacity_bar = 2.0 * capacity_new - capacity

    prices_all = jnp.concatenate([gathered[region, :rows, :] for region in range(regions)], axis=1)
    prices = gathered[own, :rows, :]
    gen_cost = fixed[:techs, :]
    half_weight = weight / 2.0
    primal_acc = jnp.zeros((rows, nodes), jnp.float32)
    dual_acc = jnp.zeros((rows, nodes), jnp.float32)
    supply = jnp.zeros((rows, nodes), jnp.float32)
    for tech in range(techs):
        slope = gen_cost[tech : tech + 1] + prices
        dispatch = given.dispatch[tech]
        avail = given.available[tech]
        if second:
            duals = jnp.maximum(0.5 * (2.0 * dispatch - avail * first_bar[tech : tech + 1]), 0.0)
        else:
            duals = given.cap_duals[tech]
        dispatch_new = jnp.maximum(dispatch - primal_step * (slope + duals), 0.0)
        dispatch_bar = 2.0 * dispatch_new - dispatch
        supply = supply + dispatch_bar
        if last:
            staged[pl.ds(tech, rows, stride=techs), :] = dispatch_new
            continue
        gives.dispatch[tech] = dispatch_new
        cap_rows = dispatch_bar - avail * capacity_bar[tech : tech + 1]
        primal_acc = primal_acc + (dispatch_new - dispatch) ** 2
        duals_new = jnp.maximum(duals + half_weight * cap_rows, 0.0)
        dual_acc = dual_acc + (duals_new - duals) ** 2
        gives.cap_duals[tech] = duals_new
        out_sums[tech : tech + 1, :] = row_sum(avail * duals_new)
    if last:
        copies = [
            pltpu.make_async_copy(staged, gives.dispatch, sems.at[0]),
            pltpu.make_async_copy(staged_charge, gives.charge, sems.at[1]),
        ]
        copies[0].start()

    maps_local = given.maps_local[...]
    slope_local = dot3(prices, maps_local, False)
    slope_cross = dot3(prices_all, given.maps_cross[...], False)

    energy = read_lanes(fixed, at.energy, units)
    row_id = lax.broadcasted_iota(jnp.int32, (rows, units), 0)
    next_row, prev_row = neighbour_rows(sizes, given, hour_index)
    store_duals = given.store_duals[...]
    next_duals = jnp.where(row_id == rows - 1, next_row, pltpu.roll(store_duals, rows - 1, 0))
    if second:
        charge = jnp.zeros((rows, units), jnp.float32)
        charge_before = jnp.zeros((1, units), jnp.float32)
    else:
        charge = given.charge[...]
        charge_before = read_lanes(small, at.before, units)
    charge_new = jnp.clip(charge - primal_step * (store_duals - next_duals), 0.0, energy)
    if last:
        staged_charge[...] = charge_new
        copies[1].start()
    else:
        gives.charge[...] = charge_new

    primal_row = jnp.zeros((1, LANES), jnp.float32)
    bars = []
    local, total_flows = lines + units, lines + units + regions * slots
    local_limits = read_lanes(fixed, at.limits, local)
    cross_limits = given.flows[rows + 2 : rows + 3, local:]
    for bound, slope, low, high in (
        (local_limits[:, :lines], slope_local[:, :lines], 0, lines),
        (local_limits[:, lines:], slope_local[:, lines:] + store_duals, lines, local),
        (cross_limits, slope_cross, local, total_flows),
    ):
        old = given.flows[:rows, low:high]
        new = jnp.clip(old - primal_step * slope, -bound, bound)
        bars.append(2.0 * new - old)
        if not last:
            gives.flows[:rows, low:high] = new
            change = row_sum((new - old) ** 2)
            if low == local:
                slot = lax.broadcasted_iota(jnp.int32, change.shape, 1)
                change = jnp.where(slot // slots == own, change, 0.0)
            primal_row = primal_row + fold_lanes(change)
    maps_own = given.maps_cross[pl.ds(pl.multiple_of(own * nodes, nodes), nodes), :]
    balance = dot3(jnp.concatenate(bars[:2], axis=1), maps_local, True) - given.available[techs]
    balance = balance + supply + dot3(bars[2], maps_own, True)

    step_up = weight / (techs + 8.0) * balance
    if last:
        gives.prices[...] = prices + step_up
        owned = fixed[at.owned : at.owned + 1, : gives.capacity.shape[1]].astype(jnp.int32)
        tech_hot, node_hot = owned_one_hots(owned, techs, nodes)
        chosen = dot3(capacity_new, node_hot, False)
        gives.capacity[...] = row_sum(jnp.where(tech_hot, chosen, 0.0))
        gives.negative[...] = negative
        gives.kept[:rows, :] = fixed[...]
        gives.kept[rows : rows + techs, :] = col_weight
        gives.kept[rows + techs : rows + 2 * techs, :] = cost
        for chunk in range(regions * slots // LANES):
            low = local + chunk * LANES
            first = rows + 2 * techs + 8 * chunk
            gives.kept[first : first + 8, :] = given.flows[rows:, low : low + LANES]
        for copy in copies:
            copy.wait()
        return
    gives.block[:rows, :] = prices + step_up
    gives.flows[rows:, local:] = given.flows[rows:, local:]
    gives.cap_duals[techs, :techs, :] = col_weight
    gives.cap_duals[techs, techs : 2 * techs, :] = cost
    small_new = gives.dispatch.at[techs]
    small_new[:techs, :] = capacity_new
    small_new[at.weight : at.weight + 1, :] = jnp.broadcast_to(weight, (1, LANES))
    small_new[at.negative : at.negative + 1, :] = negative
    charge_bar = 2.0 * charge_new - charge
    before_new = jnp.clip(charge_before - primal_step * (prev_row - store_duals[0:1]), 0.0, energy)
    write_lanes(small_new, at.before, before_new)
    before_bar = 2.0 * before_new - charge_before
    shifted_bar = jnp.where(row_id == 0, before_bar, pltpu.roll(charge_bar, 1, 0))
    store_step = weight / 3.0 * (charge_bar - shifted_bar + bars[1])
    store_new = store_duals + store_step
    gives.store_duals[...] = store_new
    primal_row = primal_row + row_sum(primal_acc) + fold_lanes(row_sum((charge_new - charge) ** 2))
    primal_row = primal_row + jnp.where(
        hour_index == 0, row_sum((capacity_new - capacity) ** 2), 0.0
    )
    dual_row = row_sum(dual_acc + step_up * step_up) + fold_lanes(row_sum(store_step * store_step))
    squares = jnp.concatenate(
        [primal_row, dual_row, jnp.zeros((SQUARES - 2, LANES), jnp.float32)], axis=0
    )
    out_sums[techs : techs + SQUARES, :] = squares
    write_halo(sizes, out_sums, store_new)


def call(kernel, given, outs, flops=0, left=(), scratch=(), limit=VMEM_BYTES, copied=0):
    names_in, names_out = tuple(vars(given)), tuple(vars(outs))
    values = pl.pallas_call(
        functools.partial(kernel, names_in, names_out),
        out_shape=tuple(vars(outs).values()),
        in_specs=[
            pl.BlockSpec(memory_space=pl.ANY if i in left else pltpu.VMEM)
            for i in range(len(names_in))
        ],
        out_specs=[
            pl.BlockSpec(memory_space=pl.ANY if i < copied else pltpu.VMEM)
            for i in range(len(names_out))
        ],
        scratch_shapes=scratch,
        cost_estimate=pl.CostEstimate(flops=flops, bytes_accessed=4 * flops, transcendentals=0),
        compiler_params=pltpu.CompilerParams(vmem_limit_bytes=limit),
    )(*vars(given).values())
    return Bag(**dict(zip(names_out, values)))


def swap(value, hour_bit, region_bit):
    hours, regions = lax.axis_size("hours"), lax.axis_size("region")
    pairs = [
        (hour * regions + region, (hour ^ hour_bit) * regions + (region ^ region_bit))
        for hour in range(hours)
        for region in range(regions)
    ]
    return lax.ppermute(value, ("hours", "region"), pairs)


def shifted(value, steps):
    count = lax.axis_size("hours")
    return lax.ppermute(value, "hours", [(i, (i + steps) % count) for i in range(count)])


def both_regions(block):
    if lax.axis_size("region") != 2:
        return lax.all_gather(block, "region")
    return in_order(block, swap(block, 0, 1))


def in_order(block, other):
    return jnp.where(
        lax.axis_index("region") == 0, jnp.stack([block, other]), jnp.stack([other, block])
    )


def exchange(sizes, block):
    hours, regions = lax.axis_size("hours"), lax.axis_size("region")
    techs, span = sizes.techs, sizes.units // LANES
    halo = halo_at(sizes)
    prices, sums = block[: sizes.rows], block[sizes.rows :]
    if regions != 2 or hours != 16:
        gathered = lax.all_gather(prices, "region")
        totals = lax.psum(sums, "hours")
        totals = totals.at[techs:halo].set(lax.psum(totals[techs:halo], "region"))
        next_row = shifted(sums[halo : halo + span], -1)
        prev_row = shifted(sums[halo + span : halo + 2 * span], 1)
        return gathered, Bag(totals=totals, next_row=next_row, prev_row=prev_row)

    def merged(mine, yours, mine_first):
        last = halo + span
        edges = [
            jnp.where(mine_first, mine[halo:last], yours[halo:last]),
            jnp.where(mine_first, yours[last : last + span], mine[last : last + span]),
        ]
        total = mine + yours
        return jnp.concatenate([total[:halo], *edges, total[last + span :]], axis=0)

    hour = lax.axis_index("hours")
    beside_core = swap(block, 1, 0)
    partner_prices, partner = beside_core[: sizes.rows], beside_core[sizes.rows :]
    chip = merged(sums, partner, hour % 2 == 0)
    across = swap(chip, 2 + 1, 0)
    diagonal = swap(chip[techs:halo], 2 + 1, 1)
    beside = swap(jnp.concatenate([partner_prices, chip[techs:halo]], axis=0), 1, 1)
    other, squares = beside[: sizes.rows], beside[sizes.rows :]
    slab = merged(chip, across, hour // 2 % 2 == 0)
    slab = slab + jnp.pad(squares + diagonal, ((techs, slab.shape[0] - halo), (0, 0)))
    near, middle, far = [swap(slab, 4 * step + 1, 0) for step in (1, 2, 3)]
    parts = Bag(slab=slab, near=near, middle=middle, far=far, partner=partner, across=across)
    return in_order(prices, other), parts


def shape(*dims, dtype=jnp.float32):
    return jax.ShapeDtypeStruct(dims, dtype)


def restarted(sizes, kept, args):
    rows, techs, nodes, lines = sizes.rows, sizes.techs, sizes.nodes, sizes.lines
    local, cross = lines + sizes.units, sizes.regions * sizes.slots
    at, own = places(sizes), lax.axis_index("region")
    first_hour = lax.axis_index("hours") == 0
    price_start = args.price_start
    available = args.availability.transpose(1, 0, 2)
    fixed, last = kept[:rows], rows + 2 * techs
    col_weight, cost = kept[rows : rows + techs], kept[rows + techs : last]
    info = kept[last:].reshape(-1, 8, LANES).transpose(1, 0, 2).reshape(8, cross)
    local_limits = fixed[at.limits : at.energy].reshape(1, local)
    cross_limits = info[2:3]
    ends = info[:2].astype(jnp.int32)
    maps_cross_low = incidence(ends[:1], ends[1:], sizes.regions * nodes)
    stores = args.store_node[None]
    maps_local_low = incidence(
        jnp.concatenate([args.line_ends[:1], jnp.full_like(stores, -1)], axis=1),
        jnp.concatenate([args.line_ends[1:], stores], axis=1),
        nodes,
    )
    maps_local = maps_local_low.astype(jnp.float32)
    maps_cross = maps_cross_low.astype(jnp.float32)
    maps_own = lax.dynamic_slice_in_dim(maps_cross, own * nodes, nodes)
    prices_all = jnp.concatenate(list(both_regions(price_start)), axis=1)
    highest = lax.Precision.HIGHEST

    capacity = jnp.maximum(-cost / col_weight, 0.0)
    slopes = fixed[:techs][:, None, :] + price_start[None]
    dispatch = jnp.maximum(-0.5 * slopes, 0.0)
    slope = jnp.dot(price_start, maps_local, precision=highest)
    flows_local = jnp.clip(-0.5 * slope, -local_limits, local_limits)
    slope = jnp.dot(prices_all, maps_cross, precision=highest)
    flows_cross = jnp.clip(-0.5 * slope, -cross_limits, cross_limits)
    balance = (
        jnp.sum(2.0 * dispatch, axis=0)
        + jnp.dot(2.0 * flows_local, maps_local.T, precision=highest)
        + jnp.dot(2.0 * flows_cross, maps_own.T, precision=highest)
        - args.demand
    )
    step_up = balance / (techs + 8.0)
    duals = jnp.maximum(0.5 * (2.0 * dispatch - available * (2.0 * capacity)[:, None, :]), 0.0)
    store_duals = 2.0 * flows_local[:, lines:] / 3.0
    slot = lax.broadcasted_iota(jnp.int32, (1, cross), 1) // sizes.slots
    primal = (
        jnp.sum(dispatch**2)
        + jnp.sum(flows_local**2)
        + jnp.sum(jnp.where(slot == own, flows_cross**2, 0.0))
        + jnp.where(first_hour, jnp.sum(capacity**2), 0.0)
    )
    dual = jnp.sum(step_up**2) + jnp.sum(duals**2) + jnp.sum(store_duals**2)
    rows_of = [
        jnp.sum(available * duals, axis=1),
        jnp.zeros((SQUARES, nodes)).at[0, 0].set(primal).at[1, 0].set(dual),
        store_duals[:1].reshape(-1, LANES),
        store_duals[rows - 1 :].reshape(-1, LANES),
    ]
    used = halo_at(sizes) + 2 * sizes.units // LANES
    rows_of.append(jnp.zeros((sums_rows(sizes) - used, nodes)))
    rows_of += [jnp.where(first_hour, part, 0.0) for part in (col_weight, cost)]
    block = jnp.concatenate([price_start + step_up, *rows_of], axis=0)
    gathered, parts = exchange(sizes, block)
    flows = jnp.concatenate([flows_local, flows_cross], axis=1)
    spare = jnp.concatenate([jnp.zeros((8, local)), info], axis=1)
    state = Bag(
        available=jnp.concatenate([available, args.demand[None], fixed[None]], axis=0),
        maps_local=maps_local_low,
        maps_cross=maps_cross_low,
        store_duals=store_duals,
        dispatch=jnp.concatenate([dispatch, jnp.zeros((1, rows, nodes))], axis=0),
        flows=jnp.concatenate([flows, spare], axis=0),
    )
    return state, gathered, parts


def run(args):
    rows, techs, nodes = args.availability.shape
    hours, regions = lax.axis_size("hours"), lax.axis_size("region")
    slots, owned = args.cross_limit.shape[1], args.cap_cost.shape[1]
    units, lines = args.store_node.shape[0], args.line_limit.shape[0]
    sizes = Bag(
        rows=rows, techs=techs, nodes=nodes, regions=regions, slots=slots, lines=lines, units=units
    )
    cross = regions * slots

    gathered = both_regions(
        call(
            lambda names_in, names_out, *refs: first_kernel(sizes, refs[:4], *refs[4:]),
            Bag(
                price=args.price_start,
                ends=args.cross_ends[:, 0],
                limit=args.cross_limit,
                pairs=args.pair_counts,
            ),
            Bag(block=shape(rows + 8 * max(1, slots // LANES), nodes)),
            left=(0, 1, 2, 3),
            scratch=[
                pltpu.VMEM((2, slots), jnp.int32),
                pltpu.VMEM((1, slots), jnp.float32),
                pltpu.VMEM((1, regions), jnp.int32),
                pltpu.SemaphoreType.DMA((4,)),
            ],
            limit=None,
            flops=25 * 10**5,
        ).block
    )
    state = call(
        functools.partial(start_kernel, sizes),
        Bag(
            availability=args.availability.reshape(rows * techs, nodes),
            price=args.price_start,
            demand=args.demand,
            gen_cost=args.gen_cost,
            cap_cost=args.cap_cost,
            owner=args.owner_map.reshape(hours, owned),
            line_ends=args.line_ends,
            line_limit=args.line_limit[None],
            store_node=args.store_node[None],
            store_power=args.store_power[None],
            store_energy=args.store_energy[None],
        ),
        Bag(
            available=shape(techs + 2, rows, nodes),
            maps_local=shape(nodes, lines + units, dtype=jnp.bfloat16),
            flows_local=shape(rows, lines + units),
            store_duals=shape(rows, units),
            dispatch=shape(techs + 1, rows, nodes),
            balance=shape(rows, nodes),
            sums=shape(sums_rows(sizes) + 2 * techs, nodes),
        ),
        flops=10**6,
        left=(0,),
        scratch=[pltpu.VMEM((rows * techs, nodes), jnp.float32), pltpu.SemaphoreType.DMA],
    )
    closed = call(
        lambda names_in, names_out, *refs: close_kernel(sizes, *refs),
        Bag(
            gathered=gathered,
            flows_local=state.flows_local,
            balance=state.balance,
            sums=state.sums,
        ),
        Bag(
            maps=shape(regions * nodes, cross, dtype=jnp.bfloat16),
            flows=shape(rows + 8, lines + units + cross),
            block=shape(rows + state.sums.shape[0], nodes),
        ),
    )
    del state.sums, state.balance, state.flows_local
    state.maps_cross, state.flows = closed.maps, closed.flows
    gathered, parts = exchange(sizes, closed.block)
    outputs, negative, kept = sweeps(sizes, owned, state, gathered, parts)

    def again():
        return sweeps(sizes, owned, *restarted(sizes, kept, args))[0]

    return lax.cond(negative > 0.0, again, lambda: outputs)


def sweeps(sizes, owned, state, gathered, parts):
    rows, techs, nodes, lines, units = (
        sizes.rows,
        sizes.techs,
        sizes.nodes,
        sizes.lines,
        sizes.units,
    )
    state = Bag(**vars(state))
    for iteration in range(1, ITERS):
        given = Bag(**vars(state), **vars(parts), gathered=gathered)
        if iteration < ITERS - 1:
            outs = Bag(
                dispatch=shape(techs + 1, rows, nodes),
                cap_duals=shape(techs + 1, rows, nodes),
                flows=shape(rows + 8, lines + units + sizes.regions * sizes.slots),
                store_duals=shape(rows, units),
                charge=shape(rows, units),
                block=shape(rows + sums_rows(sizes), nodes),
            )
        else:
            outs = Bag(
                dispatch=shape(rows * techs, nodes),
                charge=shape(rows, units),
                capacity=shape(1, owned),
                prices=shape(rows, nodes),
                negative=shape(1, LANES),
                kept=shape(rows + 2 * techs + 8 * (sizes.regions * sizes.slots // LANES), LANES),
            )
        final = iteration == ITERS - 1
        results = call(
            functools.partial(sweep_kernel, sizes, iteration),
            given,
            outs,
            copied=2 if final else 0,
            scratch=[
                pltpu.VMEM(outs.dispatch.shape, jnp.float32),
                pltpu.VMEM(outs.charge.shape, jnp.float32),
                pltpu.SemaphoreType.DMA((2,)),
            ]
            if final
            else [],
        )
        if iteration < ITERS - 1:
            gathered, parts = exchange(sizes, results.block)
            del results.block
            vars(state).update(vars(results))
    dispatch = results.dispatch.reshape(rows, techs, nodes)
    outputs = (dispatch, results.capacity, results.prices, results.charge)
    return outputs, results.negative[0, 0], results.kept


def body(
    availability,
    demand,
    gen_cost,
    cap_cost,
    owner_map,
    line_ends,
    line_limit,
    cross_ends,
    cross_limit,
    pair_counts,
    store_node,
    store_energy,
    store_power,
    price_start,
):
    args = Bag(**locals())
    return run(args)


def solution(mesh):
    placed = (
        P("hours", None, "region"),
        P("hours", "region"),
        P(None, "region"),
        P("region", "hours"),
        P("region", None),
        P(None, "region"),
        P("region"),
        P(None, "region", None),
        P("region", None),
        P("region", None),
        P("region"),
        P("region"),
        P("region"),
        P("hours", "region"),
    )
    return jax.shard_map(
        body,
        mesh=mesh,
        in_specs=placed,
        out_specs=(
            P("hours", None, "region"),
            P("region", "hours"),
            P("hours", "region"),
            P("hours", "region"),
        ),
        check_vma=False,
    )
```

```python
import functools
from types import SimpleNamespace as Bag

import jax
import jax.numpy as jnp
from jax import lax
from jax.experimental import pallas as pl
from jax.experimental.pallas import tpu as pltpu
from jax.sharding import PartitionSpec as P

ITERS = 4
EPSILON = 1e-06
LANES = 128
VMEM_BYTES = 24 * 1024 * 1024
SQUARES = 3


def split3(value):
    high = value.astype(jnp.bfloat16)
    rest = value - high.astype(jnp.float32)
    middle = rest.astype(jnp.bfloat16)
    low = (rest - middle.astype(jnp.float32)).astype(jnp.bfloat16)
    return jnp.concatenate([high, middle, low], axis=0)


def dot3(value, matrix, transposed):
    rows = value.shape[0]
    contract = ((1,), (1 if transposed else 0,))
    product = lax.dot_general(
        split3(value), matrix, (contract, ((), ())), preferred_element_type=jnp.float32
    )
    return product[:rows] + product[rows : 2 * rows] + product[2 * rows :]


def row_sum(value):
    return jnp.sum(value, axis=0, keepdims=True)


def fold_lanes(row):
    total = row[:, :LANES]
    for start in range(LANES, row.shape[1], LANES):
        total = total + row[:, start : start + LANES]
    return total


def owned_one_hots(owned, tech_count, node_count):
    shape_t = (tech_count, owned.shape[1])
    shape_n = (node_count, owned.shape[1])
    tech = lax.broadcasted_iota(jnp.int32, shape_t, 0) == owned // node_count
    node = lax.broadcasted_iota(jnp.int32, shape_n, 0) == owned % node_count
    return tech, node.astype(jnp.float32).astype(jnp.bfloat16)


def incidence(start, end, count):
    node = lax.broadcasted_iota(jnp.int32, (count, start.shape[1]), 0)
    maps = (node == end).astype(jnp.float32) - (node == start).astype(jnp.float32)
    return maps.astype(jnp.bfloat16)


def halo_at(sizes):
    return sizes.techs + SQUARES


def sums_rows(sizes):
    return (halo_at(sizes) + 2 * sizes.units // LANES + 7) // 8 * 8


def write_halo(sizes, sums_ref, store_new):
    halo, span, rows = halo_at(sizes), sizes.units // LANES, sizes.rows
    write_lanes(sums_ref, halo, store_new[:1])
    write_lanes(sums_ref, halo + span, store_new[rows - 1 :])
    used, end = halo + 2 * span, sums_rows(sizes)
    if used < end:
        sums_ref[used:end, :] = jnp.zeros((end - used, LANES), jnp.float32)


def write_lanes(ref, start, row):
    for i in range(row.shape[1] // LANES):
        ref[start + i : start + i + 1, :] = row[:, i * LANES : (i + 1) * LANES]


def read_lanes(ref, start, length):
    return jnp.concatenate(
        [ref[start + i : start + i + 1, :] for i in range(length // LANES)], axis=1
    )


def places(sizes):
    span = sizes.units // LANES
    limits = sizes.techs
    energy = limits + (sizes.lines + sizes.units) // LANES
    return Bag(
        limits=limits,
        energy=energy,
        owned=energy + span,
        weight=sizes.techs,
        before=sizes.techs + 1,
        negative=sizes.techs + 1 + span,
    )


def first_kernel(sizes, sources, block_ref, ends_ref, limit_ref, pairs_ref, sems):
    rows = sizes.rows
    targets = (block_ref.at[pl.ds(0, rows)], ends_ref, limit_ref, pairs_ref)
    copies = [
        pltpu.make_async_copy(source, target, sems.at[i])
        for i, (source, target) in enumerate(zip(sources, targets))
    ]
    for copy in copies:
        copy.start()
    nodes, slots, regions = sizes.nodes, sizes.slots, sizes.regions
    own = lax.axis_index("region")
    width = slots // regions
    slot = lax.broadcasted_iota(jnp.int32, (1, slots), 1)
    pair = slot // width
    for copy in copies[1:]:
        copy.wait()
    in_use = jnp.zeros((1, slots), jnp.int32)
    for target in range(regions):
        in_use = jnp.where(pair == target, pairs_ref[0:1, target : target + 1], in_use)
    bound = jnp.where(slot % width < in_use, limit_ref[...], 0.0)
    start = (ends_ref[0:1, :] + own * nodes).astype(jnp.float32)
    end = (ends_ref[1:2, :] + pair * nodes).astype(jnp.float32)
    block_ref[rows:, :] = jnp.zeros((block_ref.shape[0] - rows, LANES), jnp.float32)
    width = min(slots, LANES)
    for chunk in range(slots // width):
        at = rows + 8 * chunk
        for i, row in enumerate((start, end, bound)):
            block_ref[at + i : at + i + 1, :width] = row[:, chunk * width : (chunk + 1) * width]
    copies[0].wait()


def start_kernel(sizes, names_in, names_out, *refs):
    given = Bag(**dict(zip(names_in, refs[: len(names_in)])))
    gives = Bag(**dict(zip(names_out, refs[len(names_in) : -2])))
    availability, sem = refs[-2:]
    copy = pltpu.make_async_copy(given.availability, availability, sem)
    copy.start()
    rows, techs, nodes, lines = sizes.rows, sizes.techs, sizes.nodes, sizes.lines
    at = places(sizes)
    fixed = gives.available.at[techs + 1]
    gives.available[techs] = given.demand[...]
    fixed[:techs, :] = given.gen_cost[...]
    write_lanes(fixed, at.energy, given.store_energy[...])
    owned = given.owner[pl.ds(lax.axis_index("hours"), 1), :]
    fixed[at.owned : at.owned + 1, : owned.shape[1]] = owned.astype(jnp.float32)
    line_ends, stores = given.line_ends[...], given.store_node[...]
    start = jnp.concatenate([line_ends[0:1], jnp.full_like(stores, -1)], axis=1)
    end = jnp.concatenate([line_ends[1:2], stores], axis=1)
    maps = incidence(start, end, nodes)
    limits = jnp.concatenate([given.line_limit[...], given.store_power[...]], axis=1)
    gives.maps_local[...] = maps
    write_lanes(fixed, at.limits, limits)
    prices = given.price[...]
    flows = jnp.clip(-0.5 * dot3(prices, maps, False), -limits, limits)
    gives.flows_local[...] = flows
    store_new = (1.0 / 3.0) * (2.0 * flows[:, lines:])
    gives.store_duals[...] = store_new
    primal_row = fold_lanes(row_sum(flows * flows))
    dual_row = fold_lanes(row_sum(store_new * store_new))
    balance = dot3(2.0 * flows, maps, True) - given.demand[...]
    gen_cost = given.gen_cost[...]
    copy.wait()
    acc = jnp.zeros((rows, nodes), jnp.float32)
    weights = jnp.zeros((techs, nodes), jnp.float32)
    for hour in range(rows):
        weights = weights + availability[hour * techs : (hour + 1) * techs, :]
    for tech in range(techs):
        avail = availability[pl.ds(tech, rows, stride=techs), :]
        gives.available[tech] = avail
        dispatch = jnp.maximum(-0.5 * (gen_cost[tech : tech + 1] + prices), 0.0)
        gives.dispatch[tech] = dispatch
        dispatch_bar = 2.0 * dispatch
        balance = balance + dispatch_bar
        duals = jnp.maximum(0.5 * dispatch_bar, 0.0)
        acc = acc + dispatch * dispatch
        gives.sums[tech : tech + 1, :] = row_sum(avail * duals)
    gives.balance[...] = balance
    squares = row_sum(acc)
    cost = given.cap_cost[...]
    negative = jnp.sum((cost < 0.0).astype(jnp.float32), axis=1, keepdims=True)
    write_halo(sizes, gives.sums, store_new)
    gives.sums[techs : techs + SQUARES, :] = jnp.concatenate(
        [primal_row + squares, dual_row + squares, jnp.broadcast_to(negative, (1, LANES))], axis=0
    )
    tech_hot, node_hot = owned_one_hots(owned, techs, nodes)
    first = sums_rows(sizes)
    gives.sums[first : first + techs, :] = weights
    gives.sums[first + techs : first + 2 * techs, :] = dot3(
        jnp.where(tech_hot, cost, 0.0), node_hot, True
    )


def close_kernel(
    sizes,
    gathered,
    local_ref,
    balance_ref,
    sums_in_ref,
    maps_ref,
    flows_ref,
    block_ref,
):
    rows, techs, nodes = sizes.rows, sizes.techs, sizes.nodes
    slots, regions = sizes.slots, sizes.regions
    own = lax.axis_index("region")
    width = min(slots, LANES)
    info = jnp.concatenate(
        [
            gathered[region, rows + 8 * chunk : rows + 8 * chunk + 8, :width]
            for region in range(regions)
            for chunk in range(slots // width)
        ],
        axis=1,
    )
    maps_ref[...] = incidence(
        info[0:1].astype(jnp.int32), info[1:2].astype(jnp.int32), regions * nodes
    )
    limits = info[2:3]
    prices_all = jnp.concatenate([gathered[region, :rows, :] for region in range(regions)], axis=1)
    flows = jnp.clip(-0.5 * dot3(prices_all, maps_ref[...], False), -limits, limits)
    local = local_ref.shape[1]
    flows_ref[:rows, :local] = local_ref[...]
    flows_ref[:rows, local:] = flows
    flows_ref[rows:, local:] = info
    maps_own = maps_ref[pl.ds(pl.multiple_of(own * nodes, nodes), nodes), :]
    balance = balance_ref[...] + dot3(2.0 * flows, maps_own, True)
    step_up = (1.0 / (techs + 8.0)) * balance
    block_ref[:rows, :] = gathered[own, :rows, :] + step_up
    change = row_sum(flows * flows)
    slot = lax.broadcasted_iota(jnp.int32, change.shape, 1)
    primal = fold_lanes(jnp.where(slot // slots == own, change, 0.0))
    more = jnp.concatenate(
        [primal, row_sum(step_up * step_up), jnp.zeros((SQUARES - 2, LANES), jnp.float32)], axis=0
    )
    block_ref[rows:, :] = sums_in_ref[...]
    block_ref[rows + techs : rows + techs + SQUARES, :] = (
        sums_in_ref[techs : techs + SQUARES, :] + more
    )


def neighbour_rows(sizes, given, hour_index):
    units = sizes.units
    if hasattr(given, "totals"):
        return read_lanes(given.next_row, 0, units), read_lanes(given.prev_row, 0, units)
    first = halo_at(sizes)
    last = first + units // LANES
    core, x_place, odd = hour_index % 2, hour_index // 2 % 2, hour_index // 4 % 2
    next_row = jnp.where(
        odd == 0, read_lanes(given.near, first, units), read_lanes(given.far, first, units)
    )
    prev_row = jnp.where(
        odd == 0, read_lanes(given.far, last, units), read_lanes(given.near, last, units)
    )
    next_row = jnp.where(x_place == 0, read_lanes(given.across, first, units), next_row)
    prev_row = jnp.where(x_place == 0, prev_row, read_lanes(given.across, last, units))
    next_row = jnp.where(core == 0, read_lanes(given.partner, first, units), next_row)
    prev_row = jnp.where(core == 0, prev_row, read_lanes(given.partner, last, units))
    return next_row, prev_row


def total_of(parts):
    if hasattr(parts, "totals"):
        return parts.totals[...]
    return (parts.slab[...] + parts.near[...]) + (parts.middle[...] + parts.far[...])


def slopes_kernel(sizes, names_in, names_out, gathered, maps_local, maps_cross, slopes_ref):
    rows, regions = sizes.rows, sizes.regions
    local = sizes.lines + sizes.units
    prices_all = jnp.concatenate([gathered[region, :rows, :] for region in range(regions)], axis=1)
    prices = gathered[lax.axis_index("region"), :rows, :]
    slopes_ref[:, :local] = dot3(prices, maps_local[...], False)
    slopes_ref[:, local:] = dot3(prices_all, maps_cross[...], False)


def sweep_kernel(sizes, iteration, names_in, names_out, *refs):
    rows, techs, nodes = sizes.rows, sizes.techs, sizes.nodes
    slots, regions, lines, units = sizes.slots, sizes.regions, sizes.lines, sizes.units
    second = iteration == 1
    last = iteration == ITERS - 1
    given = Bag(**dict(zip(names_in, refs[: len(names_in)])))
    gives = Bag(**dict(zip(names_out, refs[len(names_in) :])))
    if last:
        staged, sem = refs[-2:]
    own = lax.axis_index("region")
    hour_index = lax.axis_index("hours")
    gathered = given.gathered

    at = places(sizes)
    fixed = given.available.at[techs + 1]
    small = given.dispatch.at[techs]
    out_sums = None if last else gives.block.at[pl.ds(rows, sums_rows(sizes))]
    sums = total_of(given)
    squares = jnp.sum(sums[techs : techs + 2], axis=1, keepdims=True)
    old_weight = jnp.ones((1, 1), jnp.float32) if second else small[at.weight : at.weight + 1, :1]
    weight = jnp.sqrt(
        old_weight * jnp.sqrt((squares[1:2] + EPSILON) / (squares[0:1] + EPSILON))
    )
    primal_step = 0.5 / weight
    if second:
        first = sums_rows(sizes)
        col_weight, cost = sums[first : first + techs], sums[first + techs : first + 2 * techs]
        negative = sums[techs + 2 : techs + 3]
        capacity = jnp.maximum(-cost / col_weight, 0.0)
        first_bar = 2.0 * capacity
    else:
        col_weight = given.cap_duals[techs, :techs, :]
        cost = given.cap_duals[techs, techs : 2 * techs, :]
        capacity = small[:techs, :]
        negative = small[at.negative : at.negative + 1, :]
    capacity_new = jnp.maximum(capacity - (cost - sums[:techs]) / (weight * col_weight), 0.0)
    capacity_bar = 2.0 * capacity_new - capacity

    prices = gathered[own, :rows, :]
    gen_cost = fixed[:techs, :]
    half_weight = weight / 2.0
    primal_acc = jnp.zeros((rows, nodes), jnp.float32)
    dual_acc = jnp.zeros((rows, nodes), jnp.float32)
    supply = jnp.zeros((rows, nodes), jnp.float32)
    for tech in range(techs):
        slope = gen_cost[tech : tech + 1] + prices
        dispatch = given.dispatch[tech]
        avail = given.available[tech]
        if second:
            duals = jnp.maximum(0.5 * (2.0 * dispatch - avail * first_bar[tech : tech + 1]), 0.0)
        else:
            duals = given.cap_duals[tech]
        dispatch_new = jnp.maximum(dispatch - primal_step * (slope + duals), 0.0)
        dispatch_bar = 2.0 * dispatch_new - dispatch
        supply = supply + dispatch_bar
        if last:
            staged[pl.ds(tech, rows, stride=techs), :] = dispatch_new
            continue
        gives.dispatch[tech] = dispatch_new
        cap_rows = dispatch_bar - avail * capacity_bar[tech : tech + 1]
        primal_acc = primal_acc + (dispatch_new - dispatch) ** 2
        duals_new = jnp.maximum(duals + half_weight * cap_rows, 0.0)
        dual_acc = dual_acc + (duals_new - duals) ** 2
        gives.cap_duals[tech] = duals_new
        out_sums[tech : tech + 1, :] = row_sum(avail * duals_new)
    if last:
        copy = pltpu.make_async_copy(staged, gives.dispatch, sem)
        copy.start()

    maps_local = given.maps_local[...]

    energy = read_lanes(fixed, at.energy, units)
    row_id = lax.broadcasted_iota(jnp.int32, (rows, units), 0)
    next_row, prev_row = neighbour_rows(sizes, given, hour_index)
    store_duals = given.store_duals[...]
    next_duals = jnp.where(row_id == rows - 1, next_row, pltpu.roll(store_duals, rows - 1, 0))
    if second:
        charge = jnp.zeros((rows, units), jnp.float32)
        charge_before = jnp.zeros((1, units), jnp.float32)
    else:
        charge = given.charge[...]
        charge_before = read_lanes(small, at.before, units)
    charge_new = jnp.clip(charge - primal_step * (store_duals - next_duals), 0.0, energy)
    gives.charge[...] = charge_new

    primal_row = jnp.zeros((1, LANES), jnp.float32)
    bars = []
    local, total_flows = lines + units, lines + units + regions * slots
    local_limits = read_lanes(fixed, at.limits, local)
    cross_limits = given.flows[rows + 2 : rows + 3, local:]
    for bound, low, high in (
        (local_limits[:, :lines], 0, lines),
        (local_limits[:, lines:], lines, local),
        (cross_limits, local, total_flows),
    ):
        slope = given.slopes[:, low:high]
        if low == lines:
            slope = slope + store_duals
        old = given.flows[:rows, low:high]
        new = jnp.clip(old - primal_step * slope, -bound, bound)
        bars.append(2.0 * new - old)
        if not last:
            gives.flows[:rows, low:high] = new
            change = row_sum((new - old) ** 2)
            if low == local:
                slot = lax.broadcasted_iota(jnp.int32, change.shape, 1)
                change = jnp.where(slot // slots == own, change, 0.0)
            primal_row = primal_row + fold_lanes(change)
    maps_own = given.maps_cross[pl.ds(pl.multiple_of(own * nodes, nodes), nodes), :]
    balance = dot3(jnp.concatenate(bars[:2], axis=1), maps_local, True) - given.available[techs]
    balance = balance + supply + dot3(bars[2], maps_own, True)

    step_up = weight / (techs + 8.0) * balance
    if last:
        gives.prices[...] = prices + step_up
        owned = fixed[at.owned : at.owned + 1, : gives.capacity.shape[1]].astype(jnp.int32)
        tech_hot, node_hot = owned_one_hots(owned, techs, nodes)
        chosen = dot3(capacity_new, node_hot, False)
        gives.capacity[...] = row_sum(jnp.where(tech_hot, chosen, 0.0))
        gives.negative[...] = negative
        gives.kept[:rows, :] = fixed[...]
        gives.kept[rows : rows + techs, :] = col_weight
        gives.kept[rows + techs : rows + 2 * techs, :] = cost
        for chunk in range(regions * slots // LANES):
            low = local + chunk * LANES
            first = rows + 2 * techs + 8 * chunk
            gives.kept[first : first + 8, :] = given.flows[rows:, low : low + LANES]
        copy.wait()
        return
    gives.block[:rows, :] = prices + step_up
    gives.flows[rows:, local:] = given.flows[rows:, local:]
    gives.cap_duals[techs, :techs, :] = col_weight
    gives.cap_duals[techs, techs : 2 * techs, :] = cost
    small_new = gives.dispatch.at[techs]
    small_new[:techs, :] = capacity_new
    small_new[at.weight : at.weight + 1, :] = jnp.broadcast_to(weight, (1, LANES))
    small_new[at.negative : at.negative + 1, :] = negative
    charge_bar = 2.0 * charge_new - charge
    before_new = jnp.clip(charge_before - primal_step * (prev_row - store_duals[0:1]), 0.0, energy)
    write_lanes(small_new, at.before, before_new)
    before_bar = 2.0 * before_new - charge_before
    shifted_bar = jnp.where(row_id == 0, before_bar, pltpu.roll(charge_bar, 1, 0))
    store_step = weight / 3.0 * (charge_bar - shifted_bar + bars[1])
    store_new = store_duals + store_step
    gives.store_duals[...] = store_new
    primal_row = primal_row + row_sum(primal_acc) + fold_lanes(row_sum((charge_new - charge) ** 2))
    primal_row = primal_row + jnp.where(
        hour_index == 0, row_sum((capacity_new - capacity) ** 2), 0.0
    )
    dual_row = row_sum(dual_acc + step_up * step_up) + fold_lanes(row_sum(store_step * store_step))
    squares = jnp.concatenate(
        [primal_row, dual_row, jnp.zeros((SQUARES - 2, LANES), jnp.float32)], axis=0
    )
    out_sums[techs : techs + SQUARES, :] = squares
    write_halo(sizes, out_sums, store_new)


def call(kernel, given, outs, flops=0, left=(), scratch=(), limit=VMEM_BYTES, copied=0):
    names_in, names_out = tuple(vars(given)), tuple(vars(outs))
    values = pl.pallas_call(
        functools.partial(kernel, names_in, names_out),
        out_shape=tuple(vars(outs).values()),
        in_specs=[
            pl.BlockSpec(memory_space=pl.ANY if i in left else pltpu.VMEM)
            for i in range(len(names_in))
        ],
        out_specs=[
            pl.BlockSpec(memory_space=pl.ANY if i < copied else pltpu.VMEM)
            for i in range(len(names_out))
        ],
        scratch_shapes=scratch,
        cost_estimate=pl.CostEstimate(flops=flops, bytes_accessed=4 * flops, transcendentals=0),
        compiler_params=pltpu.CompilerParams(vmem_limit_bytes=limit),
    )(*vars(given).values())
    return Bag(**dict(zip(names_out, values)))


def swap(value, hour_bit, region_bit):
    hours, regions = lax.axis_size("hours"), lax.axis_size("region")
    pairs = [
        (hour * regions + region, (hour ^ hour_bit) * regions + (region ^ region_bit))
        for hour in range(hours)
        for region in range(regions)
    ]
    return lax.ppermute(value, ("hours", "region"), pairs)


def shifted(value, steps):
    count = lax.axis_size("hours")
    return lax.ppermute(value, "hours", [(i, (i + steps) % count) for i in range(count)])


def both_regions(block):
    if lax.axis_size("region") != 2:
        return lax.all_gather(block, "region")
    return in_order(block, swap(block, 0, 1))


def in_order(block, other):
    return jnp.where(
        lax.axis_index("region") == 0, jnp.stack([block, other]), jnp.stack([other, block])
    )


def exchange(sizes, block):
    hours, regions = lax.axis_size("hours"), lax.axis_size("region")
    techs, span = sizes.techs, sizes.units // LANES
    halo = halo_at(sizes)
    prices, sums = block[: sizes.rows], block[sizes.rows :]
    if regions != 2 or hours != 16:
        gathered = lax.all_gather(prices, "region")
        totals = lax.psum(sums, "hours")
        totals = totals.at[techs:halo].set(lax.psum(totals[techs:halo], "region"))
        next_row = shifted(sums[halo : halo + span], -1)
        prev_row = shifted(sums[halo + span : halo + 2 * span], 1)
        return gathered, Bag(totals=totals, next_row=next_row, prev_row=prev_row)

    def merged(mine, yours, mine_first):
        last = halo + span
        edges = [
            jnp.where(mine_first, mine[halo:last], yours[halo:last]),
            jnp.where(mine_first, yours[last : last + span], mine[last : last + span]),
        ]
        total = mine + yours
        return jnp.concatenate([total[:halo], *edges, total[last + span :]], axis=0)

    hour = lax.axis_index("hours")
    beside_core = swap(block, 1, 0)
    partner_prices, partner = beside_core[: sizes.rows], beside_core[sizes.rows :]
    chip = merged(sums, partner, hour % 2 == 0)
    across = swap(chip, 2 + 1, 0)
    diagonal = swap(chip[techs:halo], 2 + 1, 1)
    beside = swap(jnp.concatenate([partner_prices, chip[techs:halo]], axis=0), 1, 1)
    other, squares = beside[: sizes.rows], beside[sizes.rows :]
    slab = merged(chip, across, hour // 2 % 2 == 0)
    slab = slab + jnp.pad(squares + diagonal, ((techs, slab.shape[0] - halo), (0, 0)))
    near, middle, far = [swap(slab, 4 * step + 1, 0) for step in (1, 2, 3)]
    parts = Bag(slab=slab, near=near, middle=middle, far=far, partner=partner, across=across)
    return in_order(prices, other), parts


def shape(*dims, dtype=jnp.float32):
    return jax.ShapeDtypeStruct(dims, dtype)


def restarted(sizes, kept, args):
    rows, techs, nodes, lines = sizes.rows, sizes.techs, sizes.nodes, sizes.lines
    local, cross = lines + sizes.units, sizes.regions * sizes.slots
    at, own = places(sizes), lax.axis_index("region")
    first_hour = lax.axis_index("hours") == 0
    price_start = args.price_start
    available = args.availability.transpose(1, 0, 2)
    fixed, last = kept[:rows], rows + 2 * techs
    col_weight, cost = kept[rows : rows + techs], kept[rows + techs : last]
    info = kept[last:].reshape(-1, 8, LANES).transpose(1, 0, 2).reshape(8, cross)
    local_limits = fixed[at.limits : at.energy].reshape(1, local)
    cross_limits = info[2:3]
    ends = info[:2].astype(jnp.int32)
    maps_cross_low = incidence(ends[:1], ends[1:], sizes.regions * nodes)
    stores = args.store_node[None]
    maps_local_low = incidence(
        jnp.concatenate([args.line_ends[:1], jnp.full_like(stores, -1)], axis=1),
        jnp.concatenate([args.line_ends[1:], stores], axis=1),
        nodes,
    )
    maps_local = maps_local_low.astype(jnp.float32)
    maps_cross = maps_cross_low.astype(jnp.float32)
    maps_own = lax.dynamic_slice_in_dim(maps_cross, own * nodes, nodes)
    prices_all = jnp.concatenate(list(both_regions(price_start)), axis=1)
    highest = lax.Precision.HIGHEST

    capacity = jnp.maximum(-cost / col_weight, 0.0)
    slopes = fixed[:techs][:, None, :] + price_start[None]
    dispatch = jnp.maximum(-0.5 * slopes, 0.0)
    slope = jnp.dot(price_start, maps_local, precision=highest)
    flows_local = jnp.clip(-0.5 * slope, -local_limits, local_limits)
    slope = jnp.dot(prices_all, maps_cross, precision=highest)
    flows_cross = jnp.clip(-0.5 * slope, -cross_limits, cross_limits)
    balance = (
        jnp.sum(2.0 * dispatch, axis=0)
        + jnp.dot(2.0 * flows_local, maps_local.T, precision=highest)
        + jnp.dot(2.0 * flows_cross, maps_own.T, precision=highest)
        - args.demand
    )
    step_up = balance / (techs + 8.0)
    duals = jnp.maximum(0.5 * (2.0 * dispatch - available * (2.0 * capacity)[:, None, :]), 0.0)
    store_duals = 2.0 * flows_local[:, lines:] / 3.0
    slot = lax.broadcasted_iota(jnp.int32, (1, cross), 1) // sizes.slots
    primal = (
        jnp.sum(dispatch**2)
        + jnp.sum(flows_local**2)
        + jnp.sum(jnp.where(slot == own, flows_cross**2, 0.0))
        + jnp.where(first_hour, jnp.sum(capacity**2), 0.0)
    )
    dual = jnp.sum(step_up**2) + jnp.sum(duals**2) + jnp.sum(store_duals**2)
    rows_of = [
        jnp.sum(available * duals, axis=1),
        jnp.zeros((SQUARES, nodes)).at[0, 0].set(primal).at[1, 0].set(dual),
        store_duals[:1].reshape(-1, LANES),
        store_duals[rows - 1 :].reshape(-1, LANES),
    ]
    used = halo_at(sizes) + 2 * sizes.units // LANES
    rows_of.append(jnp.zeros((sums_rows(sizes) - used, nodes)))
    rows_of += [jnp.where(first_hour, part, 0.0) for part in (col_weight, cost)]
    block = jnp.concatenate([price_start + step_up, *rows_of], axis=0)
    gathered, parts = exchange(sizes, block)
    flows = jnp.concatenate([flows_local, flows_cross], axis=1)
    spare = jnp.concatenate([jnp.zeros((8, local)), info], axis=1)
    state = Bag(
        available=jnp.concatenate([available, args.demand[None], fixed[None]], axis=0),
        maps_local=maps_local_low,
        maps_cross=maps_cross_low,
        store_duals=store_duals,
        dispatch=jnp.concatenate([dispatch, jnp.zeros((1, rows, nodes))], axis=0),
        flows=jnp.concatenate([flows, spare], axis=0),
    )
    return state, gathered, parts


def run(args):
    rows, techs, nodes = args.availability.shape
    hours, regions = lax.axis_size("hours"), lax.axis_size("region")
    slots, owned = args.cross_limit.shape[1], args.cap_cost.shape[1]
    units, lines = args.store_node.shape[0], args.line_limit.shape[0]
    sizes = Bag(
        rows=rows, techs=techs, nodes=nodes, regions=regions, slots=slots, lines=lines, units=units
    )
    cross = regions * slots

    gathered = both_regions(
        call(
            lambda names_in, names_out, *refs: first_kernel(sizes, refs[:4], *refs[4:]),
            Bag(
                price=args.price_start,
                ends=args.cross_ends[:, 0],
                limit=args.cross_limit,
                pairs=args.pair_counts,
            ),
            Bag(block=shape(rows + 8 * max(1, slots // LANES), nodes)),
            left=(0, 1, 2, 3),
            scratch=[
                pltpu.VMEM((2, slots), jnp.int32),
                pltpu.VMEM((1, slots), jnp.float32),
                pltpu.VMEM((1, regions), jnp.int32),
                pltpu.SemaphoreType.DMA((4,)),
            ],
            limit=None,
        ).block
    )
    state = call(
        functools.partial(start_kernel, sizes),
        Bag(
            availability=args.availability.reshape(rows * techs, nodes),
            price=args.price_start,
            demand=args.demand,
            gen_cost=args.gen_cost,
            cap_cost=args.cap_cost,
            owner=args.owner_map.reshape(hours, owned),
            line_ends=args.line_ends,
            line_limit=args.line_limit[None],
            store_node=args.store_node[None],
            store_power=args.store_power[None],
            store_energy=args.store_energy[None],
        ),
        Bag(
            available=shape(techs + 2, rows, nodes),
            maps_local=shape(nodes, lines + units, dtype=jnp.bfloat16),
            flows_local=shape(rows, lines + units),
            store_duals=shape(rows, units),
            dispatch=shape(techs + 1, rows, nodes),
            balance=shape(rows, nodes),
            sums=shape(sums_rows(sizes) + 2 * techs, nodes),
        ),
        flops=10**6,
        left=(0,),
        scratch=[pltpu.VMEM((rows * techs, nodes), jnp.float32), pltpu.SemaphoreType.DMA],
    )
    closed = call(
        lambda names_in, names_out, *refs: close_kernel(sizes, *refs),
        Bag(
            gathered=gathered,
            flows_local=state.flows_local,
            balance=state.balance,
            sums=state.sums,
        ),
        Bag(
            maps=shape(regions * nodes, cross, dtype=jnp.bfloat16),
            flows=shape(rows + 8, lines + units + cross),
            block=shape(rows + state.sums.shape[0], nodes),
        ),
    )
    del state.sums, state.balance, state.flows_local
    state.maps_cross, state.flows = closed.maps, closed.flows
    gathered, parts = exchange(sizes, closed.block)
    outputs, negative, kept = sweeps(sizes, owned, state, gathered, parts)

    def again():
        return sweeps(sizes, owned, *restarted(sizes, kept, args))[0]

    return lax.cond(negative > 0.0, again, lambda: outputs)


def sweeps(sizes, owned, state, gathered, parts):
    rows, techs, nodes, lines, units = (
        sizes.rows,
        sizes.techs,
        sizes.nodes,
        sizes.lines,
        sizes.units,
    )
    state = Bag(**vars(state))
    for iteration in range(1, ITERS):
        slopes = call(
            functools.partial(slopes_kernel, sizes),
            Bag(gathered=gathered, maps_local=state.maps_local, maps_cross=state.maps_cross),
            Bag(slopes=shape(rows, lines + units + sizes.regions * sizes.slots)),
        ).slopes
        given = Bag(**vars(state), **vars(parts), gathered=gathered, slopes=slopes)
        if iteration < ITERS - 1:
            outs = Bag(
                dispatch=shape(techs + 1, rows, nodes),
                cap_duals=shape(techs + 1, rows, nodes),
                flows=shape(rows + 8, lines + units + sizes.regions * sizes.slots),
                store_duals=shape(rows, units),
                charge=shape(rows, units),
                block=shape(rows + sums_rows(sizes), nodes),
            )
        else:
            outs = Bag(
                dispatch=shape(rows * techs, nodes),
                capacity=shape(1, owned),
                prices=shape(rows, nodes),
                charge=shape(rows, units),
                negative=shape(1, LANES),
                kept=shape(rows + 2 * techs + 8 * (sizes.regions * sizes.slots // LANES), LANES),
            )
        final = iteration == ITERS - 1
        results = call(
            functools.partial(sweep_kernel, sizes, iteration),
            given,
            outs,
            copied=int(final),
            scratch=[pltpu.VMEM(outs.dispatch.shape, jnp.float32), pltpu.SemaphoreType.DMA]
            if final
            else [],
        )
        if iteration < ITERS - 1:
            gathered, parts = exchange(sizes, results.block)
            del results.block
            vars(state).update(vars(results))
    dispatch = results.dispatch.reshape(rows, techs, nodes)
    outputs = (dispatch, results.capacity, results.prices, results.charge)
    return outputs, results.negative[0, 0], results.kept


def body(
    availability,
    demand,
    gen_cost,
    cap_cost,
    owner_map,
    line_ends,
    line_limit,
    cross_ends,
    cross_limit,
    pair_counts,
    store_node,
    store_energy,
    store_power,
    price_start,
):
    args = Bag(**locals())
    return run(args)


def solution(mesh):
    placed = (
        P("hours", None, "region"),
        P("hours", "region"),
        P(None, "region"),
        P("region", "hours"),
        P("region", None),
        P(None, "region"),
        P("region"),
        P(None, "region", None),
        P("region", None),
        P("region", None),
        P("region"),
        P("region"),
        P("region"),
        P("hours", "region"),
    )
    return jax.shard_map(
        body,
        mesh=mesh,
        in_specs=placed,
        out_specs=(
            P("hours", None, "region"),
            P("region", "hours"),
            P("hours", "region"),
            P("hours", "region"),
        ),
        check_vma=False,
    )
```

```python
import functools
from types import SimpleNamespace as Bag

import jax
import jax.numpy as jnp
from jax import lax
from jax.experimental import pallas as pl
from jax.experimental.pallas import tpu as pltpu
from jax.sharding import PartitionSpec as P

ITERS = 4
EPSILON = 1e-06
LANES = 128
VMEM_BYTES = 24 * 1024 * 1024
PARTS = 4
SQUARES = 3


def split3(value):
    high = value.astype(jnp.bfloat16)
    rest = value - high.astype(jnp.float32)
    middle = rest.astype(jnp.bfloat16)
    low = (rest - middle.astype(jnp.float32)).astype(jnp.bfloat16)
    return jnp.concatenate([high, middle, low], axis=0)


def dot3(value, matrix, transposed):
    rows = value.shape[0]
    contract = ((1,), (1 if transposed else 0,))
    product = lax.dot_general(
        split3(value), matrix, (contract, ((), ())), preferred_element_type=jnp.float32
    )
    return product[:rows] + product[rows : 2 * rows] + product[2 * rows :]


def row_sum(value):
    return jnp.sum(value, axis=0, keepdims=True)


def fold_lanes(row):
    total = row[:, :LANES]
    for start in range(LANES, row.shape[1], LANES):
        total = total + row[:, start : start + LANES]
    return total


def owned_one_hots(owned, tech_count, node_count):
    shape_t = (tech_count, owned.shape[1])
    shape_n = (node_count, owned.shape[1])
    tech = lax.broadcasted_iota(jnp.int32, shape_t, 0) == owned // node_count
    node = lax.broadcasted_iota(jnp.int32, shape_n, 0) == owned % node_count
    return tech, node.astype(jnp.float32).astype(jnp.bfloat16)


def incidence(start, end, count):
    node = lax.broadcasted_iota(jnp.int32, (count, start.shape[1]), 0)
    maps = (node == end).astype(jnp.float32) - (node == start).astype(jnp.float32)
    return maps.astype(jnp.bfloat16)


def halo_at(sizes):
    return sizes.techs + SQUARES


def sums_rows(sizes):
    return (halo_at(sizes) + 2 * sizes.units // LANES + 7) // 8 * 8


def write_halo(sizes, sums_ref, store_new):
    halo, span, rows = halo_at(sizes), sizes.units // LANES, sizes.rows
    write_lanes(sums_ref, halo, store_new[:1])
    write_lanes(sums_ref, halo + span, store_new[rows - 1 :])
    used, end = halo + 2 * span, sums_rows(sizes)
    if used < end:
        sums_ref[used:end, :] = jnp.zeros((end - used, LANES), jnp.float32)


def write_lanes(ref, start, row):
    for i in range(row.shape[1] // LANES):
        ref[start + i : start + i + 1, :] = row[:, i * LANES : (i + 1) * LANES]


def part_copies(source, target, sems):
    rows = source.shape[0] // PARTS
    spans = [pl.ds(part * rows, rows) for part in range(PARTS)]
    return [
        pltpu.make_async_copy(source.at[span], target.at[span], sems.at[part])
        for part, span in enumerate(spans)
    ]


def read_lanes(ref, start, length):
    return jnp.concatenate(
        [ref[start + i : start + i + 1, :] for i in range(length // LANES)], axis=1
    )


def places(sizes):
    span = sizes.units // LANES
    limits = sizes.techs
    energy = limits + (sizes.lines + sizes.units) // LANES
    return Bag(
        limits=limits,
        energy=energy,
        owned=energy + span,
        weight=sizes.techs,
        before=sizes.techs + 1,
        negative=sizes.techs + 1 + span,
    )


def first_kernel(sizes, sources, block_ref, ends_ref, limit_ref, pairs_ref, info_ref, sems):
    rows = sizes.rows
    targets = (block_ref.at[pl.ds(0, rows)], ends_ref, limit_ref, pairs_ref)
    copies = [
        pltpu.make_async_copy(source, target, sems.at[i])
        for i, (source, target) in enumerate(zip(sources, targets))
    ]
    for copy in copies:
        copy.start()
    nodes, slots, regions = sizes.nodes, sizes.slots, sizes.regions
    own = lax.axis_index("region")
    width = slots // regions
    slot = lax.broadcasted_iota(jnp.int32, (1, slots), 1)
    pair = slot // width
    for copy in copies[1:]:
        copy.wait()
    in_use = jnp.zeros((1, slots), jnp.int32)
    for target in range(regions):
        in_use = jnp.where(pair == target, pairs_ref[0:1, target : target + 1], in_use)
    bound = jnp.where(slot % width < in_use, limit_ref[...], 0.0)
    start = (ends_ref[0:1, :] + own * nodes).astype(jnp.float32)
    end = (ends_ref[1:2, :] + pair * nodes).astype(jnp.float32)
    info_ref[...] = jnp.zeros(info_ref.shape, jnp.float32)
    width = min(slots, LANES)
    for chunk in range(slots // width):
        for i, row in enumerate((start, end, bound)):
            at = 8 * chunk + i
            info_ref[at : at + 1, :width] = row[:, chunk * width : (chunk + 1) * width]
    target = block_ref.at[pl.ds(rows, info_ref.shape[0])]
    copy = pltpu.make_async_copy(info_ref, target, sems.at[len(copies)])
    copy.start()
    copies[0].wait()
    copy.wait()


def start_kernel(sizes, names_in, names_out, *refs):
    given = Bag(**dict(zip(names_in, refs[: len(names_in)])))
    gives = Bag(**dict(zip(names_out, refs[len(names_in) : -2])))
    availability, sems = refs[-2:]
    copies = part_copies(given.availability, availability, sems)
    for copy in copies:
        copy.start()
    rows, techs, nodes, lines = sizes.rows, sizes.techs, sizes.nodes, sizes.lines
    at = places(sizes)
    fixed = gives.available.at[techs + 1]
    gives.available[techs] = given.demand[...]
    fixed[:techs, :] = given.gen_cost[...]
    write_lanes(fixed, at.energy, given.store_energy[...])
    owned = given.owner[pl.ds(lax.axis_index("hours"), 1), :]
    fixed[at.owned : at.owned + 1, : owned.shape[1]] = owned.astype(jnp.float32)
    line_ends, stores = given.line_ends[...], given.store_node[...]
    start = jnp.concatenate([line_ends[0:1], jnp.full_like(stores, -1)], axis=1)
    end = jnp.concatenate([line_ends[1:2], stores], axis=1)
    maps = incidence(start, end, nodes)
    limits = jnp.concatenate([given.line_limit[...], given.store_power[...]], axis=1)
    gives.maps_local[...] = maps
    write_lanes(fixed, at.limits, limits)
    prices = given.price[...]
    flows = jnp.clip(-0.5 * dot3(prices, maps, False), -limits, limits)
    gives.flows_local[...] = flows
    store_new = (1.0 / 3.0) * (2.0 * flows[:, lines:])
    gives.store_duals[...] = store_new
    primal_row = fold_lanes(row_sum(flows * flows))
    dual_row = fold_lanes(row_sum(store_new * store_new))
    balance = dot3(2.0 * flows, maps, True) - given.demand[...]
    gen_cost = given.gen_cost[...]
    for copy in copies:
        copy.wait()
    acc = jnp.zeros((rows, nodes), jnp.float32)
    weights = jnp.zeros((techs, nodes), jnp.float32)
    for hour in range(rows):
        weights = weights + availability[hour * techs : (hour + 1) * techs, :]
    for tech in range(techs):
        avail = availability[pl.ds(tech, rows, stride=techs), :]
        gives.available[tech] = avail
        dispatch = jnp.maximum(-0.5 * (gen_cost[tech : tech + 1] + prices), 0.0)
        gives.dispatch[tech] = dispatch
        dispatch_bar = 2.0 * dispatch
        balance = balance + dispatch_bar
        duals = jnp.maximum(0.5 * dispatch_bar, 0.0)
        acc = acc + dispatch * dispatch
        gives.sums[tech : tech + 1, :] = row_sum(avail * duals)
    gives.balance[...] = balance
    squares = row_sum(acc)
    cost = given.cap_cost[...]
    negative = jnp.sum((cost < 0.0).astype(jnp.float32), axis=1, keepdims=True)
    write_halo(sizes, gives.sums, store_new)
    gives.sums[techs : techs + SQUARES, :] = jnp.concatenate(
        [primal_row + squares, dual_row + squares, jnp.broadcast_to(negative, (1, LANES))], axis=0
    )
    tech_hot, node_hot = owned_one_hots(owned, techs, nodes)
    first = sums_rows(sizes)
    gives.sums[first : first + techs, :] = weights
    gives.sums[first + techs : first + 2 * techs, :] = dot3(
        jnp.where(tech_hot, cost, 0.0), node_hot, True
    )


def close_kernel(
    sizes,
    gathered,
    local_ref,
    balance_ref,
    sums_in_ref,
    maps_ref,
    flows_ref,
    block_ref,
):
    rows, techs, nodes = sizes.rows, sizes.techs, sizes.nodes
    slots, regions = sizes.slots, sizes.regions
    own = lax.axis_index("region")
    width = min(slots, LANES)
    info = jnp.concatenate(
        [
            gathered[region, rows + 8 * chunk : rows + 8 * chunk + 8, :width]
            for region in range(regions)
            for chunk in range(slots // width)
        ],
        axis=1,
    )
    maps_ref[...] = incidence(
        info[0:1].astype(jnp.int32), info[1:2].astype(jnp.int32), regions * nodes
    )
    limits = info[2:3]
    prices_all = jnp.concatenate([gathered[region, :rows, :] for region in range(regions)], axis=1)
    flows = jnp.clip(-0.5 * dot3(prices_all, maps_ref[...], False), -limits, limits)
    local = local_ref.shape[1]
    flows_ref[:rows, :local] = local_ref[...]
    flows_ref[:rows, local:] = flows
    flows_ref[rows:, local:] = info
    maps_own = maps_ref[pl.ds(pl.multiple_of(own * nodes, nodes), nodes), :]
    balance = balance_ref[...] + dot3(2.0 * flows, maps_own, True)
    step_up = (1.0 / (techs + 8.0)) * balance
    block_ref[:rows, :] = gathered[own, :rows, :] + step_up
    change = row_sum(flows * flows)
    slot = lax.broadcasted_iota(jnp.int32, change.shape, 1)
    primal = fold_lanes(jnp.where(slot // slots == own, change, 0.0))
    more = jnp.concatenate(
        [primal, row_sum(step_up * step_up), jnp.zeros((SQUARES - 2, LANES), jnp.float32)], axis=0
    )
    block_ref[rows:, :] = sums_in_ref[...]
    block_ref[rows + techs : rows + techs + SQUARES, :] = (
        sums_in_ref[techs : techs + SQUARES, :] + more
    )


def neighbour_rows(sizes, given, hour_index):
    units = sizes.units
    if hasattr(given, "totals"):
        return read_lanes(given.next_row, 0, units), read_lanes(given.prev_row, 0, units)
    first = halo_at(sizes)
    last = first + units // LANES
    core, x_place, odd = hour_index % 2, hour_index // 2 % 2, hour_index // 4 % 2
    next_row = jnp.where(
        odd == 0, read_lanes(given.near, first, units), read_lanes(given.far, first, units)
    )
    prev_row = jnp.where(
        odd == 0, read_lanes(given.far, last, units), read_lanes(given.near, last, units)
    )
    next_row = jnp.where(x_place == 0, read_lanes(given.across, first, units), next_row)
    prev_row = jnp.where(x_place == 0, prev_row, read_lanes(given.across, last, units))
    next_row = jnp.where(core == 0, read_lanes(given.partner, first, units), next_row)
    prev_row = jnp.where(core == 0, prev_row, read_lanes(given.partner, last, units))
    return next_row, prev_row


def total_of(parts):
    if hasattr(parts, "totals"):
        return parts.totals[...]
    return (parts.slab[...] + parts.near[...]) + (parts.middle[...] + parts.far[...])


def slopes_kernel(sizes, names_in, names_out, gathered, maps_local, maps_cross, slopes_ref):
    rows, regions = sizes.rows, sizes.regions
    local = sizes.lines + sizes.units
    prices_all = jnp.concatenate([gathered[region, :rows, :] for region in range(regions)], axis=1)
    prices = gathered[lax.axis_index("region"), :rows, :]
    slopes_ref[:, :local] = dot3(prices, maps_local[...], False)
    slopes_ref[:, local:] = dot3(prices_all, maps_cross[...], False)


def sweep_kernel(sizes, iteration, names_in, names_out, *refs):
    rows, techs, nodes = sizes.rows, sizes.techs, sizes.nodes
    slots, regions, lines, units = sizes.slots, sizes.regions, sizes.lines, sizes.units
    second = iteration == 1
    last = iteration == ITERS - 1
    given = Bag(**dict(zip(names_in, refs[: len(names_in)])))
    gives = Bag(**dict(zip(names_out, refs[len(names_in) :])))
    if last:
        staged, sems = refs[-2:]
    own = lax.axis_index("region")
    hour_index = lax.axis_index("hours")
    gathered = given.gathered

    at = places(sizes)
    fixed = given.available.at[techs + 1]
    small = given.dispatch.at[techs]
    out_sums = None if last else gives.block.at[pl.ds(rows, sums_rows(sizes))]
    sums = total_of(given)
    squares = jnp.sum(sums[techs : techs + 2], axis=1, keepdims=True)
    old_weight = jnp.ones((1, 1), jnp.float32) if second else small[at.weight : at.weight + 1, :1]
    weight = jnp.sqrt(
        old_weight * jnp.sqrt((squares[1:2] + EPSILON) / (squares[0:1] + EPSILON))
    )
    primal_step = 0.5 / weight
    if second:
        first = sums_rows(sizes)
        col_weight, cost = sums[first : first + techs], sums[first + techs : first + 2 * techs]
        negative = sums[techs + 2 : techs + 3]
        capacity = jnp.maximum(-cost / col_weight, 0.0)
        first_bar = 2.0 * capacity
    else:
        col_weight = given.cap_duals[techs, :techs, :]
        cost = given.cap_duals[techs, techs : 2 * techs, :]
        capacity = small[:techs, :]
        negative = small[at.negative : at.negative + 1, :]
    capacity_new = jnp.maximum(capacity - (cost - sums[:techs]) / (weight * col_weight), 0.0)
    capacity_bar = 2.0 * capacity_new - capacity

    prices = gathered[own, :rows, :]
    gen_cost = fixed[:techs, :]
    half_weight = weight / 2.0
    primal_acc = jnp.zeros((rows, nodes), jnp.float32)
    dual_acc = jnp.zeros((rows, nodes), jnp.float32)
    supply = jnp.zeros((rows, nodes), jnp.float32)
    if last:
        copies = part_copies(staged, gives.dispatch, sems)
        count, pieces = rows // PARTS, []
        for part in range(PARTS):
            hours = slice(part * count, (part + 1) * count)
            piece = jnp.zeros((count, nodes), jnp.float32)
            for tech in range(techs):
                slope = gen_cost[tech : tech + 1] + prices[hours]
                dispatch = given.dispatch[tech, hours, :]
                duals = given.cap_duals[tech, hours, :]
                dispatch_new = jnp.maximum(dispatch - primal_step * (slope + duals), 0.0)
                piece = piece + (2.0 * dispatch_new - dispatch)
                staged[pl.ds(part * count * techs + tech, count, stride=techs), :] = dispatch_new
            copies[part].start()
            pieces.append(piece)
        supply = jnp.concatenate(pieces, axis=0)
    for tech in range(0 if last else techs):
        slope = gen_cost[tech : tech + 1] + prices
        dispatch = given.dispatch[tech]
        avail = given.available[tech]
        if second:
            duals = jnp.maximum(0.5 * (2.0 * dispatch - avail * first_bar[tech : tech + 1]), 0.0)
        else:
            duals = given.cap_duals[tech]
        dispatch_new = jnp.maximum(dispatch - primal_step * (slope + duals), 0.0)
        dispatch_bar = 2.0 * dispatch_new - dispatch
        supply = supply + dispatch_bar
        gives.dispatch[tech] = dispatch_new
        cap_rows = dispatch_bar - avail * capacity_bar[tech : tech + 1]
        primal_acc = primal_acc + (dispatch_new - dispatch) ** 2
        duals_new = jnp.maximum(duals + half_weight * cap_rows, 0.0)
        dual_acc = dual_acc + (duals_new - duals) ** 2
        gives.cap_duals[tech] = duals_new
        out_sums[tech : tech + 1, :] = row_sum(avail * duals_new)

    maps_local = given.maps_local[...]

    energy = read_lanes(fixed, at.energy, units)
    row_id = lax.broadcasted_iota(jnp.int32, (rows, units), 0)
    next_row, prev_row = neighbour_rows(sizes, given, hour_index)
    store_duals = given.store_duals[...]
    next_duals = jnp.where(row_id == rows - 1, next_row, pltpu.roll(store_duals, rows - 1, 0))
    if second:
        charge = jnp.zeros((rows, units), jnp.float32)
        charge_before = jnp.zeros((1, units), jnp.float32)
    else:
        charge = given.charge[...]
        charge_before = read_lanes(small, at.before, units)
    charge_new = jnp.clip(charge - primal_step * (store_duals - next_duals), 0.0, energy)
    gives.charge[...] = charge_new

    primal_row = jnp.zeros((1, LANES), jnp.float32)
    bars = []
    local, total_flows = lines + units, lines + units + regions * slots
    local_limits = read_lanes(fixed, at.limits, local)
    cross_limits = given.flows[rows + 2 : rows + 3, local:]
    for bound, low, high in (
        (local_limits[:, :lines], 0, lines),
        (local_limits[:, lines:], lines, local),
        (cross_limits, local, total_flows),
    ):
        slope = given.slopes[:, low:high]
        if low == lines:
            slope = slope + store_duals
        old = given.flows[:rows, low:high]
        new = jnp.clip(old - primal_step * slope, -bound, bound)
        bars.append(2.0 * new - old)
        if not last:
            gives.flows[:rows, low:high] = new
            change = row_sum((new - old) ** 2)
            if low == local:
                slot = lax.broadcasted_iota(jnp.int32, change.shape, 1)
                change = jnp.where(slot // slots == own, change, 0.0)
            primal_row = primal_row + fold_lanes(change)
    maps_own = given.maps_cross[pl.ds(pl.multiple_of(own * nodes, nodes), nodes), :]
    balance = dot3(jnp.concatenate(bars[:2], axis=1), maps_local, True) - given.available[techs]
    balance = balance + supply + dot3(bars[2], maps_own, True)

    step_up = weight / (techs + 8.0) * balance
    if last:
        gives.prices[...] = prices + step_up
        owned = fixed[at.owned : at.owned + 1, : gives.capacity.shape[1]].astype(jnp.int32)
        tech_hot, node_hot = owned_one_hots(owned, techs, nodes)
        chosen = dot3(capacity_new, node_hot, False)
        gives.capacity[...] = row_sum(jnp.where(tech_hot, chosen, 0.0))
        gives.negative[...] = negative
        gives.kept[:rows, :] = fixed[...]
        gives.kept[rows : rows + techs, :] = col_weight
        gives.kept[rows + techs : rows + 2 * techs, :] = cost
        for chunk in range(regions * slots // LANES):
            low = local + chunk * LANES
            first = rows + 2 * techs + 8 * chunk
            gives.kept[first : first + 8, :] = given.flows[rows:, low : low + LANES]
        for copy in copies:
            copy.wait()
        return
    gives.block[:rows, :] = prices + step_up
    gives.flows[rows:, local:] = given.flows[rows:, local:]
    gives.cap_duals[techs, :techs, :] = col_weight
    gives.cap_duals[techs, techs : 2 * techs, :] = cost
    small_new = gives.dispatch.at[techs]
    small_new[:techs, :] = capacity_new
    small_new[at.weight : at.weight + 1, :] = jnp.broadcast_to(weight, (1, LANES))
    small_new[at.negative : at.negative + 1, :] = negative
    charge_bar = 2.0 * charge_new - charge
    before_new = jnp.clip(charge_before - primal_step * (prev_row - store_duals[0:1]), 0.0, energy)
    write_lanes(small_new, at.before, before_new)
    before_bar = 2.0 * before_new - charge_before
    shifted_bar = jnp.where(row_id == 0, before_bar, pltpu.roll(charge_bar, 1, 0))
    store_step = weight / 3.0 * (charge_bar - shifted_bar + bars[1])
    store_new = store_duals + store_step
    gives.store_duals[...] = store_new
    primal_row = primal_row + row_sum(primal_acc) + fold_lanes(row_sum((charge_new - charge) ** 2))
    primal_row = primal_row + jnp.where(
        hour_index == 0, row_sum((capacity_new - capacity) ** 2), 0.0
    )
    dual_row = row_sum(dual_acc + step_up * step_up) + fold_lanes(row_sum(store_step * store_step))
    squares = jnp.concatenate(
        [primal_row, dual_row, jnp.zeros((SQUARES - 2, LANES), jnp.float32)], axis=0
    )
    out_sums[techs : techs + SQUARES, :] = squares
    write_halo(sizes, out_sums, store_new)


def call(kernel, given, outs, flops=0, left=(), scratch=(), limit=VMEM_BYTES, copied=0):
    names_in, names_out = tuple(vars(given)), tuple(vars(outs))
    values = pl.pallas_call(
        functools.partial(kernel, names_in, names_out),
        out_shape=tuple(vars(outs).values()),
        in_specs=[
            pl.BlockSpec(memory_space=pl.ANY if i in left else pltpu.VMEM)
            for i in range(len(names_in))
        ],
        out_specs=[
            pl.BlockSpec(memory_space=pl.ANY if i < copied else pltpu.VMEM)
            for i in range(len(names_out))
        ],
        scratch_shapes=scratch,
        cost_estimate=pl.CostEstimate(flops=flops, bytes_accessed=4 * flops, transcendentals=0),
        compiler_params=pltpu.CompilerParams(vmem_limit_bytes=limit),
    )(*vars(given).values())
    return Bag(**dict(zip(names_out, values)))


def swap(value, hour_bit, region_bit):
    hours, regions = lax.axis_size("hours"), lax.axis_size("region")
    pairs = [
        (hour * regions + region, (hour ^ hour_bit) * regions + (region ^ region_bit))
        for hour in range(hours)
        for region in range(regions)
    ]
    return lax.ppermute(value, ("hours", "region"), pairs)


def shifted(value, steps):
    count = lax.axis_size("hours")
    return lax.ppermute(value, "hours", [(i, (i + steps) % count) for i in range(count)])


def both_regions(block):
    if lax.axis_size("region") != 2:
        return lax.all_gather(block, "region")
    return in_order(block, swap(block, 0, 1))


def in_order(block, other):
    return jnp.where(
        lax.axis_index("region") == 0, jnp.stack([block, other]), jnp.stack([other, block])
    )


def exchange(sizes, block):
    hours, regions = lax.axis_size("hours"), lax.axis_size("region")
    techs, span = sizes.techs, sizes.units // LANES
    halo = halo_at(sizes)
    prices, sums = block[: sizes.rows], block[sizes.rows :]
    if regions != 2 or hours != 16:
        gathered = lax.all_gather(prices, "region")
        totals = lax.psum(sums, "hours")
        totals = totals.at[techs:halo].set(lax.psum(totals[techs:halo], "region"))
        next_row = shifted(sums[halo : halo + span], -1)
        prev_row = shifted(sums[halo + span : halo + 2 * span], 1)
        return gathered, Bag(totals=totals, next_row=next_row, prev_row=prev_row)

    def merged(mine, yours, mine_first):
        last = halo + span
        edges = [
            jnp.where(mine_first, mine[halo:last], yours[halo:last]),
            jnp.where(mine_first, yours[last : last + span], mine[last : last + span]),
        ]
        total = mine + yours
        return jnp.concatenate([total[:halo], *edges, total[last + span :]], axis=0)

    hour = lax.axis_index("hours")
    beside_core = swap(block, 1, 0)
    partner_prices, partner = beside_core[: sizes.rows], beside_core[sizes.rows :]
    chip = merged(sums, partner, hour % 2 == 0)
    across = swap(chip, 2 + 1, 0)
    diagonal = swap(chip[techs:halo], 2 + 1, 1)
    beside = swap(jnp.concatenate([partner_prices, chip[techs:halo]], axis=0), 1, 1)
    other, squares = beside[: sizes.rows], beside[sizes.rows :]
    slab = merged(chip, across, hour // 2 % 2 == 0)
    slab = slab + jnp.pad(squares + diagonal, ((techs, slab.shape[0] - halo), (0, 0)))
    near, middle, far = [swap(slab, 4 * step + 1, 0) for step in (1, 2, 3)]
    parts = Bag(slab=slab, near=near, middle=middle, far=far, partner=partner, across=across)
    return in_order(prices, other), parts


def shape(*dims, dtype=jnp.float32):
    return jax.ShapeDtypeStruct(dims, dtype)


def restarted(sizes, kept, args):
    rows, techs, nodes, lines = sizes.rows, sizes.techs, sizes.nodes, sizes.lines
    local, cross = lines + sizes.units, sizes.regions * sizes.slots
    at, own = places(sizes), lax.axis_index("region")
    first_hour = lax.axis_index("hours") == 0
    price_start = args.price_start
    available = args.availability.transpose(1, 0, 2)
    fixed, last = kept[:rows], rows + 2 * techs
    col_weight, cost = kept[rows : rows + techs], kept[rows + techs : last]
    info = kept[last:].reshape(-1, 8, LANES).transpose(1, 0, 2).reshape(8, cross)
    local_limits = fixed[at.limits : at.energy].reshape(1, local)
    cross_limits = info[2:3]
    ends = info[:2].astype(jnp.int32)
    maps_cross_low = incidence(ends[:1], ends[1:], sizes.regions * nodes)
    stores = args.store_node[None]
    maps_local_low = incidence(
        jnp.concatenate([args.line_ends[:1], jnp.full_like(stores, -1)], axis=1),
        jnp.concatenate([args.line_ends[1:], stores], axis=1),
        nodes,
    )
    maps_local = maps_local_low.astype(jnp.float32)
    maps_cross = maps_cross_low.astype(jnp.float32)
    maps_own = lax.dynamic_slice_in_dim(maps_cross, own * nodes, nodes)
    prices_all = jnp.concatenate(list(both_regions(price_start)), axis=1)
    highest = lax.Precision.HIGHEST

    capacity = jnp.maximum(-cost / col_weight, 0.0)
    slopes = fixed[:techs][:, None, :] + price_start[None]
    dispatch = jnp.maximum(-0.5 * slopes, 0.0)
    slope = jnp.dot(price_start, maps_local, precision=highest)
    flows_local = jnp.clip(-0.5 * slope, -local_limits, local_limits)
    slope = jnp.dot(prices_all, maps_cross, precision=highest)
    flows_cross = jnp.clip(-0.5 * slope, -cross_limits, cross_limits)
    balance = (
        jnp.sum(2.0 * dispatch, axis=0)
        + jnp.dot(2.0 * flows_local, maps_local.T, precision=highest)
        + jnp.dot(2.0 * flows_cross, maps_own.T, precision=highest)
        - args.demand
    )
    step_up = balance / (techs + 8.0)
    duals = jnp.maximum(0.5 * (2.0 * dispatch - available * (2.0 * capacity)[:, None, :]), 0.0)
    store_duals = 2.0 * flows_local[:, lines:] / 3.0
    slot = lax.broadcasted_iota(jnp.int32, (1, cross), 1) // sizes.slots
    primal = (
        jnp.sum(dispatch**2)
        + jnp.sum(flows_local**2)
        + jnp.sum(jnp.where(slot == own, flows_cross**2, 0.0))
        + jnp.where(first_hour, jnp.sum(capacity**2), 0.0)
    )
    dual = jnp.sum(step_up**2) + jnp.sum(duals**2) + jnp.sum(store_duals**2)
    rows_of = [
        jnp.sum(available * duals, axis=1),
        jnp.zeros((SQUARES, nodes)).at[0, 0].set(primal).at[1, 0].set(dual),
        store_duals[:1].reshape(-1, LANES),
        store_duals[rows - 1 :].reshape(-1, LANES),
    ]
    used = halo_at(sizes) + 2 * sizes.units // LANES
    rows_of.append(jnp.zeros((sums_rows(sizes) - used, nodes)))
    rows_of += [jnp.where(first_hour, part, 0.0) for part in (col_weight, cost)]
    block = jnp.concatenate([price_start + step_up, *rows_of], axis=0)
    gathered, parts = exchange(sizes, block)
    flows = jnp.concatenate([flows_local, flows_cross], axis=1)
    spare = jnp.concatenate([jnp.zeros((8, local)), info], axis=1)
    state = Bag(
        available=jnp.concatenate([available, args.demand[None], fixed[None]], axis=0),
        maps_local=maps_local_low,
        maps_cross=maps_cross_low,
        store_duals=store_duals,
        dispatch=jnp.concatenate([dispatch, jnp.zeros((1, rows, nodes))], axis=0),
        flows=jnp.concatenate([flows, spare], axis=0),
    )
    return state, gathered, parts


def run(args):
    rows, techs, nodes = args.availability.shape
    hours, regions = lax.axis_size("hours"), lax.axis_size("region")
    slots, owned = args.cross_limit.shape[1], args.cap_cost.shape[1]
    units, lines = args.store_node.shape[0], args.line_limit.shape[0]
    sizes = Bag(
        rows=rows, techs=techs, nodes=nodes, regions=regions, slots=slots, lines=lines, units=units
    )
    cross = regions * slots

    gathered = both_regions(
        call(
            lambda names_in, names_out, *refs: first_kernel(sizes, refs[:4], *refs[4:]),
            Bag(
                price=args.price_start,
                ends=args.cross_ends[:, 0],
                limit=args.cross_limit,
                pairs=args.pair_counts,
            ),
            Bag(block=shape(rows + 8 * max(1, slots // LANES), nodes)),
            left=(0, 1, 2, 3),
            scratch=[
                pltpu.VMEM((2, slots), jnp.int32),
                pltpu.VMEM((1, slots), jnp.float32),
                pltpu.VMEM((1, regions), jnp.int32),
                pltpu.VMEM((8 * max(1, slots // LANES), nodes), jnp.float32),
                pltpu.SemaphoreType.DMA((5,)),
            ],
            limit=None,
            copied=1,
        ).block
    )
    state = call(
        functools.partial(start_kernel, sizes),
        Bag(
            availability=args.availability.reshape(rows * techs, nodes),
            price=args.price_start,
            demand=args.demand,
            gen_cost=args.gen_cost,
            cap_cost=args.cap_cost,
            owner=args.owner_map.reshape(hours, owned),
            line_ends=args.line_ends,
            line_limit=args.line_limit[None],
            store_node=args.store_node[None],
            store_power=args.store_power[None],
            store_energy=args.store_energy[None],
        ),
        Bag(
            available=shape(techs + 2, rows, nodes),
            maps_local=shape(nodes, lines + units, dtype=jnp.bfloat16),
            flows_local=shape(rows, lines + units),
            store_duals=shape(rows, units),
            dispatch=shape(techs + 1, rows, nodes),
            balance=shape(rows, nodes),
            sums=shape(sums_rows(sizes) + 2 * techs, nodes),
        ),
        flops=10**6,
        left=(0,),
        scratch=[
            pltpu.VMEM((rows * techs, nodes), jnp.float32),
            pltpu.SemaphoreType.DMA((PARTS,)),
        ],
    )
    closed = call(
        lambda names_in, names_out, *refs: close_kernel(sizes, *refs),
        Bag(
            gathered=gathered,
            flows_local=state.flows_local,
            balance=state.balance,
            sums=state.sums,
        ),
        Bag(
            maps=shape(regions * nodes, cross, dtype=jnp.bfloat16),
            flows=shape(rows + 8, lines + units + cross),
            block=shape(rows + state.sums.shape[0], nodes),
        ),
    )
    del state.sums, state.balance, state.flows_local
    state.maps_cross, state.flows = closed.maps, closed.flows
    gathered, parts = exchange(sizes, closed.block)
    outputs, negative, kept = sweeps(sizes, owned, state, gathered, parts)

    def again():
        return sweeps(sizes, owned, *restarted(sizes, kept, args))[0]

    return lax.cond(negative > 0.0, again, lambda: outputs)


def sweeps(sizes, owned, state, gathered, parts):
    rows, techs, nodes, lines, units = (
        sizes.rows,
        sizes.techs,
        sizes.nodes,
        sizes.lines,
        sizes.units,
    )
    state = Bag(**vars(state))
    for iteration in range(1, ITERS):
        slopes = call(
            functools.partial(slopes_kernel, sizes),
            Bag(gathered=gathered, maps_local=state.maps_local, maps_cross=state.maps_cross),
            Bag(slopes=shape(rows, lines + units + sizes.regions * sizes.slots)),
        ).slopes
        given = Bag(**vars(state), **vars(parts), gathered=gathered, slopes=slopes)
        if iteration < ITERS - 1:
            outs = Bag(
                dispatch=shape(techs + 1, rows, nodes),
                cap_duals=shape(techs + 1, rows, nodes),
                flows=shape(rows + 8, lines + units + sizes.regions * sizes.slots),
                store_duals=shape(rows, units),
                charge=shape(rows, units),
                block=shape(rows + sums_rows(sizes), nodes),
            )
        else:
            outs = Bag(
                dispatch=shape(rows * techs, nodes),
                capacity=shape(1, owned),
                prices=shape(rows, nodes),
                charge=shape(rows, units),
                negative=shape(1, LANES),
                kept=shape(rows + 2 * techs + 8 * (sizes.regions * sizes.slots // LANES), LANES),
            )
        final = iteration == ITERS - 1
        results = call(
            functools.partial(sweep_kernel, sizes, iteration),
            given,
            outs,
            copied=int(final),
            scratch=[
                pltpu.VMEM(outs.dispatch.shape, jnp.float32),
                pltpu.SemaphoreType.DMA((PARTS,)),
            ]
            if final
            else [],
        )
        if iteration < ITERS - 1:
            gathered, parts = exchange(sizes, results.block)
            del results.block
            vars(state).update(vars(results))
    dispatch = results.dispatch.reshape(rows, techs, nodes)
    outputs = (dispatch, results.capacity, results.prices, results.charge)
    return outputs, results.negative[0, 0], results.kept


def body(
    availability,
    demand,
    gen_cost,
    cap_cost,
    owner_map,
    line_ends,
    line_limit,
    cross_ends,
    cross_limit,
    pair_counts,
    store_node,
    store_energy,
    store_power,
    price_start,
):
    args = Bag(**locals())
    return run(args)


def solution(mesh):
    placed = (
        P("hours", None, "region"),
        P("hours", "region"),
        P(None, "region"),
        P("region", "hours"),
        P("region", None),
        P(None, "region"),
        P("region"),
        P(None, "region", None),
        P("region", None),
        P("region", None),
        P("region"),
        P("region"),
        P("region"),
        P("hours", "region"),
    )
    return jax.shard_map(
        body,
        mesh=mesh,
        in_specs=placed,
        out_specs=(
            P("hours", None, "region"),
            P("region", "hours"),
            P("hours", "region"),
            P("hours", "region"),
        ),
        check_vma=False,
    )
```

```python
import functools
from types import SimpleNamespace as Bag

import jax
import jax.numpy as jnp
from jax import lax
from jax.experimental import pallas as pl
from jax.experimental.pallas import tpu as pltpu
from jax.sharding import PartitionSpec as P

ITERS = 4
EPSILON = 1e-06
LANES = 128
VMEM_BYTES = 24 * 1024 * 1024
FIRST_BYTES = 56 * 1024 * 1024
PARTS = 4
SQUARES = 3


def split3(value):
    high = value.astype(jnp.bfloat16)
    rest = value - high.astype(jnp.float32)
    middle = rest.astype(jnp.bfloat16)
    low = (rest - middle.astype(jnp.float32)).astype(jnp.bfloat16)
    return jnp.concatenate([high, middle, low], axis=0)


def dot3(value, matrix, transposed):
    rows = value.shape[0]
    contract = ((1,), (1 if transposed else 0,))
    product = lax.dot_general(
        split3(value), matrix, (contract, ((), ())), preferred_element_type=jnp.float32
    )
    return product[:rows] + product[rows : 2 * rows] + product[2 * rows :]


def row_sum(value):
    return jnp.sum(value, axis=0, keepdims=True)


def fold_lanes(row):
    total = row[:, :LANES]
    for start in range(LANES, row.shape[1], LANES):
        total = total + row[:, start : start + LANES]
    return total


def owned_one_hots(owned, tech_count, node_count):
    shape_t = (tech_count, owned.shape[1])
    shape_n = (node_count, owned.shape[1])
    tech = lax.broadcasted_iota(jnp.int32, shape_t, 0) == owned // node_count
    node = lax.broadcasted_iota(jnp.int32, shape_n, 0) == owned % node_count
    return tech, node.astype(jnp.float32).astype(jnp.bfloat16)


def incidence(start, end, count):
    node = lax.broadcasted_iota(jnp.int32, (count, start.shape[1]), 0)
    maps = (node == end).astype(jnp.float32) - (node == start).astype(jnp.float32)
    return maps.astype(jnp.bfloat16)


def halo_at(sizes):
    return sizes.techs + SQUARES


def sums_rows(sizes):
    return (halo_at(sizes) + 2 * sizes.units // LANES + 7) // 8 * 8


def write_halo(sizes, sums_ref, store_new):
    halo, span, rows = halo_at(sizes), sizes.units // LANES, sizes.rows
    write_lanes(sums_ref, halo, store_new[:1])
    write_lanes(sums_ref, halo + span, store_new[rows - 1 :])
    used, end = halo + 2 * span, sums_rows(sizes)
    if used < end:
        sums_ref[used:end, :] = jnp.zeros((end - used, LANES), jnp.float32)


def write_lanes(ref, start, row):
    for i in range(row.shape[1] // LANES):
        ref[start + i : start + i + 1, :] = row[:, i * LANES : (i + 1) * LANES]


def part_copies(source, target, sems):
    rows = source.shape[0] // PARTS
    spans = [pl.ds(part * rows, rows) for part in range(PARTS)]
    return [
        pltpu.make_async_copy(source.at[span], target.at[span], sems.at[part])
        for part, span in enumerate(spans)
    ]


def read_lanes(ref, start, length):
    return jnp.concatenate(
        [ref[start + i : start + i + 1, :] for i in range(length // LANES)], axis=1
    )


def places(sizes):
    span = sizes.units // LANES
    limits = sizes.techs
    energy = limits + (sizes.lines + sizes.units) // LANES
    return Bag(
        limits=limits,
        energy=energy,
        owned=energy + span,
        weight=sizes.techs,
        before=sizes.techs + 1,
        negative=sizes.techs + 1 + span,
    )


def first_kernel(sizes, sources, block_ref, ends_ref, limit_ref, pairs_ref, sems):
    rows = sizes.rows
    targets = (block_ref.at[pl.ds(0, rows)], ends_ref, limit_ref, pairs_ref)
    copies = [
        pltpu.make_async_copy(source, target, sems.at[i])
        for i, (source, target) in enumerate(zip(sources, targets))
    ]
    for copy in copies:
        copy.start()
    nodes, slots, regions = sizes.nodes, sizes.slots, sizes.regions
    own = lax.axis_index("region")
    width = slots // regions
    slot = lax.broadcasted_iota(jnp.int32, (1, slots), 1)
    pair = slot // width
    for copy in copies[1:]:
        copy.wait()
    in_use = jnp.zeros((1, slots), jnp.int32)
    for target in range(regions):
        in_use = jnp.where(pair == target, pairs_ref[0:1, target : target + 1], in_use)
    bound = jnp.where(slot % width < in_use, limit_ref[...], 0.0)
    start = (ends_ref[0:1, :] + own * nodes).astype(jnp.float32)
    end = (ends_ref[1:2, :] + pair * nodes).astype(jnp.float32)
    block_ref[rows:, :] = jnp.zeros((block_ref.shape[0] - rows, LANES), jnp.float32)
    width = min(slots, LANES)
    for chunk in range(slots // width):
        at = rows + 8 * chunk
        for i, row in enumerate((start, end, bound)):
            block_ref[at + i : at + i + 1, :width] = row[:, chunk * width : (chunk + 1) * width]
    copies[0].wait()


def start_kernel(sizes, names_in, names_out, *refs):
    given = Bag(**dict(zip(names_in, refs[: len(names_in)])))
    gives = Bag(**dict(zip(names_out, refs[len(names_in) : -2])))
    availability, sem = refs[-2:]
    copy = pltpu.make_async_copy(given.availability, availability, sem)
    copy.start()
    rows, techs, nodes, lines = sizes.rows, sizes.techs, sizes.nodes, sizes.lines
    at = places(sizes)
    fixed = gives.available.at[techs + 1]
    gives.available[techs] = given.demand[...]
    fixed[:techs, :] = given.gen_cost[...]
    write_lanes(fixed, at.energy, given.store_energy[...])
    owned = given.owner[pl.ds(lax.axis_index("hours"), 1), :]
    fixed[at.owned : at.owned + 1, : owned.shape[1]] = owned.astype(jnp.float32)
    line_ends, stores = given.line_ends[...], given.store_node[...]
    start = jnp.concatenate([line_ends[0:1], jnp.full_like(stores, -1)], axis=1)
    end = jnp.concatenate([line_ends[1:2], stores], axis=1)
    maps = incidence(start, end, nodes)
    limits = jnp.concatenate([given.line_limit[...], given.store_power[...]], axis=1)
    gives.maps_local[...] = maps
    write_lanes(fixed, at.limits, limits)
    prices = given.price[...]
    flows = jnp.clip(-0.5 * dot3(prices, maps, False), -limits, limits)
    gives.flows_local[...] = flows
    store_new = (1.0 / 3.0) * (2.0 * flows[:, lines:])
    gives.store_duals[...] = store_new
    primal_row = fold_lanes(row_sum(flows * flows))
    dual_row = fold_lanes(row_sum(store_new * store_new))
    balance = dot3(2.0 * flows, maps, True) - given.demand[...]
    gen_cost = given.gen_cost[...]
    copy.wait()
    acc = jnp.zeros((rows, nodes), jnp.float32)
    weights = jnp.zeros((techs, nodes), jnp.float32)
    for hour in range(rows):
        weights = weights + availability[hour * techs : (hour + 1) * techs, :]
    for tech in range(techs):
        avail = availability[pl.ds(tech, rows, stride=techs), :]
        gives.available[tech] = avail
        dispatch = jnp.maximum(-0.5 * (gen_cost[tech : tech + 1] + prices), 0.0)
        gives.dispatch[tech] = dispatch
        dispatch_bar = 2.0 * dispatch
        balance = balance + dispatch_bar
        duals = jnp.maximum(0.5 * dispatch_bar, 0.0)
        acc = acc + dispatch * dispatch
        gives.sums[tech : tech + 1, :] = row_sum(avail * duals)
    gives.balance[...] = balance
    squares = row_sum(acc)
    cost = given.cap_cost[...]
    negative = jnp.sum((cost < 0.0).astype(jnp.float32), axis=1, keepdims=True)
    write_halo(sizes, gives.sums, store_new)
    gives.sums[techs : techs + SQUARES, :] = jnp.concatenate(
        [primal_row + squares, dual_row + squares, jnp.broadcast_to(negative, (1, LANES))], axis=0
    )
    tech_hot, node_hot = owned_one_hots(owned, techs, nodes)
    first = sums_rows(sizes)
    gives.sums[first : first + techs, :] = weights
    gives.sums[first + techs : first + 2 * techs, :] = dot3(
        jnp.where(tech_hot, cost, 0.0), node_hot, True
    )


def close_kernel(
    sizes,
    gathered,
    local_ref,
    balance_ref,
    sums_in_ref,
    maps_ref,
    flows_ref,
    block_ref,
):
    rows, techs, nodes = sizes.rows, sizes.techs, sizes.nodes
    slots, regions = sizes.slots, sizes.regions
    own = lax.axis_index("region")
    width = min(slots, LANES)
    info = jnp.concatenate(
        [
            gathered[region, rows + 8 * chunk : rows + 8 * chunk + 8, :width]
            for region in range(regions)
            for chunk in range(slots // width)
        ],
        axis=1,
    )
    maps_ref[...] = incidence(
        info[0:1].astype(jnp.int32), info[1:2].astype(jnp.int32), regions * nodes
    )
    limits = info[2:3]
    prices_all = jnp.concatenate([gathered[region, :rows, :] for region in range(regions)], axis=1)
    flows = jnp.clip(-0.5 * dot3(prices_all, maps_ref[...], False), -limits, limits)
    local = local_ref.shape[1]
    flows_ref[:rows, :local] = local_ref[...]
    flows_ref[:rows, local:] = flows
    flows_ref[rows:, local:] = info
    maps_own = maps_ref[pl.ds(pl.multiple_of(own * nodes, nodes), nodes), :]
    balance = balance_ref[...] + dot3(2.0 * flows, maps_own, True)
    step_up = (1.0 / (techs + 8.0)) * balance
    block_ref[:rows, :] = gathered[own, :rows, :] + step_up
    change = row_sum(flows * flows)
    slot = lax.broadcasted_iota(jnp.int32, change.shape, 1)
    primal = fold_lanes(jnp.where(slot // slots == own, change, 0.0))
    more = jnp.concatenate(
        [primal, row_sum(step_up * step_up), jnp.zeros((SQUARES - 2, LANES), jnp.float32)], axis=0
    )
    block_ref[rows:, :] = sums_in_ref[...]
    block_ref[rows + techs : rows + techs + SQUARES, :] = (
        sums_in_ref[techs : techs + SQUARES, :] + more
    )


def neighbour_rows(sizes, given, hour_index):
    units = sizes.units
    if hasattr(given, "totals"):
        return read_lanes(given.next_row, 0, units), read_lanes(given.prev_row, 0, units)
    first = halo_at(sizes)
    last = first + units // LANES
    core, x_place, odd = hour_index % 2, hour_index // 2 % 2, hour_index // 4 % 2
    next_row = jnp.where(
        odd == 0, read_lanes(given.near, first, units), read_lanes(given.far, first, units)
    )
    prev_row = jnp.where(
        odd == 0, read_lanes(given.far, last, units), read_lanes(given.near, last, units)
    )
    next_row = jnp.where(x_place == 0, read_lanes(given.across, first, units), next_row)
    prev_row = jnp.where(x_place == 0, prev_row, read_lanes(given.across, last, units))
    next_row = jnp.where(core == 0, read_lanes(given.partner, first, units), next_row)
    prev_row = jnp.where(core == 0, prev_row, read_lanes(given.partner, last, units))
    return next_row, prev_row


def total_of(parts):
    if hasattr(parts, "totals"):
        return parts.totals[...]
    return (parts.slab[...] + parts.near[...]) + (parts.middle[...] + parts.far[...])


def slopes_kernel(sizes, names_in, names_out, gathered, maps_local, maps_cross, slopes_ref):
    rows, regions = sizes.rows, sizes.regions
    local = sizes.lines + sizes.units
    prices_all = jnp.concatenate([gathered[region, :rows, :] for region in range(regions)], axis=1)
    prices = gathered[lax.axis_index("region"), :rows, :]
    slopes_ref[:, :local] = dot3(prices, maps_local[...], False)
    slopes_ref[:, local:] = dot3(prices_all, maps_cross[...], False)


def sweep_kernel(sizes, iteration, names_in, names_out, *refs):
    rows, techs, nodes = sizes.rows, sizes.techs, sizes.nodes
    slots, regions, lines, units = sizes.slots, sizes.regions, sizes.lines, sizes.units
    second = iteration == 1
    last = iteration == ITERS - 1
    given = Bag(**dict(zip(names_in, refs[: len(names_in)])))
    gives = Bag(**dict(zip(names_out, refs[len(names_in) :])))
    if last:
        staged, sems = refs[-2:]
    own = lax.axis_index("region")
    hour_index = lax.axis_index("hours")
    gathered = given.gathered

    at = places(sizes)
    fixed = given.available.at[techs + 1]
    small = given.dispatch.at[techs]
    out_sums = None if last else gives.block.at[pl.ds(rows, sums_rows(sizes))]
    sums = total_of(given)
    squares = jnp.sum(sums[techs : techs + 2], axis=1, keepdims=True)
    old_weight = jnp.ones((1, 1), jnp.float32) if second else small[at.weight : at.weight + 1, :1]
    weight = jnp.sqrt(
        old_weight * jnp.sqrt((squares[1:2] + EPSILON) / (squares[0:1] + EPSILON))
    )
    primal_step = 0.5 / weight
    if second:
        first = sums_rows(sizes)
        col_weight, cost = sums[first : first + techs], sums[first + techs : first + 2 * techs]
        negative = sums[techs + 2 : techs + 3]
        capacity = jnp.maximum(-cost / col_weight, 0.0)
        first_bar = 2.0 * capacity
    else:
        col_weight = given.cap_duals[techs, :techs, :]
        cost = given.cap_duals[techs, techs : 2 * techs, :]
        capacity = small[:techs, :]
        negative = small[at.negative : at.negative + 1, :]
    capacity_new = jnp.maximum(capacity - (cost - sums[:techs]) / (weight * col_weight), 0.0)
    capacity_bar = 2.0 * capacity_new - capacity

    prices = gathered[own, :rows, :]
    gen_cost = fixed[:techs, :]
    half_weight = weight / 2.0
    primal_acc = jnp.zeros((rows, nodes), jnp.float32)
    dual_acc = jnp.zeros((rows, nodes), jnp.float32)
    supply = jnp.zeros((rows, nodes), jnp.float32)
    if last:
        copies = part_copies(staged, gives.dispatch, sems)
        count, pieces = rows // PARTS, []
        for part in range(PARTS):
            hours = slice(part * count, (part + 1) * count)
            piece = jnp.zeros((count, nodes), jnp.float32)
            for tech in range(techs):
                slope = gen_cost[tech : tech + 1] + prices[hours]
                dispatch = given.dispatch[tech, hours, :]
                duals = given.cap_duals[tech, hours, :]
                dispatch_new = jnp.maximum(dispatch - primal_step * (slope + duals), 0.0)
                piece = piece + (2.0 * dispatch_new - dispatch)
                staged[pl.ds(part * count * techs + tech, count, stride=techs), :] = dispatch_new
            copies[part].start()
            pieces.append(piece)
        supply = jnp.concatenate(pieces, axis=0)
    for tech in range(0 if last else techs):
        slope = gen_cost[tech : tech + 1] + prices
        dispatch = given.dispatch[tech]
        avail = given.available[tech]
        if second:
            duals = jnp.maximum(0.5 * (2.0 * dispatch - avail * first_bar[tech : tech + 1]), 0.0)
        else:
            duals = given.cap_duals[tech]
        dispatch_new = jnp.maximum(dispatch - primal_step * (slope + duals), 0.0)
        dispatch_bar = 2.0 * dispatch_new - dispatch
        supply = supply + dispatch_bar
        gives.dispatch[tech] = dispatch_new
        cap_rows = dispatch_bar - avail * capacity_bar[tech : tech + 1]
        primal_acc = primal_acc + (dispatch_new - dispatch) ** 2
        duals_new = jnp.maximum(duals + half_weight * cap_rows, 0.0)
        dual_acc = dual_acc + (duals_new - duals) ** 2
        gives.cap_duals[tech] = duals_new
        out_sums[tech : tech + 1, :] = row_sum(avail * duals_new)

    maps_local = given.maps_local[...]

    energy = read_lanes(fixed, at.energy, units)
    row_id = lax.broadcasted_iota(jnp.int32, (rows, units), 0)
    next_row, prev_row = neighbour_rows(sizes, given, hour_index)
    store_duals = given.store_duals[...]
    next_duals = jnp.where(row_id == rows - 1, next_row, pltpu.roll(store_duals, rows - 1, 0))
    if second:
        charge = jnp.zeros((rows, units), jnp.float32)
        charge_before = jnp.zeros((1, units), jnp.float32)
    else:
        charge = given.charge[...]
        charge_before = read_lanes(small, at.before, units)
    charge_new = jnp.clip(charge - primal_step * (store_duals - next_duals), 0.0, energy)
    gives.charge[...] = charge_new

    primal_row = jnp.zeros((1, LANES), jnp.float32)
    bars = []
    local, total_flows = lines + units, lines + units + regions * slots
    local_limits = read_lanes(fixed, at.limits, local)
    cross_limits = given.flows[rows + 2 : rows + 3, local:]
    for bound, low, high in (
        (local_limits[:, :lines], 0, lines),
        (local_limits[:, lines:], lines, local),
        (cross_limits, local, total_flows),
    ):
        slope = given.slopes[:, low:high]
        if low == lines:
            slope = slope + store_duals
        old = given.flows[:rows, low:high]
        new = jnp.clip(old - primal_step * slope, -bound, bound)
        bars.append(2.0 * new - old)
        if not last:
            gives.flows[:rows, low:high] = new
            change = row_sum((new - old) ** 2)
            if low == local:
                slot = lax.broadcasted_iota(jnp.int32, change.shape, 1)
                change = jnp.where(slot // slots == own, change, 0.0)
            primal_row = primal_row + fold_lanes(change)
    maps_own = given.maps_cross[pl.ds(pl.multiple_of(own * nodes, nodes), nodes), :]
    balance = dot3(jnp.concatenate(bars[:2], axis=1), maps_local, True) - given.available[techs]
    balance = balance + supply + dot3(bars[2], maps_own, True)

    step_up = weight / (techs + 8.0) * balance
    if last:
        gives.prices[...] = prices + step_up
        owned = fixed[at.owned : at.owned + 1, : gives.capacity.shape[1]].astype(jnp.int32)
        tech_hot, node_hot = owned_one_hots(owned, techs, nodes)
        chosen = dot3(capacity_new, node_hot, False)
        gives.capacity[...] = row_sum(jnp.where(tech_hot, chosen, 0.0))
        gives.negative[...] = negative
        gives.kept[:rows, :] = fixed[...]
        gives.kept[rows : rows + techs, :] = col_weight
        gives.kept[rows + techs : rows + 2 * techs, :] = cost
        for chunk in range(regions * slots // LANES):
            low = local + chunk * LANES
            first = rows + 2 * techs + 8 * chunk
            gives.kept[first : first + 8, :] = given.flows[rows:, low : low + LANES]
        for copy in copies:
            copy.wait()
        return
    gives.block[:rows, :] = prices + step_up
    gives.flows[rows:, local:] = given.flows[rows:, local:]
    gives.cap_duals[techs, :techs, :] = col_weight
    gives.cap_duals[techs, techs : 2 * techs, :] = cost
    small_new = gives.dispatch.at[techs]
    small_new[:techs, :] = capacity_new
    small_new[at.weight : at.weight + 1, :] = jnp.broadcast_to(weight, (1, LANES))
    small_new[at.negative : at.negative + 1, :] = negative
    charge_bar = 2.0 * charge_new - charge
    before_new = jnp.clip(charge_before - primal_step * (prev_row - store_duals[0:1]), 0.0, energy)
    write_lanes(small_new, at.before, before_new)
    before_bar = 2.0 * before_new - charge_before
    shifted_bar = jnp.where(row_id == 0, before_bar, pltpu.roll(charge_bar, 1, 0))
    store_step = weight / 3.0 * (charge_bar - shifted_bar + bars[1])
    store_new = store_duals + store_step
    gives.store_duals[...] = store_new
    primal_row = primal_row + row_sum(primal_acc) + fold_lanes(row_sum((charge_new - charge) ** 2))
    primal_row = primal_row + jnp.where(
        hour_index == 0, row_sum((capacity_new - capacity) ** 2), 0.0
    )
    dual_row = row_sum(dual_acc + step_up * step_up) + fold_lanes(row_sum(store_step * store_step))
    squares = jnp.concatenate(
        [primal_row, dual_row, jnp.zeros((SQUARES - 2, LANES), jnp.float32)], axis=0
    )
    out_sums[techs : techs + SQUARES, :] = squares
    write_halo(sizes, out_sums, store_new)


def call(kernel, given, outs, flops=0, left=(), scratch=(), limit=VMEM_BYTES, copied=0):
    names_in, names_out = tuple(vars(given)), tuple(vars(outs))
    values = pl.pallas_call(
        functools.partial(kernel, names_in, names_out),
        out_shape=tuple(vars(outs).values()),
        in_specs=[
            pl.BlockSpec(memory_space=pl.ANY if i in left else pltpu.VMEM)
            for i in range(len(names_in))
        ],
        out_specs=[
            pl.BlockSpec(memory_space=pl.ANY if i < copied else pltpu.VMEM)
            for i in range(len(names_out))
        ],
        scratch_shapes=scratch,
        cost_estimate=pl.CostEstimate(flops=flops, bytes_accessed=4 * flops, transcendentals=0),
        compiler_params=pltpu.CompilerParams(vmem_limit_bytes=limit),
    )(*vars(given).values())
    return Bag(**dict(zip(names_out, values)))


def swap(value, hour_bit, region_bit):
    hours, regions = lax.axis_size("hours"), lax.axis_size("region")
    pairs = [
        (hour * regions + region, (hour ^ hour_bit) * regions + (region ^ region_bit))
        for hour in range(hours)
        for region in range(regions)
    ]
    return lax.ppermute(value, ("hours", "region"), pairs)


def shifted(value, steps):
    count = lax.axis_size("hours")
    return lax.ppermute(value, "hours", [(i, (i + steps) % count) for i in range(count)])


def both_regions(block):
    if lax.axis_size("region") != 2:
        return lax.all_gather(block, "region")
    return in_order(block, swap(block, 0, 1))


def in_order(block, other):
    return jnp.where(
        lax.axis_index("region") == 0, jnp.stack([block, other]), jnp.stack([other, block])
    )


def exchange(sizes, block):
    hours, regions = lax.axis_size("hours"), lax.axis_size("region")
    techs, span = sizes.techs, sizes.units // LANES
    halo = halo_at(sizes)
    prices, sums = block[: sizes.rows], block[sizes.rows :]
    if regions != 2 or hours != 16:
        gathered = lax.all_gather(prices, "region")
        totals = lax.psum(sums, "hours")
        totals = totals.at[techs:halo].set(lax.psum(totals[techs:halo], "region"))
        next_row = shifted(sums[halo : halo + span], -1)
        prev_row = shifted(sums[halo + span : halo + 2 * span], 1)
        return gathered, Bag(totals=totals, next_row=next_row, prev_row=prev_row)

    def merged(mine, yours, mine_first):
        last = halo + span
        edges = [
            jnp.where(mine_first, mine[halo:last], yours[halo:last]),
            jnp.where(mine_first, yours[last : last + span], mine[last : last + span]),
        ]
        total = mine + yours
        return jnp.concatenate([total[:halo], *edges, total[last + span :]], axis=0)

    hour = lax.axis_index("hours")
    beside_core = swap(block, 1, 0)
    partner_prices, partner = beside_core[: sizes.rows], beside_core[sizes.rows :]
    chip = merged(sums, partner, hour % 2 == 0)
    across = swap(chip, 2 + 1, 0)
    diagonal = swap(chip[techs:halo], 2 + 1, 1)
    beside = swap(jnp.concatenate([partner_prices, chip[techs:halo]], axis=0), 1, 1)
    other, squares = beside[: sizes.rows], beside[sizes.rows :]
    slab = merged(chip, across, hour // 2 % 2 == 0)
    slab = slab + jnp.pad(squares + diagonal, ((techs, slab.shape[0] - halo), (0, 0)))
    near, middle, far = [swap(slab, 4 * step + 1, 0) for step in (1, 2, 3)]
    parts = Bag(slab=slab, near=near, middle=middle, far=far, partner=partner, across=across)
    return in_order(prices, other), parts


def shape(*dims, dtype=jnp.float32):
    return jax.ShapeDtypeStruct(dims, dtype)


def restarted(sizes, kept, args):
    rows, techs, nodes, lines = sizes.rows, sizes.techs, sizes.nodes, sizes.lines
    local, cross = lines + sizes.units, sizes.regions * sizes.slots
    at, own = places(sizes), lax.axis_index("region")
    first_hour = lax.axis_index("hours") == 0
    price_start = args.price_start
    available = args.availability.transpose(1, 0, 2)
    fixed, last = kept[:rows], rows + 2 * techs
    col_weight, cost = kept[rows : rows + techs], kept[rows + techs : last]
    info = kept[last:].reshape(-1, 8, LANES).transpose(1, 0, 2).reshape(8, cross)
    local_limits = fixed[at.limits : at.energy].reshape(1, local)
    cross_limits = info[2:3]
    ends = info[:2].astype(jnp.int32)
    maps_cross_low = incidence(ends[:1], ends[1:], sizes.regions * nodes)
    stores = args.store_node[None]
    maps_local_low = incidence(
        jnp.concatenate([args.line_ends[:1], jnp.full_like(stores, -1)], axis=1),
        jnp.concatenate([args.line_ends[1:], stores], axis=1),
        nodes,
    )
    maps_local = maps_local_low.astype(jnp.float32)
    maps_cross = maps_cross_low.astype(jnp.float32)
    maps_own = lax.dynamic_slice_in_dim(maps_cross, own * nodes, nodes)
    prices_all = jnp.concatenate(list(both_regions(price_start)), axis=1)
    highest = lax.Precision.HIGHEST

    capacity = jnp.maximum(-cost / col_weight, 0.0)
    slopes = fixed[:techs][:, None, :] + price_start[None]
    dispatch = jnp.maximum(-0.5 * slopes, 0.0)
    slope = jnp.dot(price_start, maps_local, precision=highest)
    flows_local = jnp.clip(-0.5 * slope, -local_limits, local_limits)
    slope = jnp.dot(prices_all, maps_cross, precision=highest)
    flows_cross = jnp.clip(-0.5 * slope, -cross_limits, cross_limits)
    balance = (
        jnp.sum(2.0 * dispatch, axis=0)
        + jnp.dot(2.0 * flows_local, maps_local.T, precision=highest)
        + jnp.dot(2.0 * flows_cross, maps_own.T, precision=highest)
        - args.demand
    )
    step_up = balance / (techs + 8.0)
    duals = jnp.maximum(0.5 * (2.0 * dispatch - available * (2.0 * capacity)[:, None, :]), 0.0)
    store_duals = 2.0 * flows_local[:, lines:] / 3.0
    slot = lax.broadcasted_iota(jnp.int32, (1, cross), 1) // sizes.slots
    primal = (
        jnp.sum(dispatch**2)
        + jnp.sum(flows_local**2)
        + jnp.sum(jnp.where(slot == own, flows_cross**2, 0.0))
        + jnp.where(first_hour, jnp.sum(capacity**2), 0.0)
    )
    dual = jnp.sum(step_up**2) + jnp.sum(duals**2) + jnp.sum(store_duals**2)
    rows_of = [
        jnp.sum(available * duals, axis=1),
        jnp.zeros((SQUARES, nodes)).at[0, 0].set(primal).at[1, 0].set(dual),
        store_duals[:1].reshape(-1, LANES),
        store_duals[rows - 1 :].reshape(-1, LANES),
    ]
    used = halo_at(sizes) + 2 * sizes.units // LANES
    rows_of.append(jnp.zeros((sums_rows(sizes) - used, nodes)))
    rows_of += [jnp.where(first_hour, part, 0.0) for part in (col_weight, cost)]
    block = jnp.concatenate([price_start + step_up, *rows_of], axis=0)
    gathered, parts = exchange(sizes, block)
    flows = jnp.concatenate([flows_local, flows_cross], axis=1)
    spare = jnp.concatenate([jnp.zeros((8, local)), info], axis=1)
    state = Bag(
        available=jnp.concatenate([available, args.demand[None], fixed[None]], axis=0),
        maps_local=maps_local_low,
        maps_cross=maps_cross_low,
        store_duals=store_duals,
        dispatch=jnp.concatenate([dispatch, jnp.zeros((1, rows, nodes))], axis=0),
        flows=jnp.concatenate([flows, spare], axis=0),
    )
    return state, gathered, parts


def run(args):
    rows, techs, nodes = args.availability.shape
    hours, regions = lax.axis_size("hours"), lax.axis_size("region")
    slots, owned = args.cross_limit.shape[1], args.cap_cost.shape[1]
    units, lines = args.store_node.shape[0], args.line_limit.shape[0]
    sizes = Bag(
        rows=rows, techs=techs, nodes=nodes, regions=regions, slots=slots, lines=lines, units=units
    )
    cross = regions * slots

    gathered = both_regions(
        call(
            lambda names_in, names_out, *refs: first_kernel(sizes, refs[:4], *refs[4:]),
            Bag(
                price=args.price_start,
                ends=args.cross_ends[:, 0],
                limit=args.cross_limit,
                pairs=args.pair_counts,
            ),
            Bag(block=shape(rows + 8 * max(1, slots // LANES), nodes)),
            left=(0, 1, 2, 3),
            scratch=[
                pltpu.VMEM((2, slots), jnp.int32),
                pltpu.VMEM((1, slots), jnp.float32),
                pltpu.VMEM((1, regions), jnp.int32),
                pltpu.SemaphoreType.DMA((4,)),
            ],
            limit=FIRST_BYTES,
        ).block
    )
    state = call(
        functools.partial(start_kernel, sizes),
        Bag(
            availability=args.availability.reshape(rows * techs, nodes),
            price=args.price_start,
            demand=args.demand,
            gen_cost=args.gen_cost,
            cap_cost=args.cap_cost,
            owner=args.owner_map.reshape(hours, owned),
            line_ends=args.line_ends,
            line_limit=args.line_limit[None],
            store_node=args.store_node[None],
            store_power=args.store_power[None],
            store_energy=args.store_energy[None],
        ),
        Bag(
            available=shape(techs + 2, rows, nodes),
            maps_local=shape(nodes, lines + units, dtype=jnp.bfloat16),
            flows_local=shape(rows, lines + units),
            store_duals=shape(rows, units),
            dispatch=shape(techs + 1, rows, nodes),
            balance=shape(rows, nodes),
            sums=shape(sums_rows(sizes) + 2 * techs, nodes),
        ),
        flops=10**6,
        left=(0,),
        scratch=[pltpu.VMEM((rows * techs, nodes), jnp.float32), pltpu.SemaphoreType.DMA],
    )
    closed = call(
        lambda names_in, names_out, *refs: close_kernel(sizes, *refs),
        Bag(
            gathered=gathered,
            flows_local=state.flows_local,
            balance=state.balance,
            sums=state.sums,
        ),
        Bag(
            maps=shape(regions * nodes, cross, dtype=jnp.bfloat16),
            flows=shape(rows + 8, lines + units + cross),
            block=shape(rows + state.sums.shape[0], nodes),
        ),
    )
    del state.sums, state.balance, state.flows_local
    state.maps_cross, state.flows = closed.maps, closed.flows
    gathered, parts = exchange(sizes, closed.block)
    outputs, negative, kept = sweeps(sizes, owned, state, gathered, parts)

    def again():
        return sweeps(sizes, owned, *restarted(sizes, kept, args))[0]

    return lax.cond(negative > 0.0, again, lambda: outputs)


def sweeps(sizes, owned, state, gathered, parts):
    rows, techs, nodes, lines, units = (
        sizes.rows,
        sizes.techs,
        sizes.nodes,
        sizes.lines,
        sizes.units,
    )
    state = Bag(**vars(state))
    for iteration in range(1, ITERS):
        slopes = call(
            functools.partial(slopes_kernel, sizes),
            Bag(gathered=gathered, maps_local=state.maps_local, maps_cross=state.maps_cross),
            Bag(slopes=shape(rows, lines + units + sizes.regions * sizes.slots)),
        ).slopes
        given = Bag(**vars(state), **vars(parts), gathered=gathered, slopes=slopes)
        if iteration < ITERS - 1:
            outs = Bag(
                dispatch=shape(techs + 1, rows, nodes),
                cap_duals=shape(techs + 1, rows, nodes),
                flows=shape(rows + 8, lines + units + sizes.regions * sizes.slots),
                store_duals=shape(rows, units),
                charge=shape(rows, units),
                block=shape(rows + sums_rows(sizes), nodes),
            )
        else:
            outs = Bag(
                dispatch=shape(rows * techs, nodes),
                capacity=shape(1, owned),
                prices=shape(rows, nodes),
                charge=shape(rows, units),
                negative=shape(1, LANES),
                kept=shape(rows + 2 * techs + 8 * (sizes.regions * sizes.slots // LANES), LANES),
            )
        final = iteration == ITERS - 1
        results = call(
            functools.partial(sweep_kernel, sizes, iteration),
            given,
            outs,
            copied=int(final),
            scratch=[
                pltpu.VMEM(outs.dispatch.shape, jnp.float32),
                pltpu.SemaphoreType.DMA((PARTS,)),
            ]
            if final
            else [],
        )
        if iteration < ITERS - 1:
            gathered, parts = exchange(sizes, results.block)
            del results.block
            vars(state).update(vars(results))
    dispatch = results.dispatch.reshape(rows, techs, nodes)
    outputs = (dispatch, results.capacity, results.prices, results.charge)
    return outputs, results.negative[0, 0], results.kept


def body(
    availability,
    demand,
    gen_cost,
    cap_cost,
    owner_map,
    line_ends,
    line_limit,
    cross_ends,
    cross_limit,
    pair_counts,
    store_node,
    store_energy,
    store_power,
    price_start,
):
    args = Bag(**locals())
    return run(args)


def solution(mesh):
    placed = (
        P("hours", None, "region"),
        P("hours", "region"),
        P(None, "region"),
        P("region", "hours"),
        P("region", None),
        P(None, "region"),
        P("region"),
        P(None, "region", None),
        P("region", None),
        P("region", None),
        P("region"),
        P("region"),
        P("region"),
        P("hours", "region"),
    )
    return jax.shard_map(
        body,
        mesh=mesh,
        in_specs=placed,
        out_specs=(
            P("hours", None, "region"),
            P("region", "hours"),
            P("hours", "region"),
            P("hours", "region"),
        ),
        check_vma=False,
    )
```

```python
import functools
from types import SimpleNamespace as Bag

import jax
import jax.numpy as jnp
from jax import lax
from jax.experimental import pallas as pl
from jax.experimental.pallas import tpu as pltpu
from jax.sharding import PartitionSpec as P

ITERS = 4
EPSILON = 1e-06
LANES = 128
VMEM_BYTES = 24 * 1024 * 1024
FIRST_BYTES = 56 * 1024 * 1024
PARTS = 4
SQUARES = 3


def split3(value):
    high = value.astype(jnp.bfloat16)
    rest = value - high.astype(jnp.float32)
    middle = rest.astype(jnp.bfloat16)
    low = (rest - middle.astype(jnp.float32)).astype(jnp.bfloat16)
    return jnp.concatenate([high, middle, low], axis=0)


def dot3(value, matrix, transposed):
    rows = value.shape[0]
    contract = ((1,), (1 if transposed else 0,))
    product = lax.dot_general(
        split3(value), matrix, (contract, ((), ())), preferred_element_type=jnp.float32
    )
    return product[:rows] + product[rows : 2 * rows] + product[2 * rows :]


def row_sum(value):
    return jnp.sum(value, axis=0, keepdims=True)


def fold_lanes(row):
    total = row[:, :LANES]
    for start in range(LANES, row.shape[1], LANES):
        total = total + row[:, start : start + LANES]
    return total


def owned_one_hots(owned, tech_count, node_count):
    shape_t = (tech_count, owned.shape[1])
    shape_n = (node_count, owned.shape[1])
    tech = lax.broadcasted_iota(jnp.int32, shape_t, 0) == owned // node_count
    node = lax.broadcasted_iota(jnp.int32, shape_n, 0) == owned % node_count
    return tech, node.astype(jnp.float32).astype(jnp.bfloat16)


def incidence(start, end, count):
    node = lax.broadcasted_iota(jnp.int32, (count, start.shape[1]), 0)
    maps = (node == end).astype(jnp.float32) - (node == start).astype(jnp.float32)
    return maps.astype(jnp.bfloat16)


def halo_at(sizes):
    return sizes.techs + SQUARES


def sums_rows(sizes):
    return (halo_at(sizes) + 2 * sizes.units // LANES + 7) // 8 * 8


def write_halo(sizes, sums_ref, store_new):
    halo, span, rows = halo_at(sizes), sizes.units // LANES, sizes.rows
    write_lanes(sums_ref, halo, store_new[:1])
    write_lanes(sums_ref, halo + span, store_new[rows - 1 :])
    used, end = halo + 2 * span, sums_rows(sizes)
    if used < end:
        sums_ref[used:end, :] = jnp.zeros((end - used, LANES), jnp.float32)


def write_lanes(ref, start, row):
    for i in range(row.shape[1] // LANES):
        ref[start + i : start + i + 1, :] = row[:, i * LANES : (i + 1) * LANES]


def part_copies(source, target, sems):
    rows = source.shape[0] // PARTS
    spans = [pl.ds(part * rows, rows) for part in range(PARTS)]
    return [
        pltpu.make_async_copy(source.at[span], target.at[span], sems.at[part])
        for part, span in enumerate(spans)
    ]


def read_lanes(ref, start, length):
    return jnp.concatenate(
        [ref[start + i : start + i + 1, :] for i in range(length // LANES)], axis=1
    )


def places(sizes):
    span = sizes.units // LANES
    limits = sizes.techs
    energy = limits + (sizes.lines + sizes.units) // LANES
    return Bag(
        limits=limits,
        energy=energy,
        owned=energy + span,
        cost=energy + span + 1,
        weight=sizes.techs,
        before=sizes.techs + 1,
        negative=sizes.techs + 1 + span,
    )


def first_kernel(sizes, sources, block_ref, ends_ref, limit_ref, pairs_ref, sems):
    rows = sizes.rows
    targets = (block_ref.at[pl.ds(0, rows)], ends_ref, limit_ref, pairs_ref)
    copies = [
        pltpu.make_async_copy(source, target, sems.at[i])
        for i, (source, target) in enumerate(zip(sources, targets))
    ]
    for copy in copies:
        copy.start()
    nodes, slots, regions = sizes.nodes, sizes.slots, sizes.regions
    own = lax.axis_index("region")
    width = slots // regions
    slot = lax.broadcasted_iota(jnp.int32, (1, slots), 1)
    pair = slot // width
    for copy in copies[1:]:
        copy.wait()
    in_use = jnp.zeros((1, slots), jnp.int32)
    for target in range(regions):
        in_use = jnp.where(pair == target, pairs_ref[0:1, target : target + 1], in_use)
    bound = jnp.where(slot % width < in_use, limit_ref[...], 0.0)
    start = (ends_ref[0:1, :] + own * nodes).astype(jnp.float32)
    end = (ends_ref[1:2, :] + pair * nodes).astype(jnp.float32)
    block_ref[rows:, :] = jnp.zeros((block_ref.shape[0] - rows, LANES), jnp.float32)
    width = min(slots, LANES)
    for chunk in range(slots // width):
        at = rows + 8 * chunk
        for i, row in enumerate((start, end, bound)):
            block_ref[at + i : at + i + 1, :width] = row[:, chunk * width : (chunk + 1) * width]
    copies[0].wait()


def start_kernel(sizes, names_in, names_out, *refs):
    given = Bag(**dict(zip(names_in, refs[: len(names_in)])))
    gives = Bag(**dict(zip(names_out, refs[len(names_in) : -2])))
    availability, sem = refs[-2:]
    copy = pltpu.make_async_copy(given.availability, availability, sem)
    copy.start()
    rows, techs, nodes, lines = sizes.rows, sizes.techs, sizes.nodes, sizes.lines
    at = places(sizes)
    fixed = gives.available.at[techs + 1]
    gives.available[techs] = given.demand[...]
    fixed[:techs, :] = given.gen_cost[...]
    write_lanes(fixed, at.energy, given.store_energy[...])
    owned = given.owner[pl.ds(lax.axis_index("hours"), 1), :]
    fixed[at.owned : at.owned + 1, : owned.shape[1]] = owned.astype(jnp.float32)
    line_ends, stores = given.line_ends[...], given.store_node[...]
    start = jnp.concatenate([line_ends[0:1], jnp.full_like(stores, -1)], axis=1)
    end = jnp.concatenate([line_ends[1:2], stores], axis=1)
    maps = incidence(start, end, nodes)
    limits = jnp.concatenate([given.line_limit[...], given.store_power[...]], axis=1)
    gives.maps_local[...] = maps
    write_lanes(fixed, at.limits, limits)
    prices = given.price[...]
    flows = jnp.clip(-0.5 * dot3(prices, maps, False), -limits, limits)
    gives.flows_local[...] = flows
    store_new = (1.0 / 3.0) * (2.0 * flows[:, lines:])
    gives.store_duals[...] = store_new
    primal_row = fold_lanes(row_sum(flows * flows))
    dual_row = fold_lanes(row_sum(store_new * store_new))
    balance = dot3(2.0 * flows, maps, True) - given.demand[...]
    gen_cost = given.gen_cost[...]
    copy.wait()
    cost = given.cap_cost[...]
    tech_hot, node_hot = owned_one_hots(owned, techs, nodes)
    own_cost = dot3(jnp.where(tech_hot, cost, 0.0), node_hot, True)
    fixed[at.cost : at.cost + techs, :] = own_cost
    gives.dispatch[techs] = jnp.zeros((rows, nodes), jnp.float32)
    acc = jnp.zeros((rows, nodes), jnp.float32)
    weights = jnp.zeros((techs, nodes), jnp.float32)
    for hour in range(rows):
        weights = weights + availability[hour * techs : (hour + 1) * techs, :]
    for tech in range(techs):
        avail = availability[pl.ds(tech, rows, stride=techs), :]
        gives.available[tech] = avail
        dispatch = jnp.maximum(-0.5 * (gen_cost[tech : tech + 1] + prices), 0.0)
        gives.dispatch[tech] = dispatch
        dispatch_bar = 2.0 * dispatch
        balance = balance + dispatch_bar
        duals = jnp.maximum(0.5 * dispatch_bar, 0.0)
        acc = acc + dispatch * dispatch
        gives.sums[tech : tech + 1, :] = own_cost[tech : tech + 1] - row_sum(avail * duals)
    gives.balance[...] = balance
    squares = row_sum(acc)
    negative = jnp.sum((cost < 0.0).astype(jnp.float32), axis=1, keepdims=True)
    write_halo(sizes, gives.sums, store_new)
    gives.sums[techs : techs + SQUARES, :] = jnp.concatenate(
        [primal_row + squares, dual_row + squares, jnp.broadcast_to(negative, (1, LANES))], axis=0
    )
    first = sums_rows(sizes)
    gives.sums[first : first + techs, :] = weights


def close_kernel(
    sizes,
    gathered,
    local_ref,
    balance_ref,
    sums_in_ref,
    maps_ref,
    flows_ref,
    block_ref,
):
    rows, techs, nodes = sizes.rows, sizes.techs, sizes.nodes
    slots, regions = sizes.slots, sizes.regions
    own = lax.axis_index("region")
    width = min(slots, LANES)
    info = jnp.concatenate(
        [
            gathered[region, rows + 8 * chunk : rows + 8 * chunk + 8, :width]
            for region in range(regions)
            for chunk in range(slots // width)
        ],
        axis=1,
    )
    maps_ref[...] = incidence(
        info[0:1].astype(jnp.int32), info[1:2].astype(jnp.int32), regions * nodes
    )
    limits = info[2:3]
    prices_all = jnp.concatenate([gathered[region, :rows, :] for region in range(regions)], axis=1)
    flows = jnp.clip(-0.5 * dot3(prices_all, maps_ref[...], False), -limits, limits)
    local = local_ref.shape[1]
    flows_ref[:rows, :local] = local_ref[...]
    flows_ref[:rows, local:] = flows
    flows_ref[rows:, local:] = info
    maps_own = maps_ref[pl.ds(pl.multiple_of(own * nodes, nodes), nodes), :]
    balance = balance_ref[...] + dot3(2.0 * flows, maps_own, True)
    step_up = (1.0 / (techs + 8.0)) * balance
    block_ref[:rows, :] = gathered[own, :rows, :] + step_up
    change = row_sum(flows * flows)
    slot = lax.broadcasted_iota(jnp.int32, change.shape, 1)
    primal = fold_lanes(jnp.where(slot // slots == own, change, 0.0))
    more = jnp.concatenate(
        [primal, row_sum(step_up * step_up), jnp.zeros((SQUARES - 2, LANES), jnp.float32)], axis=0
    )
    block_ref[rows:, :] = sums_in_ref[...]
    block_ref[rows + techs : rows + techs + SQUARES, :] = (
        sums_in_ref[techs : techs + SQUARES, :] + more
    )


def neighbour_rows(sizes, given, hour_index):
    units = sizes.units
    if hasattr(given, "totals"):
        return read_lanes(given.next_row, 0, units), read_lanes(given.prev_row, 0, units)
    first = halo_at(sizes)
    last = first + units // LANES
    core, x_place, odd = hour_index % 2, hour_index // 2 % 2, hour_index // 4 % 2
    next_row = jnp.where(
        odd == 0, read_lanes(given.near, first, units), read_lanes(given.far, first, units)
    )
    prev_row = jnp.where(
        odd == 0, read_lanes(given.far, last, units), read_lanes(given.near, last, units)
    )
    next_row = jnp.where(x_place == 0, read_lanes(given.across, first, units), next_row)
    prev_row = jnp.where(x_place == 0, prev_row, read_lanes(given.across, last, units))
    next_row = jnp.where(core == 0, read_lanes(given.partner, first, units), next_row)
    prev_row = jnp.where(core == 0, prev_row, read_lanes(given.partner, last, units))
    return next_row, prev_row


def total_of(parts):
    if hasattr(parts, "totals"):
        return parts.totals[...]
    return (parts.slab[...] + parts.near[...]) + (parts.middle[...] + parts.far[...])


def slopes_kernel(sizes, names_in, names_out, gathered, maps_local, maps_cross, slopes_ref):
    rows, regions = sizes.rows, sizes.regions
    local = sizes.lines + sizes.units
    prices_all = jnp.concatenate([gathered[region, :rows, :] for region in range(regions)], axis=1)
    prices = gathered[lax.axis_index("region"), :rows, :]
    slopes_ref[:, :local] = dot3(prices, maps_local[...], False)
    slopes_ref[:, local:] = dot3(prices_all, maps_cross[...], False)


def sweep_kernel(sizes, iteration, names_in, names_out, *refs):
    rows, techs, nodes = sizes.rows, sizes.techs, sizes.nodes
    slots, regions, lines, units = sizes.slots, sizes.regions, sizes.lines, sizes.units
    second = iteration == 1
    last = iteration == ITERS - 1
    given = Bag(**dict(zip(names_in, refs[: len(names_in)])))
    gives = Bag(**dict(zip(names_out, refs[len(names_in) :])))
    if last:
        staged, sems = refs[-2:]
    own = lax.axis_index("region")
    hour_index = lax.axis_index("hours")
    gathered = given.gathered

    at = places(sizes)
    fixed = given.available.at[techs + 1]
    small = given.dispatch.at[techs]
    out_sums = None if last else gives.block.at[pl.ds(rows, sums_rows(sizes))]
    sums = total_of(given)
    squares = jnp.sum(sums[techs : techs + 2], axis=1, keepdims=True)
    old_weight = jnp.ones((1, 1), jnp.float32) if second else small[at.weight : at.weight + 1, :1]
    weight = jnp.sqrt(
        old_weight * jnp.sqrt((squares[1:2] + EPSILON) / (squares[0:1] + EPSILON))
    )
    primal_step = 0.5 / weight
    if second:
        first = sums_rows(sizes)
        col_weight = sums[first : first + techs]
        negative = sums[techs + 2 : techs + 3]
    else:
        col_weight = given.cap_duals[techs, :techs, :]
        negative = small[at.negative : at.negative + 1, :]
    capacity = small[:techs, :]
    first_bar = 2.0 * capacity
    capacity_new = jnp.maximum(capacity - sums[:techs] / (weight * col_weight), 0.0)
    capacity_bar = 2.0 * capacity_new - capacity

    prices = gathered[own, :rows, :]
    gen_cost = fixed[:techs, :]
    half_weight = weight / 2.0
    primal_acc = jnp.zeros((rows, nodes), jnp.float32)
    dual_acc = jnp.zeros((rows, nodes), jnp.float32)
    supply = jnp.zeros((rows, nodes), jnp.float32)
    if last:
        copies = part_copies(staged, gives.dispatch, sems)
        count, pieces = rows // PARTS, []
        for part in range(PARTS):
            hours = slice(part * count, (part + 1) * count)
            piece = jnp.zeros((count, nodes), jnp.float32)
            for tech in range(techs):
                slope = gen_cost[tech : tech + 1] + prices[hours]
                dispatch = given.dispatch[tech, hours, :]
                duals = given.cap_duals[tech, hours, :]
                dispatch_new = jnp.maximum(dispatch - primal_step * (slope + duals), 0.0)
                piece = piece + (2.0 * dispatch_new - dispatch)
                staged[pl.ds(part * count * techs + tech, count, stride=techs), :] = dispatch_new
            copies[part].start()
            pieces.append(piece)
        supply = jnp.concatenate(pieces, axis=0)
    for tech in range(0 if last else techs):
        slope = gen_cost[tech : tech + 1] + prices
        dispatch = given.dispatch[tech]
        avail = given.available[tech]
        if second:
            duals = jnp.maximum(0.5 * (2.0 * dispatch - avail * first_bar[tech : tech + 1]), 0.0)
        else:
            duals = given.cap_duals[tech]
        dispatch_new = jnp.maximum(dispatch - primal_step * (slope + duals), 0.0)
        dispatch_bar = 2.0 * dispatch_new - dispatch
        supply = supply + dispatch_bar
        gives.dispatch[tech] = dispatch_new
        cap_rows = dispatch_bar - avail * capacity_bar[tech : tech + 1]
        primal_acc = primal_acc + (dispatch_new - dispatch) ** 2
        duals_new = jnp.maximum(duals + half_weight * cap_rows, 0.0)
        dual_acc = dual_acc + (duals_new - duals) ** 2
        gives.cap_duals[tech] = duals_new
        cost = fixed[at.cost + tech : at.cost + tech + 1, :]
        out_sums[tech : tech + 1, :] = cost - row_sum(avail * duals_new)

    maps_local = given.maps_local[...]

    energy = read_lanes(fixed, at.energy, units)
    row_id = lax.broadcasted_iota(jnp.int32, (rows, units), 0)
    next_row, prev_row = neighbour_rows(sizes, given, hour_index)
    store_duals = given.store_duals[...]
    next_duals = jnp.where(row_id == rows - 1, next_row, pltpu.roll(store_duals, rows - 1, 0))
    if second:
        charge = jnp.zeros((rows, units), jnp.float32)
        charge_before = jnp.zeros((1, units), jnp.float32)
    else:
        charge = given.charge[...]
        charge_before = read_lanes(small, at.before, units)
    charge_new = jnp.clip(charge - primal_step * (store_duals - next_duals), 0.0, energy)
    gives.charge[...] = charge_new

    primal_row = jnp.zeros((1, LANES), jnp.float32)
    bars = []
    local, total_flows = lines + units, lines + units + regions * slots
    local_limits = read_lanes(fixed, at.limits, local)
    cross_limits = given.flows[rows + 2 : rows + 3, local:]
    for bound, low, high in (
        (local_limits[:, :lines], 0, lines),
        (local_limits[:, lines:], lines, local),
        (cross_limits, local, total_flows),
    ):
        slope = given.slopes[:, low:high]
        if low == lines:
            slope = slope + store_duals
        old = given.flows[:rows, low:high]
        new = jnp.clip(old - primal_step * slope, -bound, bound)
        bars.append(2.0 * new - old)
        if not last:
            gives.flows[:rows, low:high] = new
            change = row_sum((new - old) ** 2)
            if low == local:
                slot = lax.broadcasted_iota(jnp.int32, change.shape, 1)
                change = jnp.where(slot // slots == own, change, 0.0)
            primal_row = primal_row + fold_lanes(change)
    maps_own = given.maps_cross[pl.ds(pl.multiple_of(own * nodes, nodes), nodes), :]
    balance = dot3(jnp.concatenate(bars[:2], axis=1), maps_local, True) - given.available[techs]
    balance = balance + supply + dot3(bars[2], maps_own, True)

    step_up = weight / (techs + 8.0) * balance
    if last:
        gives.prices[...] = prices + step_up
        owned = fixed[at.owned : at.owned + 1, : gives.capacity.shape[1]].astype(jnp.int32)
        tech_hot, node_hot = owned_one_hots(owned, techs, nodes)
        chosen = dot3(capacity_new, node_hot, False)
        gives.capacity[...] = row_sum(jnp.where(tech_hot, chosen, 0.0))
        gives.negative[...] = negative
        gives.kept[:rows, :] = fixed[...]
        gives.kept[rows : rows + techs, :] = col_weight
        for chunk in range(regions * slots // LANES):
            low = local + chunk * LANES
            first = rows + techs + 8 * chunk
            gives.kept[first : first + 8, :] = given.flows[rows:, low : low + LANES]
        for copy in copies:
            copy.wait()
        return
    gives.block[:rows, :] = prices + step_up
    gives.flows[rows:, local:] = given.flows[rows:, local:]
    gives.cap_duals[techs, :techs, :] = col_weight
    small_new = gives.dispatch.at[techs]
    small_new[:techs, :] = capacity_new
    small_new[at.weight : at.weight + 1, :] = jnp.broadcast_to(weight, (1, LANES))
    small_new[at.negative : at.negative + 1, :] = negative
    charge_bar = 2.0 * charge_new - charge
    before_new = jnp.clip(charge_before - primal_step * (prev_row - store_duals[0:1]), 0.0, energy)
    write_lanes(small_new, at.before, before_new)
    before_bar = 2.0 * before_new - charge_before
    shifted_bar = jnp.where(row_id == 0, before_bar, pltpu.roll(charge_bar, 1, 0))
    store_step = weight / 3.0 * (charge_bar - shifted_bar + bars[1])
    store_new = store_duals + store_step
    gives.store_duals[...] = store_new
    primal_row = primal_row + row_sum(primal_acc) + fold_lanes(row_sum((charge_new - charge) ** 2))
    primal_row = primal_row + jnp.where(
        hour_index == 0, row_sum((capacity_new - capacity) ** 2), 0.0
    )
    dual_row = row_sum(dual_acc + step_up * step_up) + fold_lanes(row_sum(store_step * store_step))
    squares = jnp.concatenate(
        [primal_row, dual_row, jnp.zeros((SQUARES - 2, LANES), jnp.float32)], axis=0
    )
    out_sums[techs : techs + SQUARES, :] = squares
    write_halo(sizes, out_sums, store_new)


def call(kernel, given, outs, flops=0, left=(), scratch=(), limit=VMEM_BYTES, copied=0):
    names_in, names_out = tuple(vars(given)), tuple(vars(outs))
    values = pl.pallas_call(
        functools.partial(kernel, names_in, names_out),
        out_shape=tuple(vars(outs).values()),
        in_specs=[
            pl.BlockSpec(memory_space=pl.ANY if i in left else pltpu.VMEM)
            for i in range(len(names_in))
        ],
        out_specs=[
            pl.BlockSpec(memory_space=pl.ANY if i < copied else pltpu.VMEM)
            for i in range(len(names_out))
        ],
        scratch_shapes=scratch,
        cost_estimate=pl.CostEstimate(flops=flops, bytes_accessed=4 * flops, transcendentals=0),
        compiler_params=pltpu.CompilerParams(vmem_limit_bytes=limit),
    )(*vars(given).values())
    return Bag(**dict(zip(names_out, values)))


def swap(value, hour_bit, region_bit):
    hours, regions = lax.axis_size("hours"), lax.axis_size("region")
    pairs = [
        (hour * regions + region, (hour ^ hour_bit) * regions + (region ^ region_bit))
        for hour in range(hours)
        for region in range(regions)
    ]
    return lax.ppermute(value, ("hours", "region"), pairs)


def shifted(value, steps):
    count = lax.axis_size("hours")
    return lax.ppermute(value, "hours", [(i, (i + steps) % count) for i in range(count)])


def both_regions(block):
    if lax.axis_size("region") != 2:
        return lax.all_gather(block, "region")
    return in_order(block, swap(block, 0, 1))


def in_order(block, other):
    return jnp.where(
        lax.axis_index("region") == 0, jnp.stack([block, other]), jnp.stack([other, block])
    )


def exchange(sizes, block):
    hours, regions = lax.axis_size("hours"), lax.axis_size("region")
    techs, span = sizes.techs, sizes.units // LANES
    halo = halo_at(sizes)
    prices, sums = block[: sizes.rows], block[sizes.rows :]
    if regions != 2 or hours != 16:
        gathered = lax.all_gather(prices, "region")
        totals = lax.psum(sums, "hours")
        totals = totals.at[techs:halo].set(lax.psum(totals[techs:halo], "region"))
        next_row = shifted(sums[halo : halo + span], -1)
        prev_row = shifted(sums[halo + span : halo + 2 * span], 1)
        return gathered, Bag(totals=totals, next_row=next_row, prev_row=prev_row)

    def merged(mine, yours, mine_first):
        last = halo + span
        edges = [
            jnp.where(mine_first, mine[halo:last], yours[halo:last]),
            jnp.where(mine_first, yours[last : last + span], mine[last : last + span]),
        ]
        total = mine + yours
        return jnp.concatenate([total[:halo], *edges, total[last + span :]], axis=0)

    hour = lax.axis_index("hours")
    beside_core = swap(block, 1, 0)
    partner_prices, partner = beside_core[: sizes.rows], beside_core[sizes.rows :]
    chip = merged(sums, partner, hour % 2 == 0)
    across = swap(chip, 2 + 1, 0)
    diagonal = swap(chip[techs:halo], 2 + 1, 1)
    beside = swap(jnp.concatenate([partner_prices, chip[techs:halo]], axis=0), 1, 1)
    other, squares = beside[: sizes.rows], beside[sizes.rows :]
    slab = merged(chip, across, hour // 2 % 2 == 0)
    slab = slab + jnp.pad(squares + diagonal, ((techs, slab.shape[0] - halo), (0, 0)))
    near, middle, far = [swap(slab, 4 * step + 1, 0) for step in (1, 2, 3)]
    parts = Bag(slab=slab, near=near, middle=middle, far=far, partner=partner, across=across)
    return in_order(prices, other), parts


def shape(*dims, dtype=jnp.float32):
    return jax.ShapeDtypeStruct(dims, dtype)


def restarted(sizes, kept, args):
    rows, techs, nodes, lines = sizes.rows, sizes.techs, sizes.nodes, sizes.lines
    local, cross = lines + sizes.units, sizes.regions * sizes.slots
    at, own = places(sizes), lax.axis_index("region")
    first_hour = lax.axis_index("hours") == 0
    price_start = args.price_start
    available = args.availability.transpose(1, 0, 2)
    fixed, last = kept[:rows], rows + techs
    col_weight = kept[rows:last]
    own_cost = fixed[at.cost : at.cost + techs]
    cost = lax.psum(own_cost, "hours")
    info = kept[last:].reshape(-1, 8, LANES).transpose(1, 0, 2).reshape(8, cross)
    local_limits = fixed[at.limits : at.energy].reshape(1, local)
    cross_limits = info[2:3]
    ends = info[:2].astype(jnp.int32)
    maps_cross_low = incidence(ends[:1], ends[1:], sizes.regions * nodes)
    stores = args.store_node[None]
    maps_local_low = incidence(
        jnp.concatenate([args.line_ends[:1], jnp.full_like(stores, -1)], axis=1),
        jnp.concatenate([args.line_ends[1:], stores], axis=1),
        nodes,
    )
    maps_local = maps_local_low.astype(jnp.float32)
    maps_cross = maps_cross_low.astype(jnp.float32)
    maps_own = lax.dynamic_slice_in_dim(maps_cross, own * nodes, nodes)
    prices_all = jnp.concatenate(list(both_regions(price_start)), axis=1)
    highest = lax.Precision.HIGHEST

    capacity = jnp.maximum(-cost / col_weight, 0.0)
    slopes = fixed[:techs][:, None, :] + price_start[None]
    dispatch = jnp.maximum(-0.5 * slopes, 0.0)
    slope = jnp.dot(price_start, maps_local, precision=highest)
    flows_local = jnp.clip(-0.5 * slope, -local_limits, local_limits)
    slope = jnp.dot(prices_all, maps_cross, precision=highest)
    flows_cross = jnp.clip(-0.5 * slope, -cross_limits, cross_limits)
    balance = (
        jnp.sum(2.0 * dispatch, axis=0)
        + jnp.dot(2.0 * flows_local, maps_local.T, precision=highest)
        + jnp.dot(2.0 * flows_cross, maps_own.T, precision=highest)
        - args.demand
    )
    step_up = balance / (techs + 8.0)
    duals = jnp.maximum(0.5 * (2.0 * dispatch - available * (2.0 * capacity)[:, None, :]), 0.0)
    store_duals = 2.0 * flows_local[:, lines:] / 3.0
    slot = lax.broadcasted_iota(jnp.int32, (1, cross), 1) // sizes.slots
    primal = (
        jnp.sum(dispatch**2)
        + jnp.sum(flows_local**2)
        + jnp.sum(jnp.where(slot == own, flows_cross**2, 0.0))
        + jnp.where(first_hour, jnp.sum(capacity**2), 0.0)
    )
    dual = jnp.sum(step_up**2) + jnp.sum(duals**2) + jnp.sum(store_duals**2)
    rows_of = [
        own_cost - jnp.sum(available * duals, axis=1),
        jnp.zeros((SQUARES, nodes)).at[0, 0].set(primal).at[1, 0].set(dual),
        store_duals[:1].reshape(-1, LANES),
        store_duals[rows - 1 :].reshape(-1, LANES),
    ]
    used = halo_at(sizes) + 2 * sizes.units // LANES
    rows_of.append(jnp.zeros((sums_rows(sizes) - used, nodes)))
    rows_of.append(jnp.where(first_hour, col_weight, 0.0))
    block = jnp.concatenate([price_start + step_up, *rows_of], axis=0)
    gathered, parts = exchange(sizes, block)
    flows = jnp.concatenate([flows_local, flows_cross], axis=1)
    slab = jnp.pad(capacity, ((0, rows - techs), (0, 0)))
    spare = jnp.concatenate([jnp.zeros((8, local)), info], axis=1)
    state = Bag(
        available=jnp.concatenate([available, args.demand[None], fixed[None]], axis=0),
        maps_local=maps_local_low,
        maps_cross=maps_cross_low,
        store_duals=store_duals,
        dispatch=jnp.concatenate([dispatch, slab[None]], axis=0),
        flows=jnp.concatenate([flows, spare], axis=0),
    )
    return state, gathered, parts


def run(args):
    rows, techs, nodes = args.availability.shape
    hours, regions = lax.axis_size("hours"), lax.axis_size("region")
    slots, owned = args.cross_limit.shape[1], args.cap_cost.shape[1]
    units, lines = args.store_node.shape[0], args.line_limit.shape[0]
    sizes = Bag(
        rows=rows, techs=techs, nodes=nodes, regions=regions, slots=slots, lines=lines, units=units
    )
    cross = regions * slots

    gathered = both_regions(
        call(
            lambda names_in, names_out, *refs: first_kernel(sizes, refs[:4], *refs[4:]),
            Bag(
                price=args.price_start,
                ends=args.cross_ends[:, 0],
                limit=args.cross_limit,
                pairs=args.pair_counts,
            ),
            Bag(block=shape(rows + 8 * max(1, slots // LANES), nodes)),
            left=(0, 1, 2, 3),
            scratch=[
                pltpu.VMEM((2, slots), jnp.int32),
                pltpu.VMEM((1, slots), jnp.float32),
                pltpu.VMEM((1, regions), jnp.int32),
                pltpu.SemaphoreType.DMA((4,)),
            ],
            limit=FIRST_BYTES,
        ).block
    )
    state = call(
        functools.partial(start_kernel, sizes),
        Bag(
            availability=args.availability.reshape(rows * techs, nodes),
            price=args.price_start,
            demand=args.demand,
            gen_cost=args.gen_cost,
            cap_cost=args.cap_cost,
            owner=args.owner_map.reshape(hours, owned),
            line_ends=args.line_ends,
            line_limit=args.line_limit[None],
            store_node=args.store_node[None],
            store_power=args.store_power[None],
            store_energy=args.store_energy[None],
        ),
        Bag(
            available=shape(techs + 2, rows, nodes),
            maps_local=shape(nodes, lines + units, dtype=jnp.bfloat16),
            flows_local=shape(rows, lines + units),
            store_duals=shape(rows, units),
            dispatch=shape(techs + 1, rows, nodes),
            balance=shape(rows, nodes),
            sums=shape(sums_rows(sizes) + techs, nodes),
        ),
        flops=10**6,
        left=(0,),
        scratch=[pltpu.VMEM((rows * techs, nodes), jnp.float32), pltpu.SemaphoreType.DMA],
    )
    closed = call(
        lambda names_in, names_out, *refs: close_kernel(sizes, *refs),
        Bag(
            gathered=gathered,
            flows_local=state.flows_local,
            balance=state.balance,
            sums=state.sums,
        ),
        Bag(
            maps=shape(regions * nodes, cross, dtype=jnp.bfloat16),
            flows=shape(rows + 8, lines + units + cross),
            block=shape(rows + state.sums.shape[0], nodes),
        ),
    )
    del state.sums, state.balance, state.flows_local
    state.maps_cross, state.flows = closed.maps, closed.flows
    gathered, parts = exchange(sizes, closed.block)
    outputs, negative, kept = sweeps(sizes, owned, state, gathered, parts)

    def again():
        return sweeps(sizes, owned, *restarted(sizes, kept, args))[0]

    return lax.cond(negative > 0.0, again, lambda: outputs)


def sweeps(sizes, owned, state, gathered, parts):
    rows, techs, nodes, lines, units = (
        sizes.rows,
        sizes.techs,
        sizes.nodes,
        sizes.lines,
        sizes.units,
    )
    state = Bag(**vars(state))
    for iteration in range(1, ITERS):
        slopes = call(
            functools.partial(slopes_kernel, sizes),
            Bag(gathered=gathered, maps_local=state.maps_local, maps_cross=state.maps_cross),
            Bag(slopes=shape(rows, lines + units + sizes.regions * sizes.slots)),
        ).slopes
        given = Bag(**vars(state), **vars(parts), gathered=gathered, slopes=slopes)
        if iteration < ITERS - 1:
            outs = Bag(
                dispatch=shape(techs + 1, rows, nodes),
                cap_duals=shape(techs + 1, rows, nodes),
                flows=shape(rows + 8, lines + units + sizes.regions * sizes.slots),
                store_duals=shape(rows, units),
                charge=shape(rows, units),
                block=shape(rows + sums_rows(sizes), nodes),
            )
        else:
            outs = Bag(
                dispatch=shape(rows * techs, nodes),
                capacity=shape(1, owned),
                prices=shape(rows, nodes),
                charge=shape(rows, units),
                negative=shape(1, LANES),
                kept=shape(rows + techs + 8 * (sizes.regions * sizes.slots // LANES), LANES),
            )
        final = iteration == ITERS - 1
        results = call(
            functools.partial(sweep_kernel, sizes, iteration),
            given,
            outs,
            copied=int(final),
            scratch=[
                pltpu.VMEM(outs.dispatch.shape, jnp.float32),
                pltpu.SemaphoreType.DMA((PARTS,)),
            ]
            if final
            else [],
        )
        if iteration < ITERS - 1:
            gathered, parts = exchange(sizes, results.block)
            del results.block
            vars(state).update(vars(results))
    dispatch = results.dispatch.reshape(rows, techs, nodes)
    outputs = (dispatch, results.capacity, results.prices, results.charge)
    return outputs, results.negative[0, 0], results.kept


def body(
    availability,
    demand,
    gen_cost,
    cap_cost,
    owner_map,
    line_ends,
    line_limit,
    cross_ends,
    cross_limit,
    pair_counts,
    store_node,
    store_energy,
    store_power,
    price_start,
):
    args = Bag(**locals())
    return run(args)


def solution(mesh):
    placed = (
        P("hours", None, "region"),
        P("hours", "region"),
        P(None, "region"),
        P("region", "hours"),
        P("region", None),
        P(None, "region"),
        P("region"),
        P(None, "region", None),
        P("region", None),
        P("region", None),
        P("region"),
        P("region"),
        P("region"),
        P("hours", "region"),
    )
    return jax.shard_map(
        body,
        mesh=mesh,
        in_specs=placed,
        out_specs=(
            P("hours", None, "region"),
            P("region", "hours"),
            P("hours", "region"),
            P("hours", "region"),
        ),
        check_vma=False,
    )
```

```python
import functools
from types import SimpleNamespace as Bag

import jax
import jax.numpy as jnp
from jax import lax
from jax.experimental import pallas as pl
from jax.experimental.pallas import tpu as pltpu
from jax.sharding import PartitionSpec as P

ITERS = 4
EPSILON = 1e-06
LANES = 128
VMEM_BYTES = 24 * 1024 * 1024
FIRST_BYTES = 56 * 1024 * 1024
PARTS = 4
SQUARES = 3


def split3(value):
    high = value.astype(jnp.bfloat16)
    rest = value - high.astype(jnp.float32)
    middle = rest.astype(jnp.bfloat16)
    low = (rest - middle.astype(jnp.float32)).astype(jnp.bfloat16)
    return jnp.concatenate([high, middle, low], axis=0)


def dot3(value, matrix, transposed):
    rows = value.shape[0]
    contract = ((1,), (1 if transposed else 0,))
    product = lax.dot_general(
        split3(value), matrix, (contract, ((), ())), preferred_element_type=jnp.float32
    )
    return product[:rows] + product[rows : 2 * rows] + product[2 * rows :]


def row_sum(value):
    return jnp.sum(value, axis=0, keepdims=True)


def fold_lanes(row):
    total = row[:, :LANES]
    for start in range(LANES, row.shape[1], LANES):
        total = total + row[:, start : start + LANES]
    return total


def owned_one_hots(owned, tech_count, node_count):
    shape_t = (tech_count, owned.shape[1])
    shape_n = (node_count, owned.shape[1])
    tech = lax.broadcasted_iota(jnp.int32, shape_t, 0) == owned // node_count
    node = lax.broadcasted_iota(jnp.int32, shape_n, 0) == owned % node_count
    return tech, node.astype(jnp.float32).astype(jnp.bfloat16)


def incidence(start, end, count):
    node = lax.broadcasted_iota(jnp.int32, (count, start.shape[1]), 0)
    maps = (node == end).astype(jnp.float32) - (node == start).astype(jnp.float32)
    return maps.astype(jnp.bfloat16)


def halo_at(sizes):
    return sizes.techs + SQUARES


def sums_rows(sizes):
    return (halo_at(sizes) + 2 * sizes.units // LANES + 7) // 8 * 8


def write_halo(sizes, sums_ref, store_new):
    halo, span, rows = halo_at(sizes), sizes.units // LANES, sizes.rows
    write_lanes(sums_ref, halo, store_new[:1])
    write_lanes(sums_ref, halo + span, store_new[rows - 1 :])
    used, end = halo + 2 * span, sums_rows(sizes)
    if used < end:
        sums_ref[used:end, :] = jnp.zeros((end - used, LANES), jnp.float32)


def write_lanes(ref, start, row):
    for i in range(row.shape[1] // LANES):
        ref[start + i : start + i + 1, :] = row[:, i * LANES : (i + 1) * LANES]


def part_copies(source, target, sems):
    rows = source.shape[0] // PARTS
    spans = [pl.ds(part * rows, rows) for part in range(PARTS)]
    return [
        pltpu.make_async_copy(source.at[span], target.at[span], sems.at[part])
        for part, span in enumerate(spans)
    ]


def read_lanes(ref, start, length):
    return jnp.concatenate(
        [ref[start + i : start + i + 1, :] for i in range(length // LANES)], axis=1
    )


def places(sizes):
    span = sizes.units // LANES
    limits = sizes.techs
    energy = limits + (sizes.lines + sizes.units) // LANES
    return Bag(
        limits=limits,
        energy=energy,
        owned=energy + span,
        cost=energy + span + 1,
        weight=sizes.techs,
        before=sizes.techs + 1,
        negative=sizes.techs + 1 + span,
    )


def first_kernel(sizes, sources, block_ref, ends_ref, limit_ref, pairs_ref, sems):
    rows = sizes.rows
    targets = (block_ref.at[pl.ds(0, rows)], ends_ref, limit_ref, pairs_ref)
    copies = [
        pltpu.make_async_copy(source, target, sems.at[i])
        for i, (source, target) in enumerate(zip(sources, targets))
    ]
    for copy in copies:
        copy.start()
    nodes, slots, regions = sizes.nodes, sizes.slots, sizes.regions
    own = lax.axis_index("region")
    width = slots // regions
    slot = lax.broadcasted_iota(jnp.int32, (1, slots), 1)
    pair = slot // width
    for copy in copies[1:]:
        copy.wait()
    in_use = jnp.zeros((1, slots), jnp.int32)
    for target in range(regions):
        in_use = jnp.where(pair == target, pairs_ref[0:1, target : target + 1], in_use)
    bound = jnp.where(slot % width < in_use, limit_ref[...], 0.0)
    start = (ends_ref[0:1, :] + own * nodes).astype(jnp.float32)
    end = (ends_ref[1:2, :] + pair * nodes).astype(jnp.float32)
    block_ref[rows:, :] = jnp.zeros((block_ref.shape[0] - rows, LANES), jnp.float32)
    width = min(slots, LANES)
    for chunk in range(slots // width):
        at = rows + 8 * chunk
        for i, row in enumerate((start, end, bound)):
            block_ref[at + i : at + i + 1, :width] = row[:, chunk * width : (chunk + 1) * width]
    copies[0].wait()


def start_kernel(sizes, names_in, names_out, *refs):
    given = Bag(**dict(zip(names_in, refs[: len(names_in)])))
    gives = Bag(**dict(zip(names_out, refs[len(names_in) : -2])))
    availability, sem = refs[-2:]
    copy = pltpu.make_async_copy(given.availability, availability, sem)
    copy.start()
    rows, techs, nodes, lines = sizes.rows, sizes.techs, sizes.nodes, sizes.lines
    at = places(sizes)
    fixed = gives.available.at[techs + 1]
    gives.available[techs] = given.demand[...]
    fixed[:techs, :] = given.gen_cost[...]
    write_lanes(fixed, at.energy, given.store_energy[...])
    owned = given.owner[pl.ds(lax.axis_index("hours"), 1), :]
    fixed[at.owned : at.owned + 1, : owned.shape[1]] = owned.astype(jnp.float32)
    line_ends, stores = given.line_ends[...], given.store_node[...]
    start = jnp.concatenate([line_ends[0:1], jnp.full_like(stores, -1)], axis=1)
    end = jnp.concatenate([line_ends[1:2], stores], axis=1)
    maps = incidence(start, end, nodes)
    limits = jnp.concatenate([given.line_limit[...], given.store_power[...]], axis=1)
    gives.maps_local[...] = maps
    write_lanes(fixed, at.limits, limits)
    prices = given.price[...]
    flows = jnp.clip(-0.5 * dot3(prices, maps, False), -limits, limits)
    gives.flows_local[...] = flows
    store_new = (1.0 / 3.0) * (2.0 * flows[:, lines:])
    gives.store_duals[...] = store_new
    primal_row = fold_lanes(row_sum(flows * flows))
    dual_row = fold_lanes(row_sum(store_new * store_new))
    balance = dot3(2.0 * flows, maps, True) - given.demand[...]
    gen_cost = given.gen_cost[...]
    copy.wait()
    cost = given.cap_cost[...]
    tech_hot, node_hot = owned_one_hots(owned, techs, nodes)
    own_cost = dot3(jnp.where(tech_hot, cost, 0.0), node_hot, True)
    fixed[at.cost : at.cost + techs, :] = own_cost
    gives.dispatch[techs] = jnp.zeros((rows, nodes), jnp.float32)
    acc = jnp.zeros((rows, nodes), jnp.float32)
    weights = jnp.zeros((techs, nodes), jnp.float32)
    for hour in range(rows):
        weights = weights + availability[hour * techs : (hour + 1) * techs, :]
    for tech in range(techs):
        avail = availability[pl.ds(tech, rows, stride=techs), :]
        gives.available[tech] = avail
        dispatch = jnp.maximum(-0.5 * (gen_cost[tech : tech + 1] + prices), 0.0)
        gives.dispatch[tech] = dispatch
        dispatch_bar = 2.0 * dispatch
        balance = balance + dispatch_bar
        duals = jnp.maximum(0.5 * dispatch_bar, 0.0)
        acc = acc + dispatch * dispatch
        gives.sums[tech : tech + 1, :] = own_cost[tech : tech + 1] - row_sum(avail * duals)
    gives.balance[...] = balance
    squares = row_sum(acc)
    negative = jnp.sum((cost < 0.0).astype(jnp.float32), axis=1, keepdims=True)
    write_halo(sizes, gives.sums, store_new)
    gives.sums[techs : techs + SQUARES, :] = jnp.concatenate(
        [primal_row + squares, dual_row + squares, jnp.broadcast_to(negative, (1, LANES))], axis=0
    )
    first = sums_rows(sizes)
    gives.sums[first : first + techs, :] = weights


def close_kernel(
    sizes,
    gathered,
    local_ref,
    balance_ref,
    sums_in_ref,
    maps_ref,
    flows_ref,
    block_ref,
):
    rows, techs, nodes = sizes.rows, sizes.techs, sizes.nodes
    slots, regions = sizes.slots, sizes.regions
    own = lax.axis_index("region")
    width = min(slots, LANES)
    info = jnp.concatenate(
        [
            gathered[region, rows + 8 * chunk : rows + 8 * chunk + 8, :width]
            for region in range(regions)
            for chunk in range(slots // width)
        ],
        axis=1,
    )
    maps_ref[...] = incidence(
        info[0:1].astype(jnp.int32), info[1:2].astype(jnp.int32), regions * nodes
    )
    limits = info[2:3]
    prices_all = jnp.concatenate([gathered[region, :rows, :] for region in range(regions)], axis=1)
    flows = jnp.clip(-0.5 * dot3(prices_all, maps_ref[...], False), -limits, limits)
    local = local_ref.shape[1]
    flows_ref[:rows, :local] = local_ref[...]
    flows_ref[:rows, local:] = flows
    flows_ref[rows:, local:] = info
    maps_own = maps_ref[pl.ds(pl.multiple_of(own * nodes, nodes), nodes), :]
    balance = balance_ref[...] + dot3(2.0 * flows, maps_own, True)
    step_up = (1.0 / (techs + 8.0)) * balance
    block_ref[:rows, :] = gathered[own, :rows, :] + step_up
    change = row_sum(flows * flows)
    slot = lax.broadcasted_iota(jnp.int32, change.shape, 1)
    primal = fold_lanes(jnp.where(slot // slots == own, change, 0.0))
    more = jnp.concatenate(
        [primal, row_sum(step_up * step_up), jnp.zeros((SQUARES - 2, LANES), jnp.float32)], axis=0
    )
    block_ref[rows:, :] = sums_in_ref[...]
    block_ref[rows + techs : rows + techs + SQUARES, :] = (
        sums_in_ref[techs : techs + SQUARES, :] + more
    )


def neighbour_rows(sizes, given, hour_index):
    units = sizes.units
    if hasattr(given, "totals"):
        return read_lanes(given.next_row, 0, units), read_lanes(given.prev_row, 0, units)
    first = halo_at(sizes)
    last = first + units // LANES
    core, x_place, odd = hour_index % 2, hour_index // 2 % 2, hour_index // 4 % 2
    next_row = jnp.where(
        odd == 0, read_lanes(given.near, first, units), read_lanes(given.far, first, units)
    )
    prev_row = jnp.where(
        odd == 0, read_lanes(given.far, last, units), read_lanes(given.near, last, units)
    )
    next_row = jnp.where(x_place == 0, read_lanes(given.across, first, units), next_row)
    prev_row = jnp.where(x_place == 0, prev_row, read_lanes(given.across, last, units))
    next_row = jnp.where(core == 0, read_lanes(given.partner, first, units), next_row)
    prev_row = jnp.where(core == 0, prev_row, read_lanes(given.partner, last, units))
    return next_row, prev_row


def total_of(parts):
    if hasattr(parts, "totals"):
        return parts.totals[...]
    return (parts.slab[...] + parts.near[...]) + (parts.middle[...] + parts.far[...])


def slopes_kernel(sizes, names_in, names_out, gathered, maps_local, maps_cross, slopes_ref):
    rows, regions = sizes.rows, sizes.regions
    local = sizes.lines + sizes.units
    prices_all = jnp.concatenate([gathered[region, :rows, :] for region in range(regions)], axis=1)
    prices = gathered[lax.axis_index("region"), :rows, :]
    slopes_ref[:, :local] = dot3(prices, maps_local[...], False)
    slopes_ref[:, local:] = dot3(prices_all, maps_cross[...], False)


def sweep_kernel(sizes, iteration, names_in, names_out, *refs):
    rows, techs, nodes = sizes.rows, sizes.techs, sizes.nodes
    slots, regions, lines, units = sizes.slots, sizes.regions, sizes.lines, sizes.units
    second = iteration == 1
    last = iteration == ITERS - 1
    given = Bag(**dict(zip(names_in, refs[: len(names_in)])))
    gives = Bag(**dict(zip(names_out, refs[len(names_in) :])))
    if last:
        staged, sems = refs[-2:]
    own = lax.axis_index("region")
    hour_index = lax.axis_index("hours")
    gathered = given.gathered

    at = places(sizes)
    fixed = given.available.at[techs + 1]
    small = given.dispatch.at[techs]
    out_sums = None if last else gives.block.at[pl.ds(rows, sums_rows(sizes))]
    sums = total_of(given)
    squares = jnp.sum(sums[techs : techs + 2], axis=1, keepdims=True)
    old_weight = jnp.ones((1, 1), jnp.float32) if second else small[at.weight : at.weight + 1, :1]
    weight = jnp.sqrt(
        old_weight * jnp.sqrt((squares[1:2] + EPSILON) / (squares[0:1] + EPSILON))
    )
    primal_step = 0.5 / weight
    if second:
        first = sums_rows(sizes)
        col_weight = sums[first : first + techs]
        negative = sums[techs + 2 : techs + 3]
    else:
        col_weight = given.cap_duals[techs, :techs, :]
        negative = small[at.negative : at.negative + 1, :]
    capacity = small[:techs, :]
    first_bar = 2.0 * capacity
    capacity_new = jnp.maximum(capacity - sums[:techs] / (weight * col_weight), 0.0)
    capacity_bar = 2.0 * capacity_new - capacity

    prices = gathered[own, :rows, :]
    gen_cost = fixed[:techs, :]
    half_weight = weight / 2.0
    primal_acc = jnp.zeros((rows, nodes), jnp.float32)
    dual_acc = jnp.zeros((rows, nodes), jnp.float32)
    supply = jnp.zeros((rows, nodes), jnp.float32)
    if last:
        copies = part_copies(staged, gives.dispatch, sems)
        count, pieces = rows // PARTS, []
        for part in range(PARTS):
            hours = slice(part * count, (part + 1) * count)
            piece = jnp.zeros((count, nodes), jnp.float32)
            for tech in range(techs):
                slope = gen_cost[tech : tech + 1] + prices[hours]
                dispatch = given.dispatch[tech, hours, :]
                duals = given.cap_duals[tech, hours, :]
                dispatch_new = jnp.maximum(dispatch - primal_step * (slope + duals), 0.0)
                piece = piece + (2.0 * dispatch_new - dispatch)
                staged[pl.ds(part * count * techs + tech, count, stride=techs), :] = dispatch_new
            copies[part].start()
            pieces.append(piece)
        supply = jnp.concatenate(pieces, axis=0)
    for tech in range(0 if last else techs):
        slope = gen_cost[tech : tech + 1] + prices
        dispatch = given.dispatch[tech]
        avail = given.available[tech]
        if second:
            duals = jnp.maximum(0.5 * (2.0 * dispatch - avail * first_bar[tech : tech + 1]), 0.0)
        else:
            duals = given.cap_duals[tech]
        dispatch_new = jnp.maximum(dispatch - primal_step * (slope + duals), 0.0)
        dispatch_bar = 2.0 * dispatch_new - dispatch
        supply = supply + dispatch_bar
        gives.dispatch[tech] = dispatch_new
        cap_rows = dispatch_bar - avail * capacity_bar[tech : tech + 1]
        primal_acc = primal_acc + (dispatch_new - dispatch) ** 2
        duals_new = jnp.maximum(duals + half_weight * cap_rows, 0.0)
        dual_acc = dual_acc + (duals_new - duals) ** 2
        gives.cap_duals[tech] = duals_new
        cost = fixed[at.cost + tech : at.cost + tech + 1, :]
        out_sums[tech : tech + 1, :] = cost - row_sum(avail * duals_new)

    maps_local = given.maps_local[...]

    energy = read_lanes(fixed, at.energy, units)
    row_id = lax.broadcasted_iota(jnp.int32, (rows, units), 0)
    next_row, prev_row = neighbour_rows(sizes, given, hour_index)
    store_duals = given.store_duals[...]
    next_duals = jnp.where(row_id == rows - 1, next_row, pltpu.roll(store_duals, rows - 1, 0))
    if second:
        charge = jnp.zeros((rows, units), jnp.float32)
        charge_before = jnp.zeros((1, units), jnp.float32)
    else:
        charge = given.charge[...]
        charge_before = read_lanes(small, at.before, units)
    charge_new = jnp.clip(charge - primal_step * (store_duals - next_duals), 0.0, energy)
    gives.charge[...] = charge_new

    primal_row = jnp.zeros((1, LANES), jnp.float32)
    bars = []
    local, total_flows = lines + units, lines + units + regions * slots
    local_limits = read_lanes(fixed, at.limits, local)
    cross_limits = given.flows[rows + 2 : rows + 3, local:]
    for bound, low, high in (
        (local_limits[:, :lines], 0, lines),
        (local_limits[:, lines:], lines, local),
        (cross_limits, local, total_flows),
    ):
        slope = given.slopes[:, low:high]
        if low == lines:
            slope = slope + store_duals
        old = given.flows[:rows, low:high]
        new = jnp.clip(old - primal_step * slope, -bound, bound)
        bars.append(2.0 * new - old)
        if not last:
            gives.flows[:rows, low:high] = new
            change = row_sum((new - old) ** 2)
            if low == local:
                slot = lax.broadcasted_iota(jnp.int32, change.shape, 1)
                change = jnp.where(slot // slots == own, change, 0.0)
            primal_row = primal_row + fold_lanes(change)
    maps_own = given.maps_cross[pl.ds(pl.multiple_of(own * nodes, nodes), nodes), :]
    balance = dot3(jnp.concatenate(bars[:2], axis=1), maps_local, True) - given.available[techs]
    balance = balance + supply + dot3(bars[2], maps_own, True)

    step_up = weight / (techs + 8.0) * balance
    if last:
        gives.prices[...] = prices + step_up
        owned = fixed[at.owned : at.owned + 1, : gives.capacity.shape[1]].astype(jnp.int32)
        tech_hot, node_hot = owned_one_hots(owned, techs, nodes)
        chosen = dot3(capacity_new, node_hot, False)
        gives.capacity[...] = row_sum(jnp.where(tech_hot, chosen, 0.0))
        gives.negative[...] = negative
        gives.kept[:rows, :] = fixed[...]
        gives.kept[rows : rows + techs, :] = col_weight
        for chunk in range(regions * slots // LANES):
            low = local + chunk * LANES
            first = rows + techs + 8 * chunk
            gives.kept[first : first + 8, :] = given.flows[rows:, low : low + LANES]
        for copy in copies:
            copy.wait()
        return
    gives.block[:rows, :] = prices + step_up
    gives.flows[rows:, local:] = given.flows[rows:, local:]
    gives.cap_duals[techs, :techs, :] = col_weight
    small_new = gives.dispatch.at[techs]
    small_new[:techs, :] = capacity_new
    small_new[at.weight : at.weight + 1, :] = jnp.broadcast_to(weight, (1, LANES))
    small_new[at.negative : at.negative + 1, :] = negative
    charge_bar = 2.0 * charge_new - charge
    before_new = jnp.clip(charge_before - primal_step * (prev_row - store_duals[0:1]), 0.0, energy)
    write_lanes(small_new, at.before, before_new)
    before_bar = 2.0 * before_new - charge_before
    shifted_bar = jnp.where(row_id == 0, before_bar, pltpu.roll(charge_bar, 1, 0))
    store_step = weight / 3.0 * (charge_bar - shifted_bar + bars[1])
    store_new = store_duals + store_step
    gives.store_duals[...] = store_new
    primal_row = primal_row + row_sum(primal_acc) + fold_lanes(row_sum((charge_new - charge) ** 2))
    primal_row = primal_row + jnp.where(
        hour_index == 0, row_sum((capacity_new - capacity) ** 2), 0.0
    )
    dual_row = row_sum(dual_acc + step_up * step_up) + fold_lanes(row_sum(store_step * store_step))
    squares = jnp.concatenate(
        [primal_row, dual_row, jnp.zeros((SQUARES - 2, LANES), jnp.float32)], axis=0
    )
    out_sums[techs : techs + SQUARES, :] = squares
    write_halo(sizes, out_sums, store_new)


def call(kernel, given, outs, flops=0, left=(), scratch=(), limit=VMEM_BYTES, copied=0):
    names_in, names_out = tuple(vars(given)), tuple(vars(outs))
    values = pl.pallas_call(
        functools.partial(kernel, names_in, names_out),
        out_shape=tuple(vars(outs).values()),
        in_specs=[
            pl.BlockSpec(memory_space=pl.ANY if i in left else pltpu.VMEM)
            for i in range(len(names_in))
        ],
        out_specs=[
            pl.BlockSpec(memory_space=pl.ANY if i < copied else pltpu.VMEM)
            for i in range(len(names_out))
        ],
        scratch_shapes=scratch,
        cost_estimate=pl.CostEstimate(flops=flops, bytes_accessed=4 * flops, transcendentals=0),
        compiler_params=pltpu.CompilerParams(vmem_limit_bytes=limit),
    )(*vars(given).values())
    return Bag(**dict(zip(names_out, values)))


def swap(value, hour_bit, region_bit):
    hours, regions = lax.axis_size("hours"), lax.axis_size("region")
    pairs = [
        (hour * regions + region, (hour ^ hour_bit) * regions + (region ^ region_bit))
        for hour in range(hours)
        for region in range(regions)
    ]
    return lax.ppermute(value, ("hours", "region"), pairs)


def shifted(value, steps):
    count = lax.axis_size("hours")
    return lax.ppermute(value, "hours", [(i, (i + steps) % count) for i in range(count)])


def both_regions(block):
    if lax.axis_size("region") != 2:
        return lax.all_gather(block, "region")
    return in_order(block, swap(block, 0, 1))


def in_order(block, other):
    return jnp.where(
        lax.axis_index("region") == 0, jnp.stack([block, other]), jnp.stack([other, block])
    )


def exchange(sizes, block):
    hours, regions = lax.axis_size("hours"), lax.axis_size("region")
    techs, span = sizes.techs, sizes.units // LANES
    halo = halo_at(sizes)
    prices, sums = block[: sizes.rows], block[sizes.rows :]
    if regions != 2 or hours != 16:
        gathered = lax.all_gather(prices, "region")
        totals = lax.psum(sums, "hours")
        totals = totals.at[techs:halo].set(lax.psum(totals[techs:halo], "region"))
        next_row = shifted(sums[halo : halo + span], -1)
        prev_row = shifted(sums[halo + span : halo + 2 * span], 1)
        return gathered, Bag(totals=totals, next_row=next_row, prev_row=prev_row)

    def merged(mine, yours, mine_first):
        last = halo + span
        edges = [
            jnp.where(mine_first, mine[halo:last], yours[halo:last]),
            jnp.where(mine_first, yours[last : last + span], mine[last : last + span]),
        ]
        total = mine + yours
        return jnp.concatenate([total[:halo], *edges, total[last + span :]], axis=0)

    hour = lax.axis_index("hours")
    beside_core = swap(block, 1, 0)
    partner_prices, partner = beside_core[: sizes.rows], beside_core[sizes.rows :]
    chip = merged(sums, partner, hour % 2 == 0)
    across = swap(chip, 2 + 1, 0)
    diagonal = swap(chip[techs:halo], 2 + 1, 1)
    beside = swap(jnp.concatenate([partner_prices, chip[techs:halo]], axis=0), 1, 1)
    other, squares = beside[: sizes.rows], beside[sizes.rows :]
    chip = chip + jnp.pad(squares + diagonal, ((techs, chip.shape[0] - halo), (0, 0)))
    slab = merged(chip, across, hour // 2 % 2 == 0)
    near, middle, far = [swap(slab, 4 * step + 1, 0) for step in (1, 2, 3)]
    parts = Bag(slab=slab, near=near, middle=middle, far=far, partner=partner, across=across)
    return in_order(prices, other), parts


def shape(*dims, dtype=jnp.float32):
    return jax.ShapeDtypeStruct(dims, dtype)


def restarted(sizes, kept, args):
    rows, techs, nodes, lines = sizes.rows, sizes.techs, sizes.nodes, sizes.lines
    local, cross = lines + sizes.units, sizes.regions * sizes.slots
    at, own = places(sizes), lax.axis_index("region")
    first_hour = lax.axis_index("hours") == 0
    price_start = args.price_start
    available = args.availability.transpose(1, 0, 2)
    fixed, last = kept[:rows], rows + techs
    col_weight = kept[rows:last]
    own_cost = fixed[at.cost : at.cost + techs]
    cost = lax.psum(own_cost, "hours")
    info = kept[last:].reshape(-1, 8, LANES).transpose(1, 0, 2).reshape(8, cross)
    local_limits = fixed[at.limits : at.energy].reshape(1, local)
    cross_limits = info[2:3]
    ends = info[:2].astype(jnp.int32)
    maps_cross_low = incidence(ends[:1], ends[1:], sizes.regions * nodes)
    stores = args.store_node[None]
    maps_local_low = incidence(
        jnp.concatenate([args.line_ends[:1], jnp.full_like(stores, -1)], axis=1),
        jnp.concatenate([args.line_ends[1:], stores], axis=1),
        nodes,
    )
    maps_local = maps_local_low.astype(jnp.float32)
    maps_cross = maps_cross_low.astype(jnp.float32)
    maps_own = lax.dynamic_slice_in_dim(maps_cross, own * nodes, nodes)
    prices_all = jnp.concatenate(list(both_regions(price_start)), axis=1)
    highest = lax.Precision.HIGHEST

    capacity = jnp.maximum(-cost / col_weight, 0.0)
    slopes = fixed[:techs][:, None, :] + price_start[None]
    dispatch = jnp.maximum(-0.5 * slopes, 0.0)
    slope = jnp.dot(price_start, maps_local, precision=highest)
    flows_local = jnp.clip(-0.5 * slope, -local_limits, local_limits)
    slope = jnp.dot(prices_all, maps_cross, precision=highest)
    flows_cross = jnp.clip(-0.5 * slope, -cross_limits, cross_limits)
    balance = (
        jnp.sum(2.0 * dispatch, axis=0)
        + jnp.dot(2.0 * flows_local, maps_local.T, precision=highest)
        + jnp.dot(2.0 * flows_cross, maps_own.T, precision=highest)
        - args.demand
    )
    step_up = balance / (techs + 8.0)
    duals = jnp.maximum(0.5 * (2.0 * dispatch - available * (2.0 * capacity)[:, None, :]), 0.0)
    store_duals = 2.0 * flows_local[:, lines:] / 3.0
    slot = lax.broadcasted_iota(jnp.int32, (1, cross), 1) // sizes.slots
    primal = (
        jnp.sum(dispatch**2)
        + jnp.sum(flows_local**2)
        + jnp.sum(jnp.where(slot == own, flows_cross**2, 0.0))
        + jnp.where(first_hour, jnp.sum(capacity**2), 0.0)
    )
    dual = jnp.sum(step_up**2) + jnp.sum(duals**2) + jnp.sum(store_duals**2)
    rows_of = [
        own_cost - jnp.sum(available * duals, axis=1),
        jnp.zeros((SQUARES, nodes)).at[0, 0].set(primal).at[1, 0].set(dual),
        store_duals[:1].reshape(-1, LANES),
        store_duals[rows - 1 :].reshape(-1, LANES),
    ]
    used = halo_at(sizes) + 2 * sizes.units // LANES
    rows_of.append(jnp.zeros((sums_rows(sizes) - used, nodes)))
    rows_of.append(jnp.where(first_hour, col_weight, 0.0))
    block = jnp.concatenate([price_start + step_up, *rows_of], axis=0)
    gathered, parts = exchange(sizes, block)
    flows = jnp.concatenate([flows_local, flows_cross], axis=1)
    slab = jnp.pad(capacity, ((0, rows - techs), (0, 0)))
    spare = jnp.concatenate([jnp.zeros((8, local)), info], axis=1)
    state = Bag(
        available=jnp.concatenate([available, args.demand[None], fixed[None]], axis=0),
        maps_local=maps_local_low,
        maps_cross=maps_cross_low,
        store_duals=store_duals,
        dispatch=jnp.concatenate([dispatch, slab[None]], axis=0),
        flows=jnp.concatenate([flows, spare], axis=0),
    )
    return state, gathered, parts


def run(args):
    rows, techs, nodes = args.availability.shape
    hours, regions = lax.axis_size("hours"), lax.axis_size("region")
    slots, owned = args.cross_limit.shape[1], args.cap_cost.shape[1]
    units, lines = args.store_node.shape[0], args.line_limit.shape[0]
    sizes = Bag(
        rows=rows, techs=techs, nodes=nodes, regions=regions, slots=slots, lines=lines, units=units
    )
    cross = regions * slots

    gathered = both_regions(
        call(
            lambda names_in, names_out, *refs: first_kernel(sizes, refs[:4], *refs[4:]),
            Bag(
                price=args.price_start,
                ends=args.cross_ends[:, 0],
                limit=args.cross_limit,
                pairs=args.pair_counts,
            ),
            Bag(block=shape(rows + 8 * max(1, slots // LANES), nodes)),
            left=(0, 1, 2, 3),
            scratch=[
                pltpu.VMEM((2, slots), jnp.int32),
                pltpu.VMEM((1, slots), jnp.float32),
                pltpu.VMEM((1, regions), jnp.int32),
                pltpu.SemaphoreType.DMA((4,)),
            ],
            limit=FIRST_BYTES,
        ).block
    )
    state = call(
        functools.partial(start_kernel, sizes),
        Bag(
            availability=args.availability.reshape(rows * techs, nodes),
            price=args.price_start,
            demand=args.demand,
            gen_cost=args.gen_cost,
            cap_cost=args.cap_cost,
            owner=args.owner_map.reshape(hours, owned),
            line_ends=args.line_ends,
            line_limit=args.line_limit[None],
            store_node=args.store_node[None],
            store_power=args.store_power[None],
            store_energy=args.store_energy[None],
        ),
        Bag(
            available=shape(techs + 2, rows, nodes),
            maps_local=shape(nodes, lines + units, dtype=jnp.bfloat16),
            flows_local=shape(rows, lines + units),
            store_duals=shape(rows, units),
            dispatch=shape(techs + 1, rows, nodes),
            balance=shape(rows, nodes),
            sums=shape(sums_rows(sizes) + techs, nodes),
        ),
        flops=10**6,
        left=(0,),
        scratch=[pltpu.VMEM((rows * techs, nodes), jnp.float32), pltpu.SemaphoreType.DMA],
    )
    closed = call(
        lambda names_in, names_out, *refs: close_kernel(sizes, *refs),
        Bag(
            gathered=gathered,
            flows_local=state.flows_local,
            balance=state.balance,
            sums=state.sums,
        ),
        Bag(
            maps=shape(regions * nodes, cross, dtype=jnp.bfloat16),
            flows=shape(rows + 8, lines + units + cross),
            block=shape(rows + state.sums.shape[0], nodes),
        ),
    )
    del state.sums, state.balance, state.flows_local
    state.maps_cross, state.flows = closed.maps, closed.flows
    gathered, parts = exchange(sizes, closed.block)
    outputs, negative, kept = sweeps(sizes, owned, state, gathered, parts)

    def again():
        return sweeps(sizes, owned, *restarted(sizes, kept, args))[0]

    return lax.cond(negative > 0.0, again, lambda: outputs)


def sweeps(sizes, owned, state, gathered, parts):
    rows, techs, nodes, lines, units = (
        sizes.rows,
        sizes.techs,
        sizes.nodes,
        sizes.lines,
        sizes.units,
    )
    state = Bag(**vars(state))
    for iteration in range(1, ITERS):
        slopes = call(
            functools.partial(slopes_kernel, sizes),
            Bag(gathered=gathered, maps_local=state.maps_local, maps_cross=state.maps_cross),
            Bag(slopes=shape(rows, lines + units + sizes.regions * sizes.slots)),
        ).slopes
        given = Bag(**vars(state), **vars(parts), gathered=gathered, slopes=slopes)
        if iteration < ITERS - 1:
            outs = Bag(
                dispatch=shape(techs + 1, rows, nodes),
                cap_duals=shape(techs + 1, rows, nodes),
                flows=shape(rows + 8, lines + units + sizes.regions * sizes.slots),
                store_duals=shape(rows, units),
                charge=shape(rows, units),
                block=shape(rows + sums_rows(sizes), nodes),
            )
        else:
            outs = Bag(
                dispatch=shape(rows * techs, nodes),
                capacity=shape(1, owned),
                prices=shape(rows, nodes),
                charge=shape(rows, units),
                negative=shape(1, LANES),
                kept=shape(rows + techs + 8 * (sizes.regions * sizes.slots // LANES), LANES),
            )
        final = iteration == ITERS - 1
        results = call(
            functools.partial(sweep_kernel, sizes, iteration),
            given,
            outs,
            copied=int(final),
            scratch=[
                pltpu.VMEM(outs.dispatch.shape, jnp.float32),
                pltpu.SemaphoreType.DMA((PARTS,)),
            ]
            if final
            else [],
        )
        if iteration < ITERS - 1:
            gathered, parts = exchange(sizes, results.block)
            del results.block
            vars(state).update(vars(results))
    dispatch = results.dispatch.reshape(rows, techs, nodes)
    outputs = (dispatch, results.capacity, results.prices, results.charge)
    return outputs, results.negative[0, 0], results.kept


def body(
    availability,
    demand,
    gen_cost,
    cap_cost,
    owner_map,
    line_ends,
    line_limit,
    cross_ends,
    cross_limit,
    pair_counts,
    store_node,
    store_energy,
    store_power,
    price_start,
):
    args = Bag(**locals())
    return run(args)


def solution(mesh):
    placed = (
        P("hours", None, "region"),
        P("hours", "region"),
        P(None, "region"),
        P("region", "hours"),
        P("region", None),
        P(None, "region"),
        P("region"),
        P(None, "region", None),
        P("region", None),
        P("region", None),
        P("region"),
        P("region"),
        P("region"),
        P("hours", "region"),
    )
    return jax.shard_map(
        body,
        mesh=mesh,
        in_specs=placed,
        out_specs=(
            P("hours", None, "region"),
            P("region", "hours"),
            P("hours", "region"),
            P("hours", "region"),
        ),
        check_vma=False,
    )
```

```python
import functools
from types import SimpleNamespace as Bag

import jax
import jax.numpy as jnp
from jax import lax
from jax.experimental import pallas as pl
from jax.experimental.pallas import tpu as pltpu
from jax.sharding import PartitionSpec as P

ITERS = 4
EPSILON = 1e-06
LANES = 128
VMEM_BYTES = 24 * 1024 * 1024
FIRST_BYTES = 56 * 1024 * 1024
PARTS = 8
SQUARES = 3


def split3(value):
    high = value.astype(jnp.bfloat16)
    rest = value - high.astype(jnp.float32)
    middle = rest.astype(jnp.bfloat16)
    low = (rest - middle.astype(jnp.float32)).astype(jnp.bfloat16)
    return jnp.concatenate([high, middle, low], axis=0)


def dot3(value, matrix, transposed):
    rows = value.shape[0]
    contract = ((1,), (1 if transposed else 0,))
    product = lax.dot_general(
        split3(value), matrix, (contract, ((), ())), preferred_element_type=jnp.float32
    )
    return product[:rows] + product[rows : 2 * rows] + product[2 * rows :]


def row_sum(value):
    return jnp.sum(value, axis=0, keepdims=True)


def fold_lanes(row):
    total = row[:, :LANES]
    for start in range(LANES, row.shape[1], LANES):
        total = total + row[:, start : start + LANES]
    return total


def owned_one_hots(owned, tech_count, node_count):
    shape_t = (tech_count, owned.shape[1])
    shape_n = (node_count, owned.shape[1])
    tech = lax.broadcasted_iota(jnp.int32, shape_t, 0) == owned // node_count
    node = lax.broadcasted_iota(jnp.int32, shape_n, 0) == owned % node_count
    return tech, node.astype(jnp.float32).astype(jnp.bfloat16)


def incidence(start, end, count):
    node = lax.broadcasted_iota(jnp.int32, (count, start.shape[1]), 0)
    maps = (node == end).astype(jnp.float32) - (node == start).astype(jnp.float32)
    return maps.astype(jnp.bfloat16)


def halo_at(sizes):
    return sizes.techs + SQUARES


def sums_rows(sizes):
    return (halo_at(sizes) + 2 * sizes.units // LANES + 7) // 8 * 8


def write_halo(sizes, sums_ref, store_new):
    halo, span, rows = halo_at(sizes), sizes.units // LANES, sizes.rows
    write_lanes(sums_ref, halo, store_new[:1])
    write_lanes(sums_ref, halo + span, store_new[rows - 1 :])
    used, end = halo + 2 * span, sums_rows(sizes)
    if used < end:
        sums_ref[used:end, :] = jnp.zeros((end - used, LANES), jnp.float32)


def write_lanes(ref, start, row):
    for i in range(row.shape[1] // LANES):
        ref[start + i : start + i + 1, :] = row[:, i * LANES : (i + 1) * LANES]


def part_copies(source, target, sems):
    rows = source.shape[0] // PARTS
    spans = [pl.ds(part * rows, rows) for part in range(PARTS)]
    return [
        pltpu.make_async_copy(source.at[span], target.at[span], sems.at[part])
        for part, span in enumerate(spans)
    ]


def read_lanes(ref, start, length):
    return jnp.concatenate(
        [ref[start + i : start + i + 1, :] for i in range(length // LANES)], axis=1
    )


def places(sizes):
    span = sizes.units // LANES
    limits = sizes.techs
    energy = limits + (sizes.lines + sizes.units) // LANES
    return Bag(
        limits=limits,
        energy=energy,
        owned=energy + span,
        cost=energy + span + 1,
        weight=sizes.techs,
        before=sizes.techs + 1,
        negative=sizes.techs + 1 + span,
    )


def first_kernel(sizes, sources, block_ref, ends_ref, limit_ref, pairs_ref, sems):
    rows = sizes.rows
    targets = (block_ref.at[pl.ds(0, rows)], ends_ref, limit_ref, pairs_ref)
    copies = [
        pltpu.make_async_copy(source, target, sems.at[i])
        for i, (source, target) in enumerate(zip(sources, targets))
    ]
    for copy in copies:
        copy.start()
    nodes, slots, regions = sizes.nodes, sizes.slots, sizes.regions
    own = lax.axis_index("region")
    width = slots // regions
    slot = lax.broadcasted_iota(jnp.int32, (1, slots), 1)
    pair = slot // width
    for copy in copies[1:]:
        copy.wait()
    in_use = jnp.zeros((1, slots), jnp.int32)
    for target in range(regions):
        in_use = jnp.where(pair == target, pairs_ref[0:1, target : target + 1], in_use)
    bound = jnp.where(slot % width < in_use, limit_ref[...], 0.0)
    start = (ends_ref[0:1, :] + own * nodes).astype(jnp.float32)
    end = (ends_ref[1:2, :] + pair * nodes).astype(jnp.float32)
    block_ref[rows:, :] = jnp.zeros((block_ref.shape[0] - rows, LANES), jnp.float32)
    width = min(slots, LANES)
    for chunk in range(slots // width):
        at = rows + 8 * chunk
        for i, row in enumerate((start, end, bound)):
            block_ref[at + i : at + i + 1, :width] = row[:, chunk * width : (chunk + 1) * width]
    copies[0].wait()


def start_kernel(sizes, names_in, names_out, *refs):
    given = Bag(**dict(zip(names_in, refs[: len(names_in)])))
    gives = Bag(**dict(zip(names_out, refs[len(names_in) : -2])))
    availability, sem = refs[-2:]
    copy = pltpu.make_async_copy(given.availability, availability, sem)
    copy.start()
    rows, techs, nodes, lines = sizes.rows, sizes.techs, sizes.nodes, sizes.lines
    at = places(sizes)
    fixed = gives.available.at[techs + 1]
    gives.available[techs] = given.demand[...]
    fixed[:techs, :] = given.gen_cost[...]
    write_lanes(fixed, at.energy, given.store_energy[...])
    owned = given.owner[pl.ds(lax.axis_index("hours"), 1), :]
    fixed[at.owned : at.owned + 1, : owned.shape[1]] = owned.astype(jnp.float32)
    line_ends, stores = given.line_ends[...], given.store_node[...]
    start = jnp.concatenate([line_ends[0:1], jnp.full_like(stores, -1)], axis=1)
    end = jnp.concatenate([line_ends[1:2], stores], axis=1)
    maps = incidence(start, end, nodes)
    limits = jnp.concatenate([given.line_limit[...], given.store_power[...]], axis=1)
    gives.maps_local[...] = maps
    write_lanes(fixed, at.limits, limits)
    prices = given.price[...]
    flows = jnp.clip(-0.5 * dot3(prices, maps, False), -limits, limits)
    gives.flows_local[...] = flows
    store_new = (1.0 / 3.0) * (2.0 * flows[:, lines:])
    gives.store_duals[...] = store_new
    primal_row = fold_lanes(row_sum(flows * flows))
    dual_row = fold_lanes(row_sum(store_new * store_new))
    balance = dot3(2.0 * flows, maps, True) - given.demand[...]
    gen_cost = given.gen_cost[...]
    copy.wait()
    cost = given.cap_cost[...]
    tech_hot, node_hot = owned_one_hots(owned, techs, nodes)
    own_cost = dot3(jnp.where(tech_hot, cost, 0.0), node_hot, True)
    fixed[at.cost : at.cost + techs, :] = own_cost
    gives.dispatch[techs] = jnp.zeros((rows, nodes), jnp.float32)
    acc = jnp.zeros((rows, nodes), jnp.float32)
    weights = jnp.zeros((techs, nodes), jnp.float32)
    for hour in range(rows):
        weights = weights + availability[hour * techs : (hour + 1) * techs, :]
    for tech in range(techs):
        avail = availability[pl.ds(tech, rows, stride=techs), :]
        gives.available[tech] = avail
        dispatch = jnp.maximum(-0.5 * (gen_cost[tech : tech + 1] + prices), 0.0)
        gives.dispatch[tech] = dispatch
        dispatch_bar = 2.0 * dispatch
        balance = balance + dispatch_bar
        duals = jnp.maximum(0.5 * dispatch_bar, 0.0)
        acc = acc + dispatch * dispatch
        gives.sums[tech : tech + 1, :] = own_cost[tech : tech + 1] - row_sum(avail * duals)
    gives.balance[...] = balance
    squares = row_sum(acc)
    negative = jnp.sum((cost < 0.0).astype(jnp.float32), axis=1, keepdims=True)
    write_halo(sizes, gives.sums, store_new)
    gives.sums[techs : techs + SQUARES, :] = jnp.concatenate(
        [primal_row + squares, dual_row + squares, jnp.broadcast_to(negative, (1, LANES))], axis=0
    )
    first = sums_rows(sizes)
    gives.sums[first : first + techs, :] = weights


def close_kernel(
    sizes,
    gathered,
    local_ref,
    balance_ref,
    sums_in_ref,
    maps_ref,
    flows_ref,
    block_ref,
):
    rows, techs, nodes = sizes.rows, sizes.techs, sizes.nodes
    slots, regions = sizes.slots, sizes.regions
    own = lax.axis_index("region")
    width = min(slots, LANES)
    info = jnp.concatenate(
        [
            gathered[region, rows + 8 * chunk : rows + 8 * chunk + 8, :width]
            for region in range(regions)
            for chunk in range(slots // width)
        ],
        axis=1,
    )
    maps_ref[...] = incidence(
        info[0:1].astype(jnp.int32), info[1:2].astype(jnp.int32), regions * nodes
    )
    limits = info[2:3]
    prices_all = jnp.concatenate([gathered[region, :rows, :] for region in range(regions)], axis=1)
    flows = jnp.clip(-0.5 * dot3(prices_all, maps_ref[...], False), -limits, limits)
    local = local_ref.shape[1]
    flows_ref[:rows, :local] = local_ref[...]
    flows_ref[:rows, local:] = flows
    flows_ref[rows:, local:] = info
    maps_own = maps_ref[pl.ds(pl.multiple_of(own * nodes, nodes), nodes), :]
    balance = balance_ref[...] + dot3(2.0 * flows, maps_own, True)
    step_up = (1.0 / (techs + 8.0)) * balance
    block_ref[:rows, :] = gathered[own, :rows, :] + step_up
    change = row_sum(flows * flows)
    slot = lax.broadcasted_iota(jnp.int32, change.shape, 1)
    primal = fold_lanes(jnp.where(slot // slots == own, change, 0.0))
    more = jnp.concatenate(
        [primal, row_sum(step_up * step_up), jnp.zeros((SQUARES - 2, LANES), jnp.float32)], axis=0
    )
    block_ref[rows:, :] = sums_in_ref[...]
    block_ref[rows + techs : rows + techs + SQUARES, :] = (
        sums_in_ref[techs : techs + SQUARES, :] + more
    )


def neighbour_rows(sizes, given, hour_index):
    units = sizes.units
    if hasattr(given, "totals"):
        return read_lanes(given.next_row, 0, units), read_lanes(given.prev_row, 0, units)
    first = halo_at(sizes)
    last = first + units // LANES
    core, x_place, odd = hour_index % 2, hour_index // 2 % 2, hour_index // 4 % 2
    next_row = jnp.where(
        odd == 0, read_lanes(given.near, first, units), read_lanes(given.far, first, units)
    )
    prev_row = jnp.where(
        odd == 0, read_lanes(given.far, last, units), read_lanes(given.near, last, units)
    )
    next_row = jnp.where(x_place == 0, read_lanes(given.across, first, units), next_row)
    prev_row = jnp.where(x_place == 0, prev_row, read_lanes(given.across, last, units))
    next_row = jnp.where(core == 0, read_lanes(given.partner, first, units), next_row)
    prev_row = jnp.where(core == 0, prev_row, read_lanes(given.partner, last, units))
    return next_row, prev_row


def total_of(parts):
    if hasattr(parts, "totals"):
        return parts.totals[...]
    return (parts.slab[...] + parts.near[...]) + (parts.middle[...] + parts.far[...])


def slopes_kernel(sizes, names_in, names_out, gathered, maps_local, maps_cross, slopes_ref):
    rows, regions = sizes.rows, sizes.regions
    local = sizes.lines + sizes.units
    prices_all = jnp.concatenate([gathered[region, :rows, :] for region in range(regions)], axis=1)
    prices = gathered[lax.axis_index("region"), :rows, :]
    slopes_ref[:, :local] = dot3(prices, maps_local[...], False)
    slopes_ref[:, local:] = dot3(prices_all, maps_cross[...], False)


def sweep_kernel(sizes, iteration, names_in, names_out, *refs):
    rows, techs, nodes = sizes.rows, sizes.techs, sizes.nodes
    slots, regions, lines, units = sizes.slots, sizes.regions, sizes.lines, sizes.units
    second = iteration == 1
    last = iteration == ITERS - 1
    given = Bag(**dict(zip(names_in, refs[: len(names_in)])))
    gives = Bag(**dict(zip(names_out, refs[len(names_in) :])))
    if last:
        staged, sems = refs[-2:]
    own = lax.axis_index("region")
    hour_index = lax.axis_index("hours")
    gathered = given.gathered

    at = places(sizes)
    fixed = given.available.at[techs + 1]
    small = given.dispatch.at[techs]
    out_sums = None if last else gives.block.at[pl.ds(rows, sums_rows(sizes))]
    sums = total_of(given)
    squares = jnp.sum(sums[techs : techs + 2], axis=1, keepdims=True)
    old_weight = jnp.ones((1, 1), jnp.float32) if second else small[at.weight : at.weight + 1, :1]
    weight = jnp.sqrt(
        old_weight * jnp.sqrt((squares[1:2] + EPSILON) / (squares[0:1] + EPSILON))
    )
    primal_step = 0.5 / weight
    if second:
        first = sums_rows(sizes)
        col_weight = sums[first : first + techs]
        negative = sums[techs + 2 : techs + 3]
    else:
        col_weight = given.cap_duals[techs, :techs, :]
        negative = small[at.negative : at.negative + 1, :]
    capacity = small[:techs, :]
    first_bar = 2.0 * capacity
    capacity_new = jnp.maximum(capacity - sums[:techs] / (weight * col_weight), 0.0)
    capacity_bar = 2.0 * capacity_new - capacity

    prices = gathered[own, :rows, :]
    gen_cost = fixed[:techs, :]
    half_weight = weight / 2.0
    primal_acc = jnp.zeros((rows, nodes), jnp.float32)
    dual_acc = jnp.zeros((rows, nodes), jnp.float32)
    supply = jnp.zeros((rows, nodes), jnp.float32)
    if last:
        copies = part_copies(staged, gives.dispatch, sems)
        count, pieces = rows // PARTS, []
        for part in range(PARTS):
            hours = slice(part * count, (part + 1) * count)
            piece = jnp.zeros((count, nodes), jnp.float32)
            for tech in range(techs):
                slope = gen_cost[tech : tech + 1] + prices[hours]
                dispatch = given.dispatch[tech, hours, :]
                duals = given.cap_duals[tech, hours, :]
                dispatch_new = jnp.maximum(dispatch - primal_step * (slope + duals), 0.0)
                piece = piece + (2.0 * dispatch_new - dispatch)
                staged[pl.ds(part * count * techs + tech, count, stride=techs), :] = dispatch_new
            copies[part].start()
            pieces.append(piece)
        supply = jnp.concatenate(pieces, axis=0)
    for tech in range(0 if last else techs):
        slope = gen_cost[tech : tech + 1] + prices
        dispatch = given.dispatch[tech]
        avail = given.available[tech]
        if second:
            duals = jnp.maximum(0.5 * (2.0 * dispatch - avail * first_bar[tech : tech + 1]), 0.0)
        else:
            duals = given.cap_duals[tech]
        dispatch_new = jnp.maximum(dispatch - primal_step * (slope + duals), 0.0)
        dispatch_bar = 2.0 * dispatch_new - dispatch
        supply = supply + dispatch_bar
        gives.dispatch[tech] = dispatch_new
        cap_rows = dispatch_bar - avail * capacity_bar[tech : tech + 1]
        primal_acc = primal_acc + (dispatch_new - dispatch) ** 2
        duals_new = jnp.maximum(duals + half_weight * cap_rows, 0.0)
        dual_acc = dual_acc + (duals_new - duals) ** 2
        gives.cap_duals[tech] = duals_new
        cost = fixed[at.cost + tech : at.cost + tech + 1, :]
        out_sums[tech : tech + 1, :] = cost - row_sum(avail * duals_new)

    maps_local = given.maps_local[...]

    energy = read_lanes(fixed, at.energy, units)
    row_id = lax.broadcasted_iota(jnp.int32, (rows, units), 0)
    next_row, prev_row = neighbour_rows(sizes, given, hour_index)
    store_duals = given.store_duals[...]
    next_duals = jnp.where(row_id == rows - 1, next_row, pltpu.roll(store_duals, rows - 1, 0))
    if second:
        charge = jnp.zeros((rows, units), jnp.float32)
        charge_before = jnp.zeros((1, units), jnp.float32)
    else:
        charge = given.charge[...]
        charge_before = read_lanes(small, at.before, units)
    charge_new = jnp.clip(charge - primal_step * (store_duals - next_duals), 0.0, energy)
    gives.charge[...] = charge_new

    primal_row = jnp.zeros((1, LANES), jnp.float32)
    bars = []
    local, total_flows = lines + units, lines + units + regions * slots
    local_limits = read_lanes(fixed, at.limits, local)
    cross_limits = given.flows[rows + 2 : rows + 3, local:]
    for bound, low, high in (
        (local_limits[:, :lines], 0, lines),
        (local_limits[:, lines:], lines, local),
        (cross_limits, local, total_flows),
    ):
        slope = given.slopes[:, low:high]
        if low == lines:
            slope = slope + store_duals
        old = given.flows[:rows, low:high]
        new = jnp.clip(old - primal_step * slope, -bound, bound)
        bars.append(2.0 * new - old)
        if not last:
            gives.flows[:rows, low:high] = new
            change = row_sum((new - old) ** 2)
            if low == local:
                slot = lax.broadcasted_iota(jnp.int32, change.shape, 1)
                change = jnp.where(slot // slots == own, change, 0.0)
            primal_row = primal_row + fold_lanes(change)
    maps_own = given.maps_cross[pl.ds(pl.multiple_of(own * nodes, nodes), nodes), :]
    balance = dot3(jnp.concatenate(bars[:2], axis=1), maps_local, True) - given.available[techs]
    balance = balance + supply + dot3(bars[2], maps_own, True)

    step_up = weight / (techs + 8.0) * balance
    if last:
        gives.prices[...] = prices + step_up
        owned = fixed[at.owned : at.owned + 1, : gives.capacity.shape[1]].astype(jnp.int32)
        tech_hot, node_hot = owned_one_hots(owned, techs, nodes)
        chosen = dot3(capacity_new, node_hot, False)
        gives.capacity[...] = row_sum(jnp.where(tech_hot, chosen, 0.0))
        gives.negative[...] = negative
        gives.kept[:rows, :] = fixed[...]
        gives.kept[rows : rows + techs, :] = col_weight
        for chunk in range(regions * slots // LANES):
            low = local + chunk * LANES
            first = rows + techs + 8 * chunk
            gives.kept[first : first + 8, :] = given.flows[rows:, low : low + LANES]
        for copy in copies:
            copy.wait()
        return
    gives.block[:rows, :] = prices + step_up
    gives.flows[rows:, local:] = given.flows[rows:, local:]
    gives.cap_duals[techs, :techs, :] = col_weight
    small_new = gives.dispatch.at[techs]
    small_new[:techs, :] = capacity_new
    small_new[at.weight : at.weight + 1, :] = jnp.broadcast_to(weight, (1, LANES))
    small_new[at.negative : at.negative + 1, :] = negative
    charge_bar = 2.0 * charge_new - charge
    before_new = jnp.clip(charge_before - primal_step * (prev_row - store_duals[0:1]), 0.0, energy)
    write_lanes(small_new, at.before, before_new)
    before_bar = 2.0 * before_new - charge_before
    shifted_bar = jnp.where(row_id == 0, before_bar, pltpu.roll(charge_bar, 1, 0))
    store_step = weight / 3.0 * (charge_bar - shifted_bar + bars[1])
    store_new = store_duals + store_step
    gives.store_duals[...] = store_new
    primal_row = primal_row + row_sum(primal_acc) + fold_lanes(row_sum((charge_new - charge) ** 2))
    primal_row = primal_row + jnp.where(
        hour_index == 0, row_sum((capacity_new - capacity) ** 2), 0.0
    )
    dual_row = row_sum(dual_acc + step_up * step_up) + fold_lanes(row_sum(store_step * store_step))
    squares = jnp.concatenate(
        [primal_row, dual_row, jnp.zeros((SQUARES - 2, LANES), jnp.float32)], axis=0
    )
    out_sums[techs : techs + SQUARES, :] = squares
    write_halo(sizes, out_sums, store_new)


def call(kernel, given, outs, flops=0, left=(), scratch=(), limit=VMEM_BYTES, copied=0):
    names_in, names_out = tuple(vars(given)), tuple(vars(outs))
    values = pl.pallas_call(
        functools.partial(kernel, names_in, names_out),
        out_shape=tuple(vars(outs).values()),
        in_specs=[
            pl.BlockSpec(memory_space=pl.ANY if i in left else pltpu.VMEM)
            for i in range(len(names_in))
        ],
        out_specs=[
            pl.BlockSpec(memory_space=pl.ANY if i < copied else pltpu.VMEM)
            for i in range(len(names_out))
        ],
        scratch_shapes=scratch,
        cost_estimate=pl.CostEstimate(flops=flops, bytes_accessed=4 * flops, transcendentals=0),
        compiler_params=pltpu.CompilerParams(vmem_limit_bytes=limit),
    )(*vars(given).values())
    return Bag(**dict(zip(names_out, values)))


def swap(value, hour_bit, region_bit):
    hours, regions = lax.axis_size("hours"), lax.axis_size("region")
    pairs = [
        (hour * regions + region, (hour ^ hour_bit) * regions + (region ^ region_bit))
        for hour in range(hours)
        for region in range(regions)
    ]
    return lax.ppermute(value, ("hours", "region"), pairs)


def shifted(value, steps):
    count = lax.axis_size("hours")
    return lax.ppermute(value, "hours", [(i, (i + steps) % count) for i in range(count)])


def both_regions(block):
    if lax.axis_size("region") != 2:
        return lax.all_gather(block, "region")
    return in_order(block, swap(block, 0, 1))


def in_order(block, other):
    return jnp.where(
        lax.axis_index("region") == 0, jnp.stack([block, other]), jnp.stack([other, block])
    )


def exchange(sizes, block):
    hours, regions = lax.axis_size("hours"), lax.axis_size("region")
    techs, span = sizes.techs, sizes.units // LANES
    halo = halo_at(sizes)
    prices, sums = block[: sizes.rows], block[sizes.rows :]
    if regions != 2 or hours != 16:
        gathered = lax.all_gather(prices, "region")
        totals = lax.psum(sums, "hours")
        totals = totals.at[techs:halo].set(lax.psum(totals[techs:halo], "region"))
        next_row = shifted(sums[halo : halo + span], -1)
        prev_row = shifted(sums[halo + span : halo + 2 * span], 1)
        return gathered, Bag(totals=totals, next_row=next_row, prev_row=prev_row)

    def merged(mine, yours, mine_first):
        last = halo + span
        edges = [
            jnp.where(mine_first, mine[halo:last], yours[halo:last]),
            jnp.where(mine_first, yours[last : last + span], mine[last : last + span]),
        ]
        total = mine + yours
        return jnp.concatenate([total[:halo], *edges, total[last + span :]], axis=0)

    hour = lax.axis_index("hours")
    beside_core = swap(block, 1, 0)
    partner_prices, partner = beside_core[: sizes.rows], beside_core[sizes.rows :]
    chip = merged(sums, partner, hour % 2 == 0)
    across = swap(chip, 2 + 1, 0)
    diagonal = swap(chip[techs:halo], 2 + 1, 1)
    beside = swap(jnp.concatenate([partner_prices, chip[techs:halo]], axis=0), 1, 1)
    other, squares = beside[: sizes.rows], beside[sizes.rows :]
    chip = chip + jnp.pad(squares + diagonal, ((techs, chip.shape[0] - halo), (0, 0)))
    slab = merged(chip, across, hour // 2 % 2 == 0)
    near, middle, far = [swap(slab, 4 * step + 1, 0) for step in (1, 2, 3)]
    parts = Bag(slab=slab, near=near, middle=middle, far=far, partner=partner, across=across)
    return in_order(prices, other), parts


def shape(*dims, dtype=jnp.float32):
    return jax.ShapeDtypeStruct(dims, dtype)


def restarted(sizes, kept, args):
    rows, techs, nodes, lines = sizes.rows, sizes.techs, sizes.nodes, sizes.lines
    local, cross = lines + sizes.units, sizes.regions * sizes.slots
    at, own = places(sizes), lax.axis_index("region")
    first_hour = lax.axis_index("hours") == 0
    price_start = args.price_start
    available = args.availability.transpose(1, 0, 2)
    fixed, last = kept[:rows], rows + techs
    col_weight = kept[rows:last]
    own_cost = fixed[at.cost : at.cost + techs]
    cost = lax.psum(own_cost, "hours")
    info = kept[last:].reshape(-1, 8, LANES).transpose(1, 0, 2).reshape(8, cross)
    local_limits = fixed[at.limits : at.energy].reshape(1, local)
    cross_limits = info[2:3]
    ends = info[:2].astype(jnp.int32)
    maps_cross_low = incidence(ends[:1], ends[1:], sizes.regions * nodes)
    stores = args.store_node[None]
    maps_local_low = incidence(
        jnp.concatenate([args.line_ends[:1], jnp.full_like(stores, -1)], axis=1),
        jnp.concatenate([args.line_ends[1:], stores], axis=1),
        nodes,
    )
    maps_local = maps_local_low.astype(jnp.float32)
    maps_cross = maps_cross_low.astype(jnp.float32)
    maps_own = lax.dynamic_slice_in_dim(maps_cross, own * nodes, nodes)
    prices_all = jnp.concatenate(list(both_regions(price_start)), axis=1)
    highest = lax.Precision.HIGHEST

    capacity = jnp.maximum(-cost / col_weight, 0.0)
    slopes = fixed[:techs][:, None, :] + price_start[None]
    dispatch = jnp.maximum(-0.5 * slopes, 0.0)
    slope = jnp.dot(price_start, maps_local, precision=highest)
    flows_local = jnp.clip(-0.5 * slope, -local_limits, local_limits)
    slope = jnp.dot(prices_all, maps_cross, precision=highest)
    flows_cross = jnp.clip(-0.5 * slope, -cross_limits, cross_limits)
    balance = (
        jnp.sum(2.0 * dispatch, axis=0)
        + jnp.dot(2.0 * flows_local, maps_local.T, precision=highest)
        + jnp.dot(2.0 * flows_cross, maps_own.T, precision=highest)
        - args.demand
    )
    step_up = balance / (techs + 8.0)
    duals = jnp.maximum(0.5 * (2.0 * dispatch - available * (2.0 * capacity)[:, None, :]), 0.0)
    store_duals = 2.0 * flows_local[:, lines:] / 3.0
    slot = lax.broadcasted_iota(jnp.int32, (1, cross), 1) // sizes.slots
    primal = (
        jnp.sum(dispatch**2)
        + jnp.sum(flows_local**2)
        + jnp.sum(jnp.where(slot == own, flows_cross**2, 0.0))
        + jnp.where(first_hour, jnp.sum(capacity**2), 0.0)
    )
    dual = jnp.sum(step_up**2) + jnp.sum(duals**2) + jnp.sum(store_duals**2)
    rows_of = [
        own_cost - jnp.sum(available * duals, axis=1),
        jnp.zeros((SQUARES, nodes)).at[0, 0].set(primal).at[1, 0].set(dual),
        store_duals[:1].reshape(-1, LANES),
        store_duals[rows - 1 :].reshape(-1, LANES),
    ]
    used = halo_at(sizes) + 2 * sizes.units // LANES
    rows_of.append(jnp.zeros((sums_rows(sizes) - used, nodes)))
    rows_of.append(jnp.where(first_hour, col_weight, 0.0))
    block = jnp.concatenate([price_start + step_up, *rows_of], axis=0)
    gathered, parts = exchange(sizes, block)
    flows = jnp.concatenate([flows_local, flows_cross], axis=1)
    slab = jnp.pad(capacity, ((0, rows - techs), (0, 0)))
    spare = jnp.concatenate([jnp.zeros((8, local)), info], axis=1)
    state = Bag(
        available=jnp.concatenate([available, args.demand[None], fixed[None]], axis=0),
        maps_local=maps_local_low,
        maps_cross=maps_cross_low,
        store_duals=store_duals,
        dispatch=jnp.concatenate([dispatch, slab[None]], axis=0),
        flows=jnp.concatenate([flows, spare], axis=0),
    )
    return state, gathered, parts


def run(args):
    rows, techs, nodes = args.availability.shape
    hours, regions = lax.axis_size("hours"), lax.axis_size("region")
    slots, owned = args.cross_limit.shape[1], args.cap_cost.shape[1]
    units, lines = args.store_node.shape[0], args.line_limit.shape[0]
    sizes = Bag(
        rows=rows, techs=techs, nodes=nodes, regions=regions, slots=slots, lines=lines, units=units
    )
    cross = regions * slots

    gathered = both_regions(
        call(
            lambda names_in, names_out, *refs: first_kernel(sizes, refs[:4], *refs[4:]),
            Bag(
                price=args.price_start,
                ends=args.cross_ends[:, 0],
                limit=args.cross_limit,
                pairs=args.pair_counts,
            ),
            Bag(block=shape(rows + 8 * max(1, slots // LANES), nodes)),
            left=(0, 1, 2, 3),
            scratch=[
                pltpu.VMEM((2, slots), jnp.int32),
                pltpu.VMEM((1, slots), jnp.float32),
                pltpu.VMEM((1, regions), jnp.int32),
                pltpu.SemaphoreType.DMA((4,)),
            ],
            limit=FIRST_BYTES,
        ).block
    )
    state = call(
        functools.partial(start_kernel, sizes),
        Bag(
            availability=args.availability.reshape(rows * techs, nodes),
            price=args.price_start,
            demand=args.demand,
            gen_cost=args.gen_cost,
            cap_cost=args.cap_cost,
            owner=args.owner_map.reshape(hours, owned),
            line_ends=args.line_ends,
            line_limit=args.line_limit[None],
            store_node=args.store_node[None],
            store_power=args.store_power[None],
            store_energy=args.store_energy[None],
        ),
        Bag(
            available=shape(techs + 2, rows, nodes),
            maps_local=shape(nodes, lines + units, dtype=jnp.bfloat16),
            flows_local=shape(rows, lines + units),
            store_duals=shape(rows, units),
            dispatch=shape(techs + 1, rows, nodes),
            balance=shape(rows, nodes),
            sums=shape(sums_rows(sizes) + techs, nodes),
        ),
        flops=10**6,
        left=(0,),
        scratch=[pltpu.VMEM((rows * techs, nodes), jnp.float32), pltpu.SemaphoreType.DMA],
    )
    closed = call(
        lambda names_in, names_out, *refs: close_kernel(sizes, *refs),
        Bag(
            gathered=gathered,
            flows_local=state.flows_local,
            balance=state.balance,
            sums=state.sums,
        ),
        Bag(
            maps=shape(regions * nodes, cross, dtype=jnp.bfloat16),
            flows=shape(rows + 8, lines + units + cross),
            block=shape(rows + state.sums.shape[0], nodes),
        ),
    )
    del state.sums, state.balance, state.flows_local
    state.maps_cross, state.flows = closed.maps, closed.flows
    gathered, parts = exchange(sizes, closed.block)
    outputs, negative, kept = sweeps(sizes, owned, state, gathered, parts)

    def again():
        return sweeps(sizes, owned, *restarted(sizes, kept, args))[0]

    return lax.cond(negative > 0.0, again, lambda: outputs)


def sweeps(sizes, owned, state, gathered, parts):
    rows, techs, nodes, lines, units = (
        sizes.rows,
        sizes.techs,
        sizes.nodes,
        sizes.lines,
        sizes.units,
    )
    state = Bag(**vars(state))
    for iteration in range(1, ITERS):
        slopes = call(
            functools.partial(slopes_kernel, sizes),
            Bag(gathered=gathered, maps_local=state.maps_local, maps_cross=state.maps_cross),
            Bag(slopes=shape(rows, lines + units + sizes.regions * sizes.slots)),
        ).slopes
        given = Bag(**vars(state), **vars(parts), gathered=gathered, slopes=slopes)
        if iteration < ITERS - 1:
            outs = Bag(
                dispatch=shape(techs + 1, rows, nodes),
                cap_duals=shape(techs + 1, rows, nodes),
                flows=shape(rows + 8, lines + units + sizes.regions * sizes.slots),
                store_duals=shape(rows, units),
                charge=shape(rows, units),
                block=shape(rows + sums_rows(sizes), nodes),
            )
        else:
            outs = Bag(
                dispatch=shape(rows * techs, nodes),
                capacity=shape(1, owned),
                prices=shape(rows, nodes),
                charge=shape(rows, units),
                negative=shape(1, LANES),
                kept=shape(rows + techs + 8 * (sizes.regions * sizes.slots // LANES), LANES),
            )
        final = iteration == ITERS - 1
        results = call(
            functools.partial(sweep_kernel, sizes, iteration),
            given,
            outs,
            copied=int(final),
            scratch=[
                pltpu.VMEM(outs.dispatch.shape, jnp.float32),
                pltpu.SemaphoreType.DMA((PARTS,)),
            ]
            if final
            else [],
        )
        if iteration < ITERS - 1:
            gathered, parts = exchange(sizes, results.block)
            del results.block
            vars(state).update(vars(results))
    dispatch = results.dispatch.reshape(rows, techs, nodes)
    outputs = (dispatch, results.capacity, results.prices, results.charge)
    return outputs, results.negative[0, 0], results.kept


def body(
    availability,
    demand,
    gen_cost,
    cap_cost,
    owner_map,
    line_ends,
    line_limit,
    cross_ends,
    cross_limit,
    pair_counts,
    store_node,
    store_energy,
    store_power,
    price_start,
):
    args = Bag(**locals())
    return run(args)


def solution(mesh):
    placed = (
        P("hours", None, "region"),
        P("hours", "region"),
        P(None, "region"),
        P("region", "hours"),
        P("region", None),
        P(None, "region"),
        P("region"),
        P(None, "region", None),
        P("region", None),
        P("region", None),
        P("region"),
        P("region"),
        P("region"),
        P("hours", "region"),
    )
    return jax.shard_map(
        body,
        mesh=mesh,
        in_specs=placed,
        out_specs=(
            P("hours", None, "region"),
            P("region", "hours"),
            P("hours", "region"),
            P("hours", "region"),
        ),
        check_vma=False,
    )
```
